32 devices in a mesh: maps: 4 (over y, x), band: 8 (over z, core).
Axes of the slice: x: 2, y: 2, z: 4, core: 2. Of those that a mesh axis runs over, the one named last changes fastest.
Arguments:
- tokens_in: bfloat16 [512, 48, 256], P(('maps', 'band')), may hold values from -6 to 6
- cotangent: bfloat16 [512, 48, 256], P(('maps', 'band')), may hold values from -6 to 6
- map_sizes: int32 [4, 2], P('maps'), may hold values from 34 to 128, as said below
- w_qkv: float32 [256, 768], P(('maps', 'band')), may hold values from -0.375 to 0.375
- w_out: float32 [256, 256], P(('maps', 'band')), may hold values from -1 to 1
- w_up: float32 [256, 768], P(('maps', 'band')), may hold values from -0.375 to 0.375
- w_down: float32 [768, 256], P(('maps', 'band')), may hold values from -0.21875 to 0.21875
- vectors: float32 [11, 256], P(None, ('maps', 'band'))
- pos_table: float32 [8, 49], replicated, may hold values from -4 to 4
- first_qkv: float32 [256, 768], P(('maps', 'band')), may hold values from -112 to 112
- second_qkv: float32 [256, 768], P(('maps', 'band')), may hold values from 12.288 to 196.608
- first_out: float32 [256, 256], P(('maps', 'band')), may hold values from -112 to 112
- second_out: float32 [256, 256], P(('maps', 'band')), may hold values from 12.288 to 196.608
- first_up: float32 [256, 768], P(('maps', 'band')), may hold values from -112 to 112
- second_up: float32 [256, 768], P(('maps', 'band')), may hold values from 12.288 to 196.608
- first_down: float32 [768, 256], P(('maps', 'band')), may hold values from -112 to 112
- second_down: float32 [768, 256], P(('maps', 'band')), may hold values from 12.288 to 196.608
- first_vectors: float32 [11, 256], P(None, ('maps', 'band')), may hold values from -112 to 112
- second_vectors: float32 [11, 256], P(None, ('maps', 'band')), may hold values from 12.288 to 196.608
- first_table: float32 [8, 49], replicated, may hold values from -112 to 112
- second_table: float32 [8, 49], replicated, may hold values from 12.288 to 196.608
Outputs:
- layer_out: bfloat16 [512, 48, 256], P(('maps', 'band'))
- tokens_grad: bfloat16 [512, 48, 256], P(('maps', 'band'))
- next_first_qkv: float32 [256, 768], P(('maps', 'band'))
- next_second_qkv: float32 [256, 768], P(('maps', 'band'))
- next_qkv: float32 [256, 768], P(('maps', 'band'))
- next_first_out: float32 [256, 256], P(('maps', 'band'))
- next_second_out: float32 [256, 256], P(('maps', 'band'))
- next_out: float32 [256, 256], P(('maps', 'band'))
- next_first_up: float32 [256, 768], P(('maps', 'band'))
- next_second_up: float32 [256, 768], P(('maps', 'band'))
- next_up: float32 [256, 768], P(('maps', 'band'))
- next_first_down: float32 [768, 256], P(('maps', 'band'))
- next_second_down: float32 [768, 256], P(('maps', 'band'))
- next_down: float32 [768, 256], P(('maps', 'band'))
- next_first_vectors: float32 [11, 256], P(None, ('maps', 'band'))
- next_second_vectors: float32 [11, 256], P(None, ('maps', 'band'))
- next_vectors: float32 [11, 256], P(None, ('maps', 'band'))
- next_first_table: float32 [8, 49], replicated
- next_second_table: float32 [8, 49], replicated
- next_table: float32 [8, 49], replicated
- weight_norms: float32 [16], replicated
- update_norms: float32 [16], replicated
The draws below stay inside these ranges and needn't reach their ends.
Inputs may be any that keep to these rules, and one draw needn't show every extreme that they name: `map_sizes`: column 0 is a map's valid height, between 113 and 128; column 1 its valid width, at least seven tenths of 48; at least one map is valid everywhere.
All inputs are finite; a program needn't handle non-finite values.
Results may differ from the reference program's by a relative error of at most 0.012.
The reference program's roundings to bfloat16 on the way count: a program that leaves them out, or rounds other values in their place, can miss the bound.
Values may be sent and summed in bfloat16 or wider, within the bound.
No kernel may reach another device: no remote copies, remote signals or barrier semaphores. Data moves between devices by JAX's collectives and lax.ppermute only.
A program may use at most 256 MiB of HBM per device.

```python
import math
from functools import partial
import jax
import jax.numpy as jnp
from jax import lax

D = 256
HEADS = 8
FF = 768
WINDOW = 7
DILATION = 4
STEP = 10
ROWS = 16
COLS = 48
MAPS = 4
HGT = 128
NEIGH = 49
VROWS = 11


def draw_map_sizes(key, part):
    key = jax.random.fold_in(key, 11)
    key_h, key_w, key_f = jax.random.split(key, 3)
    heights = jax.random.randint(key_h, (MAPS,), HGT - ROWS + 1, HGT + 1)
    widths = jax.random.randint(key_w, (MAPS,), (7 * COLS + 9) // 10, COLS + 1)
    chosen = jax.random.randint(key_f, (), 0, MAPS)
    full = jnp.arange(MAPS) == chosen
    heights = jnp.where(full, HGT, heights)
    widths = jnp.where(full, COLS, widths)
    return jnp.stack([heights, widths], axis=1).astype(jnp.int32)


def draw_vectors(key, part):
    key = jax.random.fold_in(key, 23)
    key_g, key_b = jax.random.split(key)
    rise = 0.6 + 1.2 * jnp.arange(D, dtype=jnp.float32) / D
    gains = rise[None, :] * jax.random.uniform(key_g, (2, D), jnp.float32, 0.8, 1.2)
    biases = 0.3 * jax.random.normal(key_b, (VROWS, D), jnp.float32)
    rows = jnp.arange(VROWS)[:, None]
    table = jnp.where(rows == 0, gains[0][None, :], biases)
    table = jnp.where(rows == 5, gains[1][None, :], table)
    return table.astype(jnp.float32)


def block_scale(rng, dims, cuts, smallest, high):
    def one(position, blocks):
        draws = jax.random.uniform(jax.random.fold_in(jax.random.fold_in(rng, 6), position), (blocks,), jnp.float32, smallest / len(cuts), high / len(cuts))
        return jnp.repeat(jnp.exp(draws), dims[position] // blocks).reshape((-1,) + (1,) * (len(dims) - position - 1))

    loudness = one(*cuts[0])
    for cut in cuts[1:]:
        loudness = loudness * one(*cut)
    return loudness


def normal_values(stream_key, extent, scale, most, cuts=(), kind=jnp.bfloat16):
    entries = scale * jax.random.normal(stream_key, extent, jnp.float32)
    if cuts:
        entries = entries * block_scale(stream_key, extent, cuts, -0.22, 0.18)
    return jnp.clip(entries, -most, most).astype(kind)


def setup_inputs(seed: int = 0) -> dict:
    keys = jax.random.split(jax.random.key(seed), 22)
    tokens_in = normal_values(keys[0], (MAPS * HGT, COLS, D), 1.0, 6.0, ((0, 32),))
    cotangent = normal_values(keys[1], (MAPS * HGT, COLS, D), 1.0, 6.0, ((0, 32),))
    map_sizes = draw_map_sizes(jax.random.fold_in(keys[21], 71), 0)
    w_qkv = normal_values(keys[3], (D, 3 * D), D ** -0.5, 0.375, ((0, 32),), jnp.float32)
    w_out = normal_values(keys[4], (D, D), (D // 7) ** -0.5, 1.0, ((0, 32),), jnp.float32)
    w_up = normal_values(keys[5], (D, FF), D ** -0.5, 0.375, ((0, 32),), jnp.float32)
    w_down = normal_values(keys[6], (FF, D), FF ** -0.5, 0.21875, ((0, 32),), jnp.float32)
    vectors = draw_vectors(jax.random.fold_in(keys[21], 71), 0)
    pos_table = normal_values(keys[8], (HEADS, NEIGH), 1.0, 4.0, (), jnp.float32)
    first_qkv = normal_values(keys[9], (D, 3 * D), (0.11 * (MAPS * HGT * COLS) ** 0.5), 112.0, ((0, 32),), jnp.float32)
    second_qkv = jnp.clip(jnp.exp(math.log(196.608) - 2.7725887 * jax.random.uniform(keys[10], (D, 3 * D), jnp.float32) ** block_scale(keys[10], (D, 3 * D), ((0, 32),), -0.2, 0.2)), 12.288, 196.608)
    first_out = normal_values(keys[11], (D, D), (0.11 * (MAPS * HGT * COLS) ** 0.5), 112.0, ((0, 32),), jnp.float32)
    second_out = jnp.clip(jnp.exp(math.log(196.608) - 2.7725887 * jax.random.uniform(keys[12], (D, D), jnp.float32) ** block_scale(keys[12], (D, D), ((0, 32),), -0.2, 0.2)), 12.288, 196.608)
    first_up = normal_values(keys[13], (D, FF), (0.11 * (MAPS * HGT * COLS) ** 0.5), 112.0, ((0, 32),), jnp.float32)
    second_up = jnp.clip(jnp.exp(math.log(196.608) - 2.7725887 * jax.random.uniform(keys[14], (D, FF), jnp.float32) ** block_scale(keys[14], (D, FF), ((0, 32),), -0.2, 0.2)), 12.288, 196.608)
    first_down = normal_values(keys[15], (FF, D), (0.11 * (MAPS * HGT * COLS) ** 0.5), 112.0, ((0, 32),), jnp.float32)
    second_down = jnp.clip(jnp.exp(math.log(196.608) - 2.7725887 * jax.random.uniform(keys[16], (FF, D), jnp.float32) ** block_scale(keys[16], (FF, D), ((0, 32),), -0.2, 0.2)), 12.288, 196.608)
    first_vectors = normal_values(keys[17], (VROWS, D), (0.11 * (MAPS * HGT * COLS) ** 0.5), 112.0, ((1, 32),), jnp.float32)
    second_vectors = jnp.clip(jnp.exp(math.log(196.608) - 2.7725887 * jax.random.uniform(keys[18], (VROWS, D), jnp.float32) ** block_scale(keys[18], (VROWS, D), ((1, 32),), -0.2, 0.2)), 12.288, 196.608)
    first_table = normal_values(keys[19], (HEADS, NEIGH), (0.11 * (MAPS * HGT * COLS) ** 0.5), 112.0, (), jnp.float32)
    second_table = jnp.clip(jnp.exp(jax.random.uniform(keys[20], (HEADS, NEIGH), jnp.float32, math.log(12.288), math.log(196.608))), 12.288, 196.608)
    return dict(tokens_in=tokens_in, cotangent=cotangent, map_sizes=map_sizes, w_qkv=w_qkv, w_out=w_out, w_up=w_up, w_down=w_down, vectors=vectors, pos_table=pos_table, first_qkv=first_qkv, second_qkv=second_qkv, first_out=first_out, second_out=second_out, first_up=first_up, second_up=second_up, first_down=first_down, second_down=second_down, first_vectors=first_vectors, second_vectors=second_vectors, first_table=first_table, second_table=second_table)


NORM_EPS = 1e-05
BETA_FIRST = 0.9
BETA_SECOND = 0.999
ADAM_EPS = 1e-06
DECAY_RATE = 0.01
LEARN_RATE = 0.2
RATIO_EPS = 1e-06
MASKED = -1e+30

@jax.custom_vjp
def low(v):
    return lax.optimization_barrier(v.astype(jnp.bfloat16)).astype(jnp.float32)

@jax.custom_vjp
def low_back(v):
    return v

def low_keep(v):
    return (low(v), None)

def low_pass(kept, grad):
    return (grad,)

def back_keep(v):
    return (v, None)

def back_low(kept, grad):
    return (low(grad),)
low.defvjp(low_keep, low_pass)
low_back.defvjp(back_keep, back_low)

def hp_dot(left, right):
    return jnp.dot(left, right, precision=lax.Precision.HIGHEST, preferred_element_type=jnp.float32)

def layer_norm(values, gain, shift):
    mean = lax.optimization_barrier(jnp.mean(values, axis=-1, keepdims=True))
    centred = values - mean
    spread = lax.optimization_barrier(jnp.mean(centred * centred, axis=-1, keepdims=True))
    return centred * lax.rsqrt(spread + NORM_EPS) * gain + shift

def map_forward(weights, tokens, size_pair):
    w_qkv, w_out, w_up, w_down, vec, table = weights
    hgt, wid, width = tokens.shape
    count = hgt * wid
    head_dim = width // HEADS
    scale = head_dim ** (-0.5)
    half = WINDOW // 2
    reach = half * DILATION
    flat = tokens.reshape(count, width)
    row_ids = jnp.arange(hgt, dtype=jnp.int32)
    col_ids = jnp.arange(wid, dtype=jnp.int32)
    a_one = low(layer_norm(flat, vec[0], vec[1]))
    bias = jnp.concatenate([vec[2], jnp.zeros_like(vec[2]), vec[3]])
    qkv = low(low_back(hp_dot(a_one, w_qkv) + bias))
    query = qkv[:, :width].reshape(count, HEADS, head_dim)
    keyval = jnp.pad(qkv[:, width:].reshape(hgt, wid, 2 * width), ((reach, reach), (reach, reach), (0, 0)))
    pieces = []
    allows = []
    for row_step in range(-half, half + 1):
        for col_step in range(-half, half + 1):
            top = reach + DILATION * row_step
            left = reach + DILATION * col_step
            pieces.append(keyval[top:top + hgt, left:left + wid].reshape(count, 2, HEADS, head_dim))
            if row_step == 0 and col_step == 0:
                allows.append(jnp.ones((count,), dtype=bool))
            else:
                key_rows = row_ids + DILATION * row_step
                key_cols = col_ids + DILATION * col_step
                okay_rows = (key_rows >= 0) & (key_rows < size_pair[0])
                okay_cols = (key_cols >= 0) & (key_cols < size_pair[1])
                allows.append((okay_rows[:, None] & okay_cols[None, :]).reshape(count))
    raw = jnp.stack([jnp.einsum('thd,thd->ht', query, piece[:, 0], precision=lax.Precision.HIGHEST) for piece in pieces])
    scores = low_back(scale * raw) + table.T[:, :, None]
    scores = jnp.where(jnp.stack(allows)[:, None, :], scores, MASKED)
    probs = low(jax.nn.softmax(scores, axis=0))
    mixed = jnp.zeros((count, HEADS, head_dim), jnp.float32)
    for index, piece in enumerate(pieces):
        mixed = mixed + jnp.einsum('ht,thd->thd', probs[index], piece[:, 1], precision=lax.Precision.HIGHEST)
    mixed = low(low_back(mixed.reshape(count, width)))
    x_one = flat + low_back(hp_dot(mixed, w_out) + vec[4])
    a_two = low(layer_norm(x_one, vec[5], vec[6]))
    hidden = low_back(hp_dot(a_two, w_up) + vec[8:].reshape(-1))
    act = low(jax.nn.gelu(hidden, approximate=True))
    result = x_one + hp_dot(act, w_down) + vec[7]
    return result.reshape(hgt, wid, width)

def forward(map_sizes, x_all, w_qkv, w_out, w_up, w_down, vectors, pos_table):
    weights = (low(w_qkv), low(w_out), low(w_up), low(w_down), low(vectors), pos_table)
    maps_in = x_all.reshape(MAPS, HGT, COLS, D)
    checked = jax.checkpoint(map_forward)

    def advance(carry, item):
        return (carry, checked(weights, item[0], item[1]))
    _, outs = lax.scan(advance, jnp.zeros((), jnp.float32), (maps_in, map_sizes))
    return outs.reshape(MAPS * HGT, COLS, D)

def adam_parts(weight, grad, first, second):
    new_first = BETA_FIRST * first + (1.0 - BETA_FIRST) * grad
    new_second = BETA_SECOND * second + (1.0 - BETA_SECOND) * grad * grad
    update = new_first / (1.0 - BETA_FIRST ** STEP) / (jnp.sqrt(new_second / (1.0 - BETA_SECOND ** STEP)) + ADAM_EPS) + DECAY_RATE * weight
    return (new_first, new_second, update)

def reference(tokens_in, cotangent, map_sizes, w_qkv, w_out, w_up, w_down, vectors, pos_table, first_qkv, second_qkv, first_out, second_out, first_up, second_up, first_down, second_down, first_vectors, second_vectors, first_table, second_table):
    x_all = tokens_in.astype(jnp.float32)
    result, pullback = jax.vjp(partial(forward, map_sizes), x_all, w_qkv, w_out, w_up, w_down, vectors, pos_table)
    grads = pullback(cotangent.astype(jnp.float32))
    tokens_grad = grads[0].astype(jnp.bfloat16)
    masters = (w_qkv, w_out, w_up, w_down, vectors, pos_table)
    firsts = (first_qkv, first_out, first_up, first_down, first_vectors, first_table)
    seconds = (second_qkv, second_out, second_up, second_down, second_vectors, second_table)
    parts = [adam_parts(masters[i], grads[i + 1], firsts[i], seconds[i]) for i in range(6)]
    updates = [part[2] for part in parts]
    weight_sq = jnp.concatenate([jnp.stack([jnp.sum(item * item) for item in masters[:4]]), lax.optimization_barrier(jnp.sum(vectors * vectors, axis=1)), jnp.sum(pos_table * pos_table)[None]])
    update_sq = jnp.concatenate([jnp.stack([jnp.sum(item * item) for item in updates[:4]]), lax.optimization_barrier(jnp.sum(updates[4] * updates[4], axis=1)), jnp.sum(updates[5] * updates[5])[None]])
    weight_norms = jnp.sqrt(weight_sq)
    update_norms = jnp.sqrt(update_sq)
    ratios = weight_norms / (update_norms + RATIO_EPS)
    news = [masters[i] - LEARN_RATE * ratios[i] * updates[i] for i in range(4)]
    news.append(vectors - LEARN_RATE * ratios[4:4 + VROWS][:, None] * updates[4])
    news.append(pos_table - LEARN_RATE * ratios[4 + VROWS] * updates[5])
    return (result.astype(jnp.bfloat16), tokens_grad, parts[0][0], parts[0][1], news[0], parts[1][0], parts[1][1], news[1], parts[2][0], parts[2][1], news[2], parts[3][0], parts[3][1], news[3], parts[4][0], parts[4][1], news[4], parts[5][0], parts[5][1], news[5], weight_norms, update_norms)
```

```python
import functools

import jax
import jax.numpy as jnp
import numpy as np
from jax import lax
from jax.experimental import pallas as pl
from jax.experimental.pallas import tpu as pltpu
from jax.sharding import PartitionSpec as P

HEADS = 8
WINDOW = 7
DIL = 4
STEP = 10
NORM_EPS = 1e-05
BETA_FIRST = 0.9
BETA_SECOND = 0.999
ADAM_EPS = 1e-06
DECAY_RATE = 0.01
LEARN_RATE = 0.2
RATIO_EPS = 1e-06
MASKED = -1e30
LOG2E = 1.4426950408889634
AXES = ("maps", "band")

BF = jnp.bfloat16
F32 = jnp.float32

CLS = DIL * DIL
QN = 48
KN = 128
RIM = 40


def dot(a, b):
    return lax.dot_general(a, b, (((1,), (0,)), ((), ())), preferred_element_type=F32)


def dot_nt(a, b):
    return lax.dot_general(a, b, (((1,), (1,)), ((), ())), preferred_element_type=F32)


def dot_tn(a, b):
    return lax.dot_general(a, b, (((0,), (0,)), ((), ())), preferred_element_type=F32)


def order_own():
    sel = np.zeros((4 * QN, 4 * 48), np.float32)
    for o in range(4 * QN):
        cc, rest = divmod(o, QN)
        qr, qc = divmod(rest, 12)
        sel[o, qr * 48 + qc * 4 + cc] = 1
    return sel


def order_keys():
    sel = np.zeros((4 * KN, 480), np.float32)
    for o in range(4 * KN):
        cc, slot = divmod(o, KN)
        j = (slot + 36) % KN
        if j < 120:
            kr, kc = divmod(j, 12)
            sel[o, kr * 48 + kc * 4 + cc] = 1
    return sel


def normed(v):
    mean = jnp.mean(v, axis=-1, keepdims=True)
    cen = v - mean
    var = jnp.mean(cen * cen, axis=-1, keepdims=True)
    rstd = lax.rsqrt(var + NORM_EPS)
    return cen * rstd, rstd


def norm_back(g, xhat, rstd):
    m1 = jnp.mean(g, axis=-1, keepdims=True)
    m2 = jnp.mean(g * xhat, axis=-1, keepdims=True)
    return rstd * (g - m1 - xhat * m2)


def spread_heads(v, lane_head):
    zero = jnp.zeros_like(v)
    return jnp.concatenate([jnp.where(lane_head == h, v, zero) for h in range(HEADS)], axis=0)


def pick_heads(full, lane_head):
    out = jnp.where(lane_head == 0, full[0:QN], 0.0)
    for h in range(1, HEADS):
        out = out + jnp.where(lane_head == h, full[h * QN : (h + 1) * QN], 0.0)
    return out


def split12(v):
    q = (v * 43) >> 9
    return q, v - 12 * q


def table_slots():
    n = lax.broadcasted_iota(jnp.int32, (WINDOW * WINDOW, KN), 0)
    lane = lax.broadcasted_iota(jnp.int32, (WINDOW * WINDOW, KN), 1)
    nr = (n * 37) >> 8
    nc = n - 7 * nr
    return (((12 * (nr - 3) + nc - 3) & (KN - 1)) == lane).astype(F32)


def layer_kernel(
    where_ref,
    x_ref,
    xb_ref,
    xa_ref,
    cot_ref,
    wqkv_ref,
    wo_ref,
    wu_ref,
    wd_ref,
    vec_ref,
    table_ref,
    po_ref,
    pk_ref,
    out_ref,
    act_ref,
    dy_ref,
    dz_ref,
    a2_ref,
    mixed_ref,
    da_ref,
    a1_ref,
    dq_ref,
    dx1_ref,
    own_ref,
    rima_ref,
    rimb_ref,
    tgrad_ref,
    sums_ref,
    zsum_ref,
    xp_ref,
    q_ref,
    k_ref,
    v_ref,
    bias_ref,
    p_ref,
    x1_ref,
    dmix_ref,
    tacc_ref,
):
    row0 = where_ref[0] * 16
    height = where_ref[1]
    wide = where_ref[2]
    scale = 32 ** (-0.5)
    lane_head = lax.broadcasted_iota(jnp.int32, (QN, 256), 1) >> 5

    def vrow(i):
        return vec_ref[i : i + 1, :]

    slots = lax.dot_general(
        table_ref[...],
        table_slots(),
        (((1,), (0,)), ((), ())),
        precision=lax.Precision.HIGHEST,
        preferred_element_type=F32,
    )
    qi = lax.broadcasted_iota(jnp.int32, (QN, KN), 0)
    si = lax.broadcasted_iota(jnp.int32, (QN, KN), 1)
    ji = (si + 36) & (KN - 1)
    kr, kc = split12(ji)
    qr, qc = split12(qi)
    window = (jnp.abs(kc - qc) <= 3) & (jnp.abs(kr - qr - 3) <= 3) & (ji < 120)
    rows = []
    for h in range(HEADS):
        line = jnp.broadcast_to(slots[h : h + 1, :] * LOG2E, (QN, KN))
        line = pltpu.roll(line, 0, 1, stride=1, stride_axis=0)
        rows.append(jnp.where(window, line, MASKED))
    bias_ref[...] = jnp.concatenate(rows, axis=0).T

    def project(rc, _):
        own = jnp.concatenate([x_ref[4 * i + rc] for i in range(4)], axis=0)
        xp = dot(po_ref[...], own)
        at = pl.ds(pl.multiple_of(rc * 192, 192), 192)
        xp_ref[at, :] = xp
        a1 = (normed(xp)[0] * vrow(0) + vrow(1)).astype(BF)
        a1_ref[at, :] = a1
        q_ref[at, :] = (dot(a1, wqkv_ref[:, 0:256]) + vrow(2)).astype(BF)
        around = jnp.concatenate(
            [xb_ref[4 * i + rc] for i in range(3)]
            + [own]
            + [xa_ref[4 * i + rc] for i in range(3)],
            axis=0,
        )
        xk = dot(pk_ref[...], around)
        a1k = (normed(xk)[0] * vrow(0) + vrow(1)).astype(BF)
        at = pl.ds(pl.multiple_of(rc * 512, 512), 512)
        k_ref[at, :] = dot(a1k, wqkv_ref[:, 256:512]).astype(BF)
        v_ref[at, :] = (dot(a1k, wqkv_ref[:, 512:768]) + vrow(3)).astype(BF)
        return 0

    lax.fori_loop(0, 4, project, 0)

    ks = lax.broadcasted_iota(jnp.int32, (KN, 384), 0)
    ql = lax.broadcasted_iota(jnp.int32, (KN, 384), 1)
    kj = (ks + 36) & (KN - 1)
    krow, kcol = split12(kj)
    qin = ql - 48 * ((ql * 171) >> 13)
    same = ks == qin

    def attend(k, _):
        rc = k >> 2
        cc = k & 3
        at_q = pl.ds(pl.multiple_of(k * QN, QN), QN)
        at_k = pl.ds(pl.multiple_of(k * KN, KN), KN)
        qbd = spread_heads(q_ref[at_q, :], lane_head)
        s = dot_nt(k_ref[at_k, :], qbd) * (scale * LOG2E) + bias_ref[...]
        r = krow * 4 + (row0 + rc - 12)
        c = kcol * 4 + cc
        okay = ((r >= 0) & (r < height) & (c < wide)) | same
        s = jnp.where(okay, s, MASKED)
        top = jnp.max(s, axis=0, keepdims=True)
        e = jnp.exp2(s - top)
        p = e * (1.0 / jnp.sum(e, axis=0, keepdims=True))
        p_ref[at_k, :] = p
        full = dot_tn(p.astype(BF), v_ref[at_k, :])
        mixed_ref[at_q, :] = pick_heads(full, lane_head).astype(BF)
        return 0

    lax.fori_loop(0, CLS, attend, 0)

    sums_ref[...] = jnp.zeros_like(sums_ref)
    zsum_ref[...] = jnp.zeros_like(zsum_ref)

    def feed(rc, _):
        at = pl.ds(pl.multiple_of(rc * 192, 192), 192)
        x1 = xp_ref[at, :] + (dot(mixed_ref[at, :], wo_ref[...]) + vrow(4))
        xhat, rstd = normed(x1)
        a2 = (xhat * vrow(5) + vrow(6)).astype(BF)
        a2_ref[at, :] = a2
        bias = jnp.concatenate([vrow(8), vrow(9), vrow(10)], axis=1)
        z = dot(a2, wu_ref[...]) + bias
        c0 = 0.7978845608028654
        c1 = 0.044715
        z2 = z * z
        t = jnp.tanh(c0 * (z + c1 * z2 * z))
        act = (0.5 * z * (1.0 + t)).astype(BF)
        act_ref[at, :] = act
        res = x1 + dot(act, wd_ref[...]) + vrow(7)
        back = dot_tn(po_ref[...], res.astype(BF)).astype(BF)
        for i in range(4):
            out_ref[4 * i + rc] = back[48 * i : 48 * i + 48]
        dyf = dot(po_ref[...], jnp.concatenate([cot_ref[4 * i + rc] for i in range(4)], axis=0))
        dy = dyf.astype(BF)
        dy_ref[at, :] = dy
        slope = 0.5 * (1.0 + t) + 0.5 * z * (1.0 - t * t) * (c0 * (1.0 + 3.0 * c1 * z2))
        dz = (dot_nt(dy, wd_ref[...]) * slope).astype(BF)
        dz_ref[at, :] = dz
        zsum_ref[...] += jnp.sum(dz.astype(F32), axis=0, keepdims=True)
        dn = dot_nt(dz, wu_ref[...])
        dx1 = dyf + norm_back(dn * vrow(5), xhat, rstd)
        dx1_ref[at, :] = dx1
        da = dx1.astype(BF)
        da_ref[at, :] = da
        dmix_ref[at, :] = dot_nt(da, wo_ref[...]).astype(BF)
        sums_ref[4:5, :] += jnp.sum(da.astype(F32), axis=0, keepdims=True)
        sums_ref[5:6, :] += jnp.sum(dn * xhat, axis=0, keepdims=True)
        sums_ref[6:7, :] += jnp.sum(dn, axis=0, keepdims=True)
        sums_ref[7:8, :] += jnp.sum(dyf, axis=0, keepdims=True)
        return 0

    lax.fori_loop(0, 4, feed, 0)

    tacc_ref[...] = jnp.zeros_like(tacc_ref)

    def back_class(k):
        at_q = pl.ds(pl.multiple_of(k * QN, QN), QN)
        at_k = pl.ds(pl.multiple_of(k * KN, KN), KN)
        qbd = spread_heads(q_ref[at_q, :], lane_head)
        dobd = spread_heads(dmix_ref[at_q, :], lane_head)
        p = p_ref[at_k, :]
        dp = dot_nt(v_ref[at_k, :], dobd)
        dv = dot(p.astype(BF), dobd)
        pdp = p * dp
        ds = pdp - p * jnp.sum(pdp, axis=0, keepdims=True)
        tacc_ref[...] += ds
        dsl = ds.astype(BF)
        dk = dot(dsl, qbd) * scale
        dq = pick_heads(dot_tn(dsl, k_ref[at_k, :]), lane_head) * scale
        dq_ref[at_q, :] = dq.astype(BF)
        own_ref[at_q, 0:256] = dk[0:QN]
        own_ref[at_q, 256:512] = dv[0:QN]
        after = jnp.concatenate([dk[QN : QN + RIM], dv[QN : QN + RIM]], axis=1)
        before = jnp.concatenate([dk[KN - RIM :], dv[KN - RIM :]], axis=1)
        return after, before

    def attend_back(pair, _):
        after0, before0 = back_class(pair * 2)
        after1, before1 = back_class(pair * 2 + 1)
        at = pl.ds(pl.multiple_of(pair * 2 * RIM, 2 * RIM), 2 * RIM)
        rima_ref[at, :] = jnp.concatenate([after0, after1], axis=0).astype(BF)
        rimb_ref[at, :] = jnp.concatenate([before0, before1], axis=0).astype(BF)
        return 0

    lax.fori_loop(0, CLS // 2, attend_back, 0)
    sums_ref[2:3, :] = jnp.sum(dq_ref[...].astype(F32), axis=0, keepdims=True)

    flat = tacc_ref[...].T
    lines = []
    for h in range(HEADS):
        part = flat[h * QN : (h + 1) * QN]
        for bit in range(6):
            turned = pltpu.roll(part, KN - (1 << bit), 1)
            part = jnp.where((qi >> bit) & 1 == 1, turned, part)
        lines.append(jnp.sum(part, axis=0, keepdims=True))
    tgrad_ref[...] = jnp.concatenate(lines, axis=0)


def finish_kernel(
    own_ref,
    fa_ref,
    fb_ref,
    dq_ref,
    dx1_ref,
    x_ref,
    wqkv_ref,
    vec_ref,
    po_ref,
    tok_ref,
    dqkv_ref,
    sums_ref,
):
    sums_ref[...] = jnp.zeros_like(sums_ref)

    def block(rc, _):
        own = jnp.concatenate([x_ref[4 * i + rc] for i in range(4)], axis=0)
        xp = dot(po_ref[...], own)
        xhat, rstd = normed(xp)
        at = pl.ds(pl.multiple_of(rc * 192, 192), 192)
        mine = own_ref[at, :]
        got_a = fa_ref[pl.ds(pl.multiple_of(rc * 160, 160), 160), :].astype(F32)
        got_b = fb_ref[pl.ds(pl.multiple_of(rc * 160, 160), 160), :].astype(F32)
        gap = jnp.zeros((QN - RIM, 512), F32)
        parts = []
        for i in range(4):
            a = jnp.concatenate([got_a[i * RIM : (i + 1) * RIM], gap], axis=0)
            b = jnp.concatenate([gap, got_b[i * RIM : (i + 1) * RIM]], axis=0)
            parts.append(mine[i * QN : (i + 1) * QN] + a + b)
        dkv = jnp.concatenate(parts, axis=0).astype(BF)
        dqkv = jnp.concatenate([dq_ref[at, :], dkv], axis=1)
        dqkv_ref[at, :] = dqkv
        dn = dot_nt(dqkv, wqkv_ref[...])
        gain = vec_ref[0:1, :]
        dx = dx1_ref[at, :] + norm_back(dn * gain, xhat, rstd)
        back = dot_tn(po_ref[...], dx.astype(BF)).astype(BF)
        for i in range(4):
            tok_ref[4 * i + rc] = back[48 * i : 48 * i + 48]
        sums_ref[0:1, :] += jnp.sum(dn * xhat, axis=0, keepdims=True)
        sums_ref[1:2, :] += jnp.sum(dn, axis=0, keepdims=True)
        sums_ref[3:4, :] += jnp.sum(dkv[:, 256:512].astype(F32), axis=0, keepdims=True)
        return 0

    lax.fori_loop(0, 4, block, 0)


def call(kernel, out_shape, scratch, *args, smem=0, flops=10**8):
    vm = pl.BlockSpec(memory_space=pltpu.VMEM)
    specs = [pl.BlockSpec(memory_space=pltpu.SMEM)] * smem + [vm] * (len(args) - smem)
    return pl.pallas_call(
        kernel,
        out_shape=out_shape,
        in_specs=specs,
        out_specs=jax.tree.map(lambda _: vm, out_shape),
        scratch_shapes=scratch,
        compiler_params=pltpu.CompilerParams(vmem_limit_bytes=48 * 2**20),
        cost_estimate=pl.CostEstimate(flops=flops, bytes_accessed=10**6, transcendentals=0),
    )(*args)


def sds(shape, dtype=BF):
    return jax.ShapeDtypeStruct(shape, dtype)


def exchange_groups(maps, band):
    zbits = band.bit_length() - 2
    mbits = maps.bit_length() - 1
    cut = lambda lo, n: [(lo + i, min(2, n - i)) for i in range(0, n, 2)]
    return cut(1, zbits) + cut(1 + zbits, mbits) + [(0, 1)]


def swap(block, mask, count):
    return lax.ppermute(block, AXES, [(k, k ^ mask) for k in range(count)])


def frame_masks(groups):
    masks = [0]
    for lo, bits in groups:
        masks = [m ^ (d << lo) for d in range(1 << bits) for m in masks]
    return masks


def gather_all(slab, groups, count):
    block = slab[None]
    for lo, bits in groups:
        block = jnp.concatenate(
            [block] + [swap(block, d << lo, count) for d in range(1, 1 << bits)], axis=0
        )
    return block


def scatter_sum(grads, groups, count):
    for lo, bits in reversed(groups):
        low = grads.astype(BF).reshape((1 << bits, -1) + grads.shape[1:])
        total = grads.reshape(low.shape)[0].astype(F32)
        for d in range(1, 1 << bits):
            total = total + swap(low[d], d << lo, count).astype(F32)
        grads = total
    return grads[0]


def adam_parts(weight, grad, first, second):
    new_first = BETA_FIRST * first + (1.0 - BETA_FIRST) * grad
    new_second = BETA_SECOND * second + (1.0 - BETA_SECOND) * grad * grad
    update = (
        new_first
        / (1.0 - BETA_FIRST**STEP)
        / (jnp.sqrt(new_second / (1.0 - BETA_SECOND**STEP)) + ADAM_EPS)
        + DECAY_RATE * weight
    )
    return (new_first, new_second, update)


def squares_of(matrices, rowwise):
    return jnp.concatenate(
        [
            jnp.stack([jnp.sum(matrix * matrix) for matrix in matrices]),
            jnp.sum(rowwise * rowwise, axis=1),
        ]
    )


def per_device(
    maps,
    band,
    tokens_in,
    cotangent,
    map_sizes,
    w_qkv,
    w_out,
    w_up,
    w_down,
    vectors,
    pos_table,
    first_qkv,
    second_qkv,
    first_out,
    second_out,
    first_up,
    second_up,
    first_down,
    second_down,
    first_vectors,
    second_vectors,
    first_table,
    second_table,
):
    count = maps * band
    rows = w_qkv.shape[0]
    vrows = vectors.shape[0]
    groups = exchange_groups(maps, band)
    masks = np.array(frame_masks(groups))
    inverse = np.argsort(masks)
    me = lax.axis_index(AXES)
    band_index = lax.axis_index("band")
    reach = 3 * DIL

    up = [(i, i + 1) for i in range(band - 1)]
    down = [(i + 1, i) for i in range(band - 1)]
    x_before = lax.ppermute(tokens_in[-reach:], "band", up)
    x_after = lax.ppermute(tokens_in[:reach], "band", down)

    def pack(qkv, out, upw, dnw, vec):
        dn = dnw.reshape(3, rows, 256).transpose(1, 0, 2).reshape(rows, 768)
        vt = jnp.pad(vec.T, ((0, 0), (0, 128 - vrows)))
        return jnp.concatenate([qkv, out, upw, dn, vt], axis=1)

    slab = pack(*(w.astype(BF) for w in (w_qkv, w_out, w_up, w_down, vectors)))
    block = gather_all(slab, groups, count)
    order = jnp.asarray(inverse, jnp.int32)[jnp.arange(count, dtype=jnp.int32) ^ me]
    whole = jnp.take(block, order, axis=0).reshape(256, -1)
    big_qkv = whole[:, 0:768]
    big_out = whole[:, 768:1024]
    big_up = whole[:, 1024:1792]
    big_down = (
        whole[:, 1792:2560].reshape(count, rows, 3, 256).transpose(0, 2, 1, 3).reshape(768, 256)
    )
    vec = whole[:, 2560 : 2560 + vrows].T.astype(F32)

    po = jnp.asarray(order_own(), BF)
    pk = jnp.asarray(order_keys(), BF)
    place = jnp.stack([band_index, map_sizes[0, 0], map_sizes[0, 1]]).astype(jnp.int32)
    (
        layer_out,
        act,
        dy,
        dz,
        a2,
        mixed,
        da,
        a1,
        dq,
        dx1,
        own,
        rim_a,
        rim_b,
        table_grad,
        sums,
        zsum,
    ) = call(
        layer_kernel,
        (
            sds((16, 48, 256)),
            sds((768, 768)),
            sds((768, 256)),
            sds((768, 768)),
            sds((768, 256)),
            sds((768, 256)),
            sds((768, 256)),
            sds((768, 256)),
            sds((768, 256)),
            sds((768, 256), F32),
            sds((768, 512), F32),
            sds((CLS * RIM, 512)),
            sds((CLS * RIM, 512)),
            sds((HEADS, KN), F32),
            sds((8, 256), F32),
            sds((1, 768), F32),
        ),
        [
            pltpu.VMEM((768, 256), F32),
            pltpu.VMEM((768, 256), BF),
            pltpu.VMEM((CLS * KN, 256), BF),
            pltpu.VMEM((CLS * KN, 256), BF),
            pltpu.VMEM((KN, 384), F32),
            pltpu.VMEM((CLS * KN, 384), F32),
            pltpu.VMEM((768, 256), F32),
            pltpu.VMEM((768, 256), BF),
            pltpu.VMEM((KN, 384), F32),
        ],
        place,
        tokens_in,
        x_before,
        x_after,
        cotangent,
        big_qkv,
        big_out,
        big_up,
        big_down,
        vec,
        pos_table,
        po,
        pk,
        smem=1,
        flops=6 * 10**9,
    )
    from_prev = lax.ppermute(rim_a, "band", up)
    from_next = lax.ppermute(rim_b, "band", down)
    grad_down = dot_tn(act, dy)
    grad_up = dot_tn(a2, dz)
    grad_out = dot_tn(mixed, da)
    tokens_grad, dqkv, sums2 = call(
        finish_kernel,
        (sds((16, 48, 256)), sds((768, 768)), sds((8, 256), F32)),
        [],
        own,
        from_prev,
        from_next,
        dq,
        dx1,
        tokens_in,
        big_qkv,
        vec,
        po,
    )
    grad_qkv = dot_tn(a1, dqkv)
    grad_vec = jnp.concatenate([sums + sums2, zsum.reshape(3, 256)], axis=0)

    packed = jnp.concatenate(
        [
            grad_qkv.reshape(count, rows, 768),
            grad_out.reshape(count, rows, 256),
            grad_up.reshape(count, rows, 768),
            grad_down.reshape(count, 3, rows, 256).transpose(0, 2, 1, 3).reshape(count, rows, 768),
            jnp.pad(grad_vec.T, ((0, 0), (0, 128 - vrows))).reshape(count, rows, 128),
        ],
        axis=2,
    )
    packed = jnp.take(packed, jnp.asarray(masks, jnp.int32) ^ me, axis=0)
    red = scatter_sum(packed, groups, count)
    red_qkv = red[:, 0:768]
    red_out = red[:, 768:1024]
    red_up = red[:, 1024:1792]
    red_down = red[:, 1792:2560].reshape(rows, 3, 256).transpose(1, 0, 2).reshape(3 * rows, 256)
    red_vec = red[:, 2560 : 2560 + vrows].T

    steps = np.arange(-3, 4)
    lanes = ((12 * steps[:, None] + steps[None, :]) % KN).reshape(-1)
    table_total = lax.psum(table_grad, AXES)[:, lanes]

    part_qkv = adam_parts(w_qkv, red_qkv, first_qkv, second_qkv)
    part_out = adam_parts(w_out, red_out, first_out, second_out)
    part_up = adam_parts(w_up, red_up, first_up, second_up)
    part_down = adam_parts(w_down, red_down, first_down, second_down)
    part_vec = adam_parts(vectors, red_vec, first_vectors, second_vectors)
    part_table = adam_parts(pos_table, table_total, first_table, second_table)
    local_weight_sq = squares_of((w_qkv, w_out, w_up, w_down), vectors)
    local_update_sq = squares_of((part_qkv[2], part_out[2], part_up[2], part_down[2]), part_vec[2])
    weight_sq, update_sq = lax.psum((local_weight_sq, local_update_sq), AXES)
    table_weight = jnp.sqrt(jnp.sum(pos_table * pos_table))
    table_update = jnp.sqrt(jnp.sum(part_table[2] * part_table[2]))
    weight_norms = jnp.concatenate([jnp.sqrt(weight_sq), table_weight[None]])
    update_norms = jnp.concatenate([jnp.sqrt(update_sq), table_update[None]])
    ratios = weight_norms / (update_norms + RATIO_EPS)
    next_qkv = w_qkv - LEARN_RATE * ratios[0] * part_qkv[2]
    next_out = w_out - LEARN_RATE * ratios[1] * part_out[2]
    next_up = w_up - LEARN_RATE * ratios[2] * part_up[2]
    next_down = w_down - LEARN_RATE * ratios[3] * part_down[2]
    next_vectors = vectors - LEARN_RATE * ratios[4 : 4 + vrows][:, None] * part_vec[2]
    next_table = pos_table - LEARN_RATE * ratios[4 + vrows] * part_table[2]
    return (
        layer_out,
        tokens_grad,
        part_qkv[0],
        part_qkv[1],
        next_qkv,
        part_out[0],
        part_out[1],
        next_out,
        part_up[0],
        part_up[1],
        next_up,
        part_down[0],
        part_down[1],
        next_down,
        part_vec[0],
        part_vec[1],
        next_vectors,
        part_table[0],
        part_table[1],
        next_table,
        weight_norms,
        update_norms,
    )


def solution(mesh):
    both = P(AXES, None)
    side = P(None, AXES)
    tall = P(AXES, None, None)
    copied = P()
    return jax.shard_map(
        functools.partial(per_device, mesh.shape["maps"], mesh.shape["band"]),
        mesh=mesh,
        in_specs=(tall, tall, P("maps", None))
        + (both,) * 4
        + (side, copied)
        + (both,) * 8
        + (side, side, copied, copied),
        out_specs=(tall, tall) + (both,) * 12 + (side,) * 3 + (copied,) * 5,
        check_vma=False,
    )
```

```python
import functools

import jax
import jax.numpy as jnp
import numpy as np
from jax import lax
from jax.experimental import pallas as pl
from jax.experimental.pallas import tpu as pltpu
from jax.sharding import PartitionSpec as P

HEADS = 8
WINDOW = 7
DIL = 4
STEP = 10
NORM_EPS = 1e-05
BETA_FIRST = 0.9
BETA_SECOND = 0.999
ADAM_EPS = 1e-06
DECAY_RATE = 0.01
LEARN_RATE = 0.2
RATIO_EPS = 1e-06
MASKED = -1e30
LOG2E = 1.4426950408889634
AXES = ("maps", "band")

BF = jnp.bfloat16
F32 = jnp.float32

CLS = DIL * DIL
QN = 48
KN = 128
RIM = 40


def dot(a, b):
    return lax.dot_general(a, b, (((1,), (0,)), ((), ())), preferred_element_type=F32)


def dot_nt(a, b):
    return lax.dot_general(a, b, (((1,), (1,)), ((), ())), preferred_element_type=F32)


def dot_tn(a, b):
    return lax.dot_general(a, b, (((0,), (0,)), ((), ())), preferred_element_type=F32)


def order_own():
    sel = np.zeros((4 * QN, 4 * 48), np.float32)
    for o in range(4 * QN):
        cc, rest = divmod(o, QN)
        qr, qc = divmod(rest, 12)
        sel[o, qr * 48 + qc * 4 + cc] = 1
    return sel


def order_keys():
    sel = np.zeros((4 * KN, 480), np.float32)
    for o in range(4 * KN):
        cc, slot = divmod(o, KN)
        j = (slot + 36) % KN
        if j < 120:
            kr, kc = divmod(j, 12)
            sel[o, kr * 48 + kc * 4 + cc] = 1
    return sel


def normed(v):
    mean = jnp.mean(v, axis=-1, keepdims=True)
    cen = v - mean
    var = jnp.mean(cen * cen, axis=-1, keepdims=True)
    rstd = lax.rsqrt(var + NORM_EPS)
    return cen * rstd, rstd


def norm_back(g, xhat, rstd):
    m1 = jnp.mean(g, axis=-1, keepdims=True)
    m2 = jnp.mean(g * xhat, axis=-1, keepdims=True)
    return rstd * (g - m1 - xhat * m2)


def spread_heads(v, lane_head):
    zero = jnp.zeros_like(v)
    return jnp.concatenate([jnp.where(lane_head == h, v, zero) for h in range(HEADS)], axis=0)


def pick_heads(full, lane_head):
    out = jnp.where(lane_head == 0, full[0:QN], 0.0)
    for h in range(1, HEADS):
        out = out + jnp.where(lane_head == h, full[h * QN : (h + 1) * QN], 0.0)
    return out


def split12(v):
    q = (v * 43) >> 9
    return q, v - 12 * q


def table_slots():
    n = lax.broadcasted_iota(jnp.int32, (WINDOW * WINDOW, KN), 0)
    lane = lax.broadcasted_iota(jnp.int32, (WINDOW * WINDOW, KN), 1)
    nr = (n * 37) >> 8
    nc = n - 7 * nr
    return (((12 * (nr - 3) + nc - 3) & (KN - 1)) == lane).astype(F32)


def layer_kernel(
    where_ref,
    x_ref,
    xb_ref,
    xa_ref,
    cot_ref,
    wqkv_ref,
    wo_ref,
    wu_ref,
    wd_ref,
    vec_ref,
    table_ref,
    po_ref,
    pk_ref,
    out_ref,
    act_ref,
    dy_ref,
    dz_ref,
    a2_ref,
    mixed_ref,
    da_ref,
    a1_ref,
    dq_ref,
    dx1_ref,
    own_ref,
    rima_ref,
    rimb_ref,
    tgrad_ref,
    sums_ref,
    zsum_ref,
    xp_ref,
    q_ref,
    k_ref,
    v_ref,
    bias_ref,
    p_ref,
    dmix_ref,
    tacc_ref,
):
    row0 = where_ref[0] * 16
    height = where_ref[1]
    wide = where_ref[2]
    scale = 32 ** (-0.5)
    lane_head = lax.broadcasted_iota(jnp.int32, (QN, 256), 1) >> 5

    def vrow(i):
        return vec_ref[i : i + 1, :]

    slots = lax.dot_general(
        table_ref[...],
        table_slots(),
        (((1,), (0,)), ((), ())),
        precision=lax.Precision.HIGHEST,
        preferred_element_type=F32,
    )
    qi = lax.broadcasted_iota(jnp.int32, (QN, KN), 0)
    si = lax.broadcasted_iota(jnp.int32, (QN, KN), 1)
    ji = (si + 36) & (KN - 1)
    kr, kc = split12(ji)
    qr, qc = split12(qi)
    window = (jnp.abs(kc - qc) <= 3) & (jnp.abs(kr - qr - 3) <= 3) & (ji < 120)
    rows = []
    for h in range(HEADS):
        line = jnp.broadcast_to(slots[h : h + 1, :] * LOG2E, (QN, KN))
        line = pltpu.roll(line, 0, 1, stride=1, stride_axis=0)
        rows.append(jnp.where(window, line, MASKED))
    bias_ref[...] = jnp.concatenate(rows, axis=0).T

    def project(rc, _):
        own = jnp.concatenate([x_ref[4 * i + rc] for i in range(4)], axis=0)
        xp = dot(po_ref[...], own)
        at = pl.ds(pl.multiple_of(rc * 192, 192), 192)
        xp_ref[at, :] = xp
        a1 = (normed(xp)[0] * vrow(0) + vrow(1)).astype(BF)
        a1_ref[at, :] = a1
        q_ref[at, :] = (dot(a1, wqkv_ref[:, 0:256]) + vrow(2)).astype(BF)
        around = jnp.concatenate(
            [xb_ref[4 * i + rc] for i in range(3)]
            + [own]
            + [xa_ref[4 * i + rc] for i in range(3)],
            axis=0,
        )
        xk = dot(pk_ref[...], around)
        a1k = (normed(xk)[0] * vrow(0) + vrow(1)).astype(BF)
        at = pl.ds(pl.multiple_of(rc * 512, 512), 512)
        k_ref[at, :] = dot(a1k, wqkv_ref[:, 256:512]).astype(BF)
        v_ref[at, :] = (dot(a1k, wqkv_ref[:, 512:768]) + vrow(3)).astype(BF)
        return 0

    lax.fori_loop(0, 4, project, 0)

    ks = lax.broadcasted_iota(jnp.int32, (KN, 384), 0)
    ql = lax.broadcasted_iota(jnp.int32, (KN, 384), 1)
    kj = (ks + 36) & (KN - 1)
    krow, kcol = split12(kj)
    qin = ql - 48 * ((ql * 171) >> 13)
    same = ks == qin

    def attend(k, _):
        rc = k >> 2
        cc = k & 3
        at_q = pl.ds(pl.multiple_of(k * QN, QN), QN)
        at_k = pl.ds(pl.multiple_of(k * KN, KN), KN)
        qbd = spread_heads(q_ref[at_q, :], lane_head)
        s = dot_nt(k_ref[at_k, :], qbd) * (scale * LOG2E) + bias_ref[...]
        r = krow * 4 + (row0 + rc - 12)
        c = kcol * 4 + cc
        okay = ((r >= 0) & (r < height) & (c < wide)) | same
        s = jnp.where(okay, s, MASKED)
        top = jnp.max(s, axis=0, keepdims=True)
        e = jnp.exp2(s - top)
        p = e * (1.0 / jnp.sum(e, axis=0, keepdims=True))
        p_ref[at_k, :] = p
        full = dot_tn(p.astype(BF), v_ref[at_k, :])
        mixed_ref[at_q, :] = pick_heads(full, lane_head).astype(BF)
        return 0

    lax.fori_loop(0, CLS, attend, 0)

    sums_ref[...] = jnp.zeros_like(sums_ref)
    zsum_ref[...] = jnp.zeros_like(zsum_ref)

    def feed(rc, _):
        at = pl.ds(pl.multiple_of(rc * 192, 192), 192)
        x1 = xp_ref[at, :] + (dot(mixed_ref[at, :], wo_ref[...]) + vrow(4))
        xhat, rstd = normed(x1)
        a2 = (xhat * vrow(5) + vrow(6)).astype(BF)
        a2_ref[at, :] = a2
        bias = jnp.concatenate([vrow(8), vrow(9), vrow(10)], axis=1)
        z = dot(a2, wu_ref[...]) + bias
        c0 = 0.7978845608028654
        c1 = 0.044715
        z2 = z * z
        t = jnp.tanh(c0 * (z + c1 * z2 * z))
        act = (0.5 * z * (1.0 + t)).astype(BF)
        act_ref[at, :] = act
        res = x1 + dot(act, wd_ref[...]) + vrow(7)
        back = dot_tn(po_ref[...], res.astype(BF)).astype(BF)
        for i in range(4):
            out_ref[4 * i + rc] = back[48 * i : 48 * i + 48]
        dyf = dot(po_ref[...], jnp.concatenate([cot_ref[4 * i + rc] for i in range(4)], axis=0))
        dy = dyf.astype(BF)
        dy_ref[at, :] = dy
        slope = 0.5 * (1.0 + t) + 0.5 * z * (1.0 - t * t) * (c0 * (1.0 + 3.0 * c1 * z2))
        dz = (dot_nt(dy, wd_ref[...]) * slope).astype(BF)
        dz_ref[at, :] = dz
        zsum_ref[...] += jnp.sum(dz.astype(F32), axis=0, keepdims=True)
        dn = dot_nt(dz, wu_ref[...])
        dx1 = dyf + norm_back(dn * vrow(5), xhat, rstd)
        dx1_ref[at, :] = dx1
        da = dx1.astype(BF)
        da_ref[at, :] = da
        dmix_ref[at, :] = dot_nt(da, wo_ref[...]).astype(BF)
        sums_ref[4:5, :] += jnp.sum(da.astype(F32), axis=0, keepdims=True)
        sums_ref[5:6, :] += jnp.sum(dn * xhat, axis=0, keepdims=True)
        sums_ref[6:7, :] += jnp.sum(dn, axis=0, keepdims=True)
        sums_ref[7:8, :] += jnp.sum(dyf, axis=0, keepdims=True)
        return 0

    lax.fori_loop(0, 4, feed, 0)

    tacc_ref[...] = jnp.zeros_like(tacc_ref)

    def back_class(k):
        at_q = pl.ds(pl.multiple_of(k * QN, QN), QN)
        at_k = pl.ds(pl.multiple_of(k * KN, KN), KN)
        qbd = spread_heads(q_ref[at_q, :], lane_head)
        dobd = spread_heads(dmix_ref[at_q, :], lane_head)
        p = p_ref[at_k, :]
        dp = dot_nt(v_ref[at_k, :], dobd)
        dv = dot(p.astype(BF), dobd)
        pdp = p * dp
        ds = pdp - p * jnp.sum(pdp, axis=0, keepdims=True)
        tacc_ref[...] += ds
        dsl = ds.astype(BF)
        dk = dot(dsl, qbd) * scale
        dq = pick_heads(dot_tn(dsl, k_ref[at_k, :]), lane_head) * scale
        dq_ref[at_q, :] = dq.astype(BF)
        own_ref[at_q, 0:256] = dk[0:QN]
        own_ref[at_q, 256:512] = dv[0:QN]
        after = jnp.concatenate([dk[QN : QN + RIM], dv[QN : QN + RIM]], axis=1)
        before = jnp.concatenate([dk[KN - RIM :], dv[KN - RIM :]], axis=1)
        return after, before

    def attend_back(pair, _):
        after0, before0 = back_class(pair * 2)
        after1, before1 = back_class(pair * 2 + 1)
        at = pl.ds(pl.multiple_of(pair * 2 * RIM, 2 * RIM), 2 * RIM)
        rima_ref[at, :] = jnp.concatenate([after0, after1], axis=0).astype(BF)
        rimb_ref[at, :] = jnp.concatenate([before0, before1], axis=0).astype(BF)
        return 0

    lax.fori_loop(0, CLS // 2, attend_back, 0)
    sums_ref[2:3, :] = jnp.sum(dq_ref[...].astype(F32), axis=0, keepdims=True)

    flat = tacc_ref[...].T
    lines = []
    for h in range(HEADS):
        part = flat[h * QN : (h + 1) * QN]
        for bit in range(6):
            turned = pltpu.roll(part, KN - (1 << bit), 1)
            part = jnp.where((qi >> bit) & 1 == 1, turned, part)
        lines.append(jnp.sum(part, axis=0, keepdims=True))
    tgrad_ref[...] = jnp.concatenate(lines, axis=0)


def finish_kernel(
    own_ref,
    fa_ref,
    fb_ref,
    dq_ref,
    dx1_ref,
    x_ref,
    wqkv_ref,
    vec_ref,
    po_ref,
    tok_ref,
    dqkv_ref,
    sums_ref,
):
    sums_ref[...] = jnp.zeros_like(sums_ref)

    def block(rc, _):
        own = jnp.concatenate([x_ref[4 * i + rc] for i in range(4)], axis=0)
        xp = dot(po_ref[...], own)
        xhat, rstd = normed(xp)
        at = pl.ds(pl.multiple_of(rc * 192, 192), 192)
        mine = own_ref[at, :]
        got_a = fa_ref[pl.ds(pl.multiple_of(rc * 160, 160), 160), :].astype(F32)
        got_b = fb_ref[pl.ds(pl.multiple_of(rc * 160, 160), 160), :].astype(F32)
        gap = jnp.zeros((QN - RIM, 512), F32)
        parts = []
        for i in range(4):
            a = jnp.concatenate([got_a[i * RIM : (i + 1) * RIM], gap], axis=0)
            b = jnp.concatenate([gap, got_b[i * RIM : (i + 1) * RIM]], axis=0)
            parts.append(mine[i * QN : (i + 1) * QN] + a + b)
        dkv = jnp.concatenate(parts, axis=0).astype(BF)
        dqkv = jnp.concatenate([dq_ref[at, :], dkv], axis=1)
        dqkv_ref[at, :] = dqkv
        dn = dot_nt(dqkv, wqkv_ref[...])
        gain = vec_ref[0:1, :]
        dx = dx1_ref[at, :] + norm_back(dn * gain, xhat, rstd)
        back = dot_tn(po_ref[...], dx.astype(BF)).astype(BF)
        for i in range(4):
            tok_ref[4 * i + rc] = back[48 * i : 48 * i + 48]
        sums_ref[0:1, :] += jnp.sum(dn * xhat, axis=0, keepdims=True)
        sums_ref[1:2, :] += jnp.sum(dn, axis=0, keepdims=True)
        sums_ref[3:4, :] += jnp.sum(dkv[:, 256:512].astype(F32), axis=0, keepdims=True)
        return 0

    lax.fori_loop(0, 4, block, 0)


EARLY = 896
LATE = 512


def pack_kernel(wqkv_ref, wo_ref, wu_ref, wd_ref, vec_ref, out_ref):
    vrows = vec_ref.shape[0]
    lane = lax.broadcasted_iota(jnp.int32, (vrows, 128), 1)
    row = lax.broadcasted_iota(jnp.int32, (vrows, 128), 0)
    turned = dot_tn(vec_ref[...].astype(BF), (lane == row).astype(BF))
    top = [wd_ref[8 * b : 8 * b + 8, :] for b in range(3)]
    top += [wo_ref[:, 0:128], wqkv_ref[:, 0:512]]
    low = [wu_ref[...], wo_ref[:, 128:256], wqkv_ref[:, 512:768], turned, jnp.zeros((8, 128), F32)]
    both = jnp.concatenate([jnp.concatenate(top, axis=1), jnp.concatenate(low, axis=1)], axis=0)
    out_ref[...] = both.astype(BF)


def unpack(me, blocks, refs):
    wqkv_ref, wo_ref, wu_ref, wd_ref, vec_ref, fq, fo, fu, fd, fv = refs
    for index, block in enumerate(blocks):
        core, across = divmod(index, 4)
        for z in range(4):
            o = me ^ (core | (z << 1) | (across << 3))
            slab = block[z].astype(F32)
            at = pl.ds(pl.multiple_of(o * 8, 8), 8)
            for b in range(3):
                fd[pl.ds(pl.multiple_of(o * 24 + 8 * b, 8), 8), :] = slab[0:8, 256 * b : 256 * b + 256]
            fo[at, 0:128] = slab[0:8, 768:896]
            fo[at, 128:256] = slab[8:16, 768:896]
            fu[at, :] = slab[8:16, 0:768]
            fq[at, 0:512] = slab[0:8, 896:1408]
            fq[at, 512:768] = slab[8:16, 896:1152]
            fv[at, :] = slab[8:16, 1152:1280]
    wqkv_ref[...] = fq[...].astype(BF)
    wo_ref[...] = fo[...].astype(BF)
    wu_ref[...] = fu[...].astype(BF)
    wd_ref[...] = fd[...].astype(BF)
    vec_ref[...] = fv[...].T[0 : vec_ref.shape[0]]


def layer_packed(
    where_ref, x_ref, xb_ref, xa_ref, cot_ref, b0, b1, b2, b3, b4, b5, b6, b7, table_ref, po_ref, pk_ref, *rest
):
    weights = rest[-10:]
    unpack(where_ref[3], (b0, b1, b2, b3, b4, b5, b6, b7), weights)
    outs, scratch = rest[:16], rest[18:-10]
    rest[16][...] = weights[0][...]
    rest[17][...] = weights[4][...]
    layer_kernel(
        where_ref, x_ref, xb_ref, xa_ref, cot_ref, *weights[:5], table_ref, po_ref, pk_ref, *outs, *scratch
    )


def frame_slot(me, o):
    m = me ^ o
    return (m & 1) * 16 + (m >> 3) * 4 + ((m >> 1) & 3)


def early_kernel(where_ref, act_ref, dy_ref, a2_ref, dz_ref, mixed_ref, da_ref, out_ref, fd, fu, fo):
    fd[...] = dot_tn(act_ref[...], dy_ref[...])
    fu[...] = dot_tn(a2_ref[...], dz_ref[...])
    fo[...] = dot_tn(mixed_ref[...], da_ref[...])
    me = where_ref[3]
    for o in range(32):
        at = slice(8 * o, 8 * o + 8)
        top = [fd[24 * o + 8 * b : 24 * o + 8 * b + 8, :] for b in range(3)] + [fo[at, 0:128]]
        low = [fu[at, :], fo[at, 128:256]]
        both = jnp.concatenate([jnp.concatenate(top, axis=1), jnp.concatenate(low, axis=1)], axis=0)
        out_ref[frame_slot(me, o)] = both.astype(BF)


def late_kernel(where_ref, *refs):
    own, fa, fb, dq, dx1, x, wqkv, vec, po, a1, sums, zsum, tgrad = refs[:13]
    tok_ref, out_ref, dqkv, sums2, fq, fv = refs[13:]
    finish_kernel(own, fa, fb, dq, dx1, x, wqkv, vec, po, tok_ref, dqkv, sums2)
    fq[...] = dot_tn(a1[...], dqkv[...])
    lines = jnp.concatenate(
        [sums[...] + sums2[...]]
        + [zsum[:, 256 * i : 256 * i + 256] for i in range(3)]
        + [jnp.zeros((117, 256), F32)],
        axis=0,
    )
    fv[...] = lines.T
    table = tgrad[...]
    me = where_ref[3]
    for o in range(32):
        at = slice(8 * o, 8 * o + 8)
        low = jnp.concatenate([fq[at, 512:768], fv[at, :], table], axis=1)
        out_ref[frame_slot(me, o)] = jnp.concatenate([fq[at, 0:512], low], axis=0).astype(BF)


def adam_kernel(*refs):
    w, first, second = refs[4:10], refs[10:16], refs[16:22]
    outs = refs[22:]
    total = refs[0][...] + sum(ref[...].astype(F32) for ref in refs[1:4])
    early, late = total[:, :EARLY], total[:, EARLY:]
    vrows = w[4].shape[0]
    grads = [
        jnp.concatenate([late[0:8], late[8:16, 0:256]], axis=1),
        jnp.concatenate([early[0:8, 768:896], early[8:16, 768:896]], axis=1),
        early[8:16, 0:768],
        jnp.concatenate([early[0:8, 256 * b : 256 * b + 256] for b in range(3)], axis=0),
        late[8:16, 256:384].T[0:vrows],
        lax.dot_general(
            late[8:16, 384:512],
            table_slots(),
            (((1,), (1,)), ((), ())),
            precision=lax.Precision.HIGHEST,
            preferred_element_type=F32,
        ),
    ]
    row = lax.broadcasted_iota(jnp.int32, (16, 128), 0)
    lane = lax.broadcasted_iota(jnp.int32, (16, 128), 1)
    norms = jnp.zeros((16, 128), F32)
    for i in range(6):
        new_first, new_second, update = adam_parts(w[i][...], grads[i], first[i][...], second[i][...])
        outs[3 * i][...] = new_first
        outs[3 * i + 1][...] = new_second
        outs[3 * i + 2][...] = update
        for col, v in ((0, w[i][...]), (1, update)):
            if i == 4:
                per_row = jnp.sum(v * v, axis=1, keepdims=True)
                tall = jnp.concatenate([jnp.zeros((4, 1), F32), per_row, jnp.zeros((12 - vrows, 1), F32)], axis=0)
                norms = jnp.where((lane == col) & (row >= 4) & (row < 4 + vrows), tall, norms)
            else:
                total = jnp.sum(v * v)
                at = i if i < 4 else 4 + vrows
                norms = jnp.where((lane == col) & (row == at), total, norms)
    outs[18][...] = norms


def step_kernel(mine_ref, a_ref, b_ref, c_ref, d_ref, *refs):
    w, update, outs = refs[0:6], refs[6:12], refs[12:]
    vrows = w[4].shape[0]
    total = a_ref[...] + b_ref[...] + c_ref[...] + d_ref[...]
    row = lax.broadcasted_iota(jnp.int32, (16, 128), 0)
    norms = jnp.sqrt(jnp.where(row == 4 + vrows, mine_ref[...], total))
    turned = norms.T
    outs[6][...] = turned[0:1]
    outs[7][...] = turned[1:2]
    rate = LEARN_RATE * norms[:, 0:1] / (norms[:, 1:2] + RATIO_EPS)
    for i in range(6):
        if i == 4:
            r = rate[4 : 4 + vrows]
        else:
            r = rate[i : i + 1] if i < 4 else rate[4 + vrows : 5 + vrows]
        outs[i][...] = w[i][...] - r * update[i][...]


def stack_kernel(*refs):
    for i, ref in enumerate(refs[:-1]):
        refs[-1][i] = ref[...]


def call(kernel, out_shape, scratch, *args, smem=0, flops=10**8, vmem=16):
    vm = pl.BlockSpec(memory_space=pltpu.VMEM)
    specs = [pl.BlockSpec(memory_space=pltpu.SMEM)] * smem + [vm] * (len(args) - smem)
    return pl.pallas_call(
        kernel,
        out_shape=out_shape,
        in_specs=specs,
        out_specs=jax.tree.map(lambda _: vm, out_shape),
        scratch_shapes=scratch,
        compiler_params=pltpu.CompilerParams(vmem_limit_bytes=vmem * 2**20),
        cost_estimate=pl.CostEstimate(flops=flops, bytes_accessed=10**6, transcendentals=0),
    )(*args)


def sds(shape, dtype=BF):
    return jax.ShapeDtypeStruct(shape, dtype)


def exchange_groups(maps, band):
    zbits = band.bit_length() - 2
    mbits = maps.bit_length() - 1
    cut = lambda lo, n: [(lo + i, min(2, n - i)) for i in range(0, n, 2)]
    return cut(1, zbits) + cut(1 + zbits, mbits) + [(0, 1)]


def swap(block, mask, count):
    return lax.ppermute(block, AXES, [(k, k ^ mask) for k in range(count)])


def frame_masks(groups):
    masks = [0]
    for lo, bits in groups:
        masks = [m ^ (d << lo) for d in range(1 << bits) for m in masks]
    return masks


def gather_all(slab, groups, count):
    block = slab[None]
    for lo, bits in groups:
        block = jnp.concatenate(
            [block] + [swap(block, d << lo, count) for d in range(1, 1 << bits)], axis=0
        )
    return block


def scatter_sum(grads, groups, count):
    for lo, bits in reversed(groups):
        grads = add_stage(grads, lo, bits, count)
    return grads[0]


def adam_parts(weight, grad, first, second):
    new_first = BETA_FIRST * first + (1.0 - BETA_FIRST) * grad
    new_second = BETA_SECOND * second + (1.0 - BETA_SECOND) * grad * grad
    update = (
        new_first
        / (1.0 - BETA_FIRST**STEP)
        / (jnp.sqrt(new_second / (1.0 - BETA_SECOND**STEP)) + ADAM_EPS)
        + DECAY_RATE * weight
    )
    return (new_first, new_second, update)


def squares_of(matrices, rowwise):
    return jnp.concatenate(
        [
            jnp.stack([jnp.sum(matrix * matrix) for matrix in matrices]),
            jnp.sum(rowwise * rowwise, axis=1),
        ]
    )


def layer_outputs():
    return (
        sds((16, 48, 256)),
        sds((768, 768)),
        sds((768, 256)),
        sds((768, 768)),
        sds((768, 256)),
        sds((768, 256)),
        sds((768, 256)),
        sds((768, 256)),
        sds((768, 256)),
        sds((768, 256), F32),
        sds((768, 512), F32),
        sds((CLS * RIM, 512)),
        sds((CLS * RIM, 512)),
        sds((HEADS, KN), F32),
        sds((8, 256), F32),
        sds((1, 768), F32),
    )


def layer_scratch():
    return [
        pltpu.VMEM((768, 256), F32),
        pltpu.VMEM((768, 256), BF),
        pltpu.VMEM((CLS * KN, 256), BF),
        pltpu.VMEM((CLS * KN, 256), BF),
        pltpu.VMEM((KN, 384), F32),
        pltpu.VMEM((CLS * KN, 384), F32),
        pltpu.VMEM((768, 256), BF),
        pltpu.VMEM((KN, 384), F32),
    ]


def packed_step(tokens_in, cotangent, map_sizes, weights, firsts, seconds):
    count = 32
    me = lax.axis_index(AXES)
    band_index = lax.axis_index("band")
    vrows = weights[4].shape[0]
    up = [(i, i + 1) for i in range(7)]
    down = [(i + 1, i) for i in range(7)]
    x_before = lax.ppermute(tokens_in[-12:], "band", up)
    x_after = lax.ppermute(tokens_in[:12], "band", down)

    slab = call(pack_kernel, sds((16, EARLY + LATE)), [], *weights[:5])
    column = call(
        stack_kernel,
        sds((4, 16, EARLY + LATE)),
        [],
        slab,
        *[swap(slab, d << 1, count) for d in (1, 2, 3)],
    )
    blocks = [column] + [swap(column, d << 3, count) for d in (1, 2, 3)]
    blocks += [swap(block, 1, count) for block in blocks]

    po = jnp.asarray(order_own(), BF)
    pk = jnp.asarray(order_keys(), BF)
    place = jnp.stack([band_index, map_sizes[0, 0], map_sizes[0, 1], me]).astype(jnp.int32)
    matrices = [(256, 768), (256, 256), (256, 768), (768, 256)]
    (
        layer_out, act, dy, dz, a2, mixed, da, a1, dq, dx1, own, rim_a, rim_b, tgrad, sums, zsum, big_qkv, vec,
    ) = call(
        layer_packed,
        layer_outputs() + (sds((256, 768)), sds((vrows, 256), F32)),
        layer_scratch()
        + [pltpu.VMEM(m, BF) for m in matrices]
        + [pltpu.VMEM((vrows, 256), F32)]
        + [pltpu.VMEM(m, F32) for m in matrices]
        + [pltpu.VMEM((256, 128), F32)],
        place, tokens_in, x_before, x_after, cotangent, *blocks, weights[5], po, pk,
        smem=1, flops=6 * 10**9, vmem=24,
    )
    from_prev = lax.ppermute(rim_a, "band", up)
    from_next = lax.ppermute(rim_b, "band", down)
    early = call(
        early_kernel,
        sds((count, 16, EARLY)),
        [pltpu.VMEM((768, 256), F32), pltpu.VMEM((256, 768), F32), pltpu.VMEM((256, 256), F32)],
        place, act, dy, a2, dz, mixed, da,
        smem=1, flops=10**9,
    )
    tokens_grad, late = call(
        late_kernel,
        (sds((16, 48, 256)), sds((count, 16, LATE))),
        [
            pltpu.VMEM((768, 768), BF),
            pltpu.VMEM((8, 256), F32),
            pltpu.VMEM((256, 768), F32),
            pltpu.VMEM((256, 128), F32),
        ],
        place, own, from_prev, from_next, dq, dx1, tokens_in, big_qkv, vec, po, a1, sums, zsum, tgrad,
        smem=1, flops=10**9,
    )
    early = add_stage(add_stage(early, 0, 1, count), 3, 2, count)
    late = add_stage(add_stage(late, 0, 1, count), 3, 2, count)
    grads = jnp.concatenate([early, late], axis=-1)
    low = grads.astype(BF)
    parts = [grads[0]] + [swap(low[d], d << 1, count) for d in (1, 2, 3)]

    shapes = [sds(w.shape, F32) for w in weights]
    moments = call(
        adam_kernel,
        tuple(shape for shape in shapes for _ in range(3)) + (sds((16, 128), F32),),
        [],
        *parts, *weights, *firsts, *seconds,
    )
    mine = moments[18]
    squares = mine + swap(mine, 1, count)
    squares = squares + swap(squares, 8, count) + swap(squares, 16, count) + swap(squares, 24, count)
    news = call(
        step_kernel,
        tuple(shapes) + (sds((1, 16), F32),) * 2,
        [],
        mine, squares, *[swap(squares, d << 1, count) for d in (1, 2, 3)], *weights, *moments[2:18:3],
    )
    results = [layer_out, tokens_grad]
    for i in range(6):
        results += [moments[3 * i], moments[3 * i + 1], news[i]]
    return tuple(results) + (news[6].reshape(16), news[7].reshape(16))


def add_stage(grads, lo, bits, count):
    low = grads.astype(BF).reshape((1 << bits, -1) + grads.shape[1:])
    total = grads.reshape(low.shape)[0].astype(F32)
    for d in range(1, 1 << bits):
        total = total + swap(low[d], d << lo, count).astype(F32)
    return total


def per_device(
    maps,
    band,
    tokens_in,
    cotangent,
    map_sizes,
    w_qkv,
    w_out,
    w_up,
    w_down,
    vectors,
    pos_table,
    first_qkv,
    second_qkv,
    first_out,
    second_out,
    first_up,
    second_up,
    first_down,
    second_down,
    first_vectors,
    second_vectors,
    first_table,
    second_table,
):
    if w_qkv.shape[0] == 8 and (maps, band) == (4, 8):
        return packed_step(
            tokens_in, cotangent, map_sizes,
            (w_qkv, w_out, w_up, w_down, vectors, pos_table),
            (first_qkv, first_out, first_up, first_down, first_vectors, first_table),
            (second_qkv, second_out, second_up, second_down, second_vectors, second_table),
        )
    count = maps * band
    rows = w_qkv.shape[0]
    vrows = vectors.shape[0]
    groups = exchange_groups(maps, band)
    masks = np.array(frame_masks(groups))
    inverse = np.argsort(masks)
    me = lax.axis_index(AXES)
    band_index = lax.axis_index("band")
    reach = 3 * DIL

    up = [(i, i + 1) for i in range(band - 1)]
    down = [(i + 1, i) for i in range(band - 1)]
    x_before = lax.ppermute(tokens_in[-reach:], "band", up)
    x_after = lax.ppermute(tokens_in[:reach], "band", down)

    def pack(qkv, out, upw, dnw, vec):
        dn = dnw.reshape(3, rows, 256).transpose(1, 0, 2).reshape(rows, 768)
        vt = jnp.pad(vec.T, ((0, 0), (0, 128 - vrows)))
        return jnp.concatenate([qkv, out, upw, dn, vt], axis=1)

    slab = pack(*(w.astype(BF) for w in (w_qkv, w_out, w_up, w_down, vectors)))
    block = gather_all(slab, groups, count)
    order = jnp.asarray(inverse, jnp.int32)[jnp.arange(count, dtype=jnp.int32) ^ me]
    whole = jnp.take(block, order, axis=0).reshape(256, -1)
    big_qkv = whole[:, 0:768]
    big_out = whole[:, 768:1024]
    big_up = whole[:, 1024:1792]
    big_down = (
        whole[:, 1792:2560].reshape(count, rows, 3, 256).transpose(0, 2, 1, 3).reshape(768, 256)
    )
    vec = whole[:, 2560 : 2560 + vrows].T.astype(F32)

    po = jnp.asarray(order_own(), BF)
    pk = jnp.asarray(order_keys(), BF)
    place = jnp.stack([band_index, map_sizes[0, 0], map_sizes[0, 1]]).astype(jnp.int32)
    (
        layer_out,
        act,
        dy,
        dz,
        a2,
        mixed,
        da,
        a1,
        dq,
        dx1,
        own,
        rim_a,
        rim_b,
        table_grad,
        sums,
        zsum,
    ) = call(
        layer_kernel,
        layer_outputs(),
        layer_scratch(),
        place,
        tokens_in,
        x_before,
        x_after,
        cotangent,
        big_qkv,
        big_out,
        big_up,
        big_down,
        vec,
        pos_table,
        po,
        pk,
        smem=1,
        flops=6 * 10**9,
    )
    from_prev = lax.ppermute(rim_a, "band", up)
    from_next = lax.ppermute(rim_b, "band", down)
    grad_down = dot_tn(act, dy)
    grad_up = dot_tn(a2, dz)
    grad_out = dot_tn(mixed, da)
    tokens_grad, dqkv, sums2 = call(
        finish_kernel,
        (sds((16, 48, 256)), sds((768, 768)), sds((8, 256), F32)),
        [],
        own,
        from_prev,
        from_next,
        dq,
        dx1,
        tokens_in,
        big_qkv,
        vec,
        po,
    )
    grad_qkv = dot_tn(a1, dqkv)
    grad_vec = jnp.concatenate([sums + sums2, zsum.reshape(3, 256)], axis=0)

    packed = jnp.concatenate(
        [
            grad_qkv.reshape(count, rows, 768),
            grad_out.reshape(count, rows, 256),
            grad_up.reshape(count, rows, 768),
            grad_down.reshape(count, 3, rows, 256).transpose(0, 2, 1, 3).reshape(count, rows, 768),
            jnp.pad(grad_vec.T, ((0, 0), (0, 128 - vrows))).reshape(count, rows, 128),
        ],
        axis=2,
    )
    packed = jnp.take(packed, jnp.asarray(masks, jnp.int32) ^ me, axis=0)
    red = scatter_sum(packed, groups, count)
    red_qkv = red[:, 0:768]
    red_out = red[:, 768:1024]
    red_up = red[:, 1024:1792]
    red_down = red[:, 1792:2560].reshape(rows, 3, 256).transpose(1, 0, 2).reshape(3 * rows, 256)
    red_vec = red[:, 2560 : 2560 + vrows].T

    steps = np.arange(-3, 4)
    lanes = ((12 * steps[:, None] + steps[None, :]) % KN).reshape(-1)
    table_total = lax.psum(table_grad, AXES)[:, lanes]

    part_qkv = adam_parts(w_qkv, red_qkv, first_qkv, second_qkv)
    part_out = adam_parts(w_out, red_out, first_out, second_out)
    part_up = adam_parts(w_up, red_up, first_up, second_up)
    part_down = adam_parts(w_down, red_down, first_down, second_down)
    part_vec = adam_parts(vectors, red_vec, first_vectors, second_vectors)
    part_table = adam_parts(pos_table, table_total, first_table, second_table)
    local_weight_sq = squares_of((w_qkv, w_out, w_up, w_down), vectors)
    local_update_sq = squares_of((part_qkv[2], part_out[2], part_up[2], part_down[2]), part_vec[2])
    weight_sq, update_sq = lax.psum((local_weight_sq, local_update_sq), AXES)
    table_weight = jnp.sqrt(jnp.sum(pos_table * pos_table))
    table_update = jnp.sqrt(jnp.sum(part_table[2] * part_table[2]))
    weight_norms = jnp.concatenate([jnp.sqrt(weight_sq), table_weight[None]])
    update_norms = jnp.concatenate([jnp.sqrt(update_sq), table_update[None]])
    ratios = weight_norms / (update_norms + RATIO_EPS)
    next_qkv = w_qkv - LEARN_RATE * ratios[0] * part_qkv[2]
    next_out = w_out - LEARN_RATE * ratios[1] * part_out[2]
    next_up = w_up - LEARN_RATE * ratios[2] * part_up[2]
    next_down = w_down - LEARN_RATE * ratios[3] * part_down[2]
    next_vectors = vectors - LEARN_RATE * ratios[4 : 4 + vrows][:, None] * part_vec[2]
    next_table = pos_table - LEARN_RATE * ratios[4 + vrows] * part_table[2]
    return (
        layer_out,
        tokens_grad,
        part_qkv[0],
        part_qkv[1],
        next_qkv,
        part_out[0],
        part_out[1],
        next_out,
        part_up[0],
        part_up[1],
        next_up,
        part_down[0],
        part_down[1],
        next_down,
        part_vec[0],
        part_vec[1],
        next_vectors,
        part_table[0],
        part_table[1],
        next_table,
        weight_norms,
        update_norms,
    )


def solution(mesh):
    both = P(AXES, None)
    side = P(None, AXES)
    tall = P(AXES, None, None)
    copied = P()
    return jax.shard_map(
        functools.partial(per_device, mesh.shape["maps"], mesh.shape["band"]),
        mesh=mesh,
        in_specs=(tall, tall, P("maps", None))
        + (both,) * 4
        + (side, copied)
        + (both,) * 8
        + (side, side, copied, copied),
        out_specs=(tall, tall) + (both,) * 12 + (side,) * 3 + (copied,) * 5,
        check_vma=False,
    )
```

```python
import functools

import jax
import jax.numpy as jnp
import numpy as np
from jax import lax
from jax.experimental import pallas as pl
from jax.experimental.pallas import tpu as pltpu
from jax.sharding import PartitionSpec as P

HEADS = 8
WINDOW = 7
DIL = 4
STEP = 10
NORM_EPS = 1e-05
BETA_FIRST = 0.9
BETA_SECOND = 0.999
ADAM_EPS = 1e-06
DECAY_RATE = 0.01
LEARN_RATE = 0.2
RATIO_EPS = 1e-06
MASKED = -1e30
LOG2E = 1.4426950408889634
AXES = ("maps", "band")

BF = jnp.bfloat16
F32 = jnp.float32

CLS = DIL * DIL
QN = 48
KN = 128
RIM = 40


def dot(a, b):
    return lax.dot_general(a, b, (((1,), (0,)), ((), ())), preferred_element_type=F32)


def dot_nt(a, b):
    return lax.dot_general(a, b, (((1,), (1,)), ((), ())), preferred_element_type=F32)


def dot_tn(a, b):
    return lax.dot_general(a, b, (((0,), (0,)), ((), ())), preferred_element_type=F32)


def order_own():
    sel = np.zeros((4 * QN, 4 * 48), np.float32)
    for o in range(4 * QN):
        cc, rest = divmod(o, QN)
        qr, qc = divmod(rest, 12)
        sel[o, qr * 48 + qc * 4 + cc] = 1
    return sel


def order_keys():
    sel = np.zeros((4 * KN, 480), np.float32)
    for o in range(4 * KN):
        cc, slot = divmod(o, KN)
        j = (slot + 36) % KN
        if j < 120:
            kr, kc = divmod(j, 12)
            sel[o, kr * 48 + kc * 4 + cc] = 1
    return sel


def normed(v):
    mean = jnp.mean(v, axis=-1, keepdims=True)
    cen = v - mean
    var = jnp.mean(cen * cen, axis=-1, keepdims=True)
    rstd = lax.rsqrt(var + NORM_EPS)
    return cen * rstd, rstd


def norm_back(g, xhat, rstd):
    m1 = jnp.mean(g, axis=-1, keepdims=True)
    m2 = jnp.mean(g * xhat, axis=-1, keepdims=True)
    return rstd * (g - m1 - xhat * m2)


def spread_heads(v, lane_head):
    zero = jnp.zeros_like(v)
    return jnp.concatenate([jnp.where(lane_head == h, v, zero) for h in range(HEADS)], axis=0)


def pick_heads(full, lane_head):
    out = jnp.where(lane_head == 0, full[0:QN], 0.0)
    for h in range(1, HEADS):
        out = out + jnp.where(lane_head == h, full[h * QN : (h + 1) * QN], 0.0)
    return out


def split12(v):
    q = (v * 43) >> 9
    return q, v - 12 * q


def table_slots():
    n = lax.broadcasted_iota(jnp.int32, (WINDOW * WINDOW, KN), 0)
    lane = lax.broadcasted_iota(jnp.int32, (WINDOW * WINDOW, KN), 1)
    nr = (n * 37) >> 8
    nc = n - 7 * nr
    return (((12 * (nr - 3) + nc - 3) & (KN - 1)) == lane).astype(F32)


def layer_kernel(
    sizes_ref,
    x_ref,
    xb_ref,
    xa_ref,
    cot_ref,
    wqkv_ref,
    wo_ref,
    wu_ref,
    wd_ref,
    vec_ref,
    table_ref,
    po_ref,
    pk_ref,
    out_ref,
    act_ref,
    dy_ref,
    dz_ref,
    a2_ref,
    mixed_ref,
    da_ref,
    a1_ref,
    dq_ref,
    dx1_ref,
    own_ref,
    rima_ref,
    rimb_ref,
    tgrad_ref,
    sums_ref,
    zsum_ref,
    xp_ref,
    q_ref,
    k_ref,
    v_ref,
    bias_ref,
    p_ref,
    dmix_ref,
    tacc_ref,
):
    row0 = lax.axis_index("band") * 16
    height = sizes_ref[0, 0]
    wide = sizes_ref[0, 1]
    scale = 32 ** (-0.5)
    lane_head = lax.broadcasted_iota(jnp.int32, (QN, 256), 1) >> 5

    def vrow(i):
        return vec_ref[i : i + 1, :]

    slots = lax.dot_general(
        table_ref[...],
        table_slots(),
        (((1,), (0,)), ((), ())),
        precision=lax.Precision.HIGHEST,
        preferred_element_type=F32,
    )
    qi = lax.broadcasted_iota(jnp.int32, (QN, KN), 0)
    si = lax.broadcasted_iota(jnp.int32, (QN, KN), 1)
    ji = (si + 36) & (KN - 1)
    kr, kc = split12(ji)
    qr, qc = split12(qi)
    window = (jnp.abs(kc - qc) <= 3) & (jnp.abs(kr - qr - 3) <= 3) & (ji < 120)
    rows = []
    for h in range(HEADS):
        line = jnp.broadcast_to(slots[h : h + 1, :] * LOG2E, (QN, KN))
        line = pltpu.roll(line, 0, 1, stride=1, stride_axis=0)
        rows.append(jnp.where(window, line, MASKED))
    bias_ref[...] = jnp.concatenate(rows, axis=0).T

    def project(rc, _):
        own = jnp.concatenate([x_ref[4 * i + rc] for i in range(4)], axis=0)
        xp = dot(po_ref[...], own)
        at = pl.ds(pl.multiple_of(rc * 192, 192), 192)
        xp_ref[at, :] = xp
        a1 = (normed(xp)[0] * vrow(0) + vrow(1)).astype(BF)
        a1_ref[at, :] = a1
        q_ref[at, :] = (dot(a1, wqkv_ref[:, 0:256]) + vrow(2)).astype(BF)
        around = jnp.concatenate(
            [xb_ref[4 * i + rc] for i in range(3)]
            + [own]
            + [xa_ref[4 * i + rc] for i in range(3)],
            axis=0,
        )
        xk = dot(pk_ref[...], around)
        a1k = (normed(xk)[0] * vrow(0) + vrow(1)).astype(BF)
        at = pl.ds(pl.multiple_of(rc * 512, 512), 512)
        k_ref[at, :] = dot(a1k, wqkv_ref[:, 256:512]).astype(BF)
        v_ref[at, :] = (dot(a1k, wqkv_ref[:, 512:768]) + vrow(3)).astype(BF)
        return 0

    lax.fori_loop(0, 4, project, 0)

    ks = lax.broadcasted_iota(jnp.int32, (KN, 384), 0)
    ql = lax.broadcasted_iota(jnp.int32, (KN, 384), 1)
    kj = (ks + 36) & (KN - 1)
    krow, kcol = split12(kj)
    qin = ql - 48 * ((ql * 171) >> 13)
    same = ks == qin

    def attend(k, _):
        rc = k >> 2
        cc = k & 3
        at_q = pl.ds(pl.multiple_of(k * QN, QN), QN)
        at_k = pl.ds(pl.multiple_of(k * KN, KN), KN)
        qbd = spread_heads(q_ref[at_q, :], lane_head)
        s = dot_nt(k_ref[at_k, :], qbd) * (scale * LOG2E) + bias_ref[...]
        r = krow * 4 + (row0 + rc - 12)
        c = kcol * 4 + cc
        okay = ((r >= 0) & (r < height) & (c < wide)) | same
        s = jnp.where(okay, s, MASKED)
        top = jnp.max(s, axis=0, keepdims=True)
        e = jnp.exp2(s - top)
        p = e * (1.0 / jnp.sum(e, axis=0, keepdims=True))
        p_ref[at_k, :] = p
        full = dot_tn(p.astype(BF), v_ref[at_k, :])
        mixed_ref[at_q, :] = pick_heads(full, lane_head).astype(BF)
        return 0

    lax.fori_loop(0, CLS, attend, 0)

    sums_ref[...] = jnp.zeros_like(sums_ref)
    zsum_ref[...] = jnp.zeros_like(zsum_ref)

    def feed(rc, _):
        at = pl.ds(pl.multiple_of(rc * 192, 192), 192)
        x1 = xp_ref[at, :] + (dot(mixed_ref[at, :], wo_ref[...]) + vrow(4))
        xhat, rstd = normed(x1)
        a2 = (xhat * vrow(5) + vrow(6)).astype(BF)
        a2_ref[at, :] = a2
        bias = jnp.concatenate([vrow(8), vrow(9), vrow(10)], axis=1)
        z = dot(a2, wu_ref[...]) + bias
        c0 = 0.7978845608028654
        c1 = 0.044715
        z2 = z * z
        t = jnp.tanh(c0 * (z + c1 * z2 * z))
        act = (0.5 * z * (1.0 + t)).astype(BF)
        act_ref[at, :] = act
        res = x1 + dot(act, wd_ref[...]) + vrow(7)
        back = dot_tn(po_ref[...], res.astype(BF)).astype(BF)
        for i in range(4):
            out_ref[4 * i + rc] = back[48 * i : 48 * i + 48]
        dyf = dot(po_ref[...], jnp.concatenate([cot_ref[4 * i + rc] for i in range(4)], axis=0))
        dy = dyf.astype(BF)
        dy_ref[at, :] = dy
        slope = 0.5 * (1.0 + t) + 0.5 * z * (1.0 - t * t) * (c0 * (1.0 + 3.0 * c1 * z2))
        dz = (dot_nt(dy, wd_ref[...]) * slope).astype(BF)
        dz_ref[at, :] = dz
        zsum_ref[...] += jnp.sum(dz.astype(F32), axis=0, keepdims=True)
        dn = dot_nt(dz, wu_ref[...])
        dx1 = dyf + norm_back(dn * vrow(5), xhat, rstd)
        dx1_ref[at, :] = dx1
        da = dx1.astype(BF)
        da_ref[at, :] = da
        dmix_ref[at, :] = dot_nt(da, wo_ref[...]).astype(BF)
        sums_ref[4:5, :] += jnp.sum(da.astype(F32), axis=0, keepdims=True)
        sums_ref[5:6, :] += jnp.sum(dn * xhat, axis=0, keepdims=True)
        sums_ref[6:7, :] += jnp.sum(dn, axis=0, keepdims=True)
        sums_ref[7:8, :] += jnp.sum(dyf, axis=0, keepdims=True)
        return 0

    lax.fori_loop(0, 4, feed, 0)

    tacc_ref[...] = jnp.zeros_like(tacc_ref)

    def back_class(k):
        at_q = pl.ds(pl.multiple_of(k * QN, QN), QN)
        at_k = pl.ds(pl.multiple_of(k * KN, KN), KN)
        qbd = spread_heads(q_ref[at_q, :], lane_head)
        dobd = spread_heads(dmix_ref[at_q, :], lane_head)
        p = p_ref[at_k, :]
        dp = dot_nt(v_ref[at_k, :], dobd)
        dv = dot(p.astype(BF), dobd)
        pdp = p * dp
        ds = pdp - p * jnp.sum(pdp, axis=0, keepdims=True)
        tacc_ref[...] += ds
        dsl = ds.astype(BF)
        dk = dot(dsl, qbd) * scale
        dq = pick_heads(dot_tn(dsl, k_ref[at_k, :]), lane_head) * scale
        dq_ref[at_q, :] = dq.astype(BF)
        own_ref[at_q, 0:256] = dk[0:QN]
        own_ref[at_q, 256:512] = dv[0:QN]
        after = jnp.concatenate([dk[QN : QN + RIM], dv[QN : QN + RIM]], axis=1)
        before = jnp.concatenate([dk[KN - RIM :], dv[KN - RIM :]], axis=1)
        return after, before

    def attend_back(pair, _):
        after0, before0 = back_class(pair * 2)
        after1, before1 = back_class(pair * 2 + 1)
        at = pl.ds(pl.multiple_of(pair * 2 * RIM, 2 * RIM), 2 * RIM)
        rima_ref[at, :] = jnp.concatenate([after0, after1], axis=0).astype(BF)
        rimb_ref[at, :] = jnp.concatenate([before0, before1], axis=0).astype(BF)
        return 0

    lax.fori_loop(0, CLS // 2, attend_back, 0)
    sums_ref[2:3, :] = jnp.sum(dq_ref[...].astype(F32), axis=0, keepdims=True)

    flat = tacc_ref[...].T
    lines = []
    for h in range(HEADS):
        part = flat[h * QN : (h + 1) * QN]
        for bit in range(6):
            turned = pltpu.roll(part, KN - (1 << bit), 1)
            part = jnp.where((qi >> bit) & 1 == 1, turned, part)
        lines.append(jnp.sum(part, axis=0, keepdims=True))
    tgrad_ref[...] = jnp.concatenate(lines, axis=0)


def finish_kernel(
    own_ref,
    fa_ref,
    fb_ref,
    dq_ref,
    dx1_ref,
    x_ref,
    wqkv_ref,
    vec_ref,
    po_ref,
    tok_ref,
    dqkv_ref,
    sums_ref,
):
    sums_ref[...] = jnp.zeros_like(sums_ref)

    def block(rc, _):
        own = jnp.concatenate([x_ref[4 * i + rc] for i in range(4)], axis=0)
        xp = dot(po_ref[...], own)
        xhat, rstd = normed(xp)
        at = pl.ds(pl.multiple_of(rc * 192, 192), 192)
        mine = own_ref[at, :]
        got_a = fa_ref[pl.ds(pl.multiple_of(rc * 160, 160), 160), :].astype(F32)
        got_b = fb_ref[pl.ds(pl.multiple_of(rc * 160, 160), 160), :].astype(F32)
        gap = jnp.zeros((QN - RIM, 512), F32)
        parts = []
        for i in range(4):
            a = jnp.concatenate([got_a[i * RIM : (i + 1) * RIM], gap], axis=0)
            b = jnp.concatenate([gap, got_b[i * RIM : (i + 1) * RIM]], axis=0)
            parts.append(mine[i * QN : (i + 1) * QN] + a + b)
        dkv = jnp.concatenate(parts, axis=0).astype(BF)
        dqkv = jnp.concatenate([dq_ref[at, :], dkv], axis=1)
        dqkv_ref[at, :] = dqkv
        dn = dot_nt(dqkv, wqkv_ref[...])
        gain = vec_ref[0:1, :]
        dx = dx1_ref[at, :] + norm_back(dn * gain, xhat, rstd)
        back = dot_tn(po_ref[...], dx.astype(BF)).astype(BF)
        for i in range(4):
            tok_ref[4 * i + rc] = back[48 * i : 48 * i + 48]
        sums_ref[0:1, :] += jnp.sum(dn * xhat, axis=0, keepdims=True)
        sums_ref[1:2, :] += jnp.sum(dn, axis=0, keepdims=True)
        sums_ref[3:4, :] += jnp.sum(dkv[:, 256:512].astype(F32), axis=0, keepdims=True)
        return 0

    lax.fori_loop(0, 4, block, 0)


EARLY = 896
LATE = 512


def widen(v):
    return jnp.concatenate([v, jnp.zeros((v.shape[0], 128 - v.shape[1]), F32)], axis=1)


def pack_kernel(wqkv_ref, wo_ref, wu_ref, wd_ref, vec_ref, out_ref):
    top = [wd_ref[8 * b : 8 * b + 8, :] for b in range(3)]
    top += [wo_ref[:, 0:128], wqkv_ref[:, 0:512]]
    low = [wu_ref[...], wo_ref[:, 128:256], wqkv_ref[:, 512:768], widen(vec_ref[...]), jnp.zeros((8, 128), F32)]
    both = jnp.concatenate([jnp.concatenate(top, axis=1), jnp.concatenate(low, axis=1)], axis=0)
    out_ref[...] = both.astype(BF)


def unpack(me, blocks, refs):
    wqkv_ref, wo_ref, wu_ref, wd_ref, vec_ref, fq, fo, fu, fd, fv = refs
    for index, block in enumerate(blocks):
        core, across = divmod(index, 4)
        for z in range(4):
            o = me ^ (core | (z << 1) | (across << 3))
            slab = block[z].astype(F32)
            at = pl.ds(pl.multiple_of(o * 8, 8), 8)
            for b in range(3):
                fd[pl.ds(pl.multiple_of(o * 24 + 8 * b, 8), 8), :] = slab[0:8, 256 * b : 256 * b + 256]
            fo[at, 0:128] = slab[0:8, 768:896]
            fo[at, 128:256] = slab[8:16, 768:896]
            fu[at, :] = slab[8:16, 0:768]
            fq[at, 0:512] = slab[0:8, 896:1408]
            fq[at, 512:768] = slab[8:16, 896:1152]
            fv[at, :] = slab[8:16, 1152:1280]
    wqkv_ref[...] = fq[...].astype(BF)
    wo_ref[...] = fo[...].astype(BF)
    wu_ref[...] = fu[...].astype(BF)
    wd_ref[...] = fd[...].astype(BF)
    vec_ref[...] = fv[...].T[0 : vec_ref.shape[0]]


def own_index():
    return lax.axis_index("maps") * 8 + lax.axis_index("band")


def layer_packed(
    sizes_ref, x_ref, xb_ref, xa_ref, cot_ref, b0, b1, b2, b3, b4, b5, b6, b7, table_ref, po_ref, pk_ref, *rest
):
    weights = rest[-10:]
    unpack(own_index(), (b0, b1, b2, b3, b4, b5, b6, b7), weights)
    outs, scratch = rest[:16], rest[18:-10]
    rest[16][...] = weights[0][...]
    rest[17][...] = weights[4][...]
    layer_kernel(
        sizes_ref, x_ref, xb_ref, xa_ref, cot_ref, *weights[:5], table_ref, po_ref, pk_ref, *outs, *scratch
    )


def frame_slot(me, o):
    m = me ^ o
    return (m & 1) * 16 + (m >> 3) * 4 + ((m >> 1) & 3)


def early_kernel(act_ref, dy_ref, a2_ref, dz_ref, mixed_ref, da_ref, out_ref, fd, fu, fo):
    fd[...] = dot_tn(act_ref[...], dy_ref[...])
    fu[...] = dot_tn(a2_ref[...], dz_ref[...])
    fo[...] = dot_tn(mixed_ref[...], da_ref[...])
    me = own_index()
    for o in range(32):
        at = slice(8 * o, 8 * o + 8)
        top = [fd[24 * o + 8 * b : 24 * o + 8 * b + 8, :] for b in range(3)] + [fo[at, 0:128]]
        low = [fu[at, :], fo[at, 128:256]]
        both = jnp.concatenate([jnp.concatenate(top, axis=1), jnp.concatenate(low, axis=1)], axis=0)
        out_ref[frame_slot(me, o)] = both.astype(BF)


def late_kernel(*refs):
    own, fa, fb, dq, dx1, x, wqkv, vec, po, a1, sums, zsum, tgrad = refs[:13]
    tok_ref, out_ref, dqkv, sums2, fq, fv = refs[13:]
    finish_kernel(own, fa, fb, dq, dx1, x, wqkv, vec, po, tok_ref, dqkv, sums2)
    fq[...] = dot_tn(a1[...], dqkv[...])
    lines = jnp.concatenate(
        [sums[...] + sums2[...]]
        + [zsum[:, 256 * i : 256 * i + 256] for i in range(3)]
        + [jnp.zeros((117, 256), F32)],
        axis=0,
    )
    fv[...] = lines.T
    table = tgrad[...]
    me = own_index()
    for o in range(32):
        at = slice(8 * o, 8 * o + 8)
        low = jnp.concatenate([fq[at, 512:768], fv[at, :], table], axis=1)
        out_ref[frame_slot(me, o)] = jnp.concatenate([fq[at, 0:512], low], axis=0).astype(BF)


def adam_kernel(*refs):
    w, first, second = refs[4:10], refs[10:16], refs[16:22]
    outs = refs[22:]
    total = refs[0][...] + sum(ref[...].astype(F32) for ref in refs[1:4])
    early, late = total[:, :EARLY], total[:, EARLY:]
    vrows = w[4].shape[1]
    grads = [
        jnp.concatenate([late[0:8], late[8:16, 0:256]], axis=1),
        jnp.concatenate([early[0:8, 768:896], early[8:16, 768:896]], axis=1),
        early[8:16, 0:768],
        jnp.concatenate([early[0:8, 256 * b : 256 * b + 256] for b in range(3)], axis=0),
        late[8:16, 256 : 256 + vrows],
        lax.dot_general(
            late[8:16, 384:512],
            table_slots(),
            (((1,), (1,)), ((), ())),
            precision=lax.Precision.HIGHEST,
            preferred_element_type=F32,
        ),
    ]
    row = lax.broadcasted_iota(jnp.int32, (8, 128), 0)
    lane = lax.broadcasted_iota(jnp.int32, (8, 128), 1)
    norms = jnp.zeros((8, 128), F32)
    for i in range(6):
        new_first, new_second, update = adam_parts(w[i][...], grads[i], first[i][...], second[i][...])
        outs[3 * i][...] = new_first
        outs[3 * i + 1][...] = new_second
        outs[3 * i + 2][...] = update
        for line, v in ((0, w[i][...]), (1, update)):
            if i == 4:
                sums = pltpu.roll(widen(jnp.sum(v * v, axis=0, keepdims=True)), 4, 1)
                norms = jnp.where((row == line) & (lane >= 4) & (lane < 4 + vrows), sums, norms)
            else:
                at = i if i < 4 else 4 + vrows
                norms = jnp.where((row == line) & (lane == at), jnp.sum(v * v), norms)
    outs[18][...] = norms


def step_kernel(mine_ref, a_ref, b_ref, c_ref, d_ref, *refs):
    w, update, outs = refs[0:6], refs[6:12], refs[12:]
    vrows = w[4].shape[1]
    total = a_ref[...] + b_ref[...] + c_ref[...] + d_ref[...]
    lane = lax.broadcasted_iota(jnp.int32, (8, 128), 1)
    norms = jnp.sqrt(jnp.where(lane == 4 + vrows, mine_ref[...], total))
    outs[6][...] = norms[0:1, 0:16]
    outs[7][...] = norms[1:2, 0:16]
    rate = LEARN_RATE * norms[0:1] / (norms[1:2] + RATIO_EPS)
    for i in range(6):
        if i == 4:
            r = pltpu.roll(rate, 124, 1)[:, 0:vrows]
        else:
            at = i if i < 4 else 4 + vrows
            r = rate[:, at : at + 1]
        outs[i][...] = w[i][...] - r * update[i][...]


def stack_kernel(*refs):
    for i, ref in enumerate(refs[:-1]):
        refs[-1][i] = ref[...]


def call(kernel, out_shape, scratch, *args, smem=0, flops=10**8, vmem=16):
    vm = pl.BlockSpec(memory_space=pltpu.VMEM)
    specs = [pl.BlockSpec(memory_space=pltpu.SMEM)] * smem + [vm] * (len(args) - smem)
    return pl.pallas_call(
        kernel,
        out_shape=out_shape,
        in_specs=specs,
        out_specs=jax.tree.map(lambda _: vm, out_shape),
        scratch_shapes=scratch,
        compiler_params=pltpu.CompilerParams(vmem_limit_bytes=vmem * 2**20),
        cost_estimate=pl.CostEstimate(flops=flops, bytes_accessed=10**6, transcendentals=0),
    )(*args)


def sds(shape, dtype=BF):
    return jax.ShapeDtypeStruct(shape, dtype)


def exchange_groups(maps, band):
    zbits = band.bit_length() - 2
    mbits = maps.bit_length() - 1
    cut = lambda lo, n: [(lo + i, min(2, n - i)) for i in range(0, n, 2)]
    return cut(1, zbits) + cut(1 + zbits, mbits) + [(0, 1)]


def swap(block, mask, count):
    return lax.ppermute(block, AXES, [(k, k ^ mask) for k in range(count)])


def frame_masks(groups):
    masks = [0]
    for lo, bits in groups:
        masks = [m ^ (d << lo) for d in range(1 << bits) for m in masks]
    return masks


def gather_all(slab, groups, count):
    block = slab[None]
    for lo, bits in groups:
        block = jnp.concatenate(
            [block] + [swap(block, d << lo, count) for d in range(1, 1 << bits)], axis=0
        )
    return block


def scatter_sum(grads, groups, count):
    for lo, bits in reversed(groups):
        grads = add_stage(grads, lo, bits, count)
    return grads[0]


def adam_parts(weight, grad, first, second):
    new_first = BETA_FIRST * first + (1.0 - BETA_FIRST) * grad
    new_second = BETA_SECOND * second + (1.0 - BETA_SECOND) * grad * grad
    update = (
        new_first
        / (1.0 - BETA_FIRST**STEP)
        / (jnp.sqrt(new_second / (1.0 - BETA_SECOND**STEP)) + ADAM_EPS)
        + DECAY_RATE * weight
    )
    return (new_first, new_second, update)


def squares_of(matrices, rowwise):
    return jnp.concatenate(
        [
            jnp.stack([jnp.sum(matrix * matrix) for matrix in matrices]),
            jnp.sum(rowwise * rowwise, axis=1),
        ]
    )


def layer_outputs():
    return (
        sds((16, 48, 256)),
        sds((768, 768)),
        sds((768, 256)),
        sds((768, 768)),
        sds((768, 256)),
        sds((768, 256)),
        sds((768, 256)),
        sds((768, 256)),
        sds((768, 256)),
        sds((768, 256), F32),
        sds((768, 512), F32),
        sds((CLS * RIM, 512)),
        sds((CLS * RIM, 512)),
        sds((HEADS, KN), F32),
        sds((8, 256), F32),
        sds((1, 768), F32),
    )


def layer_scratch():
    return [
        pltpu.VMEM((768, 256), F32),
        pltpu.VMEM((768, 256), BF),
        pltpu.VMEM((CLS * KN, 256), BF),
        pltpu.VMEM((CLS * KN, 256), BF),
        pltpu.VMEM((KN, 384), F32),
        pltpu.VMEM((CLS * KN, 384), F32),
        pltpu.VMEM((768, 256), BF),
        pltpu.VMEM((KN, 384), F32),
    ]


def packed_step(tokens_in, cotangent, map_sizes, weights, firsts, seconds):
    count = 32
    vrows = weights[4].shape[0]
    turn = lambda arrays: tuple(a.T if i == 4 else a for i, a in enumerate(arrays))
    weights, firsts, seconds = turn(weights), turn(firsts), turn(seconds)
    up = [(i, i + 1) for i in range(7)]
    down = [(i + 1, i) for i in range(7)]
    x_before = lax.ppermute(tokens_in[-12:], "band", up)
    x_after = lax.ppermute(tokens_in[:12], "band", down)

    slab = call(pack_kernel, sds((16, EARLY + LATE)), [], *weights[:5])
    column = call(
        stack_kernel,
        sds((4, 16, EARLY + LATE)),
        [],
        slab,
        *[swap(slab, d << 1, count) for d in (1, 2, 3)],
    )
    blocks = [column] + [swap(column, d << 3, count) for d in (1, 2, 3)]
    blocks += [swap(block, 1, count) for block in blocks]

    po = jnp.asarray(order_own(), BF)
    pk = jnp.asarray(order_keys(), BF)
    matrices = [(256, 768), (256, 256), (256, 768), (768, 256)]
    (
        layer_out, act, dy, dz, a2, mixed, da, a1, dq, dx1, own, rim_a, rim_b, tgrad, sums, zsum, big_qkv, vec,
    ) = call(
        layer_packed,
        layer_outputs() + (sds((256, 768)), sds((vrows, 256), F32)),
        layer_scratch()
        + [pltpu.VMEM(m, BF) for m in matrices]
        + [pltpu.VMEM((vrows, 256), F32)]
        + [pltpu.VMEM(m, F32) for m in matrices]
        + [pltpu.VMEM((256, 128), F32)],
        map_sizes, tokens_in, x_before, x_after, cotangent, *blocks, weights[5], po, pk,
        smem=1, flops=6 * 10**9, vmem=24,
    )
    from_prev = lax.ppermute(rim_a, "band", up)
    from_next = lax.ppermute(rim_b, "band", down)
    early = call(
        early_kernel,
        sds((count, 16, EARLY)),
        [pltpu.VMEM((768, 256), F32), pltpu.VMEM((256, 768), F32), pltpu.VMEM((256, 256), F32)],
        act, dy, a2, dz, mixed, da,
        flops=10**9,
    )
    tokens_grad, late = call(
        late_kernel,
        (sds((16, 48, 256)), sds((count, 16, LATE))),
        [
            pltpu.VMEM((768, 768), BF),
            pltpu.VMEM((8, 256), F32),
            pltpu.VMEM((256, 768), F32),
            pltpu.VMEM((256, 128), F32),
        ],
        own, from_prev, from_next, dq, dx1, tokens_in, big_qkv, vec, po, a1, sums, zsum, tgrad,
        flops=10**9,
    )
    early = add_stage(add_stage(early, 0, 1, count), 3, 2, count)
    late = add_stage(add_stage(late, 0, 1, count), 3, 2, count)
    grads = jnp.concatenate([early, late], axis=-1)
    low = grads.astype(BF)
    parts = [grads[0]] + [swap(low[d], d << 1, count) for d in (1, 2, 3)]

    shapes = [sds(w.shape, F32) for w in weights]
    moments = call(
        adam_kernel,
        tuple(shape for shape in shapes for _ in range(3)) + (sds((8, 128), F32),),
        [],
        *parts, *weights, *firsts, *seconds,
    )
    mine = moments[18]
    squares = mine + swap(mine, 1, count)
    squares = squares + swap(squares, 8, count) + swap(squares, 16, count) + swap(squares, 24, count)
    news = call(
        step_kernel,
        tuple(shapes) + (sds((1, 16), F32),) * 2,
        [],
        mine, squares, *[swap(squares, d << 1, count) for d in (1, 2, 3)], *weights, *moments[2:18:3],
    )
    results = [layer_out, tokens_grad]
    for i in range(6):
        three = (moments[3 * i], moments[3 * i + 1], news[i])
        results += [a.T for a in three] if i == 4 else three
    return tuple(results) + (news[6].reshape(16), news[7].reshape(16))


def add_stage(grads, lo, bits, count):
    low = grads.astype(BF).reshape((1 << bits, -1) + grads.shape[1:])
    total = grads.reshape(low.shape)[0].astype(F32)
    for d in range(1, 1 << bits):
        total = total + swap(low[d], d << lo, count).astype(F32)
    return total


def per_device(
    maps,
    band,
    tokens_in,
    cotangent,
    map_sizes,
    w_qkv,
    w_out,
    w_up,
    w_down,
    vectors,
    pos_table,
    first_qkv,
    second_qkv,
    first_out,
    second_out,
    first_up,
    second_up,
    first_down,
    second_down,
    first_vectors,
    second_vectors,
    first_table,
    second_table,
):
    if w_qkv.shape[0] == 8 and (maps, band) == (4, 8):
        return packed_step(
            tokens_in, cotangent, map_sizes,
            (w_qkv, w_out, w_up, w_down, vectors, pos_table),
            (first_qkv, first_out, first_up, first_down, first_vectors, first_table),
            (second_qkv, second_out, second_up, second_down, second_vectors, second_table),
        )
    count = maps * band
    rows = w_qkv.shape[0]
    vrows = vectors.shape[0]
    groups = exchange_groups(maps, band)
    masks = np.array(frame_masks(groups))
    inverse = np.argsort(masks)
    me = lax.axis_index(AXES)
    reach = 3 * DIL

    up = [(i, i + 1) for i in range(band - 1)]
    down = [(i + 1, i) for i in range(band - 1)]
    x_before = lax.ppermute(tokens_in[-reach:], "band", up)
    x_after = lax.ppermute(tokens_in[:reach], "band", down)

    def pack(qkv, out, upw, dnw, vec):
        dn = dnw.reshape(3, rows, 256).transpose(1, 0, 2).reshape(rows, 768)
        vt = jnp.pad(vec.T, ((0, 0), (0, 128 - vrows)))
        return jnp.concatenate([qkv, out, upw, dn, vt], axis=1)

    slab = pack(*(w.astype(BF) for w in (w_qkv, w_out, w_up, w_down, vectors)))
    block = gather_all(slab, groups, count)
    order = jnp.asarray(inverse, jnp.int32)[jnp.arange(count, dtype=jnp.int32) ^ me]
    whole = jnp.take(block, order, axis=0).reshape(256, -1)
    big_qkv = whole[:, 0:768]
    big_out = whole[:, 768:1024]
    big_up = whole[:, 1024:1792]
    big_down = (
        whole[:, 1792:2560].reshape(count, rows, 3, 256).transpose(0, 2, 1, 3).reshape(768, 256)
    )
    vec = whole[:, 2560 : 2560 + vrows].T.astype(F32)

    po = jnp.asarray(order_own(), BF)
    pk = jnp.asarray(order_keys(), BF)
    (
        layer_out,
        act,
        dy,
        dz,
        a2,
        mixed,
        da,
        a1,
        dq,
        dx1,
        own,
        rim_a,
        rim_b,
        table_grad,
        sums,
        zsum,
    ) = call(
        layer_kernel,
        layer_outputs(),
        layer_scratch(),
        map_sizes,
        tokens_in,
        x_before,
        x_after,
        cotangent,
        big_qkv,
        big_out,
        big_up,
        big_down,
        vec,
        pos_table,
        po,
        pk,
        smem=1,
        flops=6 * 10**9,
    )
    from_prev = lax.ppermute(rim_a, "band", up)
    from_next = lax.ppermute(rim_b, "band", down)
    grad_down = dot_tn(act, dy)
    grad_up = dot_tn(a2, dz)
    grad_out = dot_tn(mixed, da)
    tokens_grad, dqkv, sums2 = call(
        finish_kernel,
        (sds((16, 48, 256)), sds((768, 768)), sds((8, 256), F32)),
        [],
        own,
        from_prev,
        from_next,
        dq,
        dx1,
        tokens_in,
        big_qkv,
        vec,
        po,
    )
    grad_qkv = dot_tn(a1, dqkv)
    grad_vec = jnp.concatenate([sums + sums2, zsum.reshape(3, 256)], axis=0)

    packed = jnp.concatenate(
        [
            grad_qkv.reshape(count, rows, 768),
            grad_out.reshape(count, rows, 256),
            grad_up.reshape(count, rows, 768),
            grad_down.reshape(count, 3, rows, 256).transpose(0, 2, 1, 3).reshape(count, rows, 768),
            jnp.pad(grad_vec.T, ((0, 0), (0, 128 - vrows))).reshape(count, rows, 128),
        ],
        axis=2,
    )
    packed = jnp.take(packed, jnp.asarray(masks, jnp.int32) ^ me, axis=0)
    red = scatter_sum(packed, groups, count)
    red_qkv = red[:, 0:768]
    red_out = red[:, 768:1024]
    red_up = red[:, 1024:1792]
    red_down = red[:, 1792:2560].reshape(rows, 3, 256).transpose(1, 0, 2).reshape(3 * rows, 256)
    red_vec = red[:, 2560 : 2560 + vrows].T

    steps = np.arange(-3, 4)
    lanes = ((12 * steps[:, None] + steps[None, :]) % KN).reshape(-1)
    table_total = lax.psum(table_grad, AXES)[:, lanes]

    part_qkv = adam_parts(w_qkv, red_qkv, first_qkv, second_qkv)
    part_out = adam_parts(w_out, red_out, first_out, second_out)
    part_up = adam_parts(w_up, red_up, first_up, second_up)
    part_down = adam_parts(w_down, red_down, first_down, second_down)
    part_vec = adam_parts(vectors, red_vec, first_vectors, second_vectors)
    part_table = adam_parts(pos_table, table_total, first_table, second_table)
    local_weight_sq = squares_of((w_qkv, w_out, w_up, w_down), vectors)
    local_update_sq = squares_of((part_qkv[2], part_out[2], part_up[2], part_down[2]), part_vec[2])
    weight_sq, update_sq = lax.psum((local_weight_sq, local_update_sq), AXES)
    table_weight = jnp.sqrt(jnp.sum(pos_table * pos_table))
    table_update = jnp.sqrt(jnp.sum(part_table[2] * part_table[2]))
    weight_norms = jnp.concatenate([jnp.sqrt(weight_sq), table_weight[None]])
    update_norms = jnp.concatenate([jnp.sqrt(update_sq), table_update[None]])
    ratios = weight_norms / (update_norms + RATIO_EPS)
    next_qkv = w_qkv - LEARN_RATE * ratios[0] * part_qkv[2]
    next_out = w_out - LEARN_RATE * ratios[1] * part_out[2]
    next_up = w_up - LEARN_RATE * ratios[2] * part_up[2]
    next_down = w_down - LEARN_RATE * ratios[3] * part_down[2]
    next_vectors = vectors - LEARN_RATE * ratios[4 : 4 + vrows][:, None] * part_vec[2]
    next_table = pos_table - LEARN_RATE * ratios[4 + vrows] * part_table[2]
    return (
        layer_out,
        tokens_grad,
        part_qkv[0],
        part_qkv[1],
        next_qkv,
        part_out[0],
        part_out[1],
        next_out,
        part_up[0],
        part_up[1],
        next_up,
        part_down[0],
        part_down[1],
        next_down,
        part_vec[0],
        part_vec[1],
        next_vectors,
        part_table[0],
        part_table[1],
        next_table,
        weight_norms,
        update_norms,
    )


def solution(mesh):
    both = P(AXES, None)
    side = P(None, AXES)
    tall = P(AXES, None, None)
    copied = P()
    return jax.shard_map(
        functools.partial(per_device, mesh.shape["maps"], mesh.shape["band"]),
        mesh=mesh,
        in_specs=(tall, tall, P("maps", None))
        + (both,) * 4
        + (side, copied)
        + (both,) * 8
        + (side, side, copied, copied),
        out_specs=(tall, tall) + (both,) * 12 + (side,) * 3 + (copied,) * 5,
        check_vma=False,
    )
```

```python
import functools

import jax
import jax.numpy as jnp
import numpy as np
from jax import lax
from jax.experimental import pallas as pl
from jax.experimental.pallas import tpu as pltpu
from jax.sharding import PartitionSpec as P

HEADS = 8
WINDOW = 7
DIL = 4
STEP = 10
NORM_EPS = 1e-05
BETA_FIRST = 0.9
BETA_SECOND = 0.999
ADAM_EPS = 1e-06
DECAY_RATE = 0.01
LEARN_RATE = 0.2
RATIO_EPS = 1e-06
MASKED = -1e30
LOG2E = 1.4426950408889634
AXES = ("maps", "band")

BF = jnp.bfloat16
F32 = jnp.float32

CLS = DIL * DIL
QN = 48
KN = 128
RIM = 40


def dot(a, b):
    return lax.dot_general(a, b, (((1,), (0,)), ((), ())), preferred_element_type=F32)


def dot_nt(a, b):
    return lax.dot_general(a, b, (((1,), (1,)), ((), ())), preferred_element_type=F32)


def dot_tn(a, b):
    return lax.dot_general(a, b, (((0,), (0,)), ((), ())), preferred_element_type=F32)


def select(shape, source):
    o = lax.broadcasted_iota(jnp.int32, shape, 0)
    return (source(o) == lax.broadcasted_iota(jnp.int32, shape, 1)).astype(F32).astype(BF)


def own_source(o):
    cc = (o * 171) >> 13
    qr, qc = split12(o - QN * cc)
    return qr * 48 + qc * 4 + cc


def key_source(o):
    j = ((o & (KN - 1)) + 36) & (KN - 1)
    kr, kc = split12(j)
    return jnp.where(j < 120, kr * 48 + kc * 4 + (o >> 7), -1)


def normed(v):
    mean = jnp.mean(v, axis=-1, keepdims=True)
    cen = v - mean
    var = jnp.mean(cen * cen, axis=-1, keepdims=True)
    rstd = lax.rsqrt(var + NORM_EPS)
    return cen * rstd, rstd


def norm_back(g, xhat, rstd):
    m1 = jnp.mean(g, axis=-1, keepdims=True)
    m2 = jnp.mean(g * xhat, axis=-1, keepdims=True)
    return rstd * (g - m1 - xhat * m2)


def spread_heads(v, lane_head):
    zero = jnp.zeros_like(v)
    return jnp.concatenate([jnp.where(lane_head == h, v, zero) for h in range(HEADS)], axis=0)


def pick_heads(full, lane_head):
    out = jnp.where(lane_head == 0, full[0:QN], 0.0)
    for h in range(1, HEADS):
        out = out + jnp.where(lane_head == h, full[h * QN : (h + 1) * QN], 0.0)
    return out


def split12(v):
    q = (v * 43) >> 9
    return q, v - 12 * q


def table_slots():
    n = lax.broadcasted_iota(jnp.int32, (WINDOW * WINDOW, KN), 0)
    lane = lax.broadcasted_iota(jnp.int32, (WINDOW * WINDOW, KN), 1)
    nr = (n * 37) >> 8
    nc = n - 7 * nr
    return (((12 * (nr - 3) + nc - 3) & (KN - 1)) == lane).astype(F32)


def prep_kernel(sizes_ref, table_ref, x_ref, bias_ref, limits_ref, po_ref, pk_ref, xp_ref, xhat_ref, rstd_ref):
    po_ref[...] = select((4 * QN, 4 * 48), own_source)
    pk_ref[...] = select((4 * KN, 10 * 48), key_source)
    row = lax.broadcasted_iota(jnp.int32, (8, 128), 0)
    limits_ref[...] = jnp.where(row == 0, sizes_ref[0, 0] - lax.axis_index("band") * 16, sizes_ref[0, 1])

    slots = lax.dot_general(
        table_ref[...],
        table_slots(),
        (((1,), (0,)), ((), ())),
        precision=lax.Precision.HIGHEST,
        preferred_element_type=F32,
    )
    qi = lax.broadcasted_iota(jnp.int32, (QN, KN), 0)
    si = lax.broadcasted_iota(jnp.int32, (QN, KN), 1)
    ji = (si + 36) & (KN - 1)
    kr, kc = split12(ji)
    qr, qc = split12(qi)
    window = (jnp.abs(kc - qc) <= 3) & (jnp.abs(kr - qr - 3) <= 3) & (ji < 120)
    rows = []
    for h in range(HEADS):
        line = jnp.broadcast_to(slots[h : h + 1, :] * LOG2E, (QN, KN))
        line = pltpu.roll(line, 0, 1, stride=1, stride_axis=0)
        rows.append(jnp.where(window, line, MASKED))
    bias_ref[...] = jnp.concatenate(rows, axis=0).T

    def block(rc, _):
        at = pl.ds(pl.multiple_of(rc * 192, 192), 192)
        xp = dot(po_ref[...], jnp.concatenate([x_ref[4 * i + rc] for i in range(4)], axis=0))
        xp_ref[at, :] = xp
        xhat, rstd = normed(xp)
        xhat_ref[at, :] = xhat
        rstd_ref[at, :] = jnp.broadcast_to(rstd, (192, 128))
        return 0

    lax.fori_loop(0, 4, block, 0, unroll=2)


def halo_kernel(x_ref, xc_ref, xz_ref, pk_ref, xk_ref):
    odd = (lax.axis_index("band") & 1) == 1

    def block(rc, _):
        rows = [jnp.where(odd, xc_ref[4 + 4 * i + rc], xz_ref[4 + 4 * i + rc]) for i in range(3)]
        rows += [x_ref[4 * i + rc] for i in range(4)]
        rows += [jnp.where(odd, xz_ref[4 * i + rc], xc_ref[4 * i + rc]) for i in range(3)]
        xk = dot(pk_ref[...], jnp.concatenate(rows, axis=0))
        xk_ref[pl.ds(pl.multiple_of(rc * 512, 512), 512), :] = normed(xk)[0]
        return 0

    lax.fori_loop(0, 4, block, 0, unroll=2)


def project_kernel(xhat_ref, xk_ref, wqkv_ref, vec_ref, a1_ref, q_ref, k_ref, v_ref):
    def vrow(i):
        return vec_ref[i : i + 1, :]

    def block(rc, _):
        at = pl.ds(pl.multiple_of(rc * 192, 192), 192)
        a1 = (xhat_ref[at, :] * vrow(0) + vrow(1)).astype(BF)
        a1_ref[at, :] = a1
        q_ref[at, :] = (dot(a1, wqkv_ref[:, 0:256]) + vrow(2)).astype(BF)
        at = pl.ds(pl.multiple_of(rc * 512, 512), 512)
        a1k = (xk_ref[at, :] * vrow(0) + vrow(1)).astype(BF)
        k_ref[at, :] = dot(a1k, wqkv_ref[:, 256:512]).astype(BF)
        v_ref[at, :] = (dot(a1k, wqkv_ref[:, 512:768]) + vrow(3)).astype(BF)
        return 0

    lax.fori_loop(0, 4, block, 0, unroll=2)


def attend_kernel(limits_ref, bias_ref, q_ref, k_ref, v_ref, mixed_ref, p_ref):
    scale = 32 ** (-0.5)
    lane_head = lax.broadcasted_iota(jnp.int32, (QN, 256), 1) >> 5
    row0 = lax.axis_index("band") * 16
    height = limits_ref[0:1, 0:1]
    wide = limits_ref[1:2, 0:1]
    ks = lax.broadcasted_iota(jnp.int32, (KN, 384), 0)
    ql = lax.broadcasted_iota(jnp.int32, (KN, 384), 1)
    kj = (ks + 36) & (KN - 1)
    krow, kcol = split12(kj)
    qin = ql - 48 * ((ql * 171) >> 13)
    same = ks == qin

    def attend(k, _):
        rc = k >> 2
        cc = k & 3
        at_q = pl.ds(pl.multiple_of(k * QN, QN), QN)
        at_k = pl.ds(pl.multiple_of(k * KN, KN), KN)
        qbd = spread_heads(q_ref[at_q, :], lane_head)
        s = dot_nt(k_ref[at_k, :], qbd) * (scale * LOG2E) + bias_ref[...]
        r = krow * 4 + (rc - 12)
        c = kcol * 4 + cc
        okay = ((r >= -row0) & (r < height) & (c < wide)) | same
        s = jnp.where(okay, s, MASKED)
        top = jnp.max(s, axis=0, keepdims=True)
        e = jnp.exp2(s - top)
        p = e * (1.0 / jnp.sum(e, axis=0, keepdims=True))
        p_ref[at_k, :] = p
        full = dot_tn(p.astype(BF), v_ref[at_k, :])
        mixed_ref[at_q, :] = pick_heads(full, lane_head).astype(BF)
        return 0

    lax.fori_loop(0, CLS, attend, 0, unroll=4)


def feed_kernel(
    cot_ref,
    mixed_ref,
    xp_ref,
    q_ref,
    k_ref,
    v_ref,
    p_ref,
    wo_ref,
    wu_ref,
    wd_ref,
    vec_ref,
    po_ref,
    act_ref,
    dy_ref,
    dz_ref,
    a2_ref,
    da_ref,
    dx1_ref,
    x1_ref,
    own_ref,
    rimc_ref,
    rimz_ref,
    dsl_ref,
    tacc_ref,
    sums_ref,
    zsum_ref,
    dmix_ref,
):
    odd = (lax.axis_index("band") & 1) == 1
    scale = 32 ** (-0.5)
    lane_head = lax.broadcasted_iota(jnp.int32, (QN, 256), 1) >> 5

    def vrow(i):
        return vec_ref[i : i + 1, :]

    sums_ref[...] = jnp.zeros_like(sums_ref)
    zsum_ref[...] = jnp.zeros_like(zsum_ref)

    def feed(rc, _):
        at = pl.ds(pl.multiple_of(rc * 192, 192), 192)
        x1 = xp_ref[at, :] + (dot(mixed_ref[at, :], wo_ref[...]) + vrow(4))
        x1_ref[at, :] = x1
        xhat, rstd = normed(x1)
        a2 = (xhat * vrow(5) + vrow(6)).astype(BF)
        a2_ref[at, :] = a2
        bias = jnp.concatenate([vrow(8), vrow(9), vrow(10)], axis=1)
        z = dot(a2, wu_ref[...]) + bias
        c0 = 0.7978845608028654
        c1 = 0.044715
        z2 = z * z
        t = jnp.tanh(z * (c0 + c0 * c1 * z2))
        hz = 0.5 * z
        act_ref[at, :] = (hz + hz * t).astype(BF)
        dyf = dot(po_ref[...], jnp.concatenate([cot_ref[4 * i + rc] for i in range(4)], axis=0))
        dy = dyf.astype(BF)
        dy_ref[at, :] = dy
        slope = (0.5 + 0.5 * t) + (hz - hz * (t * t)) * (c0 + 3.0 * c0 * c1 * z2)
        dz = (dot_nt(dy, wd_ref[...]) * slope).astype(BF)
        dz_ref[at, :] = dz
        zsum_ref[...] += jnp.sum(dz.astype(F32), axis=0, keepdims=True)
        dn = dot_nt(dz, wu_ref[...])
        dx1 = dyf + norm_back(dn * vrow(5), xhat, rstd)
        dx1_ref[at, :] = dx1
        da = dx1.astype(BF)
        da_ref[at, :] = da
        dmix_ref[at, :] = dot_nt(da, wo_ref[...]).astype(BF)
        sums_ref[4:5, :] += jnp.sum(da.astype(F32), axis=0, keepdims=True)
        sums_ref[5:6, :] += jnp.sum(dn * xhat, axis=0, keepdims=True)
        sums_ref[6:7, :] += jnp.sum(dn, axis=0, keepdims=True)
        sums_ref[7:8, :] += jnp.sum(dyf, axis=0, keepdims=True)
        return 0

    lax.fori_loop(0, 4, feed, 0, unroll=2)

    tacc_ref[...] = jnp.zeros_like(tacc_ref)

    def back_class(k):
        at_q = pl.ds(pl.multiple_of(k * QN, QN), QN)
        at_k = pl.ds(pl.multiple_of(k * KN, KN), KN)
        qbd = spread_heads(q_ref[at_q, :], lane_head)
        dobd = spread_heads(dmix_ref[at_q, :], lane_head)
        p = p_ref[at_k, :]
        dp = dot_nt(v_ref[at_k, :], dobd)
        dv = dot(p.astype(BF), dobd)
        pdp = p * dp
        ds = pdp - p * jnp.sum(pdp, axis=0, keepdims=True)
        tacc_ref[...] += ds
        dsl = ds.astype(BF)
        dsl_ref[at_k, :] = dsl
        dk = dot(dsl, qbd) * scale
        own_ref[at_q, 0:256] = dk[0:QN]
        own_ref[at_q, 256:512] = dv[0:QN]
        after = jnp.concatenate([dk[QN : QN + RIM], dv[QN : QN + RIM]], axis=1)
        before = jnp.concatenate([dk[KN - RIM :], dv[KN - RIM :]], axis=1)
        return after, before

    def attend_back(pair, _):
        after0, before0 = back_class(pair * 2)
        after1, before1 = back_class(pair * 2 + 1)
        at = pl.ds(pl.multiple_of(pair * 2 * RIM, 2 * RIM), 2 * RIM)
        after = jnp.concatenate([after0, after1], axis=0)
        before = jnp.concatenate([before0, before1], axis=0)
        rimc_ref[at, :] = jnp.where(odd, before, after).astype(BF)
        rimz_ref[at, :] = jnp.where(odd, after, before).astype(BF)
        return 0

    lax.fori_loop(0, CLS // 2, attend_back, 0, unroll=2)


def early_grads(act_ref, dy_ref, a2_ref, dz_ref, mixed_ref, da_ref, fd, fu, fo):
    fd[...] = dot_tn(act_ref[...], dy_ref[...])
    fu[...] = dot_tn(a2_ref[...], dz_ref[...])
    fo[...] = dot_tn(mixed_ref[...], da_ref[...])


def window_kernel(
    x1_ref,
    act_ref,
    dsl_ref,
    k_ref,
    tacc_ref,
    a1_ref,
    wd_ref,
    wqkv_ref,
    vec_ref,
    po_ref,
    out_ref,
    dnq_ref,
    fwq_ref,
    tgrad_ref,
    qsum_ref,
    dq_ref,
):
    scale = 32 ** (-0.5)
    lane_head = lax.broadcasted_iota(jnp.int32, (QN, 256), 1) >> 5

    def query(k, _):
        at_q = pl.ds(pl.multiple_of(k * QN, QN), QN)
        at_k = pl.ds(pl.multiple_of(k * KN, KN), KN)
        dq = pick_heads(dot_tn(dsl_ref[at_k, :], k_ref[at_k, :]), lane_head) * scale
        dq_ref[at_q, :] = dq.astype(BF)
        return 0

    lax.fori_loop(0, CLS, query, 0, unroll=4)
    dq = dq_ref[...]
    qsum_ref[...] = jnp.sum(dq.astype(F32), axis=0, keepdims=True)
    fwq_ref[...] = dot_tn(a1_ref[...], dq)
    dnq_ref[...] = dot_nt(dq, wqkv_ref[:, 0:256])

    def result(rc, _):
        at = pl.ds(pl.multiple_of(rc * 192, 192), 192)
        res = x1_ref[at, :] + dot(act_ref[at, :], wd_ref[...]) + vec_ref[7:8, :]
        back = dot_tn(po_ref[...], res.astype(BF)).astype(BF)
        for i in range(4):
            out_ref[4 * i + rc] = back[48 * i : 48 * i + 48]
        return 0

    lax.fori_loop(0, 4, result, 0, unroll=2)

    flat = tacc_ref[...].T
    qi = lax.broadcasted_iota(jnp.int32, (QN, KN), 0)
    lines = []
    for h in range(HEADS):
        part = flat[h * QN : (h + 1) * QN]
        for bit in range(6):
            turned = pltpu.roll(part, KN - (1 << bit), 1)
            part = jnp.where((qi >> bit) & 1 == 1, turned, part)
        lines.append(jnp.sum(part, axis=0, keepdims=True))
    tgrad_ref[...] = jnp.concatenate(lines, axis=0)


def finish_kernel(
    own_ref,
    gotc_ref,
    gotz_ref,
    dnq_ref,
    dx1_ref,
    xhat_ref,
    rstd_ref,
    wqkv_ref,
    vec_ref,
    po_ref,
    a1_ref,
    tok_ref,
    fkv_ref,
    sums_ref,
    dkv_ref,
):
    odd = (lax.axis_index("band") & 1) == 1
    sums_ref[...] = jnp.zeros_like(sums_ref)

    def block(rc, _):
        at = pl.ds(pl.multiple_of(rc * 192, 192), 192)
        mine = own_ref[at, :]
        got_c = gotc_ref[pl.ds(pl.multiple_of(rc * 160, 160), 160), :].astype(F32)
        got_z = gotz_ref[pl.ds(pl.multiple_of(rc * 160, 160), 160), :].astype(F32)
        got_a = jnp.where(odd, got_c, got_z)
        got_b = jnp.where(odd, got_z, got_c)
        gap = jnp.zeros((QN - RIM, 512), F32)
        parts = []
        for i in range(4):
            a = jnp.concatenate([got_a[i * RIM : (i + 1) * RIM], gap], axis=0)
            b = jnp.concatenate([gap, got_b[i * RIM : (i + 1) * RIM]], axis=0)
            parts.append(mine[i * QN : (i + 1) * QN] + a + b)
        dkv = jnp.concatenate(parts, axis=0).astype(BF)
        dkv_ref[at, :] = dkv
        dn = dnq_ref[at, :] + dot_nt(dkv, wqkv_ref[:, 256:768])
        xhat = xhat_ref[at, :]
        dx = dx1_ref[at, :] + norm_back(dn * vec_ref[0:1, :], xhat, rstd_ref[at, 0:1])
        back = dot_tn(po_ref[...], dx.astype(BF)).astype(BF)
        for i in range(4):
            tok_ref[4 * i + rc] = back[48 * i : 48 * i + 48]
        sums_ref[0:1, :] += jnp.sum(dn * xhat, axis=0, keepdims=True)
        sums_ref[1:2, :] += jnp.sum(dn, axis=0, keepdims=True)
        sums_ref[3:4, :] += jnp.sum(dkv[:, 256:512].astype(F32), axis=0, keepdims=True)
        return 0

    lax.fori_loop(0, 4, block, 0, unroll=2)
    fkv_ref[...] = dot_tn(a1_ref[...], dkv_ref[...])


EARLY = 896
LATE = 512


def widen(v):
    return jnp.concatenate([v, jnp.zeros((v.shape[0], 128 - v.shape[1]), F32)], axis=1)


def pack(wqkv, wo, wu, wd, vec):
    pieces = [(wqkv, 0, 0), (wo, 0, 768), (wd, 0, 1024), (vec, 0, 1280)]
    pieces += [(wu, 8, 0), (wd, 0, 768), (wd, -8, 1024)]
    total = 0.0
    for p, row, lane in pieces:
        rows, lanes = p.shape
        zero = jnp.zeros((), F32)
        if rows == 24 and lane == 1024 and row == 0:
            p = lax.pad(p, zero, ((0, -16, 0), (0, 0, 0)))
            rows = 8
        elif rows == 24:
            p = lax.pad(p, zero, ((-8 + row, -8 - row, 0), (0, 0, 0)))
            row, rows = 8, 8
        total = total + lax.pad(p, zero, ((row, 16 - row - rows, 0), (lane, EARLY + LATE - lane - lanes, 0)))
    return total.astype(BF)


def own_index():
    return lax.axis_index("maps") * 8 + lax.axis_index("band")


def sorted_slabs(blocks):
    me = own_index()
    for index, block in enumerate(blocks):
        core, across = divmod(index, 4)
        for z in range(4):
            yield me ^ (core | (z << 1) | (across << 3)), block[z].astype(F32)


def project_packed(xhat_ref, xk_ref, b0, b1, b2, b3, b4, b5, b6, b7, *rest):
    outs, big_qkv, vec, fq, fv = rest[:4], *rest[4:]
    for o, slab in sorted_slabs((b0, b1, b2, b3, b4, b5, b6, b7)):
        at = pl.ds(pl.multiple_of(o * 8, 8), 8)
        fq[at, :] = slab[0:8, 0:768]
        fv[at, :] = slab[0:8, 1280:1408]
    big_qkv[...] = fq[...].astype(BF)
    vec[...] = fv[...].T[0 : vec.shape[0]]
    project_kernel(xhat_ref, xk_ref, big_qkv, vec, *outs)


def feed_packed(
    cot_ref, mixed_ref, xp_ref, q_ref, k_ref, v_ref, p_ref, vec_ref, po_ref, b0, b1, b2, b3, b4, b5, b6, b7, *rest
):
    outs, big_down, (dmix, big_out, big_up, fo, fu, fd) = rest[:14], rest[14], rest[15:]
    for o, slab in sorted_slabs((b0, b1, b2, b3, b4, b5, b6, b7)):
        at = pl.ds(pl.multiple_of(o * 8, 8), 8)
        for b, rows in enumerate((slab[0:8, 1024:1280], slab[8:16, 768:1024], slab[8:16, 1024:1280])):
            fd[pl.ds(pl.multiple_of(o * 24 + 8 * b, 8), 8), :] = rows
        fo[at, :] = slab[0:8, 768:1024]
        fu[at, :] = slab[8:16, 0:768]
    big_out[...] = fo[...].astype(BF)
    big_up[...] = fu[...].astype(BF)
    big_down[...] = fd[...].astype(BF)
    feed_kernel(
        cot_ref, mixed_ref, xp_ref, q_ref, k_ref, v_ref, p_ref, big_out, big_up, big_down, vec_ref, po_ref, *outs, dmix
    )


def frame_slot(me, o):
    m = me ^ o
    return (m & 1) * 16 + (m >> 3) * 4 + ((m >> 1) & 3)


def early_kernel(*refs):
    out_ref, fd, fu, fo = refs[6:]
    early_grads(*refs[:6], fd, fu, fo)
    me = own_index()
    for o in range(32):
        at = slice(8 * o, 8 * o + 8)
        top = [fd[24 * o + 8 * b : 24 * o + 8 * b + 8, :] for b in range(3)] + [fo[at, 0:128]]
        low = [fu[at, :], fo[at, 128:256]]
        both = jnp.concatenate([jnp.concatenate(top, axis=1), jnp.concatenate(low, axis=1)], axis=0)
        out_ref[frame_slot(me, o)] = both.astype(BF)


def qrow(line):
    return jnp.where(lax.broadcasted_iota(jnp.int32, (8, 256), 0) == 2, line, 0.0)


def late_kernel(*refs):
    sums, zsum, qsum, fwq, tgrad = refs[11:16]
    tok_ref, out_ref, fkv, sums2, dkv, fv = refs[16:]
    finish_kernel(*refs[:11], tok_ref, fkv, sums2, dkv)
    lines = jnp.concatenate(
        [sums[...] + sums2[...] + qrow(qsum[...])]
        + [zsum[:, 256 * i : 256 * i + 256] for i in range(3)]
        + [jnp.zeros((117, 256), F32)],
        axis=0,
    )
    fv[...] = lines.T
    table = tgrad[...]
    me = own_index()
    for o in range(32):
        at = slice(8 * o, 8 * o + 8)
        top = jnp.concatenate([fwq[at, :], fkv[at, 0:256]], axis=1)
        low = jnp.concatenate([fkv[at, 256:512], fv[at, :], table], axis=1)
        out_ref[frame_slot(me, o)] = jnp.concatenate([top, low], axis=0).astype(BF)


def adam_kernel(*refs):
    w, first, second = refs[4:10], refs[10:16], refs[16:22]
    outs = refs[22:]
    total = refs[0][...] + sum(ref[...].astype(F32) for ref in refs[1:4])
    early, late = total[:, :EARLY], total[:, EARLY:]
    vrows = w[4].shape[1]
    grads = [
        jnp.concatenate([late[0:8], late[8:16, 0:256]], axis=1),
        jnp.concatenate([early[0:8, 768:896], early[8:16, 768:896]], axis=1),
        early[8:16, 0:768],
        jnp.concatenate([early[0:8, 256 * b : 256 * b + 256] for b in range(3)], axis=0),
        late[8:16, 256 : 256 + vrows],
        lax.dot_general(
            late[8:16, 384:512],
            table_slots(),
            (((1,), (1,)), ((), ())),
            precision=lax.Precision.HIGHEST,
            preferred_element_type=F32,
        ),
    ]
    row = lax.broadcasted_iota(jnp.int32, (8, 128), 0)
    lane = lax.broadcasted_iota(jnp.int32, (8, 128), 1)
    norms = jnp.zeros((8, 128), F32)
    for i in range(6):
        new_first, new_second, update = adam_parts(w[i][...], grads[i], first[i][...], second[i][...])
        outs[3 * i][...] = new_first
        outs[3 * i + 1][...] = new_second
        outs[3 * i + 2][...] = update
        for line, v in ((0, w[i][...]), (1, update)):
            if i == 4:
                sums = pltpu.roll(widen(jnp.sum(v * v, axis=0, keepdims=True)), 4, 1)
                norms = jnp.where((row == line) & (lane >= 4) & (lane < 4 + vrows), sums, norms)
            else:
                at = i if i < 4 else 4 + vrows
                norms = jnp.where((row == line) & (lane == at), jnp.sum(v * v), norms)
    outs[18][...] = norms


def step_kernel(mine_ref, a_ref, b_ref, c_ref, d_ref, *refs):
    w, update, outs = refs[0:6], refs[6:12], refs[12:]
    vrows = w[4].shape[1]
    total = a_ref[...] + b_ref[...] + c_ref[...] + d_ref[...]
    lane = lax.broadcasted_iota(jnp.int32, (8, 128), 1)
    norms = jnp.sqrt(jnp.where(lane == 4 + vrows, mine_ref[...], total))
    outs[6][...] = norms[0:1, 0:16]
    outs[7][...] = norms[1:2, 0:16]
    rate = LEARN_RATE * norms[0:1] / (norms[1:2] + RATIO_EPS)
    for i in range(6):
        if i == 4:
            r = pltpu.roll(rate, 124, 1)[:, 0:vrows]
        else:
            at = i if i < 4 else 4 + vrows
            r = rate[:, at : at + 1]
        outs[i][...] = w[i][...] - r * update[i][...]


def stack_kernel(*refs):
    for i, ref in enumerate(refs[:4]):
        refs[4][i] = ref[...]


def call(kernel, out_shape, scratch, *args, smem=0, flops=10**8, vmem=16):
    vm = pl.BlockSpec(memory_space=pltpu.VMEM)
    specs = [pl.BlockSpec(memory_space=pltpu.SMEM)] * smem + [vm] * (len(args) - smem)
    return pl.pallas_call(
        kernel,
        out_shape=out_shape,
        in_specs=specs,
        out_specs=jax.tree.map(lambda _: vm, out_shape),
        scratch_shapes=scratch,
        compiler_params=pltpu.CompilerParams(vmem_limit_bytes=vmem * 2**20),
        cost_estimate=pl.CostEstimate(flops=flops, bytes_accessed=10**6, transcendentals=0),
    )(*args)


def sds(shape, dtype=BF):
    return jax.ShapeDtypeStruct(shape, dtype)


def exchange_groups(maps, band):
    zbits = band.bit_length() - 2
    mbits = maps.bit_length() - 1
    cut = lambda lo, n: [(lo + i, min(2, n - i)) for i in range(0, n, 2)]
    return cut(1, zbits) + cut(1 + zbits, mbits) + [(0, 1)]


def swap(block, mask, count):
    return lax.ppermute(block, AXES, [(k, k ^ mask) for k in range(count)])


def frame_masks(groups):
    masks = [0]
    for lo, bits in groups:
        masks = [m ^ (d << lo) for d in range(1 << bits) for m in masks]
    return masks


def gather_all(slab, groups, count):
    block = slab[None]
    for lo, bits in groups:
        block = jnp.concatenate(
            [block] + [swap(block, d << lo, count) for d in range(1, 1 << bits)], axis=0
        )
    return block


def scatter_sum(grads, groups, count):
    for lo, bits in reversed(groups):
        grads = add_stage(grads, lo, bits, count)
    return grads[0]


def adam_parts(weight, grad, first, second):
    new_first = BETA_FIRST * first + (1.0 - BETA_FIRST) * grad
    new_second = BETA_SECOND * second + (1.0 - BETA_SECOND) * grad * grad
    update = (
        new_first
        / (1.0 - BETA_FIRST**STEP)
        / (jnp.sqrt(new_second / (1.0 - BETA_SECOND**STEP)) + ADAM_EPS)
        + DECAY_RATE * weight
    )
    return (new_first, new_second, update)


def squares_of(matrices, rowwise):
    return jnp.concatenate(
        [
            jnp.stack([jnp.sum(matrix * matrix) for matrix in matrices]),
            jnp.sum(rowwise * rowwise, axis=1),
        ]
    )


def prep_outputs():
    return (
        sds((KN, 384), F32),
        sds((8, 128), jnp.int32),
        sds((4 * QN, 4 * 48)),
        sds((4 * KN, 10 * 48)),
        sds((768, 256), F32),
        sds((768, 256), F32),
        sds((768, 128), F32),
    )


def project_outputs():
    return (sds((768, 256)), sds((768, 256)), sds((CLS * KN, 256)), sds((CLS * KN, 256)))


def attend_outputs():
    return (sds((768, 256)), sds((CLS * KN, 384), F32))


def feed_outputs():
    return (
        sds((768, 768)),
        sds((768, 256)),
        sds((768, 768)),
        sds((768, 256)),
        sds((768, 256)),
        sds((768, 256), F32),
        sds((768, 256), F32),
        sds((768, 512), F32),
        sds((CLS * RIM, 512)),
        sds((CLS * RIM, 512)),
        sds((CLS * KN, 384)),
        sds((KN, 384), F32),
        sds((8, 256), F32),
        sds((1, 768), F32),
    )


def window_outputs():
    return (
        sds((16, 48, 256)),
        sds((768, 256), F32),
        sds((256, 256), F32),
        sds((HEADS, KN), F32),
        sds((1, 256), F32),
    )


def beside(block, band):
    touching = [(b, b + 1 if b % 2 else b - 1) for b in range(band)]
    return (
        lax.ppermute(block[0], "band", [(b, b ^ 1) for b in range(band)]),
        lax.ppermute(block[1], "band", [(b, to) for b, to in touching if 0 <= to < band]),
    )


def packed_step(tokens_in, cotangent, map_sizes, weights, firsts, seconds):
    count = 32
    vrows = weights[4].shape[0]
    turn = lambda arrays: tuple(a.T if i == 4 else a for i, a in enumerate(arrays))
    weights, firsts, seconds = turn(weights), turn(firsts), turn(seconds)
    slab = pack(*weights[:5])
    column = call(
        stack_kernel,
        sds((4, 16, EARLY + LATE)),
        [],
        slab,
        *[swap(slab, d << 1, count) for d in (1, 2, 3)],
        vmem=4,
    )
    column, x = lax.optimization_barrier((column, tokens_in))
    blocks = [column] + [swap(column, d << 3, count) for d in (1, 2, 3)]
    x_core, x_next = beside((x, x), 8)
    bias, limits, po, pk, xp, xhat, rstd = call(
        prep_kernel, prep_outputs(), [], map_sizes, weights[5], x, smem=1, flops=2 * 10**9, vmem=8
    )
    xk = call(halo_kernel, sds((CLS * KN, 256), F32), [], x, x_core, x_next, pk, flops=10**9, vmem=8)
    *far, xk = lax.optimization_barrier((*blocks[1:], xk))
    blocks = [blocks[0]] + far + [swap(block, 1, count) for block in [blocks[0]] + far]
    a1, queries, keys, values, big_qkv, vec = call(
        project_packed,
        project_outputs() + (sds((256, 768)), sds((vrows, 256), F32)),
        [pltpu.VMEM((256, 768), F32), pltpu.VMEM((256, 128), F32)],
        xhat, xk, *blocks,
        flops=10**9, vmem=8,
    )
    mixed, probs = call(
        attend_kernel, attend_outputs(), [], limits, bias, queries, keys, values, flops=3 * 10**9, vmem=8
    )
    (
        act, dy, dz, a2, da, dx1, x1, own, rim_c, rim_z, dsl, tacc, sums, zsum, big_down,
    ) = call(
        feed_packed,
        feed_outputs() + (sds((768, 256)),),
        [pltpu.VMEM((768, 256), BF), pltpu.VMEM((256, 256), BF), pltpu.VMEM((256, 768), BF)]
        + [pltpu.VMEM(m, F32) for m in ((256, 256), (256, 768), (768, 256))],
        cotangent, mixed, xp, queries, keys, values, probs, vec, po, *blocks,
        flops=4 * 10**9,
    )
    got_c, got_z = beside((rim_c, rim_z), 8)
    early = call(
        early_kernel,
        sds((count, 16, EARLY)),
        [pltpu.VMEM((768, 256), F32), pltpu.VMEM((256, 768), F32), pltpu.VMEM((256, 256), F32)],
        act, dy, a2, dz, mixed, da,
        flops=10**9,
    )
    early = add_stage(early, 0, 1, count)
    early, tacc = lax.optimization_barrier((early, tacc))
    layer_out, dnq, fwq, tgrad, qsum = call(
        window_kernel,
        window_outputs(),
        [pltpu.VMEM((768, 256), BF)],
        x1, act, dsl, keys, tacc, a1, big_down, big_qkv, vec, po,
        flops=3 * 10**9,
    )
    early = add_stage(early, 3, 2, count)
    early, own = lax.optimization_barrier((early, own))
    tokens_grad, late = call(
        late_kernel,
        (sds((16, 48, 256)), sds((count, 16, LATE))),
        [
            pltpu.VMEM((256, 512), F32),
            pltpu.VMEM((8, 256), F32),
            pltpu.VMEM((768, 512), BF),
            pltpu.VMEM((256, 128), F32),
        ],
        own, got_c, got_z, dnq, dx1, xhat, rstd, big_qkv, vec, po, a1, sums, zsum, qsum, fwq, tgrad,
        flops=10**9,
    )
    late = add_stage(add_stage(late, 0, 1, count), 3, 2, count)
    grads = jnp.concatenate([early, late], axis=-1)
    low = grads.astype(BF)
    parts = [grads[0]] + [swap(low[d], d << 1, count) for d in (1, 2, 3)]

    shapes = [sds(w.shape, F32) for w in weights]
    moments = call(
        adam_kernel,
        tuple(shape for shape in shapes for _ in range(3)) + (sds((8, 128), F32),),
        [],
        *parts, *weights, *firsts, *seconds,
    )
    mine = moments[18]
    squares = mine + swap(mine, 1, count)
    squares = squares + swap(squares, 8, count) + swap(squares, 16, count) + swap(squares, 24, count)
    news = call(
        step_kernel,
        tuple(shapes) + (sds((1, 16), F32),) * 2,
        [],
        mine, squares, *[swap(squares, d << 1, count) for d in (1, 2, 3)], *weights, *moments[2:18:3],
    )
    results = [layer_out, tokens_grad]
    for i in range(6):
        three = (moments[3 * i], moments[3 * i + 1], news[i])
        results += [a.T for a in three] if i == 4 else three
    return tuple(results) + (news[6].reshape(16), news[7].reshape(16))


def add_stage(grads, lo, bits, count):
    low = grads.astype(BF).reshape((1 << bits, -1) + grads.shape[1:])
    total = grads.reshape(low.shape)[0].astype(F32)
    for d in range(1, 1 << bits):
        total = total + swap(low[d], d << lo, count).astype(F32)
    return total


def per_device(
    maps,
    band,
    tokens_in,
    cotangent,
    map_sizes,
    w_qkv,
    w_out,
    w_up,
    w_down,
    vectors,
    pos_table,
    first_qkv,
    second_qkv,
    first_out,
    second_out,
    first_up,
    second_up,
    first_down,
    second_down,
    first_vectors,
    second_vectors,
    first_table,
    second_table,
):
    if w_qkv.shape[0] == 8 and (maps, band) == (4, 8):
        return packed_step(
            tokens_in, cotangent, map_sizes,
            (w_qkv, w_out, w_up, w_down, vectors, pos_table),
            (first_qkv, first_out, first_up, first_down, first_vectors, first_table),
            (second_qkv, second_out, second_up, second_down, second_vectors, second_table),
        )
    count = maps * band
    rows = w_qkv.shape[0]
    vrows = vectors.shape[0]
    groups = exchange_groups(maps, band)
    masks = np.array(frame_masks(groups))
    inverse = np.argsort(masks)
    me = lax.axis_index(AXES)
    x_core, x_next = beside((tokens_in, tokens_in), band)

    def pack(qkv, out, upw, dnw, vec):
        dn = dnw.reshape(3, rows, 256).transpose(1, 0, 2).reshape(rows, 768)
        vt = jnp.pad(vec.T, ((0, 0), (0, 128 - vrows)))
        return jnp.concatenate([qkv, out, upw, dn, vt], axis=1)

    slab = pack(*(w.astype(BF) for w in (w_qkv, w_out, w_up, w_down, vectors)))
    block = gather_all(slab, groups, count)
    order = jnp.asarray(inverse, jnp.int32)[jnp.arange(count, dtype=jnp.int32) ^ me]
    whole = jnp.take(block, order, axis=0).reshape(256, -1)
    big_qkv = whole[:, 0:768]
    big_out = whole[:, 768:1024]
    big_up = whole[:, 1024:1792]
    big_down = (
        whole[:, 1792:2560].reshape(count, rows, 3, 256).transpose(0, 2, 1, 3).reshape(768, 256)
    )
    vec = whole[:, 2560 : 2560 + vrows].T.astype(F32)

    bias, limits, po, pk, xp, xhat, rstd = call(
        prep_kernel, prep_outputs(), [], map_sizes, pos_table, tokens_in, smem=1, flops=2 * 10**9
    )
    xk = call(halo_kernel, sds((CLS * KN, 256), F32), [], tokens_in, x_core, x_next, pk, flops=10**9)
    a1, queries, keys, values = call(project_kernel, project_outputs(), [], xhat, xk, big_qkv, vec, flops=10**9)
    mixed, probs = call(attend_kernel, attend_outputs(), [], limits, bias, queries, keys, values, flops=3 * 10**9)
    act, dy, dz, a2, da, dx1, x1, own, rim_c, rim_z, dsl, tacc, sums, zsum = call(
        feed_kernel,
        feed_outputs(),
        [pltpu.VMEM((768, 256), BF)],
        cotangent, mixed, xp, queries, keys, values, probs, big_out, big_up, big_down, vec, po,
        flops=4 * 10**9,
    )
    got_c, got_z = beside((rim_c, rim_z), band)
    grad_down, grad_up, grad_out = call(
        early_grads,
        (sds((768, 256), F32), sds((256, 768), F32), sds((256, 256), F32)),
        [],
        act, dy, a2, dz, mixed, da,
        flops=10**9,
    )
    layer_out, dnq, fwq, table_grad, qsum = call(
        window_kernel,
        window_outputs(),
        [pltpu.VMEM((768, 256), BF)],
        x1, act, dsl, keys, tacc, a1, big_down, big_qkv, vec, po,
        flops=3 * 10**9,
    )
    tokens_grad, fkv, sums2 = call(
        finish_kernel,
        (sds((16, 48, 256)), sds((256, 512), F32), sds((8, 256), F32)),
        [pltpu.VMEM((768, 512), BF)],
        own, got_c, got_z, dnq, dx1, xhat, rstd, big_qkv, vec, po, a1,
        flops=10**9,
    )
    grad_qkv = jnp.concatenate([fwq, fkv], axis=1)
    sums2 = sums2.at[2:3].add(qsum)
    grad_vec = jnp.concatenate([sums + sums2, zsum.reshape(3, 256)], axis=0)

    packed = jnp.concatenate(
        [
            grad_qkv.reshape(count, rows, 768),
            grad_out.reshape(count, rows, 256),
            grad_up.reshape(count, rows, 768),
            grad_down.reshape(count, 3, rows, 256).transpose(0, 2, 1, 3).reshape(count, rows, 768),
            jnp.pad(grad_vec.T, ((0, 0), (0, 128 - vrows))).reshape(count, rows, 128),
        ],
        axis=2,
    )
    packed = jnp.take(packed, jnp.asarray(masks, jnp.int32) ^ me, axis=0)
    red = scatter_sum(packed, groups, count)
    red_qkv = red[:, 0:768]
    red_out = red[:, 768:1024]
    red_up = red[:, 1024:1792]
    red_down = red[:, 1792:2560].reshape(rows, 3, 256).transpose(1, 0, 2).reshape(3 * rows, 256)
    red_vec = red[:, 2560 : 2560 + vrows].T

    steps = np.arange(-3, 4)
    lanes = ((12 * steps[:, None] + steps[None, :]) % KN).reshape(-1)
    table_total = lax.psum(table_grad, AXES)[:, lanes]

    part_qkv = adam_parts(w_qkv, red_qkv, first_qkv, second_qkv)
    part_out = adam_parts(w_out, red_out, first_out, second_out)
    part_up = adam_parts(w_up, red_up, first_up, second_up)
    part_down = adam_parts(w_down, red_down, first_down, second_down)
    part_vec = adam_parts(vectors, red_vec, first_vectors, second_vectors)
    part_table = adam_parts(pos_table, table_total, first_table, second_table)
    local_weight_sq = squares_of((w_qkv, w_out, w_up, w_down), vectors)
    local_update_sq = squares_of((part_qkv[2], part_out[2], part_up[2], part_down[2]), part_vec[2])
    weight_sq, update_sq = lax.psum((local_weight_sq, local_update_sq), AXES)
    table_weight = jnp.sqrt(jnp.sum(pos_table * pos_table))
    table_update = jnp.sqrt(jnp.sum(part_table[2] * part_table[2]))
    weight_norms = jnp.concatenate([jnp.sqrt(weight_sq), table_weight[None]])
    update_norms = jnp.concatenate([jnp.sqrt(update_sq), table_update[None]])
    ratios = weight_norms / (update_norms + RATIO_EPS)
    next_qkv = w_qkv - LEARN_RATE * ratios[0] * part_qkv[2]
    next_out = w_out - LEARN_RATE * ratios[1] * part_out[2]
    next_up = w_up - LEARN_RATE * ratios[2] * part_up[2]
    next_down = w_down - LEARN_RATE * ratios[3] * part_down[2]
    next_vectors = vectors - LEARN_RATE * ratios[4 : 4 + vrows][:, None] * part_vec[2]
    next_table = pos_table - LEARN_RATE * ratios[4 + vrows] * part_table[2]
    return (
        layer_out,
        tokens_grad,
        part_qkv[0],
        part_qkv[1],
        next_qkv,
        part_out[0],
        part_out[1],
        next_out,
        part_up[0],
        part_up[1],
        next_up,
        part_down[0],
        part_down[1],
        next_down,
        part_vec[0],
        part_vec[1],
        next_vectors,
        part_table[0],
        part_table[1],
        next_table,
        weight_norms,
        update_norms,
    )


def solution(mesh):
    both = P(AXES, None)
    side = P(None, AXES)
    tall = P(AXES, None, None)
    copied = P()
    return jax.shard_map(
        functools.partial(per_device, mesh.shape["maps"], mesh.shape["band"]),
        mesh=mesh,
        in_specs=(tall, tall, P("maps", None))
        + (both,) * 4
        + (side, copied)
        + (both,) * 8
        + (side, side, copied, copied),
        out_specs=(tall, tall) + (both,) * 12 + (side,) * 3 + (copied,) * 5,
        check_vma=False,
    )
```

```python
import functools

import jax
import jax.numpy as jnp
import numpy as np
from jax import lax
from jax.experimental import pallas as pl
from jax.experimental.pallas import tpu as pltpu
from jax.sharding import PartitionSpec as P

HEADS = 8
WINDOW = 7
DIL = 4
STEP = 10
NORM_EPS = 1e-05
BETA_FIRST = 0.9
BETA_SECOND = 0.999
ADAM_EPS = 1e-06
DECAY_RATE = 0.01
LEARN_RATE = 0.2
RATIO_EPS = 1e-06
MASKED = -1e30
LOG2E = 1.4426950408889634
GELU0 = 0.7978845608028654
GELU1 = 0.044715
AXES = ("maps", "band")

BF = jnp.bfloat16
F32 = jnp.float32

CLS = DIL * DIL
QN = 48
KN = 128
RIM = 40


def dot(a, b):
    return lax.dot_general(a, b, (((1,), (0,)), ((), ())), preferred_element_type=F32)


def dot_nt(a, b):
    return lax.dot_general(a, b, (((1,), (1,)), ((), ())), preferred_element_type=F32)


def dot_tn(a, b):
    return lax.dot_general(a, b, (((0,), (0,)), ((), ())), preferred_element_type=F32)


def select(shape, source):
    o = lax.broadcasted_iota(jnp.int32, shape, 0)
    return (source(o) == lax.broadcasted_iota(jnp.int32, shape, 1)).astype(F32).astype(BF)


def own_source(o):
    cc = (o * 171) >> 13
    qr, qc = split12(o - QN * cc)
    return qr * 48 + qc * 4 + cc


def key_source(o):
    j = ((o & (KN - 1)) + 36) & (KN - 1)
    kr, kc = split12(j)
    return jnp.where(j < 120, kr * 48 + kc * 4 + (o >> 7), -1)


def normed(v):
    mean = jnp.mean(v, axis=-1, keepdims=True)
    cen = v - mean
    var = jnp.mean(cen * cen, axis=-1, keepdims=True)
    rstd = lax.rsqrt(var + NORM_EPS)
    return cen * rstd, rstd


def norm_back(g, xhat, rstd):
    m1 = jnp.mean(g, axis=-1, keepdims=True)
    m2 = jnp.mean(g * xhat, axis=-1, keepdims=True)
    return rstd * (g - m1 - xhat * m2)


def spread_heads(v, lane_head):
    zero = jnp.zeros_like(v)
    return jnp.concatenate([jnp.where(lane_head == h, v, zero) for h in range(HEADS)], axis=0)


def pick_heads(full, lane_head):
    out = jnp.where(lane_head == 0, full[0:QN], 0.0)
    for h in range(1, HEADS):
        out = out + jnp.where(lane_head == h, full[h * QN : (h + 1) * QN], 0.0)
    return out


def split12(v):
    q = (v * 43) >> 9
    return q, v - 12 * q


def table_slots():
    n = lax.broadcasted_iota(jnp.int32, (WINDOW * WINDOW, KN), 0)
    lane = lax.broadcasted_iota(jnp.int32, (WINDOW * WINDOW, KN), 1)
    nr = (n * 37) >> 8
    nc = n - 7 * nr
    return (((12 * (nr - 3) + nc - 3) & (KN - 1)) == lane).astype(F32)


def prep_kernel(
    sizes_ref, table_ref, x_ref, cot_ref, bias_ref, limits_ref, po_ref, pk_ref, xp_ref, xhat_ref, rstd_ref, dy_ref, dysum_ref
):
    po_ref[...] = select((4 * QN, 4 * 48), own_source)
    pk_ref[...] = select((4 * KN, 10 * 48), key_source)
    row = lax.broadcasted_iota(jnp.int32, (8, 128), 0)
    limits_ref[...] = jnp.where(row == 0, sizes_ref[0, 0] - lax.axis_index("band") * 16, sizes_ref[0, 1])

    slots = lax.dot_general(
        table_ref[...],
        table_slots(),
        (((1,), (0,)), ((), ())),
        precision=lax.Precision.HIGHEST,
        preferred_element_type=F32,
    )
    qi = lax.broadcasted_iota(jnp.int32, (QN, KN), 0)
    si = lax.broadcasted_iota(jnp.int32, (QN, KN), 1)
    ji = (si + 36) & (KN - 1)
    kr, kc = split12(ji)
    qr, qc = split12(qi)
    window = (jnp.abs(kc - qc) <= 3) & (jnp.abs(kr - qr - 3) <= 3) & (ji < 120)
    rows = []
    for h in range(HEADS):
        line = jnp.broadcast_to(slots[h : h + 1, :] * LOG2E, (QN, KN))
        line = pltpu.roll(line, 0, 1, stride=1, stride_axis=0)
        rows.append(jnp.where(window, line, MASKED))
    bias_ref[...] = jnp.concatenate(rows, axis=0).T

    def block(rc, _):
        at = pl.ds(pl.multiple_of(rc * 192, 192), 192)
        xp = dot(po_ref[...], jnp.concatenate([x_ref[4 * i + rc] for i in range(4)], axis=0))
        xp_ref[at, :] = xp
        xhat, rstd = normed(xp)
        xhat_ref[at, :] = xhat
        rstd_ref[at, :] = jnp.broadcast_to(rstd, (192, 128))
        dy = dot(po_ref[...], jnp.concatenate([cot_ref[4 * i + rc] for i in range(4)], axis=0))
        dy_ref[at, :] = dy.astype(BF)
        dysum_ref[...] += jnp.sum(dy, axis=0, keepdims=True)
        return 0

    dysum_ref[...] = jnp.zeros_like(dysum_ref)
    lax.fori_loop(0, 4, block, 0, unroll=4)


def halo_kernel(x_ref, xc_ref, xz_ref, pk_ref, xk_ref):
    odd = (lax.axis_index("band") & 1) == 1

    def block(rc, _):
        rows = [jnp.where(odd, xc_ref[4 + 4 * i + rc], xz_ref[4 + 4 * i + rc]) for i in range(3)]
        rows += [x_ref[4 * i + rc] for i in range(4)]
        rows += [jnp.where(odd, xz_ref[4 * i + rc], xc_ref[4 * i + rc]) for i in range(3)]
        xk = dot(pk_ref[...], jnp.concatenate(rows, axis=0))
        xk_ref[pl.ds(pl.multiple_of(rc * 512, 512), 512), :] = normed(xk)[0]
        return 0

    lax.fori_loop(0, 4, block, 0, unroll=2)


def project_kernel(xhat_ref, xk_ref, wqkv_ref, vec_ref, a1_ref, q_ref, k_ref, v_ref):
    def vrow(i):
        return vec_ref[i : i + 1, :]

    def block(rc, _):
        at = pl.ds(pl.multiple_of(rc * 192, 192), 192)
        a1 = (xhat_ref[at, :] * vrow(0) + vrow(1)).astype(BF)
        a1_ref[at, :] = a1
        q_ref[at, :] = (dot(a1, wqkv_ref[:, 0:256]) + vrow(2)).astype(BF)
        at = pl.ds(pl.multiple_of(rc * 512, 512), 512)
        a1k = (xk_ref[at, :] * vrow(0) + vrow(1)).astype(BF)
        k_ref[at, :] = dot(a1k, wqkv_ref[:, 256:512]).astype(BF)
        v_ref[at, :] = (dot(a1k, wqkv_ref[:, 512:768]) + vrow(3)).astype(BF)
        return 0

    lax.fori_loop(0, 4, block, 0, unroll=2)


def attend_kernel(limits_ref, bias_ref, q_ref, k_ref, v_ref, mixed_ref, p_ref):
    scale = 32 ** (-0.5)
    lane_head = lax.broadcasted_iota(jnp.int32, (QN, 256), 1) >> 5
    row0 = lax.axis_index("band") * 16
    height = limits_ref[0:1, 0:1]
    wide = limits_ref[1:2, 0:1]
    ks = lax.broadcasted_iota(jnp.int32, (KN, 384), 0)
    ql = lax.broadcasted_iota(jnp.int32, (KN, 384), 1)
    kj = (ks + 36) & (KN - 1)
    krow, kcol = split12(kj)
    qin = ql - 48 * ((ql * 171) >> 13)
    same = ks == qin

    def attend(k, _):
        rc = k >> 2
        cc = k & 3
        at_q = pl.ds(pl.multiple_of(k * QN, QN), QN)
        at_k = pl.ds(pl.multiple_of(k * KN, KN), KN)
        qbd = spread_heads(q_ref[at_q, :], lane_head)
        s = dot_nt(k_ref[at_k, :], qbd) * (scale * LOG2E) + bias_ref[...]
        r = krow * 4 + (rc - 12)
        c = kcol * 4 + cc
        okay = ((r >= -row0) & (r < height) & (c < wide)) | same
        s = jnp.where(okay, s, MASKED)
        top = jnp.max(s, axis=0, keepdims=True)
        e = jnp.exp2(s - top)
        p = e * (1.0 / jnp.sum(e, axis=0, keepdims=True))
        p_ref[at_k, :] = p
        full = dot_tn(p.astype(BF), v_ref[at_k, :])
        mixed_ref[at_q, :] = pick_heads(full, lane_head).astype(BF)
        return 0

    lax.fori_loop(0, CLS, attend, 0, unroll=CLS)


def feed_kernel(
    dy_ref,
    dysum_ref,
    mixed_ref,
    xp_ref,
    wo_ref,
    wu_ref,
    wd_ref,
    vec_ref,
    act_ref,
    dz_ref,
    a2_ref,
    da_ref,
    dx1_ref,
    x1_ref,
    dmix_ref,
    sums_ref,
    zsum_ref,
):
    def vrow(i):
        return vec_ref[i : i + 1, :]

    sums_ref[...] = jnp.zeros_like(sums_ref)
    sums_ref[7:8, :] = dysum_ref[...]
    zsum_ref[...] = jnp.zeros_like(zsum_ref)

    def feed(rc, _):
        at = pl.ds(pl.multiple_of(rc * 192, 192), 192)
        x1 = xp_ref[at, :] + (dot(mixed_ref[at, :], wo_ref[...]) + vrow(4))
        x1_ref[at, :] = x1
        xhat, rstd = normed(x1)
        a2 = (xhat * vrow(5) + vrow(6)).astype(BF)
        a2_ref[at, :] = a2
        dy = dy_ref[at, :]
        dn = jnp.zeros((192, 256), F32)
        for part in range(3):
            cols = slice(256 * part, 256 * part + 256)
            z = dot(a2, wu_ref[:, cols]) + vrow(8 + part)
            cube = (GELU0 * GELU1) * (z * z)
            up = 1.0 + jnp.tanh(z * (GELU0 + cube))
            hz = 0.5 * z
            act_ref[at, cols] = (hz * up).astype(BF)
            slope = up * (0.5 + hz * (2.0 - up) * (GELU0 + 3.0 * cube))
            dz = (dot_nt(dy, wd_ref[cols, :]) * slope).astype(BF)
            dz_ref[at, cols] = dz
            zsum_ref[:, cols] += jnp.sum(dz.astype(F32), axis=0, keepdims=True)
            dn = dn + dot_nt(dz, wu_ref[:, cols])
        dyf = dy.astype(F32)
        dx1 = dyf + norm_back(dn * vrow(5), xhat, rstd)
        dx1_ref[at, :] = dx1
        da = dx1.astype(BF)
        da_ref[at, :] = da
        dmix_ref[at, :] = dot_nt(da, wo_ref[...]).astype(BF)
        sums_ref[4:5, :] += jnp.sum(da.astype(F32), axis=0, keepdims=True)
        sums_ref[5:6, :] += jnp.sum(dn * xhat, axis=0, keepdims=True)
        sums_ref[6:7, :] += jnp.sum(dn, axis=0, keepdims=True)
        return 0

    lax.fori_loop(0, 4, feed, 0, unroll=4)


def back_kernel(
    q_ref,
    v_ref,
    p_ref,
    dmix_ref,
    own_ref,
    rimc_ref,
    rimz_ref,
    dsl_ref,
    tacc_ref,
):
    odd = (lax.axis_index("band") & 1) == 1
    scale = 32 ** (-0.5)
    lane_head = lax.broadcasted_iota(jnp.int32, (QN, 256), 1) >> 5
    tacc_ref[...] = jnp.zeros_like(tacc_ref)

    def back_class(k):
        at_q = pl.ds(pl.multiple_of(k * QN, QN), QN)
        at_k = pl.ds(pl.multiple_of(k * KN, KN), KN)
        qbd = spread_heads(q_ref[at_q, :], lane_head)
        dobd = spread_heads(dmix_ref[at_q, :], lane_head)
        p = p_ref[at_k, :]
        dp = dot_nt(v_ref[at_k, :], dobd)
        dv = dot(p.astype(BF), dobd)
        pdp = p * dp
        ds = pdp - p * jnp.sum(pdp, axis=0, keepdims=True)
        tacc_ref[...] += ds
        dsl = ds.astype(BF)
        dsl_ref[at_k, :] = dsl
        dk = dot(dsl, qbd) * scale
        own_ref[at_q, 0:256] = dk[0:QN]
        own_ref[at_q, 256:512] = dv[0:QN]
        after = jnp.concatenate([dk[QN : QN + RIM], dv[QN : QN + RIM]], axis=1)
        before = jnp.concatenate([dk[KN - RIM :], dv[KN - RIM :]], axis=1)
        return after, before

    def attend_back(pair, _):
        after0, before0 = back_class(pair * 2)
        after1, before1 = back_class(pair * 2 + 1)
        at = pl.ds(pl.multiple_of(pair * 2 * RIM, 2 * RIM), 2 * RIM)
        after = jnp.concatenate([after0, after1], axis=0)
        before = jnp.concatenate([before0, before1], axis=0)
        rimc_ref[at, :] = jnp.where(odd, before, after).astype(BF)
        rimz_ref[at, :] = jnp.where(odd, after, before).astype(BF)
        return 0

    lax.fori_loop(0, CLS // 2, attend_back, 0, unroll=8)


def early_grads(act_ref, dy_ref, a2_ref, dz_ref, mixed_ref, da_ref, fd, fu, fo):
    fd[...] = dot_tn(act_ref[...], dy_ref[...])
    fu[...] = dot_tn(a2_ref[...], dz_ref[...])
    fo[...] = dot_tn(mixed_ref[...], da_ref[...])


def window_kernel(
    x1_ref,
    act_ref,
    dsl_ref,
    k_ref,
    tacc_ref,
    a1_ref,
    wd_ref,
    wqkv_ref,
    vec_ref,
    po_ref,
    out_ref,
    dnq_ref,
    fwq_ref,
    tgrad_ref,
    qsum_ref,
    dq_ref,
):
    scale = 32 ** (-0.5)
    lane_head = lax.broadcasted_iota(jnp.int32, (QN, 256), 1) >> 5

    def query(k, _):
        at_q = pl.ds(pl.multiple_of(k * QN, QN), QN)
        at_k = pl.ds(pl.multiple_of(k * KN, KN), KN)
        dq = pick_heads(dot_tn(dsl_ref[at_k, :], k_ref[at_k, :]), lane_head) * scale
        dq_ref[at_q, :] = dq.astype(BF)
        return 0

    lax.fori_loop(0, CLS, query, 0, unroll=16)
    dq = dq_ref[...]
    qsum_ref[...] = jnp.sum(dq.astype(F32), axis=0, keepdims=True)
    fwq_ref[...] = dot_tn(a1_ref[...], dq)
    dnq_ref[...] = dot_nt(dq, wqkv_ref[:, 0:256])

    def result(rc, _):
        at = pl.ds(pl.multiple_of(rc * 192, 192), 192)
        res = x1_ref[at, :] + dot(act_ref[at, :], wd_ref[...]) + vec_ref[7:8, :]
        back = dot_tn(po_ref[...], res.astype(BF)).astype(BF)
        for i in range(4):
            out_ref[4 * i + rc] = back[48 * i : 48 * i + 48]
        return 0

    lax.fori_loop(0, 4, result, 0, unroll=2)

    flat = tacc_ref[...].T
    qi = lax.broadcasted_iota(jnp.int32, (QN, KN), 0)
    lines = []
    for h in range(HEADS):
        part = flat[h * QN : (h + 1) * QN]
        for bit in range(6):
            turned = pltpu.roll(part, KN - (1 << bit), 1)
            part = jnp.where((qi >> bit) & 1 == 1, turned, part)
        lines.append(jnp.sum(part, axis=0, keepdims=True))
    tgrad_ref[...] = jnp.concatenate(lines, axis=0)


def finish_kernel(
    own_ref,
    gotc_ref,
    gotz_ref,
    dnq_ref,
    xhat_ref,
    wqkv_ref,
    a1_ref,
    dn_ref,
    fkv_ref,
    sums_ref,
    dkv_ref,
):
    odd = (lax.axis_index("band") & 1) == 1
    sums_ref[...] = jnp.zeros_like(sums_ref)

    def block(rc, _):
        at = pl.ds(pl.multiple_of(rc * 192, 192), 192)
        mine = own_ref[at, :]
        got_c = gotc_ref[pl.ds(pl.multiple_of(rc * 160, 160), 160), :].astype(F32)
        got_z = gotz_ref[pl.ds(pl.multiple_of(rc * 160, 160), 160), :].astype(F32)
        got_a = jnp.where(odd, got_c, got_z)
        got_b = jnp.where(odd, got_z, got_c)
        gap = jnp.zeros((QN - RIM, 512), F32)
        parts = []
        for i in range(4):
            a = jnp.concatenate([got_a[i * RIM : (i + 1) * RIM], gap], axis=0)
            b = jnp.concatenate([gap, got_b[i * RIM : (i + 1) * RIM]], axis=0)
            parts.append(mine[i * QN : (i + 1) * QN] + a + b)
        dkv = jnp.concatenate(parts, axis=0).astype(BF)
        dkv_ref[at, :] = dkv
        dn = dnq_ref[at, :] + dot_nt(dkv, wqkv_ref[:, 256:768])
        dn_ref[at, :] = dn
        sums_ref[0:1, :] += jnp.sum(dn * xhat_ref[at, :], axis=0, keepdims=True)
        sums_ref[1:2, :] += jnp.sum(dn, axis=0, keepdims=True)
        sums_ref[3:4, :] += jnp.sum(dkv[:, 256:512].astype(F32), axis=0, keepdims=True)
        return 0

    lax.fori_loop(0, 4, block, 0, unroll=4)
    fkv_ref[...] = dot_tn(a1_ref[...], dkv_ref[...])


def input_kernel(dn_ref, dx1_ref, xhat_ref, rstd_ref, vec_ref, po_ref, tok_ref):
    def block(rc, _):
        at = pl.ds(pl.multiple_of(rc * 192, 192), 192)
        dx = dx1_ref[at, :] + norm_back(dn_ref[at, :] * vec_ref[0:1, :], xhat_ref[at, :], rstd_ref[at, 0:1])
        back = dot_tn(po_ref[...], dx.astype(BF)).astype(BF)
        for i in range(4):
            tok_ref[4 * i + rc] = back[48 * i : 48 * i + 48]
        return 0

    lax.fori_loop(0, 4, block, 0, unroll=4)


EARLY = 896
LATE = 512


def widen(v):
    return jnp.concatenate([v, jnp.zeros((v.shape[0], 128 - v.shape[1]), F32)], axis=1)


def pack(wqkv, wo, wu, wd, vec):
    pieces = [(wqkv, 0, 0), (wo, 0, 768), (wd, 0, 1024), (vec, 0, 1280)]
    pieces += [(wu, 8, 0), (wd, 0, 768), (wd, -8, 1024)]
    total = 0.0
    for p, row, lane in pieces:
        rows, lanes = p.shape
        zero = jnp.zeros((), F32)
        if rows == 24 and lane == 1024 and row == 0:
            p = lax.pad(p, zero, ((0, -16, 0), (0, 0, 0)))
            rows = 8
        elif rows == 24:
            p = lax.pad(p, zero, ((-8 + row, -8 - row, 0), (0, 0, 0)))
            row, rows = 8, 8
        total = total + lax.pad(p, zero, ((row, 16 - row - rows, 0), (lane, EARLY + LATE - lane - lanes, 0)))
    return total.astype(BF)


def own_index():
    return lax.axis_index("maps") * 8 + lax.axis_index("band")


def sorted_slabs(blocks):
    me = own_index()
    for index, block in enumerate(blocks):
        core, across = divmod(index, 4)
        for z in range(4):
            yield me ^ (core | (z << 1) | (across << 3)), block[z].astype(F32)


def project_packed(xhat_ref, xk_ref, b0, b1, b2, b3, b4, b5, b6, b7, *rest):
    outs, big_qkv, vec, fq, fv = rest[:4], *rest[4:]
    for o, slab in sorted_slabs((b0, b1, b2, b3, b4, b5, b6, b7)):
        at = pl.ds(pl.multiple_of(o * 8, 8), 8)
        fq[at, :] = slab[0:8, 0:768]
        fv[at, :] = slab[0:8, 1280:1408]
    big_qkv[...] = fq[...].astype(BF)
    vec[...] = fv[...].T[0 : vec.shape[0]]
    project_kernel(xhat_ref, xk_ref, big_qkv, vec, *outs)


def feed_packed(dy_ref, dysum_ref, mixed_ref, xp_ref, vec_ref, b0, b1, b2, b3, b4, b5, b6, b7, *rest):
    outs, big_down, (big_out, big_up, fo, fu, fd) = rest[:9], rest[9], rest[10:]
    for o, slab in sorted_slabs((b0, b1, b2, b3, b4, b5, b6, b7)):
        at = pl.ds(pl.multiple_of(o * 8, 8), 8)
        for b, rows in enumerate((slab[0:8, 1024:1280], slab[8:16, 768:1024], slab[8:16, 1024:1280])):
            fd[pl.ds(pl.multiple_of(o * 24 + 8 * b, 8), 8), :] = rows
        fo[at, :] = slab[0:8, 768:1024]
        fu[at, :] = slab[8:16, 0:768]
    big_out[...] = fo[...].astype(BF)
    big_up[...] = fu[...].astype(BF)
    big_down[...] = fd[...].astype(BF)
    feed_kernel(dy_ref, dysum_ref, mixed_ref, xp_ref, big_out, big_up, big_down, vec_ref, *outs)


def frame_slot(me, o):
    m = me ^ o
    return (m & 1) * 16 + (m >> 3) * 4 + ((m >> 1) & 3)


def early_kernel(*refs):
    out_ref, fd, fu, fo = refs[6:]
    early_grads(*refs[:6], fd, fu, fo)
    me = own_index()
    for o in range(32):
        at = slice(8 * o, 8 * o + 8)
        top = [fd[24 * o + 8 * b : 24 * o + 8 * b + 8, :] for b in range(3)] + [fo[at, 0:128]]
        low = [fu[at, :], fo[at, 128:256]]
        both = jnp.concatenate([jnp.concatenate(top, axis=1), jnp.concatenate(low, axis=1)], axis=0)
        out_ref[frame_slot(me, o)] = both.astype(BF)


def qrow(line):
    return jnp.where(lax.broadcasted_iota(jnp.int32, (8, 256), 0) == 2, line, 0.0)


def late_kernel(*refs):
    sums, zsum, qsum, fwq, tgrad = refs[7:12]
    dn_ref, out_ref, fkv, sums2, dkv, fv = refs[12:]
    finish_kernel(*refs[:7], dn_ref, fkv, sums2, dkv)
    lines = jnp.concatenate(
        [sums[...] + sums2[...] + qrow(qsum[...])]
        + [zsum[:, 256 * i : 256 * i + 256] for i in range(3)]
        + [jnp.zeros((117, 256), F32)],
        axis=0,
    )
    fv[...] = lines.T
    table = tgrad[...]
    me = own_index()
    for o in range(32):
        at = slice(8 * o, 8 * o + 8)
        top = jnp.concatenate([fwq[at, :], fkv[at, 0:256]], axis=1)
        low = jnp.concatenate([fkv[at, 256:512], fv[at, :], table], axis=1)
        out_ref[frame_slot(me, o)] = jnp.concatenate([top, low], axis=0).astype(BF)


def adam_kernel(*refs):
    w, first, second = refs[4:10], refs[10:16], refs[16:22]
    outs = refs[22:]
    total = refs[0][...] + sum(ref[...].astype(F32) for ref in refs[1:4])
    early, late = total[:, :EARLY], total[:, EARLY:]
    vrows = w[4].shape[1]
    grads = [
        jnp.concatenate([late[0:8], late[8:16, 0:256]], axis=1),
        jnp.concatenate([early[0:8, 768:896], early[8:16, 768:896]], axis=1),
        early[8:16, 0:768],
        jnp.concatenate([early[0:8, 256 * b : 256 * b + 256] for b in range(3)], axis=0),
        late[8:16, 256 : 256 + vrows],
        lax.dot_general(
            late[8:16, 384:512],
            table_slots(),
            (((1,), (1,)), ((), ())),
            precision=lax.Precision.HIGHEST,
            preferred_element_type=F32,
        ),
    ]
    row = lax.broadcasted_iota(jnp.int32, (8, 128), 0)
    lane = lax.broadcasted_iota(jnp.int32, (8, 128), 1)
    norms = jnp.zeros((8, 128), F32)
    for i in range(6):
        new_first, new_second, update = adam_parts(w[i][...], grads[i], first[i][...], second[i][...])
        outs[3 * i][...] = new_first
        outs[3 * i + 1][...] = new_second
        outs[3 * i + 2][...] = update
        for line, v in ((0, w[i][...]), (1, update)):
            if i == 4:
                sums = pltpu.roll(widen(jnp.sum(v * v, axis=0, keepdims=True)), 4, 1)
                norms = jnp.where((row == line) & (lane >= 4) & (lane < 4 + vrows), sums, norms)
            else:
                at = i if i < 4 else 4 + vrows
                norms = jnp.where((row == line) & (lane == at), jnp.sum(v * v), norms)
    outs[18][...] = norms


def step_kernel(mine_ref, a_ref, b_ref, c_ref, d_ref, *refs):
    w, update, outs = refs[0:6], refs[6:12], refs[12:]
    vrows = w[4].shape[1]
    total = a_ref[...] + b_ref[...] + c_ref[...] + d_ref[...]
    lane = lax.broadcasted_iota(jnp.int32, (8, 128), 1)
    norms = jnp.sqrt(jnp.where(lane == 4 + vrows, mine_ref[...], total))
    outs[6][...] = norms[0:1, 0:16]
    outs[7][...] = norms[1:2, 0:16]
    rate = LEARN_RATE * norms[0:1] / (norms[1:2] + RATIO_EPS)
    for i in range(6):
        if i == 4:
            r = pltpu.roll(rate, 124, 1)[:, 0:vrows]
        else:
            at = i if i < 4 else 4 + vrows
            r = rate[:, at : at + 1]
        outs[i][...] = w[i][...] - r * update[i][...]


def stack_kernel(*refs):
    for i, ref in enumerate(refs[:4]):
        refs[4][i] = ref[...]


def call(kernel, out_shape, scratch, *args, smem=0, flops=10**8, vmem=16):
    vm = pl.BlockSpec(memory_space=pltpu.VMEM)
    specs = [pl.BlockSpec(memory_space=pltpu.SMEM)] * smem + [vm] * (len(args) - smem)
    return pl.pallas_call(
        kernel,
        out_shape=out_shape,
        in_specs=specs,
        out_specs=jax.tree.map(lambda _: vm, out_shape),
        scratch_shapes=scratch,
        compiler_params=pltpu.CompilerParams(vmem_limit_bytes=vmem * 2**20),
        cost_estimate=pl.CostEstimate(flops=flops, bytes_accessed=10**6, transcendentals=0),
    )(*args)


def sds(shape, dtype=BF):
    return jax.ShapeDtypeStruct(shape, dtype)


def exchange_groups(maps, band):
    zbits = band.bit_length() - 2
    mbits = maps.bit_length() - 1
    cut = lambda lo, n: [(lo + i, min(2, n - i)) for i in range(0, n, 2)]
    return cut(1, zbits) + cut(1 + zbits, mbits) + [(0, 1)]


def swap(block, mask, count):
    return lax.ppermute(block, AXES, [(k, k ^ mask) for k in range(count)])


def frame_masks(groups):
    masks = [0]
    for lo, bits in groups:
        masks = [m ^ (d << lo) for d in range(1 << bits) for m in masks]
    return masks


def gather_all(slab, groups, count):
    block = slab[None]
    for lo, bits in groups:
        block = jnp.concatenate(
            [block] + [swap(block, d << lo, count) for d in range(1, 1 << bits)], axis=0
        )
    return block


def scatter_sum(grads, groups, count):
    for lo, bits in reversed(groups):
        grads = add_stage(grads, lo, bits, count)
    return grads[0]


def adam_parts(weight, grad, first, second):
    new_first = BETA_FIRST * first + (1.0 - BETA_FIRST) * grad
    new_second = BETA_SECOND * second + (1.0 - BETA_SECOND) * grad * grad
    update = (
        new_first
        / (1.0 - BETA_FIRST**STEP)
        / (jnp.sqrt(new_second / (1.0 - BETA_SECOND**STEP)) + ADAM_EPS)
        + DECAY_RATE * weight
    )
    return (new_first, new_second, update)


def squares_of(matrices, rowwise):
    return jnp.concatenate(
        [
            jnp.stack([jnp.sum(matrix * matrix) for matrix in matrices]),
            jnp.sum(rowwise * rowwise, axis=1),
        ]
    )


def prep_outputs():
    return (
        sds((KN, 384), F32),
        sds((8, 128), jnp.int32),
        sds((4 * QN, 4 * 48)),
        sds((4 * KN, 10 * 48)),
        sds((768, 256), F32),
        sds((768, 256), F32),
        sds((768, 128), F32),
        sds((768, 256)),
        sds((1, 256), F32),
    )


def project_outputs():
    return (sds((768, 256)), sds((768, 256)), sds((CLS * KN, 256)), sds((CLS * KN, 256)))


def attend_outputs():
    return (sds((768, 256)), sds((CLS * KN, 384), F32))


def feed_outputs():
    return (
        sds((768, 768)),
        sds((768, 768)),
        sds((768, 256)),
        sds((768, 256)),
        sds((768, 256), F32),
        sds((768, 256), F32),
        sds((768, 256)),
        sds((8, 256), F32),
        sds((1, 768), F32),
    )


def back_outputs():
    return (
        sds((768, 512), F32),
        sds((CLS * RIM, 512)),
        sds((CLS * RIM, 512)),
        sds((CLS * KN, 384)),
        sds((KN, 384), F32),
    )


def window_outputs():
    return (
        sds((16, 48, 256)),
        sds((768, 256), F32),
        sds((256, 256), F32),
        sds((HEADS, KN), F32),
        sds((1, 256), F32),
    )


def beside(block, band):
    touching = [(b, b + 1 if b % 2 else b - 1) for b in range(band)]
    return (
        lax.ppermute(block[0], "band", [(b, b ^ 1) for b in range(band)]),
        lax.ppermute(block[1], "band", [(b, to) for b, to in touching if 0 <= to < band]),
    )


def packed_step(tokens_in, cotangent, map_sizes, weights, firsts, seconds):
    count = 32
    vrows = weights[4].shape[0]
    turn = lambda arrays: tuple(a.T if i == 4 else a for i, a in enumerate(arrays))
    weights, firsts, seconds = turn(weights), turn(firsts), turn(seconds)
    slab = pack(*weights[:5])
    column = call(
        stack_kernel,
        sds((4, 16, EARLY + LATE)),
        [],
        slab,
        *[swap(slab, d << 1, count) for d in (1, 2, 3)],
        vmem=4,
    )
    column, x = lax.optimization_barrier((column, tokens_in))
    blocks = [column] + [swap(column, d << 3, count) for d in (1, 2, 3)]
    x_core, x_next = beside((x, x), 8)
    bias, limits, po, pk, xp, xhat, rstd, dy, dysum = call(
        prep_kernel, prep_outputs(), [], map_sizes, weights[5], x, cotangent, smem=1, flops=2 * 10**9, vmem=8
    )
    *far, pk = lax.optimization_barrier((*blocks[1:], pk))
    xk = call(halo_kernel, sds((CLS * KN, 256), F32), [], x, x_core, x_next, pk, flops=10**9, vmem=8)
    blocks = [blocks[0]] + far + [swap(block, 1, count) for block in [blocks[0]] + far]
    a1, queries, keys, values, big_qkv, vec = call(
        project_packed,
        project_outputs() + (sds((256, 768)), sds((vrows, 256), F32)),
        [pltpu.VMEM((256, 768), F32), pltpu.VMEM((256, 128), F32)],
        xhat, xk, *blocks,
        flops=10**9, vmem=8,
    )
    mixed, probs = call(
        attend_kernel, attend_outputs(), [], limits, bias, queries, keys, values, flops=3 * 10**9, vmem=8
    )
    act, dz, a2, da, dx1, x1, dmix, sums, zsum, big_down = call(
        feed_packed,
        feed_outputs() + (sds((768, 256)),),
        [pltpu.VMEM((256, 256), BF), pltpu.VMEM((256, 768), BF)]
        + [pltpu.VMEM(m, F32) for m in ((256, 256), (256, 768), (768, 256))],
        dy, dysum, mixed, xp, vec, *blocks,
        flops=4 * 10**9, vmem=8,
    )
    early = call(
        early_kernel,
        sds((count, 16, EARLY)),
        [pltpu.VMEM((768, 256), F32), pltpu.VMEM((256, 768), F32), pltpu.VMEM((256, 256), F32)],
        act, dy, a2, dz, mixed, da,
        flops=10**9, vmem=8,
    )
    early, dmix = lax.optimization_barrier((early, dmix))
    own, rim_c, rim_z, dsl, tacc = call(
        back_kernel, back_outputs(), [], queries, values, probs, dmix, flops=4 * 10**9, vmem=8
    )
    got_c, got_z = beside((rim_c, rim_z), 8)
    early = add_stage(early, 0, 1, count)
    early, tacc = lax.optimization_barrier((early, tacc))
    layer_out, dnq, fwq, tgrad, qsum = call(
        window_kernel,
        window_outputs(),
        [pltpu.VMEM((768, 256), BF)],
        x1, act, dsl, keys, tacc, a1, big_down, big_qkv, vec, po,
        flops=3 * 10**9,
    )
    early = add_stage(early, 3, 2, count)
    early, own = lax.optimization_barrier((early, own))
    dn, late = call(
        late_kernel,
        (sds((768, 256), F32), sds((count, 16, LATE))),
        [
            pltpu.VMEM((256, 512), F32),
            pltpu.VMEM((8, 256), F32),
            pltpu.VMEM((768, 512), BF),
            pltpu.VMEM((256, 128), F32),
        ],
        own, got_c, got_z, dnq, xhat, big_qkv, a1, sums, zsum, qsum, fwq, tgrad,
        flops=10**9, vmem=8,
    )
    tokens_grad = call(input_kernel, sds((16, 48, 256)), [], dn, dx1, xhat, rstd, vec, po, flops=10**9, vmem=8)
    late = add_stage(add_stage(late, 0, 1, count), 3, 2, count)
    grads = jnp.concatenate([early, late], axis=-1)
    low = grads.astype(BF)
    parts = [grads[0]] + [swap(low[d], d << 1, count) for d in (1, 2, 3)]

    shapes = [sds(w.shape, F32) for w in weights]
    moments = call(
        adam_kernel,
        tuple(shape for shape in shapes for _ in range(3)) + (sds((8, 128), F32),),
        [],
        *parts, *weights, *firsts, *seconds,
    )
    mine = moments[18]
    squares = mine + swap(mine, 1, count)
    squares = squares + swap(squares, 8, count) + swap(squares, 16, count) + swap(squares, 24, count)
    news = call(
        step_kernel,
        tuple(shapes) + (sds((1, 16), F32),) * 2,
        [],
        mine, squares, *[swap(squares, d << 1, count) for d in (1, 2, 3)], *weights, *moments[2:18:3],
    )
    results = [layer_out, tokens_grad]
    for i in range(6):
        three = (moments[3 * i], moments[3 * i + 1], news[i])
        results += [a.T for a in three] if i == 4 else three
    return tuple(results) + (news[6].reshape(16), news[7].reshape(16))


def add_stage(grads, lo, bits, count):
    low = grads.astype(BF).reshape((1 << bits, -1) + grads.shape[1:])
    total = grads.reshape(low.shape)[0].astype(F32)
    for d in range(1, 1 << bits):
        total = total + swap(low[d], d << lo, count).astype(F32)
    return total


def per_device(
    maps,
    band,
    tokens_in,
    cotangent,
    map_sizes,
    w_qkv,
    w_out,
    w_up,
    w_down,
    vectors,
    pos_table,
    first_qkv,
    second_qkv,
    first_out,
    second_out,
    first_up,
    second_up,
    first_down,
    second_down,
    first_vectors,
    second_vectors,
    first_table,
    second_table,
):
    if w_qkv.shape[0] == 8 and (maps, band) == (4, 8):
        return packed_step(
            tokens_in, cotangent, map_sizes,
            (w_qkv, w_out, w_up, w_down, vectors, pos_table),
            (first_qkv, first_out, first_up, first_down, first_vectors, first_table),
            (second_qkv, second_out, second_up, second_down, second_vectors, second_table),
        )
    count = maps * band
    rows = w_qkv.shape[0]
    vrows = vectors.shape[0]
    groups = exchange_groups(maps, band)
    masks = np.array(frame_masks(groups))
    inverse = np.argsort(masks)
    me = lax.axis_index(AXES)
    x_core, x_next = beside((tokens_in, tokens_in), band)

    def pack(qkv, out, upw, dnw, vec):
        dn = dnw.reshape(3, rows, 256).transpose(1, 0, 2).reshape(rows, 768)
        vt = jnp.pad(vec.T, ((0, 0), (0, 128 - vrows)))
        return jnp.concatenate([qkv, out, upw, dn, vt], axis=1)

    slab = pack(*(w.astype(BF) for w in (w_qkv, w_out, w_up, w_down, vectors)))
    block = gather_all(slab, groups, count)
    order = jnp.asarray(inverse, jnp.int32)[jnp.arange(count, dtype=jnp.int32) ^ me]
    whole = jnp.take(block, order, axis=0).reshape(256, -1)
    big_qkv = whole[:, 0:768]
    big_out = whole[:, 768:1024]
    big_up = whole[:, 1024:1792]
    big_down = (
        whole[:, 1792:2560].reshape(count, rows, 3, 256).transpose(0, 2, 1, 3).reshape(768, 256)
    )
    vec = whole[:, 2560 : 2560 + vrows].T.astype(F32)

    bias, limits, po, pk, xp, xhat, rstd, dy, dysum = call(
        prep_kernel, prep_outputs(), [], map_sizes, pos_table, tokens_in, cotangent, smem=1, flops=2 * 10**9
    )
    xk = call(halo_kernel, sds((CLS * KN, 256), F32), [], tokens_in, x_core, x_next, pk, flops=10**9)
    a1, queries, keys, values = call(project_kernel, project_outputs(), [], xhat, xk, big_qkv, vec, flops=10**9)
    mixed, probs = call(attend_kernel, attend_outputs(), [], limits, bias, queries, keys, values, flops=3 * 10**9)
    act, dz, a2, da, dx1, x1, dmix, sums, zsum = call(
        feed_kernel,
        feed_outputs(),
        [],
        dy, dysum, mixed, xp, big_out, big_up, big_down, vec,
        flops=4 * 10**9,
    )
    own, rim_c, rim_z, dsl, tacc = call(back_kernel, back_outputs(), [], queries, values, probs, dmix, flops=4 * 10**9)
    got_c, got_z = beside((rim_c, rim_z), band)
    grad_down, grad_up, grad_out = call(
        early_grads,
        (sds((768, 256), F32), sds((256, 768), F32), sds((256, 256), F32)),
        [],
        act, dy, a2, dz, mixed, da,
        flops=10**9,
    )
    layer_out, dnq, fwq, table_grad, qsum = call(
        window_kernel,
        window_outputs(),
        [pltpu.VMEM((768, 256), BF)],
        x1, act, dsl, keys, tacc, a1, big_down, big_qkv, vec, po,
        flops=3 * 10**9,
    )
    dn, fkv, sums2 = call(
        finish_kernel,
        (sds((768, 256), F32), sds((256, 512), F32), sds((8, 256), F32)),
        [pltpu.VMEM((768, 512), BF)],
        own, got_c, got_z, dnq, xhat, big_qkv, a1,
        flops=10**9,
    )
    tokens_grad = call(input_kernel, sds((16, 48, 256)), [], dn, dx1, xhat, rstd, vec, po, flops=10**9)
    grad_qkv = jnp.concatenate([fwq, fkv], axis=1)
    sums2 = sums2.at[2:3].add(qsum)
    grad_vec = jnp.concatenate([sums + sums2, zsum.reshape(3, 256)], axis=0)

    packed = jnp.concatenate(
        [
            grad_qkv.reshape(count, rows, 768),
            grad_out.reshape(count, rows, 256),
            grad_up.reshape(count, rows, 768),
            grad_down.reshape(count, 3, rows, 256).transpose(0, 2, 1, 3).reshape(count, rows, 768),
            jnp.pad(grad_vec.T, ((0, 0), (0, 128 - vrows))).reshape(count, rows, 128),
        ],
        axis=2,
    )
    packed = jnp.take(packed, jnp.asarray(masks, jnp.int32) ^ me, axis=0)
    red = scatter_sum(packed, groups, count)
    red_qkv = red[:, 0:768]
    red_out = red[:, 768:1024]
    red_up = red[:, 1024:1792]
    red_down = red[:, 1792:2560].reshape(rows, 3, 256).transpose(1, 0, 2).reshape(3 * rows, 256)
    red_vec = red[:, 2560 : 2560 + vrows].T

    steps = np.arange(-3, 4)
    lanes = ((12 * steps[:, None] + steps[None, :]) % KN).reshape(-1)
    table_total = lax.psum(table_grad, AXES)[:, lanes]

    part_qkv = adam_parts(w_qkv, red_qkv, first_qkv, second_qkv)
    part_out = adam_parts(w_out, red_out, first_out, second_out)
    part_up = adam_parts(w_up, red_up, first_up, second_up)
    part_down = adam_parts(w_down, red_down, first_down, second_down)
    part_vec = adam_parts(vectors, red_vec, first_vectors, second_vectors)
    part_table = adam_parts(pos_table, table_total, first_table, second_table)
    local_weight_sq = squares_of((w_qkv, w_out, w_up, w_down), vectors)
    local_update_sq = squares_of((part_qkv[2], part_out[2], part_up[2], part_down[2]), part_vec[2])
    weight_sq, update_sq = lax.psum((local_weight_sq, local_update_sq), AXES)
    table_weight = jnp.sqrt(jnp.sum(pos_table * pos_table))
    table_update = jnp.sqrt(jnp.sum(part_table[2] * part_table[2]))
    weight_norms = jnp.concatenate([jnp.sqrt(weight_sq), table_weight[None]])
    update_norms = jnp.concatenate([jnp.sqrt(update_sq), table_update[None]])
    ratios = weight_norms / (update_norms + RATIO_EPS)
    next_qkv = w_qkv - LEARN_RATE * ratios[0] * part_qkv[2]
    next_out = w_out - LEARN_RATE * ratios[1] * part_out[2]
    next_up = w_up - LEARN_RATE * ratios[2] * part_up[2]
    next_down = w_down - LEARN_RATE * ratios[3] * part_down[2]
    next_vectors = vectors - LEARN_RATE * ratios[4 : 4 + vrows][:, None] * part_vec[2]
    next_table = pos_table - LEARN_RATE * ratios[4 + vrows] * part_table[2]
    return (
        layer_out,
        tokens_grad,
        part_qkv[0],
        part_qkv[1],
        next_qkv,
        part_out[0],
        part_out[1],
        next_out,
        part_up[0],
        part_up[1],
        next_up,
        part_down[0],
        part_down[1],
        next_down,
        part_vec[0],
        part_vec[1],
        next_vectors,
        part_table[0],
        part_table[1],
        next_table,
        weight_norms,
        update_norms,
    )


def solution(mesh):
    both = P(AXES, None)
    side = P(None, AXES)
    tall = P(AXES, None, None)
    copied = P()
    return jax.shard_map(
        functools.partial(per_device, mesh.shape["maps"], mesh.shape["band"]),
        mesh=mesh,
        in_specs=(tall, tall, P("maps", None))
        + (both,) * 4
        + (side, copied)
        + (both,) * 8
        + (side, side, copied, copied),
        out_specs=(tall, tall) + (both,) * 12 + (side,) * 3 + (copied,) * 5,
        check_vma=False,
    )
```

```python
import functools

import jax
import jax.numpy as jnp
import numpy as np
from jax import lax
from jax.experimental import pallas as pl
from jax.experimental.pallas import tpu as pltpu
from jax.sharding import PartitionSpec as P

HEADS = 8
WINDOW = 7
DIL = 4
STEP = 10
NORM_EPS = 1e-05
BETA_FIRST = 0.9
BETA_SECOND = 0.999
ADAM_EPS = 1e-06
DECAY_RATE = 0.01
LEARN_RATE = 0.2
RATIO_EPS = 1e-06
MASKED = -1e30
LOG2E = 1.4426950408889634
GELU0 = 0.7978845608028654
GELU1 = 0.044715
AXES = ("maps", "band")

BF = jnp.bfloat16
F32 = jnp.float32

CLS = DIL * DIL
QN = 48
KN = 128
RIM = 40


def dot(a, b):
    return lax.dot_general(a, b, (((1,), (0,)), ((), ())), preferred_element_type=F32)


def dot_nt(a, b):
    return lax.dot_general(a, b, (((1,), (1,)), ((), ())), preferred_element_type=F32)


def dot_tn(a, b):
    return lax.dot_general(a, b, (((0,), (0,)), ((), ())), preferred_element_type=F32)


def select(shape, source):
    o = lax.broadcasted_iota(jnp.int32, shape, 0)
    return (source(o) == lax.broadcasted_iota(jnp.int32, shape, 1)).astype(F32).astype(BF)


def own_source(o):
    cc = (o * 171) >> 13
    qr, qc = split12(o - QN * cc)
    return qr * 48 + qc * 4 + cc


def key_source(o):
    j = ((o & (KN - 1)) + 36) & (KN - 1)
    kr, kc = split12(j)
    return jnp.where(j < 120, kr * 48 + kc * 4 + (o >> 7), -1)


def normed(v):
    mean = jnp.mean(v, axis=-1, keepdims=True)
    cen = v - mean
    var = jnp.mean(cen * cen, axis=-1, keepdims=True)
    rstd = lax.rsqrt(var + NORM_EPS)
    return cen * rstd, rstd


def norm_back(g, xhat, rstd):
    m1 = jnp.mean(g, axis=-1, keepdims=True)
    m2 = jnp.mean(g * xhat, axis=-1, keepdims=True)
    return rstd * (g - m1 - xhat * m2)


def spread_heads(v, lane_head):
    zero = jnp.zeros_like(v)
    return jnp.concatenate([jnp.where(lane_head == h, v, zero) for h in range(HEADS)], axis=0)


def pick_heads(full, lane_head):
    out = jnp.where(lane_head == 0, full[0:QN], 0.0)
    for h in range(1, HEADS):
        out = out + jnp.where(lane_head == h, full[h * QN : (h + 1) * QN], 0.0)
    return out


def split12(v):
    q = (v * 43) >> 9
    return q, v - 12 * q


def table_slots():
    n = lax.broadcasted_iota(jnp.int32, (WINDOW * WINDOW, KN), 0)
    lane = lax.broadcasted_iota(jnp.int32, (WINDOW * WINDOW, KN), 1)
    nr = (n * 37) >> 8
    nc = n - 7 * nr
    return (((12 * (nr - 3) + nc - 3) & (KN - 1)) == lane).astype(F32)


def prep_kernel(
    sizes_ref, table_ref, x_ref, cot_ref, bias_ref, limits_ref, po_ref, pk_ref, xp_ref, xhat_ref, rstd_ref, dy_ref, dysum_ref
):
    po_ref[...] = select((4 * QN, 4 * 48), own_source)
    pk_ref[...] = select((4 * KN, 10 * 48), key_source)
    row = lax.broadcasted_iota(jnp.int32, (8, 128), 0)
    limits_ref[...] = jnp.where(row == 0, sizes_ref[0, 0] - lax.axis_index("band") * 16, sizes_ref[0, 1])

    slots = lax.dot_general(
        table_ref[...],
        table_slots(),
        (((1,), (0,)), ((), ())),
        precision=lax.Precision.HIGHEST,
        preferred_element_type=F32,
    )
    qi = lax.broadcasted_iota(jnp.int32, (QN, KN), 0)
    si = lax.broadcasted_iota(jnp.int32, (QN, KN), 1)
    ji = (si + 36) & (KN - 1)
    kr, kc = split12(ji)
    qr, qc = split12(qi)
    window = (jnp.abs(kc - qc) <= 3) & (jnp.abs(kr - qr - 3) <= 3) & (ji < 120)
    rows = []
    for h in range(HEADS):
        line = jnp.broadcast_to(slots[h : h + 1, :] * LOG2E, (QN, KN))
        line = pltpu.roll(line, 0, 1, stride=1, stride_axis=0)
        rows.append(jnp.where(window, line, MASKED))
    bias_ref[...] = jnp.concatenate(rows, axis=0).T

    def block(rc, _):
        at = pl.ds(pl.multiple_of(rc * 192, 192), 192)
        xp = dot(po_ref[...], jnp.concatenate([x_ref[4 * i + rc] for i in range(4)], axis=0))
        xp_ref[at, :] = xp
        xhat, rstd = normed(xp)
        xhat_ref[at, :] = xhat
        rstd_ref[at, :] = jnp.broadcast_to(rstd, (192, 128))
        dy = dot(po_ref[...], jnp.concatenate([cot_ref[4 * i + rc] for i in range(4)], axis=0))
        dy_ref[at, :] = dy.astype(BF)
        dysum_ref[...] += jnp.sum(dy, axis=0, keepdims=True)
        return 0

    dysum_ref[...] = jnp.zeros_like(dysum_ref)
    lax.fori_loop(0, 4, block, 0, unroll=4)


def halo_kernel(x_ref, xc_ref, xz_ref, pk_ref, xk_ref):
    odd = (lax.axis_index("band") & 1) == 1

    def block(rc, _):
        rows = [jnp.where(odd, xc_ref[4 + 4 * i + rc], xz_ref[4 + 4 * i + rc]) for i in range(3)]
        rows += [x_ref[4 * i + rc] for i in range(4)]
        rows += [jnp.where(odd, xz_ref[4 * i + rc], xc_ref[4 * i + rc]) for i in range(3)]
        xk = dot(pk_ref[...], jnp.concatenate(rows, axis=0))
        xk_ref[pl.ds(pl.multiple_of(rc * 512, 512), 512), :] = normed(xk)[0]
        return 0

    lax.fori_loop(0, 4, block, 0, unroll=2)


def project_kernel(xhat_ref, xk_ref, wqkv_ref, vec_ref, q_ref, k_ref, v_ref):
    def vrow(i):
        return vec_ref[i : i + 1, :]

    def block(rc, _):
        at = pl.ds(pl.multiple_of(rc * 192, 192), 192)
        a1 = (xhat_ref[at, :] * vrow(0) + vrow(1)).astype(BF)
        q_ref[at, :] = (dot(a1, wqkv_ref[:, 0:256]) + vrow(2)).astype(BF)
        at = pl.ds(pl.multiple_of(rc * 512, 512), 512)
        a1k = (xk_ref[at, :] * vrow(0) + vrow(1)).astype(BF)
        k_ref[at, :] = dot(a1k, wqkv_ref[:, 256:512]).astype(BF)
        v_ref[at, :] = (dot(a1k, wqkv_ref[:, 512:768]) + vrow(3)).astype(BF)
        return 0

    lax.fori_loop(0, 4, block, 0, unroll=2)


def attend_kernel(limits_ref, bias_ref, q_ref, k_ref, v_ref, mixed_ref, p_ref):
    scale = 32 ** (-0.5)
    lane_head = lax.broadcasted_iota(jnp.int32, (QN, 256), 1) >> 5
    row0 = lax.axis_index("band") * 16
    height = limits_ref[0:1, 0:1]
    wide = limits_ref[1:2, 0:1]
    ks = lax.broadcasted_iota(jnp.int32, (KN, 384), 0)
    ql = lax.broadcasted_iota(jnp.int32, (KN, 384), 1)
    kj = (ks + 36) & (KN - 1)
    krow, kcol = split12(kj)
    qin = ql - 48 * ((ql * 171) >> 13)
    same = ks == qin

    def attend(k, _):
        rc = k >> 2
        cc = k & 3
        at_q = pl.ds(pl.multiple_of(k * QN, QN), QN)
        at_k = pl.ds(pl.multiple_of(k * KN, KN), KN)
        qbd = spread_heads(q_ref[at_q, :], lane_head)
        s = dot_nt(k_ref[at_k, :], qbd) * (scale * LOG2E) + bias_ref[...]
        r = krow * 4 + (rc - 12)
        c = kcol * 4 + cc
        okay = ((r >= -row0) & (r < height) & (c < wide)) | same
        s = jnp.where(okay, s, MASKED)
        top = jnp.max(s, axis=0, keepdims=True)
        e = jnp.exp2(s - top)
        p = e * (1.0 / jnp.sum(e, axis=0, keepdims=True))
        p_ref[at_k, :] = p
        full = dot_tn(p.astype(BF), v_ref[at_k, :])
        mixed_ref[at_q, :] = pick_heads(full, lane_head).astype(BF)
        return 0

    lax.fori_loop(0, CLS, attend, 0, unroll=CLS)


def feed_kernel(
    dy_ref,
    dysum_ref,
    mixed_ref,
    xp_ref,
    wo_ref,
    wu_ref,
    wd_ref,
    vec_ref,
    act_ref,
    dz_ref,
    a2_ref,
    da_ref,
    dx1_ref,
    x1_ref,
    dmix_ref,
    sums_ref,
    zsum_ref,
):
    def vrow(i):
        return vec_ref[i : i + 1, :]

    sums_ref[...] = jnp.zeros_like(sums_ref)
    sums_ref[7:8, :] = dysum_ref[...]
    zsum_ref[...] = jnp.zeros_like(zsum_ref)

    def feed(rc, _):
        at = pl.ds(pl.multiple_of(rc * 192, 192), 192)
        x1 = xp_ref[at, :] + (dot(mixed_ref[at, :], wo_ref[...]) + vrow(4))
        x1_ref[at, :] = x1
        xhat, rstd = normed(x1)
        a2 = (xhat * vrow(5) + vrow(6)).astype(BF)
        a2_ref[at, :] = a2
        dy = dy_ref[at, :]
        dn = jnp.zeros((192, 256), F32)
        for part in range(3):
            cols = slice(256 * part, 256 * part + 256)
            z = dot(a2, wu_ref[:, cols]) + vrow(8 + part)
            cube = (GELU0 * GELU1) * (z * z)
            up = 1.0 + jnp.tanh(z * (GELU0 + cube))
            hz = 0.5 * z
            act_ref[at, cols] = (hz * up).astype(BF)
            slope = up * (0.5 + hz * (2.0 - up) * (GELU0 + 3.0 * cube))
            dz = (dot_nt(dy, wd_ref[cols, :]) * slope).astype(BF)
            dz_ref[at, cols] = dz
            zsum_ref[:, cols] += jnp.sum(dz.astype(F32), axis=0, keepdims=True)
            dn = dn + dot_nt(dz, wu_ref[:, cols])
        dyf = dy.astype(F32)
        dx1 = dyf + norm_back(dn * vrow(5), xhat, rstd)
        dx1_ref[at, :] = dx1
        da = dx1.astype(BF)
        da_ref[at, :] = da
        dmix_ref[at, :] = dot_nt(da, wo_ref[...]).astype(BF)
        sums_ref[4:5, :] += jnp.sum(da.astype(F32), axis=0, keepdims=True)
        sums_ref[5:6, :] += jnp.sum(dn * xhat, axis=0, keepdims=True)
        sums_ref[6:7, :] += jnp.sum(dn, axis=0, keepdims=True)
        return 0

    lax.fori_loop(0, 4, feed, 0, unroll=4)


def back_kernel(
    q_ref,
    v_ref,
    p_ref,
    dmix_ref,
    own_ref,
    rimc_ref,
    rimz_ref,
    dsl_ref,
    tacc_ref,
    dkv_ref,
):
    odd = (lax.axis_index("band") & 1) == 1
    scale = 32 ** (-0.5)
    lane_head = lax.broadcasted_iota(jnp.int32, (QN, 256), 1) >> 5
    tacc_ref[...] = jnp.zeros_like(tacc_ref)

    def back_class(k):
        at_q = pl.ds(pl.multiple_of(k * QN, QN), QN)
        at_k = pl.ds(pl.multiple_of(k * KN, KN), KN)
        qbd = spread_heads(q_ref[at_q, :], lane_head)
        dobd = spread_heads(dmix_ref[at_q, :], lane_head)
        p = p_ref[at_k, :]
        dp = dot_nt(v_ref[at_k, :], dobd)
        dv = dot(p.astype(BF), dobd)
        pdp = p * dp
        ds = pdp - p * jnp.sum(pdp, axis=0, keepdims=True)
        tacc_ref[...] += ds
        dsl = ds.astype(BF)
        dsl_ref[at_k, :] = dsl
        dk = dot(dsl, qbd) * scale
        dkv_ref[at_k, 0:256] = dk.astype(BF)
        dkv_ref[at_k, 256:512] = dv.astype(BF)
        own_ref[at_q, 0:256] = dk[0:QN]
        own_ref[at_q, 256:512] = dv[0:QN]
        after = jnp.concatenate([dk[QN : QN + RIM], dv[QN : QN + RIM]], axis=1)
        before = jnp.concatenate([dk[KN - RIM :], dv[KN - RIM :]], axis=1)
        return after, before

    def attend_back(pair, _):
        after0, before0 = back_class(pair * 2)
        after1, before1 = back_class(pair * 2 + 1)
        at = pl.ds(pl.multiple_of(pair * 2 * RIM, 2 * RIM), 2 * RIM)
        after = jnp.concatenate([after0, after1], axis=0)
        before = jnp.concatenate([before0, before1], axis=0)
        rimc_ref[at, :] = jnp.where(odd, before, after).astype(BF)
        rimz_ref[at, :] = jnp.where(odd, after, before).astype(BF)
        return 0

    lax.fori_loop(0, CLS // 2, attend_back, 0, unroll=8)


def early_grads(act_ref, dy_ref, a2_ref, dz_ref, mixed_ref, da_ref, fd, fu, fo):
    fd[...] = dot_tn(act_ref[...], dy_ref[...])
    fu[...] = dot_tn(a2_ref[...], dz_ref[...])
    fo[...] = dot_tn(mixed_ref[...], da_ref[...])


def output_kernel(x1_ref, act_ref, wd_ref, vec_ref, po_ref, out_ref):
    def result(rc, _):
        at = pl.ds(pl.multiple_of(rc * 192, 192), 192)
        res = x1_ref[at, :] + dot(act_ref[at, :], wd_ref[...]) + vec_ref[7:8, :]
        back = dot_tn(po_ref[...], res.astype(BF)).astype(BF)
        for i in range(4):
            out_ref[4 * i + rc] = back[48 * i : 48 * i + 48]
        return 0

    lax.fori_loop(0, 4, result, 0, unroll=4)


def late_grads(
    dsl_ref,
    k_ref,
    tacc_ref,
    xhat_ref,
    xk_ref,
    dkv_ref,
    wqkv_ref,
    vt_ref,
    sums_ref,
    zsum_ref,
    dq_ref,
    fq_ref,
    fv_ref,
    tgrad_ref,
):
    scale = 32 ** (-0.5)
    lane_head = lax.broadcasted_iota(jnp.int32, (QN, 256), 1) >> 5

    def query(k, _):
        at_q = pl.ds(pl.multiple_of(k * QN, QN), QN)
        at_k = pl.ds(pl.multiple_of(k * KN, KN), KN)
        dq = pick_heads(dot_tn(dsl_ref[at_k, :], k_ref[at_k, :]), lane_head) * scale
        dq_ref[at_q, :] = dq.astype(BF)
        return 0

    lax.fori_loop(0, CLS, query, 0, unroll=16)
    dq = dq_ref[...]
    gain, shift = vt_ref[:, 0:1], vt_ref[:, 1:2]
    qsum = jnp.sum(dq.astype(F32), axis=0, keepdims=True)
    m = dot_tn(xhat_ref[...].astype(BF), dq)
    weight = wqkv_ref[:, 0:256].astype(F32)
    fq_ref[:, 0:256] = gain * m + shift * qsum
    gain_grad = jnp.sum(weight * m, axis=1, keepdims=True)
    shift_grad = jnp.sum(weight * qsum, axis=1, keepdims=True)
    xk = xk_ref[...].astype(BF)
    for cols in (slice(256, 512), slice(512, 768)):
        dkv = dkv_ref[:, cols.start - 256 : cols.stop - 256]
        kvsum = jnp.sum(dkv.astype(F32), axis=0, keepdims=True)
        m = dot_tn(xk, dkv)
        weight = wqkv_ref[:, cols].astype(F32)
        fq_ref[:, cols] = gain * m + shift * kvsum
        gain_grad = gain_grad + jnp.sum(weight * m, axis=1, keepdims=True)
        shift_grad = shift_grad + jnp.sum(weight * kvsum, axis=1, keepdims=True)
    lines = jnp.concatenate(
        [jnp.zeros((2, 256), F32), qsum, kvsum, sums_ref[4:8, :]]
        + [zsum_ref[:, 256 * i : 256 * i + 256] for i in range(3)]
        + [jnp.zeros((117, 256), F32)],
        axis=0,
    )
    lane = lax.broadcasted_iota(jnp.int32, (256, 128), 1)
    fv_ref[...] = jnp.where(lane == 0, gain_grad, jnp.where(lane == 1, shift_grad, lines.T))

    flat = tacc_ref[...].T
    qi = lax.broadcasted_iota(jnp.int32, (QN, KN), 0)
    lines = []
    for h in range(HEADS):
        part = flat[h * QN : (h + 1) * QN]
        for bit in range(6):
            turned = pltpu.roll(part, KN - (1 << bit), 1)
            part = jnp.where((qi >> bit) & 1 == 1, turned, part)
        lines.append(jnp.sum(part, axis=0, keepdims=True))
    tgrad_ref[...] = jnp.concatenate(lines, axis=0)


def input_kernel(
    own_ref, gotc_ref, gotz_ref, dq_ref, dx1_ref, xhat_ref, rstd_ref, wqkv_ref, vec_ref, po_ref, tok_ref
):
    odd = (lax.axis_index("band") & 1) == 1

    def block(rc, _):
        at = pl.ds(pl.multiple_of(rc * 192, 192), 192)
        mine = own_ref[at, :]
        got_c = gotc_ref[pl.ds(pl.multiple_of(rc * 160, 160), 160), :].astype(F32)
        got_z = gotz_ref[pl.ds(pl.multiple_of(rc * 160, 160), 160), :].astype(F32)
        got_a = jnp.where(odd, got_c, got_z)
        got_b = jnp.where(odd, got_z, got_c)
        gap = jnp.zeros((QN - RIM, 512), F32)
        parts = []
        for i in range(4):
            a = jnp.concatenate([got_a[i * RIM : (i + 1) * RIM], gap], axis=0)
            b = jnp.concatenate([gap, got_b[i * RIM : (i + 1) * RIM]], axis=0)
            parts.append(mine[i * QN : (i + 1) * QN] + a + b)
        dkv = jnp.concatenate(parts, axis=0).astype(BF)
        dn = dot_nt(dq_ref[at, :], wqkv_ref[:, 0:256]) + dot_nt(dkv, wqkv_ref[:, 256:768])
        dx = dx1_ref[at, :] + norm_back(dn * vec_ref[0:1, :], xhat_ref[at, :], rstd_ref[at, 0:1])
        back = dot_tn(po_ref[...], dx.astype(BF)).astype(BF)
        for i in range(4):
            tok_ref[4 * i + rc] = back[48 * i : 48 * i + 48]
        return 0

    lax.fori_loop(0, 4, block, 0, unroll=4)


EARLY = 896
LATE = 512


def widen(v):
    return jnp.concatenate([v, jnp.zeros((v.shape[0], 128 - v.shape[1]), F32)], axis=1)


def pack(wqkv, wo, wu, wd, vec):
    pieces = [(wqkv, 0, 0), (wo, 0, 768), (wd, 0, 1024), (vec, 0, 1280)]
    pieces += [(wu, 8, 0), (wd, 0, 768), (wd, -8, 1024)]
    total = 0.0
    for p, row, lane in pieces:
        rows, lanes = p.shape
        zero = jnp.zeros((), F32)
        if rows == 24 and lane == 1024 and row == 0:
            p = lax.pad(p, zero, ((0, -16, 0), (0, 0, 0)))
            rows = 8
        elif rows == 24:
            p = lax.pad(p, zero, ((-8 + row, -8 - row, 0), (0, 0, 0)))
            row, rows = 8, 8
        total = total + lax.pad(p, zero, ((row, 16 - row - rows, 0), (lane, EARLY + LATE - lane - lanes, 0)))
    return total.astype(BF)


def own_index():
    return lax.axis_index("maps") * 8 + lax.axis_index("band")


def sorted_slabs(blocks):
    me = own_index()
    for index, block in enumerate(blocks):
        core, across = divmod(index, 4)
        for z in range(4):
            yield me ^ (core | (z << 1) | (across << 3)), block[z].astype(F32)


def project_packed(xhat_ref, xk_ref, b0, b1, b2, b3, b4, b5, b6, b7, *rest):
    outs, big_qkv, vec, fv, fq = rest[:3], *rest[3:]
    for o, slab in sorted_slabs((b0, b1, b2, b3, b4, b5, b6, b7)):
        at = pl.ds(pl.multiple_of(o * 8, 8), 8)
        fq[at, :] = slab[0:8, 0:768]
        fv[at, :] = slab[0:8, 1280:1408]
    big_qkv[...] = fq[...].astype(BF)
    vec[...] = fv[...].T[0 : vec.shape[0]]
    project_kernel(xhat_ref, xk_ref, big_qkv, vec, *outs)


def feed_packed(dy_ref, dysum_ref, mixed_ref, xp_ref, vec_ref, b0, b1, b2, b3, b4, b5, b6, b7, *rest):
    outs, big_down, (big_out, big_up, fo, fu, fd) = rest[:9], rest[9], rest[10:]
    for o, slab in sorted_slabs((b0, b1, b2, b3, b4, b5, b6, b7)):
        at = pl.ds(pl.multiple_of(o * 8, 8), 8)
        for b, rows in enumerate((slab[0:8, 1024:1280], slab[8:16, 768:1024], slab[8:16, 1024:1280])):
            fd[pl.ds(pl.multiple_of(o * 24 + 8 * b, 8), 8), :] = rows
        fo[at, :] = slab[0:8, 768:1024]
        fu[at, :] = slab[8:16, 0:768]
    big_out[...] = fo[...].astype(BF)
    big_up[...] = fu[...].astype(BF)
    big_down[...] = fd[...].astype(BF)
    feed_kernel(dy_ref, dysum_ref, mixed_ref, xp_ref, big_out, big_up, big_down, vec_ref, *outs)


def frame_slot(me, o):
    m = me ^ o
    return (m & 1) * 16 + (m >> 3) * 4 + ((m >> 1) & 3)


def grads_kernel(*refs):
    dq_ref, out_ref, fd, fu, fo, fq, fv, tgrad = refs[16:]
    early_grads(*refs[:6], fd, fu, fo)
    late_grads(*refs[6:16], dq_ref, fq, fv, tgrad)
    table = tgrad[...]
    me = own_index()
    for o in range(32):
        at = slice(8 * o, 8 * o + 8)
        top = [fd[24 * o + 8 * b : 24 * o + 8 * b + 8, :] for b in range(3)] + [fo[at, 0:128], fq[at, 0:512]]
        low = [fu[at, :], fo[at, 128:256], fq[at, 512:768], fv[at, :], table]
        both = jnp.concatenate([jnp.concatenate(top, axis=1), jnp.concatenate(low, axis=1)], axis=0)
        out_ref[frame_slot(me, o)] = both.astype(BF)


def adam_kernel(*refs):
    w, first, second = refs[4:10], refs[10:16], refs[16:22]
    outs = refs[22:]
    total = refs[0][...] + sum(ref[...].astype(F32) for ref in refs[1:4])
    early, late = total[:, :EARLY], total[:, EARLY:]
    vrows = w[4].shape[1]
    grads = [
        jnp.concatenate([late[0:8], late[8:16, 0:256]], axis=1),
        jnp.concatenate([early[0:8, 768:896], early[8:16, 768:896]], axis=1),
        early[8:16, 0:768],
        jnp.concatenate([early[0:8, 256 * b : 256 * b + 256] for b in range(3)], axis=0),
        late[8:16, 256 : 256 + vrows],
        lax.dot_general(
            late[8:16, 384:512],
            table_slots(),
            (((1,), (1,)), ((), ())),
            precision=lax.Precision.HIGHEST,
            preferred_element_type=F32,
        ),
    ]
    row = lax.broadcasted_iota(jnp.int32, (8, 128), 0)
    lane = lax.broadcasted_iota(jnp.int32, (8, 128), 1)
    norms = jnp.zeros((8, 128), F32)
    for i in range(6):
        new_first, new_second, update = adam_parts(w[i][...], grads[i], first[i][...], second[i][...])
        outs[3 * i][...] = new_first
        outs[3 * i + 1][...] = new_second
        outs[3 * i + 2][...] = update
        for line, v in ((0, w[i][...]), (1, update)):
            if i == 4:
                sums = pltpu.roll(widen(jnp.sum(v * v, axis=0, keepdims=True)), 4, 1)
                norms = jnp.where((row == line) & (lane >= 4) & (lane < 4 + vrows), sums, norms)
            else:
                at = i if i < 4 else 4 + vrows
                norms = jnp.where((row == line) & (lane == at), jnp.sum(v * v), norms)
    outs[18][...] = norms


def step_kernel(mine_ref, a_ref, b_ref, c_ref, d_ref, *refs):
    w, update, outs = refs[0:6], refs[6:12], refs[12:]
    vrows = w[4].shape[1]
    total = a_ref[...] + b_ref[...] + c_ref[...] + d_ref[...]
    lane = lax.broadcasted_iota(jnp.int32, (8, 128), 1)
    norms = jnp.sqrt(jnp.where(lane == 4 + vrows, mine_ref[...], total))
    outs[6][...] = norms[0:1, 0:16]
    outs[7][...] = norms[1:2, 0:16]
    rate = LEARN_RATE * norms[0:1] / (norms[1:2] + RATIO_EPS)
    for i in range(6):
        if i == 4:
            r = pltpu.roll(rate, 124, 1)[:, 0:vrows]
        else:
            at = i if i < 4 else 4 + vrows
            r = rate[:, at : at + 1]
        outs[i][...] = w[i][...] - r * update[i][...]


def stack_kernel(*refs):
    for i, ref in enumerate(refs[:4]):
        refs[4][i] = ref[...]


def call(kernel, out_shape, scratch, *args, smem=0, flops=10**8, vmem=16):
    vm = pl.BlockSpec(memory_space=pltpu.VMEM)
    specs = [pl.BlockSpec(memory_space=pltpu.SMEM)] * smem + [vm] * (len(args) - smem)
    return pl.pallas_call(
        kernel,
        out_shape=out_shape,
        in_specs=specs,
        out_specs=jax.tree.map(lambda _: vm, out_shape),
        scratch_shapes=scratch,
        compiler_params=pltpu.CompilerParams(vmem_limit_bytes=vmem * 2**20),
        cost_estimate=pl.CostEstimate(flops=flops, bytes_accessed=10**6, transcendentals=0),
    )(*args)


def sds(shape, dtype=BF):
    return jax.ShapeDtypeStruct(shape, dtype)


def exchange_groups(maps, band):
    zbits = band.bit_length() - 2
    mbits = maps.bit_length() - 1
    cut = lambda lo, n: [(lo + i, min(2, n - i)) for i in range(0, n, 2)]
    return cut(1, zbits) + cut(1 + zbits, mbits) + [(0, 1)]


def swap(block, mask, count):
    return lax.ppermute(block, AXES, [(k, k ^ mask) for k in range(count)])


def frame_masks(groups):
    masks = [0]
    for lo, bits in groups:
        masks = [m ^ (d << lo) for d in range(1 << bits) for m in masks]
    return masks


def gather_all(slab, groups, count):
    block = slab[None]
    for lo, bits in groups:
        block = jnp.concatenate(
            [block] + [swap(block, d << lo, count) for d in range(1, 1 << bits)], axis=0
        )
    return block


def scatter_sum(grads, groups, count):
    for lo, bits in reversed(groups):
        grads = add_stage(grads, lo, bits, count)
    return grads[0]


def adam_parts(weight, grad, first, second):
    new_first = BETA_FIRST * first + (1.0 - BETA_FIRST) * grad
    new_second = BETA_SECOND * second + (1.0 - BETA_SECOND) * grad * grad
    update = (
        new_first
        / (1.0 - BETA_FIRST**STEP)
        / (jnp.sqrt(new_second / (1.0 - BETA_SECOND**STEP)) + ADAM_EPS)
        + DECAY_RATE * weight
    )
    return (new_first, new_second, update)


def squares_of(matrices, rowwise):
    return jnp.concatenate(
        [
            jnp.stack([jnp.sum(matrix * matrix) for matrix in matrices]),
            jnp.sum(rowwise * rowwise, axis=1),
        ]
    )


def prep_outputs():
    return (
        sds((KN, 384), F32),
        sds((8, 128), jnp.int32),
        sds((4 * QN, 4 * 48)),
        sds((4 * KN, 10 * 48)),
        sds((768, 256), F32),
        sds((768, 256), F32),
        sds((768, 128), F32),
        sds((768, 256)),
        sds((1, 256), F32),
    )


def project_outputs():
    return (sds((768, 256)), sds((CLS * KN, 256)), sds((CLS * KN, 256)))


def attend_outputs():
    return (sds((768, 256)), sds((CLS * KN, 384), F32))


def feed_outputs():
    return (
        sds((768, 768)),
        sds((768, 768)),
        sds((768, 256)),
        sds((768, 256)),
        sds((768, 256), F32),
        sds((768, 256), F32),
        sds((768, 256)),
        sds((8, 256), F32),
        sds((1, 768), F32),
    )


def back_outputs():
    return (
        sds((768, 512), F32),
        sds((CLS * RIM, 512)),
        sds((CLS * RIM, 512)),
        sds((CLS * KN, 384)),
        sds((KN, 384), F32),
        sds((CLS * KN, 512)),
    )


def late_outputs():
    return (
        sds((768, 256)),
        sds((256, 768), F32),
        sds((256, 128), F32),
        sds((HEADS, KN), F32),
    )


def beside(block, band):
    touching = [(b, b + 1 if b % 2 else b - 1) for b in range(band)]
    return (
        lax.ppermute(block[0], "band", [(b, b ^ 1) for b in range(band)]),
        lax.ppermute(block[1], "band", [(b, to) for b, to in touching if 0 <= to < band]),
    )


def packed_step(tokens_in, cotangent, map_sizes, weights, firsts, seconds):
    count = 32
    vrows = weights[4].shape[0]
    turn = lambda arrays: tuple(a.T if i == 4 else a for i, a in enumerate(arrays))
    weights, firsts, seconds = turn(weights), turn(firsts), turn(seconds)
    slab = pack(*weights[:5])
    column = call(
        stack_kernel,
        sds((4, 16, EARLY + LATE)),
        [],
        slab,
        *[swap(slab, d << 1, count) for d in (1, 2, 3)],
        vmem=4,
    )
    column, x = lax.optimization_barrier((column, tokens_in))
    blocks = [column] + [swap(column, d << 3, count) for d in (1, 2, 3)]
    x_core, x_next = beside((x, x), 8)
    bias, limits, po, pk, xp, xhat, rstd, dy, dysum = call(
        prep_kernel, prep_outputs(), [], map_sizes, weights[5], x, cotangent, smem=1, flops=2 * 10**9, vmem=8
    )
    *far, pk = lax.optimization_barrier((*blocks[1:], pk))
    xk = call(halo_kernel, sds((CLS * KN, 256), F32), [], x, x_core, x_next, pk, flops=10**9, vmem=8)
    blocks = [blocks[0]] + far + [swap(block, 1, count) for block in [blocks[0]] + far]
    queries, keys, values, big_qkv, vec, vt = call(
        project_packed,
        project_outputs() + (sds((256, 768)), sds((vrows, 256), F32), sds((256, 128), F32)),
        [pltpu.VMEM((256, 768), F32)],
        xhat, xk, *blocks,
        flops=10**9, vmem=8,
    )
    mixed, probs = call(
        attend_kernel, attend_outputs(), [], limits, bias, queries, keys, values, flops=3 * 10**9, vmem=8
    )
    act, dz, a2, da, dx1, x1, dmix, sums, zsum, big_down = call(
        feed_packed,
        feed_outputs() + (sds((768, 256)),),
        [pltpu.VMEM((256, 256), BF), pltpu.VMEM((256, 768), BF)]
        + [pltpu.VMEM(m, F32) for m in ((256, 256), (256, 768), (768, 256))],
        dy, dysum, mixed, xp, vec, *blocks,
        flops=4 * 10**9, vmem=8,
    )
    own, rim_c, rim_z, dsl, tacc, dkv = call(
        back_kernel, back_outputs(), [], queries, values, probs, dmix, flops=4 * 10**9, vmem=8
    )
    dq, grads = call(
        grads_kernel,
        (sds((768, 256)), sds((count, 16, EARLY + LATE))),
        [pltpu.VMEM(m, F32) for m in ((768, 256), (256, 768), (256, 256))]
        + [pltpu.VMEM(o.shape, o.dtype) for o in late_outputs()[1:]],
        act, dy, a2, dz, mixed, da, dsl, keys, tacc, xhat, xk, dkv, big_qkv, vt, sums, zsum,
        flops=5 * 10**9, vmem=8,
    )
    layer_out = call(output_kernel, sds((16, 48, 256)), [], x1, act, big_down, vec, po, flops=10**9, vmem=8)
    got_c, got_z = beside((rim_c, rim_z), 8)
    tokens_grad = call(
        input_kernel, sds((16, 48, 256)), [], own, got_c, got_z, dq, dx1, xhat, rstd, big_qkv, vec, po,
        flops=10**9, vmem=8,
    )
    grads = add_stage(add_stage(grads, 0, 1, count), 3, 2, count)
    low = grads.astype(BF)
    parts = [grads[0]] + [swap(low[d], d << 1, count) for d in (1, 2, 3)]
    parts[0], tokens_grad = lax.optimization_barrier((parts[0], tokens_grad))

    shapes = [sds(w.shape, F32) for w in weights]
    moments = call(
        adam_kernel,
        tuple(shape for shape in shapes for _ in range(3)) + (sds((8, 128), F32),),
        [],
        *parts, *weights, *firsts, *seconds,
    )
    mine = moments[18]
    squares = mine + swap(mine, 1, count)
    squares = squares + swap(squares, 8, count) + swap(squares, 16, count) + swap(squares, 24, count)
    news = call(
        step_kernel,
        tuple(shapes) + (sds((1, 16), F32),) * 2,
        [],
        mine, squares, *[swap(squares, d << 1, count) for d in (1, 2, 3)], *weights, *moments[2:18:3],
    )
    results = [layer_out, tokens_grad]
    for i in range(6):
        three = (moments[3 * i], moments[3 * i + 1], news[i])
        results += [a.T for a in three] if i == 4 else three
    return tuple(results) + (news[6].reshape(16), news[7].reshape(16))


def add_stage(grads, lo, bits, count):
    low = grads.astype(BF).reshape((1 << bits, -1) + grads.shape[1:])
    total = grads.reshape(low.shape)[0].astype(F32)
    for d in range(1, 1 << bits):
        total = total + swap(low[d], d << lo, count).astype(F32)
    return total


def per_device(
    maps,
    band,
    tokens_in,
    cotangent,
    map_sizes,
    w_qkv,
    w_out,
    w_up,
    w_down,
    vectors,
    pos_table,
    first_qkv,
    second_qkv,
    first_out,
    second_out,
    first_up,
    second_up,
    first_down,
    second_down,
    first_vectors,
    second_vectors,
    first_table,
    second_table,
):
    if w_qkv.shape[0] == 8 and (maps, band) == (4, 8):
        return packed_step(
            tokens_in, cotangent, map_sizes,
            (w_qkv, w_out, w_up, w_down, vectors, pos_table),
            (first_qkv, first_out, first_up, first_down, first_vectors, first_table),
            (second_qkv, second_out, second_up, second_down, second_vectors, second_table),
        )
    count = maps * band
    rows = w_qkv.shape[0]
    vrows = vectors.shape[0]
    groups = exchange_groups(maps, band)
    masks = np.array(frame_masks(groups))
    inverse = np.argsort(masks)
    me = lax.axis_index(AXES)
    x_core, x_next = beside((tokens_in, tokens_in), band)

    def pack(qkv, out, upw, dnw, vec):
        dn = dnw.reshape(3, rows, 256).transpose(1, 0, 2).reshape(rows, 768)
        vt = jnp.pad(vec.T, ((0, 0), (0, 128 - vrows)))
        return jnp.concatenate([qkv, out, upw, dn, vt], axis=1)

    slab = pack(*(w.astype(BF) for w in (w_qkv, w_out, w_up, w_down, vectors)))
    block = gather_all(slab, groups, count)
    order = jnp.asarray(inverse, jnp.int32)[jnp.arange(count, dtype=jnp.int32) ^ me]
    whole = jnp.take(block, order, axis=0).reshape(256, -1)
    big_qkv = whole[:, 0:768]
    big_out = whole[:, 768:1024]
    big_up = whole[:, 1024:1792]
    big_down = (
        whole[:, 1792:2560].reshape(count, rows, 3, 256).transpose(0, 2, 1, 3).reshape(768, 256)
    )
    vt = whole[:, 2560:].astype(F32)
    vec = vt[:, :vrows].T

    bias, limits, po, pk, xp, xhat, rstd, dy, dysum = call(
        prep_kernel, prep_outputs(), [], map_sizes, pos_table, tokens_in, cotangent, smem=1, flops=2 * 10**9
    )
    xk = call(halo_kernel, sds((CLS * KN, 256), F32), [], tokens_in, x_core, x_next, pk, flops=10**9)
    queries, keys, values = call(project_kernel, project_outputs(), [], xhat, xk, big_qkv, vec, flops=10**9)
    mixed, probs = call(attend_kernel, attend_outputs(), [], limits, bias, queries, keys, values, flops=3 * 10**9)
    act, dz, a2, da, dx1, x1, dmix, sums, zsum = call(
        feed_kernel,
        feed_outputs(),
        [],
        dy, dysum, mixed, xp, big_out, big_up, big_down, vec,
        flops=4 * 10**9,
    )
    own, rim_c, rim_z, dsl, tacc, dkv = call(
        back_kernel, back_outputs(), [], queries, values, probs, dmix, flops=4 * 10**9
    )
    got_c, got_z = beside((rim_c, rim_z), band)
    grad_down, grad_up, grad_out = call(
        early_grads,
        (sds((768, 256), F32), sds((256, 768), F32), sds((256, 256), F32)),
        [],
        act, dy, a2, dz, mixed, da,
        flops=10**9,
    )
    dq, grad_qkv, grad_vec, table_grad = call(
        late_grads,
        late_outputs(),
        [],
        dsl, keys, tacc, xhat, xk, dkv, big_qkv, vt, sums, zsum,
        flops=3 * 10**9,
    )
    layer_out = call(output_kernel, sds((16, 48, 256)), [], x1, act, big_down, vec, po, flops=10**9)
    tokens_grad = call(
        input_kernel, sds((16, 48, 256)), [], own, got_c, got_z, dq, dx1, xhat, rstd, big_qkv, vec, po, flops=10**9
    )

    packed = jnp.concatenate(
        [
            grad_qkv.reshape(count, rows, 768),
            grad_out.reshape(count, rows, 256),
            grad_up.reshape(count, rows, 768),
            grad_down.reshape(count, 3, rows, 256).transpose(0, 2, 1, 3).reshape(count, rows, 768),
            grad_vec.reshape(count, rows, 128),
        ],
        axis=2,
    )
    packed = jnp.take(packed, jnp.asarray(masks, jnp.int32) ^ me, axis=0)
    red = scatter_sum(packed, groups, count)
    red_qkv = red[:, 0:768]
    red_out = red[:, 768:1024]
    red_up = red[:, 1024:1792]
    red_down = red[:, 1792:2560].reshape(rows, 3, 256).transpose(1, 0, 2).reshape(3 * rows, 256)
    red_vec = red[:, 2560 : 2560 + vrows].T

    steps = np.arange(-3, 4)
    lanes = ((12 * steps[:, None] + steps[None, :]) % KN).reshape(-1)
    table_total = lax.psum(table_grad, AXES)[:, lanes]

    part_qkv = adam_parts(w_qkv, red_qkv, first_qkv, second_qkv)
    part_out = adam_parts(w_out, red_out, first_out, second_out)
    part_up = adam_parts(w_up, red_up, first_up, second_up)
    part_down = adam_parts(w_down, red_down, first_down, second_down)
    part_vec = adam_parts(vectors, red_vec, first_vectors, second_vectors)
    part_table = adam_parts(pos_table, table_total, first_table, second_table)
    local_weight_sq = squares_of((w_qkv, w_out, w_up, w_down), vectors)
    local_update_sq = squares_of((part_qkv[2], part_out[2], part_up[2], part_down[2]), part_vec[2])
    weight_sq, update_sq = lax.psum((local_weight_sq, local_update_sq), AXES)
    table_weight = jnp.sqrt(jnp.sum(pos_table * pos_table))
    table_update = jnp.sqrt(jnp.sum(part_table[2] * part_table[2]))
    weight_norms = jnp.concatenate([jnp.sqrt(weight_sq), table_weight[None]])
    update_norms = jnp.concatenate([jnp.sqrt(update_sq), table_update[None]])
    ratios = weight_norms / (update_norms + RATIO_EPS)
    next_qkv = w_qkv - LEARN_RATE * ratios[0] * part_qkv[2]
    next_out = w_out - LEARN_RATE * ratios[1] * part_out[2]
    next_up = w_up - LEARN_RATE * ratios[2] * part_up[2]
    next_down = w_down - LEARN_RATE * ratios[3] * part_down[2]
    next_vectors = vectors - LEARN_RATE * ratios[4 : 4 + vrows][:, None] * part_vec[2]
    next_table = pos_table - LEARN_RATE * ratios[4 + vrows] * part_table[2]
    return (
        layer_out,
        tokens_grad,
        part_qkv[0],
        part_qkv[1],
        next_qkv,
        part_out[0],
        part_out[1],
        next_out,
        part_up[0],
        part_up[1],
        next_up,
        part_down[0],
        part_down[1],
        next_down,
        part_vec[0],
        part_vec[1],
        next_vectors,
        part_table[0],
        part_table[1],
        next_table,
        weight_norms,
        update_norms,
    )


def solution(mesh):
    both = P(AXES, None)
    side = P(None, AXES)
    tall = P(AXES, None, None)
    copied = P()
    return jax.shard_map(
        functools.partial(per_device, mesh.shape["maps"], mesh.shape["band"]),
        mesh=mesh,
        in_specs=(tall, tall, P("maps", None))
        + (both,) * 4
        + (side, copied)
        + (both,) * 8
        + (side, side, copied, copied),
        out_specs=(tall, tall) + (both,) * 12 + (side,) * 3 + (copied,) * 5,
        check_vma=False,
    )
```

```python
import functools

import jax
import jax.numpy as jnp
import numpy as np
from jax import lax
from jax.experimental import pallas as pl
from jax.experimental.pallas import tpu as pltpu
from jax.sharding import PartitionSpec as P

HEADS = 8
WINDOW = 7
DIL = 4
STEP = 10
NORM_EPS = 1e-05
BETA_FIRST = 0.9
BETA_SECOND = 0.999
ADAM_EPS = 1e-06
DECAY_RATE = 0.01
LEARN_RATE = 0.2
RATIO_EPS = 1e-06
MASKED = -1e30
LOG2E = 1.4426950408889634
GELU0 = 0.7978845608028654
GELU1 = 0.044715
AXES = ("maps", "band")

BF = jnp.bfloat16
F32 = jnp.float32

CLS = DIL * DIL
QN = 48
KN = 128
RIM = 40


def dot(a, b):
    return lax.dot_general(a, b, (((1,), (0,)), ((), ())), preferred_element_type=F32)


def dot_nt(a, b):
    return lax.dot_general(a, b, (((1,), (1,)), ((), ())), preferred_element_type=F32)


def dot_tn(a, b):
    return lax.dot_general(a, b, (((0,), (0,)), ((), ())), preferred_element_type=F32)


def select(shape, source):
    o = lax.broadcasted_iota(jnp.int32, shape, 0)
    return (source(o) == lax.broadcasted_iota(jnp.int32, shape, 1)).astype(F32).astype(BF)


def own_source(o):
    cc = (o * 171) >> 13
    qr, qc = split12(o - QN * cc)
    return qr * 48 + qc * 4 + cc


def key_source(o):
    j = ((o & (KN - 1)) + 36) & (KN - 1)
    kr, kc = split12(j)
    return jnp.where(j < 120, kr * 48 + kc * 4 + (o >> 7), -1)


def normed(v):
    mean = jnp.mean(v, axis=-1, keepdims=True)
    cen = v - mean
    var = jnp.mean(cen * cen, axis=-1, keepdims=True)
    rstd = lax.rsqrt(var + NORM_EPS)
    return cen * rstd, rstd


def norm_back(g, xhat, rstd):
    m1 = jnp.mean(g, axis=-1, keepdims=True)
    m2 = jnp.mean(g * xhat, axis=-1, keepdims=True)
    return rstd * (g - m1 - xhat * m2)


def spread_heads(v, lane_head):
    zero = jnp.zeros_like(v)
    return jnp.concatenate([jnp.where(lane_head == h, v, zero) for h in range(HEADS)], axis=0)


def pick_heads(full, lane_head):
    out = jnp.where(lane_head == 0, full[0:QN], 0.0)
    for h in range(1, HEADS):
        out = out + jnp.where(lane_head == h, full[h * QN : (h + 1) * QN], 0.0)
    return out


def split12(v):
    q = (v * 43) >> 9
    return q, v - 12 * q


def table_slots():
    n = lax.broadcasted_iota(jnp.int32, (WINDOW * WINDOW, KN), 0)
    lane = lax.broadcasted_iota(jnp.int32, (WINDOW * WINDOW, KN), 1)
    nr = (n * 37) >> 8
    nc = n - 7 * nr
    return (((12 * (nr - 3) + nc - 3) & (KN - 1)) == lane).astype(F32)


def bias_kernel(sizes_ref, table_ref, bias_ref, limits_ref, po_ref, pk_ref):
    po_ref[...] = select((4 * QN, 4 * 48), own_source)
    pk_ref[...] = select((4 * KN, 10 * 48), key_source)
    row = lax.broadcasted_iota(jnp.int32, (8, 128), 0)
    limits_ref[...] = jnp.where(row == 0, sizes_ref[0, 0] - lax.axis_index("band") * 16, sizes_ref[0, 1])

    slots = lax.dot_general(
        table_ref[...],
        table_slots(),
        (((1,), (0,)), ((), ())),
        precision=lax.Precision.HIGHEST,
        preferred_element_type=F32,
    )
    qi = lax.broadcasted_iota(jnp.int32, (QN, KN), 0)
    si = lax.broadcasted_iota(jnp.int32, (QN, KN), 1)
    ji = (si + 36) & (KN - 1)
    kr, kc = split12(ji)
    qr, qc = split12(qi)
    window = (jnp.abs(kc - qc) <= 3) & (jnp.abs(kr - qr - 3) <= 3) & (ji < 120)
    rows = []
    for h in range(HEADS):
        line = jnp.broadcast_to(slots[h : h + 1, :] * LOG2E, (QN, KN))
        line = pltpu.roll(line, 0, 1, stride=1, stride_axis=0)
        rows.append(jnp.where(window, line, MASKED))
    bias_ref[...] = jnp.concatenate(rows, axis=0).T


def prep_kernel(x_ref, cot_ref, po_ref, xp_ref, xhat_ref, rstd_ref, dy_ref, dysum_ref, toc_ref, toz_ref):
    odd = (lax.axis_index("band") & 1) == 1
    for i in range(12):
        toc_ref[i] = jnp.where(odd, x_ref[i], x_ref[4 + i])
        toz_ref[i] = jnp.where(odd, x_ref[4 + i], x_ref[i])

    def block(rc, _):
        at = pl.ds(pl.multiple_of(rc * 192, 192), 192)
        xp = dot(po_ref[...], jnp.concatenate([x_ref[4 * i + rc] for i in range(4)], axis=0))
        xp_ref[at, :] = xp
        xhat, rstd = normed(xp)
        xhat_ref[at, :] = xhat
        rstd_ref[at, :] = jnp.broadcast_to(rstd, (192, 128))
        dy = dot(po_ref[...], jnp.concatenate([cot_ref[4 * i + rc] for i in range(4)], axis=0))
        dy_ref[at, :] = dy.astype(BF)
        dysum_ref[...] += jnp.sum(dy, axis=0, keepdims=True)
        return 0

    dysum_ref[...] = jnp.zeros_like(dysum_ref)
    lax.fori_loop(0, 4, block, 0, unroll=4)


def halo_kernel(x_ref, xc_ref, xz_ref, pk_ref, xk_ref):
    odd = (lax.axis_index("band") & 1) == 1

    def block(rc, _):
        rows = [jnp.where(odd, xc_ref[4 * i + rc], xz_ref[4 * i + rc]) for i in range(3)]
        rows += [x_ref[4 * i + rc] for i in range(4)]
        rows += [jnp.where(odd, xz_ref[4 * i + rc], xc_ref[4 * i + rc]) for i in range(3)]
        xk = dot(pk_ref[...], jnp.concatenate(rows, axis=0))
        xk_ref[pl.ds(pl.multiple_of(rc * 512, 512), 512), :] = normed(xk)[0]
        return 0

    lax.fori_loop(0, 4, block, 0, unroll=2)


def project_kernel(xhat_ref, xk_ref, wqkv_ref, vec_ref, q_ref, k_ref, v_ref):
    def vrow(i):
        return vec_ref[i : i + 1, :]

    def block(rc, _):
        at = pl.ds(pl.multiple_of(rc * 192, 192), 192)
        a1 = (xhat_ref[at, :] * vrow(0) + vrow(1)).astype(BF)
        q_ref[at, :] = (dot(a1, wqkv_ref[:, 0:256]) + vrow(2)).astype(BF)
        at = pl.ds(pl.multiple_of(rc * 512, 512), 512)
        a1k = (xk_ref[at, :] * vrow(0) + vrow(1)).astype(BF)
        k_ref[at, :] = dot(a1k, wqkv_ref[:, 256:512]).astype(BF)
        v_ref[at, :] = (dot(a1k, wqkv_ref[:, 512:768]) + vrow(3)).astype(BF)
        return 0

    lax.fori_loop(0, 4, block, 0, unroll=2)


def attend_kernel(limits_ref, bias_ref, q_ref, k_ref, v_ref, mixed_ref, p_ref):
    scale = 32 ** (-0.5)
    lane_head = lax.broadcasted_iota(jnp.int32, (QN, 256), 1) >> 5
    row0 = lax.axis_index("band") * 16
    height = limits_ref[0:1, 0:1]
    wide = limits_ref[1:2, 0:1]
    ks = lax.broadcasted_iota(jnp.int32, (KN, 384), 0)
    ql = lax.broadcasted_iota(jnp.int32, (KN, 384), 1)
    kj = (ks + 36) & (KN - 1)
    krow, kcol = split12(kj)
    qin = ql - 48 * ((ql * 171) >> 13)
    same = ks == qin

    def attend(k, _):
        rc = k >> 2
        cc = k & 3
        at_q = pl.ds(pl.multiple_of(k * QN, QN), QN)
        at_k = pl.ds(pl.multiple_of(k * KN, KN), KN)
        qbd = spread_heads(q_ref[at_q, :], lane_head)
        s = dot_nt(k_ref[at_k, :], qbd) * (scale * LOG2E) + bias_ref[...]
        r = krow * 4 + (rc - 12)
        c = kcol * 4 + cc
        okay = ((r >= -row0) & (r < height) & (c < wide)) | same
        s = jnp.where(okay, s, MASKED)
        top = jnp.max(s, axis=0, keepdims=True)
        e = jnp.exp2(s - top)
        p = e * (1.0 / jnp.sum(e, axis=0, keepdims=True))
        p_ref[at_k, :] = p
        full = dot_tn(p.astype(BF), v_ref[at_k, :])
        mixed_ref[at_q, :] = pick_heads(full, lane_head).astype(BF)
        return 0

    lax.fori_loop(0, CLS, attend, 0, unroll=CLS)


def feed_kernel(
    dy_ref,
    dysum_ref,
    mixed_ref,
    xp_ref,
    wo_ref,
    wu_ref,
    wd_ref,
    vec_ref,
    act_ref,
    dz_ref,
    a2_ref,
    da_ref,
    dx1_ref,
    x1_ref,
    dmix_ref,
    sums_ref,
    zsum_ref,
):
    def vrow(i):
        return vec_ref[i : i + 1, :]

    sums_ref[...] = jnp.zeros_like(sums_ref)
    sums_ref[7:8, :] = dysum_ref[...]
    zsum_ref[...] = jnp.zeros_like(zsum_ref)

    def feed(rc, _):
        at = pl.ds(pl.multiple_of(rc * 192, 192), 192)
        x1 = xp_ref[at, :] + (dot(mixed_ref[at, :], wo_ref[...]) + vrow(4))
        x1_ref[at, :] = x1
        xhat, rstd = normed(x1)
        a2 = (xhat * vrow(5) + vrow(6)).astype(BF)
        a2_ref[at, :] = a2
        dy = dy_ref[at, :]
        dn = jnp.zeros((192, 256), F32)
        for part in range(3):
            cols = slice(256 * part, 256 * part + 256)
            z = dot(a2, wu_ref[:, cols]) + vrow(8 + part)
            cube = (GELU0 * GELU1) * (z * z)
            up = 1.0 + jnp.tanh(z * (GELU0 + cube))
            hz = 0.5 * z
            act_ref[at, cols] = (hz * up).astype(BF)
            slope = up * (0.5 + hz * (2.0 - up) * (GELU0 + 3.0 * cube))
            dz = (dot_nt(dy, wd_ref[cols, :]) * slope).astype(BF)
            dz_ref[at, cols] = dz
            zsum_ref[:, cols] += jnp.sum(dz.astype(F32), axis=0, keepdims=True)
            dn = dn + dot_nt(dz, wu_ref[:, cols])
        dyf = dy.astype(F32)
        dx1 = dyf + norm_back(dn * vrow(5), xhat, rstd)
        dx1_ref[at, :] = dx1
        da = dx1.astype(BF)
        da_ref[at, :] = da
        dmix_ref[at, :] = dot_nt(da, wo_ref[...]).astype(BF)
        sums_ref[4:5, :] += jnp.sum(da.astype(F32), axis=0, keepdims=True)
        sums_ref[5:6, :] += jnp.sum(dn * xhat, axis=0, keepdims=True)
        sums_ref[6:7, :] += jnp.sum(dn, axis=0, keepdims=True)
        return 0

    lax.fori_loop(0, 4, feed, 0, unroll=4)


def back_kernel(
    q_ref,
    v_ref,
    p_ref,
    dmix_ref,
    own_ref,
    rimc_ref,
    rimz_ref,
    dsl_ref,
    tacc_ref,
    dkv_ref,
):
    odd = (lax.axis_index("band") & 1) == 1
    scale = 32 ** (-0.5)
    lane_head = lax.broadcasted_iota(jnp.int32, (QN, 256), 1) >> 5
    tacc_ref[...] = jnp.zeros_like(tacc_ref)

    def back_class(k):
        at_q = pl.ds(pl.multiple_of(k * QN, QN), QN)
        at_k = pl.ds(pl.multiple_of(k * KN, KN), KN)
        qbd = spread_heads(q_ref[at_q, :], lane_head)
        dobd = spread_heads(dmix_ref[at_q, :], lane_head)
        p = p_ref[at_k, :]
        dp = dot_nt(v_ref[at_k, :], dobd)
        dv = dot(p.astype(BF), dobd)
        pdp = p * dp
        ds = pdp - p * jnp.sum(pdp, axis=0, keepdims=True)
        tacc_ref[...] += ds
        dsl = ds.astype(BF)
        dsl_ref[at_k, :] = dsl
        dk = dot(dsl, qbd) * scale
        dkv_ref[at_k, 0:256] = dk.astype(BF)
        dkv_ref[at_k, 256:512] = dv.astype(BF)
        own_ref[at_q, 0:256] = dk[0:QN]
        own_ref[at_q, 256:512] = dv[0:QN]
        after = jnp.concatenate([dk[QN : QN + RIM], dv[QN : QN + RIM]], axis=1)
        before = jnp.concatenate([dk[KN - RIM :], dv[KN - RIM :]], axis=1)
        return after, before

    def attend_back(pair, _):
        after0, before0 = back_class(pair * 2)
        after1, before1 = back_class(pair * 2 + 1)
        at = pl.ds(pl.multiple_of(pair * 2 * RIM, 2 * RIM), 2 * RIM)
        after = jnp.concatenate([after0, after1], axis=0)
        before = jnp.concatenate([before0, before1], axis=0)
        rimc_ref[at, :] = jnp.where(odd, before, after).astype(BF)
        rimz_ref[at, :] = jnp.where(odd, after, before).astype(BF)
        return 0

    lax.fori_loop(0, CLS // 2, attend_back, 0, unroll=8)


def early_grads(act_ref, dy_ref, a2_ref, dz_ref, mixed_ref, da_ref, fd, fu, fo):
    fd[...] = dot_tn(act_ref[...], dy_ref[...])
    fu[...] = dot_tn(a2_ref[...], dz_ref[...])
    fo[...] = dot_tn(mixed_ref[...], da_ref[...])


def output_kernel(x1_ref, act_ref, wd_ref, vec_ref, po_ref, out_ref):
    def result(rc, _):
        at = pl.ds(pl.multiple_of(rc * 192, 192), 192)
        res = x1_ref[at, :] + dot(act_ref[at, :], wd_ref[...]) + vec_ref[7:8, :]
        back = dot_tn(po_ref[...], res.astype(BF)).astype(BF)
        for i in range(4):
            out_ref[4 * i + rc] = back[48 * i : 48 * i + 48]
        return 0

    lax.fori_loop(0, 4, result, 0, unroll=4)


def late_grads(
    dsl_ref,
    k_ref,
    tacc_ref,
    xhat_ref,
    xk_ref,
    dkv_ref,
    wqkv_ref,
    vt_ref,
    sums_ref,
    zsum_ref,
    dq_ref,
    fq_ref,
    fv_ref,
    tgrad_ref,
):
    scale = 32 ** (-0.5)
    lane_head = lax.broadcasted_iota(jnp.int32, (QN, 256), 1) >> 5

    def query(k, _):
        at_q = pl.ds(pl.multiple_of(k * QN, QN), QN)
        at_k = pl.ds(pl.multiple_of(k * KN, KN), KN)
        dq = pick_heads(dot_tn(dsl_ref[at_k, :], k_ref[at_k, :]), lane_head) * scale
        dq_ref[at_q, :] = dq.astype(BF)
        return 0

    lax.fori_loop(0, CLS, query, 0, unroll=16)
    dq = dq_ref[...]
    gain, shift = vt_ref[:, 0:1], vt_ref[:, 1:2]
    qsum = jnp.sum(dq.astype(F32), axis=0, keepdims=True)
    m = dot_tn(xhat_ref[...].astype(BF), dq)
    weight = wqkv_ref[:, 0:256].astype(F32)
    fq_ref[:, 0:256] = gain * m + shift * qsum
    gain_grad = jnp.sum(weight * m, axis=1, keepdims=True)
    shift_grad = jnp.sum(weight * qsum, axis=1, keepdims=True)
    xk = xk_ref[...].astype(BF)
    for cols in (slice(256, 512), slice(512, 768)):
        dkv = dkv_ref[:, cols.start - 256 : cols.stop - 256]
        kvsum = jnp.sum(dkv.astype(F32), axis=0, keepdims=True)
        m = dot_tn(xk, dkv)
        weight = wqkv_ref[:, cols].astype(F32)
        fq_ref[:, cols] = gain * m + shift * kvsum
        gain_grad = gain_grad + jnp.sum(weight * m, axis=1, keepdims=True)
        shift_grad = shift_grad + jnp.sum(weight * kvsum, axis=1, keepdims=True)
    lines = jnp.concatenate(
        [jnp.zeros((2, 256), F32), qsum, kvsum, sums_ref[4:8, :]]
        + [zsum_ref[:, 256 * i : 256 * i + 256] for i in range(3)]
        + [jnp.zeros((117, 256), F32)],
        axis=0,
    )
    lane = lax.broadcasted_iota(jnp.int32, (256, 128), 1)
    fv_ref[...] = jnp.where(lane == 0, gain_grad, jnp.where(lane == 1, shift_grad, lines.T))

    flat = tacc_ref[...].T
    qi = lax.broadcasted_iota(jnp.int32, (QN, KN), 0)
    lines = []
    for h in range(HEADS):
        part = flat[h * QN : (h + 1) * QN]
        for bit in range(6):
            turned = pltpu.roll(part, KN - (1 << bit), 1)
            part = jnp.where((qi >> bit) & 1 == 1, turned, part)
        lines.append(jnp.sum(part, axis=0, keepdims=True))
    tgrad_ref[...] = jnp.concatenate(lines, axis=0)


def input_kernel(
    own_ref, gotc_ref, gotz_ref, dq_ref, dx1_ref, xhat_ref, rstd_ref, wqkv_ref, vec_ref, po_ref, tok_ref
):
    odd = (lax.axis_index("band") & 1) == 1

    def block(rc, _):
        at = pl.ds(pl.multiple_of(rc * 192, 192), 192)
        mine = own_ref[at, :]
        got_c = gotc_ref[pl.ds(pl.multiple_of(rc * 160, 160), 160), :].astype(F32)
        got_z = gotz_ref[pl.ds(pl.multiple_of(rc * 160, 160), 160), :].astype(F32)
        got_a = jnp.where(odd, got_c, got_z)
        got_b = jnp.where(odd, got_z, got_c)
        gap = jnp.zeros((QN - RIM, 512), F32)
        parts = []
        for i in range(4):
            a = jnp.concatenate([got_a[i * RIM : (i + 1) * RIM], gap], axis=0)
            b = jnp.concatenate([gap, got_b[i * RIM : (i + 1) * RIM]], axis=0)
            parts.append(mine[i * QN : (i + 1) * QN] + a + b)
        dkv = jnp.concatenate(parts, axis=0).astype(BF)
        dn = dot_nt(dq_ref[at, :], wqkv_ref[:, 0:256]) + dot_nt(dkv, wqkv_ref[:, 256:768])
        dx = dx1_ref[at, :] + norm_back(dn * vec_ref[0:1, :], xhat_ref[at, :], rstd_ref[at, 0:1])
        back = dot_tn(po_ref[...], dx.astype(BF)).astype(BF)
        for i in range(4):
            tok_ref[4 * i + rc] = back[48 * i : 48 * i + 48]
        return 0

    lax.fori_loop(0, 4, block, 0, unroll=4)


EARLY = 896
LATE = 512


def widen(v):
    return jnp.concatenate([v, jnp.zeros((v.shape[0], 128 - v.shape[1]), F32)], axis=1)


def pack(wqkv, wo, wu, wd, vec):
    pieces = [(wqkv, 0, 0), (wo, 0, 768), (wd, 0, 1024), (vec, 0, 1280)]
    pieces += [(wu, 8, 0), (wd, 0, 768), (wd, -8, 1024)]
    total = 0.0
    for p, row, lane in pieces:
        rows, lanes = p.shape
        zero = jnp.zeros((), F32)
        if rows == 24 and lane == 1024 and row == 0:
            p = lax.pad(p, zero, ((0, -16, 0), (0, 0, 0)))
            rows = 8
        elif rows == 24:
            p = lax.pad(p, zero, ((-8 + row, -8 - row, 0), (0, 0, 0)))
            row, rows = 8, 8
        total = total + lax.pad(p, zero, ((row, 16 - row - rows, 0), (lane, EARLY + LATE - lane - lanes, 0)))
    return total.astype(BF)


def own_index():
    return lax.axis_index("maps") * 8 + lax.axis_index("band")


def unpack(blocks, big_qkv, big_out, big_up, big_down, vec, vt, fq, fo, fu, fd):
    me = own_index()
    for index, block in enumerate(blocks):
        core, across = divmod(index, 4)
        for z in range(4):
            slab = block[z].astype(F32)
            o = me ^ (core | (z << 1) | (across << 3))
            at = pl.ds(pl.multiple_of(o * 8, 8), 8)
            fq[at, :] = slab[0:8, 0:768]
            vt[at, :] = slab[0:8, 1280:1408]
            for b, rows in enumerate((slab[0:8, 1024:1280], slab[8:16, 768:1024], slab[8:16, 1024:1280])):
                fd[pl.ds(pl.multiple_of(o * 24 + 8 * b, 8), 8), :] = rows
            fo[at, :] = slab[0:8, 768:1024]
            fu[at, :] = slab[8:16, 0:768]
    big_qkv[...] = fq[...].astype(BF)
    vec[...] = vt[...].T[0 : vec.shape[0]]
    big_out[...] = fo[...].astype(BF)
    big_up[...] = fu[...].astype(BF)
    big_down[...] = fd[...].astype(BF)


def main_kernel(*refs):
    blocks, (xhat, x, xz, xc, pk, xp, bias, limits, dy, dysum) = refs[:8], refs[8:18]
    act, dx1, x1, own, rimc, rimz, dq, out_ref, big_qkv, big_down, vec = refs[18:29]
    q, k, v, mixed, p, dz, a2, da, dmix, sums, zsum, dsl, tacc, dkv = refs[29:43]
    fq, fv, tgrad, fd, fu, fo, big_out, big_up, vt, xk = refs[43:]
    halo_kernel(x, xc, xz, pk, xk)
    unpack(blocks, big_qkv, big_out, big_up, big_down, vec, vt, fq, fo, fu, fd)
    project_kernel(xhat, xk, big_qkv, vec, q, k, v)
    attend_kernel(limits, bias, q, k, v, mixed, p)
    feed_kernel(dy, dysum, mixed, xp, big_out, big_up, big_down, vec, act, dz, a2, da, dx1, x1, dmix, sums, zsum)
    back_kernel(q, v, p, dmix, own, rimc, rimz, dsl, tacc, dkv)
    early_grads(act, dy, a2, dz, mixed, da, fd, fu, fo)
    late_grads(dsl, k, tacc, xhat, xk, dkv, big_qkv, vt, sums, zsum, dq, fq, fv, tgrad)
    table = tgrad[...]
    me = own_index()
    for o in range(32):
        at = slice(8 * o, 8 * o + 8)
        top = [fd[24 * o + 8 * b : 24 * o + 8 * b + 8, :] for b in range(3)] + [fo[at, 0:128], fq[at, 0:512]]
        low = [fu[at, :], fo[at, 128:256], fq[at, 512:768], fv[at, :], table]
        both = jnp.concatenate([jnp.concatenate(top, axis=1), jnp.concatenate(low, axis=1)], axis=0)
        out_ref[frame_slot(me, o)] = both.astype(BF)


def frame_slot(me, o):
    m = me ^ o
    return (m & 1) * 16 + (m >> 3) * 4 + ((m >> 1) & 3)


def shard_grads(refs, vrows):
    total = refs[0][...] + sum(ref[...].astype(F32) for ref in refs[1:4])
    early, late = total[:, :EARLY], total[:, EARLY:]
    return [
        jnp.concatenate([late[0:8], late[8:16, 0:256]], axis=1),
        jnp.concatenate([early[0:8, 768:896], early[8:16, 768:896]], axis=1),
        early[8:16, 0:768],
        jnp.concatenate([early[0:8, 256 * b : 256 * b + 256] for b in range(3)], axis=0),
        late[8:16, 256 : 256 + vrows],
        lax.dot_general(
            late[8:16, 384:512],
            table_slots(),
            (((1,), (1,)), ((), ())),
            precision=lax.Precision.HIGHEST,
            preferred_element_type=F32,
        ),
    ]


def update_kernel(*refs):
    w, first, second, outs = refs[4:10], refs[10:16], refs[16:22], refs[22:]
    vrows = w[4].shape[1]
    grads = shard_grads(refs, vrows)
    row = lax.broadcasted_iota(jnp.int32, (8, 128), 0)
    lane = lax.broadcasted_iota(jnp.int32, (8, 128), 1)
    norms = jnp.zeros((8, 128), F32)
    for i in range(6):
        update = adam_parts(w[i][...], grads[i], first[i][...], second[i][...])[2]
        outs[i][...] = update
        for line, v in ((0, w[i][...]), (1, update)):
            sums = jnp.sum(v * v, axis=0, keepdims=True)
            if i == 4:
                sums = pltpu.roll(widen(sums), 4, 1)
                norms = jnp.where((row == line) & (lane >= 4) & (lane < 4 + vrows), sums, norms)
            else:
                at = i if i < 4 else 4 + vrows
                norms = jnp.where((row == line) & (lane == at), jnp.sum(sums, axis=1, keepdims=True), norms)
    outs[6][...] = norms


def moments_kernel(*refs):
    first, second, outs = refs[4:10], refs[10:16], refs[16:]
    grads = shard_grads(refs, first[4].shape[1])
    for i in range(6):
        new_first, new_second, _ = adam_parts(0.0, grads[i], first[i][...], second[i][...])
        outs[2 * i][...] = new_first
        outs[2 * i + 1][...] = new_second


def step_kernel(mine_ref, a_ref, b_ref, c_ref, d_ref, *refs):
    w, update, outs = refs[0:6], refs[6:12], refs[12:]
    vrows = w[4].shape[1]
    total = a_ref[...] + b_ref[...] + c_ref[...] + d_ref[...]
    lane = lax.broadcasted_iota(jnp.int32, (8, 128), 1)
    norms = jnp.sqrt(jnp.where(lane == 4 + vrows, mine_ref[...], total))
    outs[6][...] = norms[0:1, 0:16]
    outs[7][...] = norms[1:2, 0:16]
    rate = LEARN_RATE * norms[0:1] / (norms[1:2] + RATIO_EPS)
    for i in range(6):
        if i == 4:
            r = pltpu.roll(rate, 124, 1)[:, 0:vrows]
        else:
            at = i if i < 4 else 4 + vrows
            r = rate[:, at : at + 1]
        outs[i][...] = w[i][...] - r * update[i][...]


def stack_kernel(*refs):
    for i, ref in enumerate(refs[:4]):
        refs[4][i] = ref[...]


def call(kernel, out_shape, scratch, *args, smem=0, flops=10**8, vmem=16):
    vm = pl.BlockSpec(memory_space=pltpu.VMEM)
    specs = [pl.BlockSpec(memory_space=pltpu.SMEM)] * smem + [vm] * (len(args) - smem)
    return pl.pallas_call(
        kernel,
        out_shape=out_shape,
        in_specs=specs,
        out_specs=jax.tree.map(lambda _: vm, out_shape),
        scratch_shapes=scratch,
        compiler_params=pltpu.CompilerParams(vmem_limit_bytes=vmem * 2**20),
        cost_estimate=pl.CostEstimate(flops=flops, bytes_accessed=10**6, transcendentals=0),
    )(*args)


def sds(shape, dtype=BF):
    return jax.ShapeDtypeStruct(shape, dtype)


def exchange_groups(maps, band):
    zbits = band.bit_length() - 2
    mbits = maps.bit_length() - 1
    cut = lambda lo, n: [(lo + i, min(2, n - i)) for i in range(0, n, 2)]
    return cut(1, zbits) + cut(1 + zbits, mbits) + [(0, 1)]


def swap(block, mask, count):
    return lax.ppermute(block, AXES, [(k, k ^ mask) for k in range(count)])


def frame_masks(groups):
    masks = [0]
    for lo, bits in groups:
        masks = [m ^ (d << lo) for d in range(1 << bits) for m in masks]
    return masks


def gather_all(slab, groups, count):
    block = slab[None]
    for lo, bits in groups:
        block = jnp.concatenate(
            [block] + [swap(block, d << lo, count) for d in range(1, 1 << bits)], axis=0
        )
    return block


def scatter_sum(grads, groups, count):
    for lo, bits in reversed(groups):
        grads = add_stage(grads, lo, bits, count)
    return grads[0]


def adam_parts(weight, grad, first, second):
    new_first = BETA_FIRST * first + (1.0 - BETA_FIRST) * grad
    new_second = BETA_SECOND * second + (1.0 - BETA_SECOND) * grad * grad
    update = (
        new_first
        / (1.0 - BETA_FIRST**STEP)
        / (jnp.sqrt(new_second / (1.0 - BETA_SECOND**STEP)) + ADAM_EPS)
        + DECAY_RATE * weight
    )
    return (new_first, new_second, update)


def squares_of(matrices, rowwise):
    return jnp.concatenate(
        [
            jnp.stack([jnp.sum(matrix * matrix) for matrix in matrices]),
            jnp.sum(rowwise * rowwise, axis=1),
        ]
    )


def bias_outputs():
    return (sds((KN, 384), F32), sds((8, 128), jnp.int32), sds((4 * QN, 4 * 48)), sds((4 * KN, 10 * 48)))


def prep_outputs():
    return (
        sds((768, 256), F32),
        sds((768, 256), F32),
        sds((768, 128), F32),
        sds((768, 256)),
        sds((1, 256), F32),
        sds((12, 48, 256)),
        sds((12, 48, 256)),
    )


def project_outputs():
    return (sds((768, 256)), sds((CLS * KN, 256)), sds((CLS * KN, 256)))


def attend_outputs():
    return (sds((768, 256)), sds((CLS * KN, 384), F32))


def feed_outputs():
    return (
        sds((768, 768)),
        sds((768, 768)),
        sds((768, 256)),
        sds((768, 256)),
        sds((768, 256), F32),
        sds((768, 256), F32),
        sds((768, 256)),
        sds((8, 256), F32),
        sds((1, 768), F32),
    )


def back_outputs():
    return (
        sds((768, 512), F32),
        sds((CLS * RIM, 512)),
        sds((CLS * RIM, 512)),
        sds((CLS * KN, 384)),
        sds((KN, 384), F32),
        sds((CLS * KN, 512)),
    )


def late_outputs():
    return (
        sds((768, 256)),
        sds((256, 768), F32),
        sds((256, 128), F32),
        sds((HEADS, KN), F32),
    )


def beside(block, band):
    touching = [(b, b + 1 if b % 2 else b - 1) for b in range(band)]
    return (
        lax.ppermute(block[0], "band", [(b, b ^ 1) for b in range(band)]),
        lax.ppermute(block[1], "band", [(b, to) for b, to in touching if 0 <= to < band]),
    )


def packed_step(tokens_in, cotangent, map_sizes, weights, firsts, seconds):
    count = 32
    vrows = weights[4].shape[0]
    turn = lambda arrays: tuple(a.T if i == 4 else a for i, a in enumerate(arrays))
    weights, firsts, seconds = turn(weights), turn(firsts), turn(seconds)
    slab = pack(*weights[:5])
    slab, sizes = lax.optimization_barrier((slab, map_sizes))
    slabs = [slab] + [swap(slab, d << 1, count) for d in (1, 2, 3)]
    bias, limits, po, pk = call(bias_kernel, bias_outputs(), [], sizes, weights[5], smem=1, flops=10**9, vmem=4)
    *slabs, bias = lax.optimization_barrier((*slabs, bias))
    column = call(stack_kernel, sds((4, 16, EARLY + LATE)), [], *slabs, vmem=4)
    column, x = lax.optimization_barrier((column, tokens_in))
    blocks = [column] + [swap(column, d << 3, count) for d in (1, 2, 3)]
    xp, xhat, rstd, dy, dysum, *edges = call(prep_kernel, prep_outputs(), [], x, cotangent, po, flops=2 * 10**9, vmem=8)
    x_core, x_next = beside(edges, 8)
    *far, xp = lax.optimization_barrier((*blocks[1:], xp))
    blocks = [blocks[0]] + far + [swap(block, 1, count) for block in [blocks[0]] + far]
    act_s, dz_s, a2_s, da_s, dx1_s, x1_s, dmix_s, sums_s, zsum_s = feed_outputs()
    own_s, rimc_s, rimz_s, dsl_s, tacc_s, dkv_s = back_outputs()
    dq_s, fq_s, fv_s, tgrad_s = late_outputs()
    act, dx1, x1, own, rim_c, rim_z, dq, grads, big_qkv, big_down, vec = call(
        main_kernel,
        (act_s, dx1_s, x1_s, own_s, rimc_s, rimz_s, dq_s)
        + (sds((count, 16, EARLY + LATE)), sds((256, 768)), sds((768, 256)), sds((vrows, 256), F32)),
        [
            pltpu.VMEM(o.shape, o.dtype)
            for o in project_outputs()
            + attend_outputs()
            + (dz_s, a2_s, da_s, dmix_s, sums_s, zsum_s, dsl_s, tacc_s, dkv_s, fq_s, fv_s, tgrad_s)
            + (sds((768, 256), F32), sds((256, 768), F32), sds((256, 256), F32))
            + (sds((256, 256)), sds((256, 768)), sds((256, 128), F32), sds((CLS * KN, 256), F32))
        ],
        *blocks, xhat, x, x_next, x_core, pk, xp, bias, limits, dy, dysum,
        flops=15 * 10**9, vmem=24,
    )
    layer_out = call(output_kernel, sds((16, 48, 256)), [], x1, act, big_down, vec, po, flops=10**9, vmem=8)
    got_c, got_z = beside((rim_c, rim_z), 8)
    grads = add_stage(add_stage(grads, 0, 1, count), 3, 2, count)
    grads, own = lax.optimization_barrier((grads, own))
    tokens_grad = call(
        input_kernel, sds((16, 48, 256)), [], own, got_c, got_z, dq, dx1, xhat, rstd, big_qkv, vec, po,
        flops=10**9, vmem=8,
    )
    low = grads.astype(BF)
    parts = [grads[0]] + [swap(low[d], d << 1, count) for d in (1, 2, 3)]
    parts[0], tokens_grad, layer_out = lax.optimization_barrier((parts[0], tokens_grad, layer_out))

    shapes = [sds(w.shape, F32) for w in weights]
    *updates, mine = call(
        update_kernel, tuple(shapes) + (sds((8, 128), F32),), [], *parts, *weights, *firsts, *seconds, vmem=4
    )
    moments = call(
        moments_kernel, tuple(shape for shape in shapes for _ in range(2)), [], *parts, *firsts, *seconds, vmem=4
    )
    squares = mine + swap(mine, 1, count)
    squares = squares + swap(squares, 8, count) + swap(squares, 16, count) + swap(squares, 24, count)
    last = [swap(squares, d << 1, count) for d in (1, 2, 3)]
    squares, *moments = lax.optimization_barrier((squares, *moments))
    news = call(
        step_kernel,
        tuple(shapes) + (sds((1, 16), F32),) * 2,
        [],
        mine, squares, *last, *weights, *updates, vmem=4,
    )
    results = [layer_out, tokens_grad]
    for i in range(6):
        three = (moments[2 * i], moments[2 * i + 1], news[i])
        results += [a.T for a in three] if i == 4 else three
    return tuple(results) + (news[6].reshape(16), news[7].reshape(16))


def add_stage(grads, lo, bits, count):
    low = grads.astype(BF).reshape((1 << bits, -1) + grads.shape[1:])
    total = grads.reshape(low.shape)[0].astype(F32)
    for d in range(1, 1 << bits):
        total = total + swap(low[d], d << lo, count).astype(F32)
    return total


def per_device(
    maps,
    band,
    tokens_in,
    cotangent,
    map_sizes,
    w_qkv,
    w_out,
    w_up,
    w_down,
    vectors,
    pos_table,
    first_qkv,
    second_qkv,
    first_out,
    second_out,
    first_up,
    second_up,
    first_down,
    second_down,
    first_vectors,
    second_vectors,
    first_table,
    second_table,
):
    if w_qkv.shape[0] == 8 and (maps, band) == (4, 8):
        return packed_step(
            tokens_in, cotangent, map_sizes,
            (w_qkv, w_out, w_up, w_down, vectors, pos_table),
            (first_qkv, first_out, first_up, first_down, first_vectors, first_table),
            (second_qkv, second_out, second_up, second_down, second_vectors, second_table),
        )
    count = maps * band
    rows = w_qkv.shape[0]
    vrows = vectors.shape[0]
    groups = exchange_groups(maps, band)
    masks = np.array(frame_masks(groups))
    inverse = np.argsort(masks)
    me = lax.axis_index(AXES)
    def pack(qkv, out, upw, dnw, vec):
        dn = dnw.reshape(3, rows, 256).transpose(1, 0, 2).reshape(rows, 768)
        vt = jnp.pad(vec.T, ((0, 0), (0, 128 - vrows)))
        return jnp.concatenate([qkv, out, upw, dn, vt], axis=1)

    slab = pack(*(w.astype(BF) for w in (w_qkv, w_out, w_up, w_down, vectors)))
    block = gather_all(slab, groups, count)
    order = jnp.asarray(inverse, jnp.int32)[jnp.arange(count, dtype=jnp.int32) ^ me]
    whole = jnp.take(block, order, axis=0).reshape(256, -1)
    big_qkv = whole[:, 0:768]
    big_out = whole[:, 768:1024]
    big_up = whole[:, 1024:1792]
    big_down = (
        whole[:, 1792:2560].reshape(count, rows, 3, 256).transpose(0, 2, 1, 3).reshape(768, 256)
    )
    vt = whole[:, 2560:].astype(F32)
    vec = vt[:, :vrows].T

    bias, limits, po, pk = call(bias_kernel, bias_outputs(), [], map_sizes, pos_table, smem=1, flops=10**9)
    xp, xhat, rstd, dy, dysum, *edges = call(prep_kernel, prep_outputs(), [], tokens_in, cotangent, po, flops=2 * 10**9)
    x_core, x_next = beside(edges, band)
    xk = call(halo_kernel, sds((CLS * KN, 256), F32), [], tokens_in, x_core, x_next, pk, flops=10**9)
    queries, keys, values = call(project_kernel, project_outputs(), [], xhat, xk, big_qkv, vec, flops=10**9)
    mixed, probs = call(attend_kernel, attend_outputs(), [], limits, bias, queries, keys, values, flops=3 * 10**9)
    act, dz, a2, da, dx1, x1, dmix, sums, zsum = call(
        feed_kernel,
        feed_outputs(),
        [],
        dy, dysum, mixed, xp, big_out, big_up, big_down, vec,
        flops=4 * 10**9,
    )
    own, rim_c, rim_z, dsl, tacc, dkv = call(
        back_kernel, back_outputs(), [], queries, values, probs, dmix, flops=4 * 10**9
    )
    got_c, got_z = beside((rim_c, rim_z), band)
    grad_down, grad_up, grad_out = call(
        early_grads,
        (sds((768, 256), F32), sds((256, 768), F32), sds((256, 256), F32)),
        [],
        act, dy, a2, dz, mixed, da,
        flops=10**9,
    )
    dq, grad_qkv, grad_vec, table_grad = call(
        late_grads,
        late_outputs(),
        [],
        dsl, keys, tacc, xhat, xk, dkv, big_qkv, vt, sums, zsum,
        flops=3 * 10**9,
    )
    layer_out = call(output_kernel, sds((16, 48, 256)), [], x1, act, big_down, vec, po, flops=10**9)
    tokens_grad = call(
        input_kernel, sds((16, 48, 256)), [], own, got_c, got_z, dq, dx1, xhat, rstd, big_qkv, vec, po, flops=10**9
    )

    packed = jnp.concatenate(
        [
            grad_qkv.reshape(count, rows, 768),
            grad_out.reshape(count, rows, 256),
            grad_up.reshape(count, rows, 768),
            grad_down.reshape(count, 3, rows, 256).transpose(0, 2, 1, 3).reshape(count, rows, 768),
            grad_vec.reshape(count, rows, 128),
        ],
        axis=2,
    )
    packed = jnp.take(packed, jnp.asarray(masks, jnp.int32) ^ me, axis=0)
    red = scatter_sum(packed, groups, count)
    red_qkv = red[:, 0:768]
    red_out = red[:, 768:1024]
    red_up = red[:, 1024:1792]
    red_down = red[:, 1792:2560].reshape(rows, 3, 256).transpose(1, 0, 2).reshape(3 * rows, 256)
    red_vec = red[:, 2560 : 2560 + vrows].T

    steps = np.arange(-3, 4)
    lanes = ((12 * steps[:, None] + steps[None, :]) % KN).reshape(-1)
    table_total = lax.psum(table_grad, AXES)[:, lanes]

    part_qkv = adam_parts(w_qkv, red_qkv, first_qkv, second_qkv)
    part_out = adam_parts(w_out, red_out, first_out, second_out)
    part_up = adam_parts(w_up, red_up, first_up, second_up)
    part_down = adam_parts(w_down, red_down, first_down, second_down)
    part_vec = adam_parts(vectors, red_vec, first_vectors, second_vectors)
    part_table = adam_parts(pos_table, table_total, first_table, second_table)
    local_weight_sq = squares_of((w_qkv, w_out, w_up, w_down), vectors)
    local_update_sq = squares_of((part_qkv[2], part_out[2], part_up[2], part_down[2]), part_vec[2])
    weight_sq, update_sq = lax.psum((local_weight_sq, local_update_sq), AXES)
    table_weight = jnp.sqrt(jnp.sum(pos_table * pos_table))
    table_update = jnp.sqrt(jnp.sum(part_table[2] * part_table[2]))
    weight_norms = jnp.concatenate([jnp.sqrt(weight_sq), table_weight[None]])
    update_norms = jnp.concatenate([jnp.sqrt(update_sq), table_update[None]])
    ratios = weight_norms / (update_norms + RATIO_EPS)
    next_qkv = w_qkv - LEARN_RATE * ratios[0] * part_qkv[2]
    next_out = w_out - LEARN_RATE * ratios[1] * part_out[2]
    next_up = w_up - LEARN_RATE * ratios[2] * part_up[2]
    next_down = w_down - LEARN_RATE * ratios[3] * part_down[2]
    next_vectors = vectors - LEARN_RATE * ratios[4 : 4 + vrows][:, None] * part_vec[2]
    next_table = pos_table - LEARN_RATE * ratios[4 + vrows] * part_table[2]
    return (
        layer_out,
        tokens_grad,
        part_qkv[0],
        part_qkv[1],
        next_qkv,
        part_out[0],
        part_out[1],
        next_out,
        part_up[0],
        part_up[1],
        next_up,
        part_down[0],
        part_down[1],
        next_down,
        part_vec[0],
        part_vec[1],
        next_vectors,
        part_table[0],
        part_table[1],
        next_table,
        weight_norms,
        update_norms,
    )


def solution(mesh):
    both = P(AXES, None)
    side = P(None, AXES)
    tall = P(AXES, None, None)
    copied = P()
    return jax.shard_map(
        functools.partial(per_device, mesh.shape["maps"], mesh.shape["band"]),
        mesh=mesh,
        in_specs=(tall, tall, P("maps", None))
        + (both,) * 4
        + (side, copied)
        + (both,) * 8
        + (side, side, copied, copied),
        out_specs=(tall, tall) + (both,) * 12 + (side,) * 3 + (copied,) * 5,
        check_vma=False,
    )
```

```python
import functools

import jax
import jax.numpy as jnp
import numpy as np
from jax import lax
from jax.experimental import pallas as pl
from jax.experimental.pallas import tpu as pltpu
from jax.sharding import PartitionSpec as P

HEADS = 8
WINDOW = 7
DIL = 4
STEP = 10
NORM_EPS = 1e-05
BETA_FIRST = 0.9
BETA_SECOND = 0.999
ADAM_EPS = 1e-06
DECAY_RATE = 0.01
LEARN_RATE = 0.2
RATIO_EPS = 1e-06
MASKED = -1e30
LOG2E = 1.4426950408889634
GELU0 = 0.7978845608028654
GELU1 = 0.044715
AXES = ("maps", "band")

BF = jnp.bfloat16
F32 = jnp.float32

CLS = DIL * DIL
QN = 48
KN = 128
RIM = 40


def dot(a, b):
    return lax.dot_general(a, b, (((1,), (0,)), ((), ())), preferred_element_type=F32)


def dot_nt(a, b):
    return lax.dot_general(a, b, (((1,), (1,)), ((), ())), preferred_element_type=F32)


def dot_tn(a, b):
    return lax.dot_general(a, b, (((0,), (0,)), ((), ())), preferred_element_type=F32)


def select(shape, source):
    o = lax.broadcasted_iota(jnp.int32, shape, 0)
    return (source(o) == lax.broadcasted_iota(jnp.int32, shape, 1)).astype(F32).astype(BF)


def own_source(o):
    cc = (o * 171) >> 13
    qr, qc = split12(o - QN * cc)
    return qr * 48 + qc * 4 + cc


def key_source(o):
    j = ((o & (KN - 1)) + 36) & (KN - 1)
    kr, kc = split12(j)
    return jnp.where(j < 120, kr * 48 + kc * 4 + (o >> 7), -1)


def normed(v):
    mean = jnp.mean(v, axis=-1, keepdims=True)
    cen = v - mean
    var = jnp.mean(cen * cen, axis=-1, keepdims=True)
    rstd = lax.rsqrt(var + NORM_EPS)
    return cen * rstd, rstd


def norm_back(g, xhat, rstd):
    m1 = jnp.mean(g, axis=-1, keepdims=True)
    m2 = jnp.mean(g * xhat, axis=-1, keepdims=True)
    return rstd * (g - m1 - xhat * m2)


def spread_heads(v, lane_head):
    zero = jnp.zeros((QN, 128), v.dtype)
    rows = []
    for h in range(HEADS):
        half = [zero, zero]
        half[h // 4] = jnp.where(lane_head == h % 4, v[:, 128 * (h // 4) : 128 * (h // 4) + 128], zero)
        rows.append(jnp.concatenate(half, axis=1))
    return jnp.concatenate(rows, axis=0)


def pick_heads(full, lane_head):
    halves = []
    for side in range(2):
        parts = [full[h * QN : (h + 1) * QN, 128 * side : 128 * side + 128] for h in range(4 * side, 4 * side + 4)]
        low = jnp.where(lane_head == 0, parts[0], parts[1])
        high = jnp.where(lane_head == 2, parts[2], parts[3])
        halves.append(jnp.where(lane_head < 2, low, high))
    return jnp.concatenate(halves, axis=1)


def split12(v):
    q = (v * 43) >> 9
    return q, v - 12 * q


def table_slots():
    n = lax.broadcasted_iota(jnp.int32, (WINDOW * WINDOW, KN), 0)
    lane = lax.broadcasted_iota(jnp.int32, (WINDOW * WINDOW, KN), 1)
    nr = (n * 37) >> 8
    nc = n - 7 * nr
    return (((12 * (nr - 3) + nc - 3) & (KN - 1)) == lane).astype(F32)


def bias_kernel(sizes_ref, table_ref, bias_ref, limits_ref, po_ref, pk_ref):
    po_ref[...] = select((4 * QN, 4 * 48), own_source)
    pk_ref[...] = select((4 * KN, 10 * 48), key_source)
    row = lax.broadcasted_iota(jnp.int32, (8, 128), 0)
    limits_ref[...] = jnp.where(row == 0, sizes_ref[0, 0] - lax.axis_index("band") * 16, sizes_ref[0, 1])

    slots = lax.dot_general(
        table_ref[...],
        table_slots(),
        (((1,), (0,)), ((), ())),
        precision=lax.Precision.HIGHEST,
        preferred_element_type=F32,
    )
    qi = lax.broadcasted_iota(jnp.int32, (QN, KN), 0)
    si = lax.broadcasted_iota(jnp.int32, (QN, KN), 1)
    ji = (si + 36) & (KN - 1)
    kr, kc = split12(ji)
    qr, qc = split12(qi)
    window = (jnp.abs(kc - qc) <= 3) & (jnp.abs(kr - qr - 3) <= 3) & (ji < 120)
    rows = []
    for h in range(HEADS):
        line = jnp.broadcast_to(slots[h : h + 1, :] * LOG2E, (QN, KN))
        line = pltpu.roll(line, 0, 1, stride=1, stride_axis=0)
        rows.append(jnp.where(window, line, MASKED))
    bias_ref[...] = jnp.concatenate(rows, axis=0).T


def prep_kernel(x_ref, cot_ref, po_ref, xp_ref, xhat_ref, rstd_ref, dy_ref, dysum_ref, toc_ref, toz_ref):
    odd = (lax.axis_index("band") & 1) == 1
    for i in range(12):
        toc_ref[i] = jnp.where(odd, x_ref[i], x_ref[4 + i])
        toz_ref[i] = jnp.where(odd, x_ref[4 + i], x_ref[i])

    def block(rc, _):
        at = pl.ds(pl.multiple_of(rc * 192, 192), 192)
        xp = dot(po_ref[...], jnp.concatenate([x_ref[4 * i + rc] for i in range(4)], axis=0))
        xp_ref[at, :] = xp
        xhat, rstd = normed(xp)
        xhat_ref[at, :] = xhat
        rstd_ref[at, :] = jnp.broadcast_to(rstd, (192, 128))
        dy = dot(po_ref[...], jnp.concatenate([cot_ref[4 * i + rc] for i in range(4)], axis=0))
        dy_ref[at, :] = dy.astype(BF)
        dysum_ref[...] += jnp.sum(dy, axis=0, keepdims=True)
        return 0

    dysum_ref[...] = jnp.zeros_like(dysum_ref)
    lax.fori_loop(0, 4, block, 0, unroll=4)


def halo_kernel(x_ref, xc_ref, xz_ref, pk_ref, xk_ref):
    odd = (lax.axis_index("band") & 1) == 1

    def block(rc, _):
        rows = [jnp.where(odd, xc_ref[4 * i + rc], xz_ref[4 * i + rc]) for i in range(3)]
        rows += [x_ref[4 * i + rc] for i in range(4)]
        rows += [jnp.where(odd, xz_ref[4 * i + rc], xc_ref[4 * i + rc]) for i in range(3)]
        xk = dot(pk_ref[...], jnp.concatenate(rows, axis=0))
        xk_ref[pl.ds(pl.multiple_of(rc * 512, 512), 512), :] = normed(xk)[0]
        return 0

    lax.fori_loop(0, 4, block, 0, unroll=2)


def project_kernel(xhat_ref, xk_ref, wqkv_ref, vec_ref, q_ref, k_ref, v_ref):
    def vrow(i):
        return vec_ref[i : i + 1, :]

    def block(rc, _):
        at = pl.ds(pl.multiple_of(rc * 192, 192), 192)
        a1 = (xhat_ref[at, :] * vrow(0) + vrow(1)).astype(BF)
        q_ref[at, :] = (dot(a1, wqkv_ref[:, 0:256]) + vrow(2)).astype(BF)
        at = pl.ds(pl.multiple_of(rc * 512, 512), 512)
        a1k = (xk_ref[at, :] * vrow(0) + vrow(1)).astype(BF)
        k_ref[at, :] = dot(a1k, wqkv_ref[:, 256:512]).astype(BF)
        v_ref[at, :] = (dot(a1k, wqkv_ref[:, 512:768]) + vrow(3)).astype(BF)
        return 0

    lax.fori_loop(0, 4, block, 0, unroll=2)


def attend_kernel(limits_ref, bias_ref, q_ref, k_ref, v_ref, mixed_ref, p_ref, other_ref):
    scale = 32 ** (-0.5)
    lane_head = lax.broadcasted_iota(jnp.int32, (QN, 128), 1) >> 5
    row0 = lax.axis_index("band") * 16
    height = limits_ref[0:1, 0:1]
    wide = limits_ref[1:2, 0:1]
    ks = lax.broadcasted_iota(jnp.int32, (KN, 384), 0)
    ql = lax.broadcasted_iota(jnp.int32, (KN, 384), 1)
    other_ref[...] = jnp.where(ks == ql - 48 * ((ql * 171) >> 13), 0.0, 1.0)
    krow, kcol = split12((lax.broadcasted_iota(jnp.int32, (KN, 128), 0) + 36) & (KN - 1))

    def attend(k, _):
        rc = k >> 2
        cc = k & 3
        at_q = pl.ds(pl.multiple_of(k * QN, QN), QN)
        at_k = pl.ds(pl.multiple_of(k * KN, KN), KN)
        qbd = spread_heads(q_ref[at_q, :], lane_head)
        r = krow * 4 + (rc - 12)
        c = kcol * 4 + cc
        off = jnp.where((r >= -row0) & (r < height) & (c < wide), 0.0, MASKED)
        off = bias_ref[...] + jnp.concatenate([off] * 3, axis=1) * other_ref[...]
        s = dot_nt(k_ref[at_k, :], qbd) * (scale * LOG2E) + off
        top = jnp.max(s, axis=0, keepdims=True)
        e = jnp.exp2(s - top)
        p = e * (1.0 / jnp.sum(e, axis=0, keepdims=True))
        p_ref[at_k, :] = p
        full = dot_tn(p.astype(BF), v_ref[at_k, :])
        mixed_ref[at_q, :] = pick_heads(full, lane_head).astype(BF)
        return 0

    lax.fori_loop(0, CLS, attend, 0, unroll=CLS)


def feed_kernel(
    dy_ref,
    dysum_ref,
    mixed_ref,
    xp_ref,
    wo_ref,
    wu_ref,
    wd_ref,
    vec_ref,
    act_ref,
    dz_ref,
    a2_ref,
    da_ref,
    dx1_ref,
    x1_ref,
    dmix_ref,
    sums_ref,
    zsum_ref,
    xhat_ref,
    rstd_ref,
):
    def vrow(i):
        return vec_ref[i : i + 1, :]

    sums_ref[...] = jnp.zeros_like(sums_ref)
    sums_ref[7:8, :] = dysum_ref[...]
    zsum_ref[...] = jnp.zeros_like(zsum_ref)

    def inner(rc, _):
        at = pl.ds(pl.multiple_of(rc * 192, 192), 192)
        x1 = xp_ref[at, :] + (dot(mixed_ref[at, :], wo_ref[...]) + vrow(4))
        x1_ref[at, :] = x1
        xhat, rstd = normed(x1)
        xhat_ref[at, :] = xhat
        rstd_ref[at, :] = jnp.broadcast_to(rstd, (192, 128))
        a2_ref[at, :] = (xhat * vrow(5) + vrow(6)).astype(BF)
        return 0

    lax.fori_loop(0, 4, inner, 0, unroll=4)

    def hidden(rc, _):
        at = pl.ds(pl.multiple_of(rc * 192, 192), 192)
        for part in range(3):
            cols = slice(256 * part, 256 * part + 256)
            z = dot(a2_ref[at, :], wu_ref[:, cols]) + vrow(8 + part)
            cube = (GELU0 * GELU1) * (z * z)
            up = 0.5 + 0.5 * jnp.tanh(z * (GELU0 + cube))
            act = z * up
            act_ref[at, cols] = act.astype(BF)
            slope = up * (1.0 + (z - act) * (2.0 * GELU0 + 6.0 * cube))
            dz = dot_nt(dy_ref[at, :], wd_ref[cols, :]) * slope
            zsum_ref[:, cols] += jnp.sum(dz, axis=0, keepdims=True)
            dz_ref[at, cols] = dz.astype(BF)
        return 0

    lax.fori_loop(0, 4, hidden, 0, unroll=4)

    def outer(rc, _):
        at = pl.ds(pl.multiple_of(rc * 192, 192), 192)
        dn = dot_nt(dz_ref[at, :], wu_ref[...])
        xhat = xhat_ref[at, :]
        dx1 = dy_ref[at, :].astype(F32) + norm_back(dn * vrow(5), xhat, rstd_ref[at, 0:1])
        dx1_ref[at, :] = dx1
        da_ref[at, :] = dx1.astype(BF)
        sums_ref[4:5, :] += jnp.sum(dx1, axis=0, keepdims=True)
        sums_ref[5:6, :] += jnp.sum(dn * xhat, axis=0, keepdims=True)
        sums_ref[6:7, :] += jnp.sum(dn, axis=0, keepdims=True)
        return 0

    lax.fori_loop(0, 4, outer, 0, unroll=4)
    dmix_ref[...] = dot_nt(da_ref[...], wo_ref[...]).astype(BF)


def back_kernel(
    q_ref,
    v_ref,
    p_ref,
    dmix_ref,
    own_ref,
    rimc_ref,
    rimz_ref,
    dsl_ref,
    tacc_ref,
    dkv_ref,
):
    odd = (lax.axis_index("band") & 1) == 1
    scale = 32 ** (-0.5)
    lane_head = lax.broadcasted_iota(jnp.int32, (QN, 128), 1) >> 5
    tacc_ref[...] = jnp.zeros_like(tacc_ref)

    def scores_back(k, _):
        at_q = pl.ds(pl.multiple_of(k * QN, QN), QN)
        at_k = pl.ds(pl.multiple_of(k * KN, KN), KN)
        dp = dot_nt(v_ref[at_k, :], spread_heads(dmix_ref[at_q, :], lane_head))
        p = p_ref[at_k, :]
        pdp = p * dp
        ds = pdp - p * jnp.sum(pdp, axis=0, keepdims=True)
        tacc_ref[...] += ds
        dsl_ref[at_k, :] = ds.astype(BF)
        return 0

    lax.fori_loop(0, CLS, scores_back, 0, unroll=CLS)

    def back_class(k):
        at_q = pl.ds(pl.multiple_of(k * QN, QN), QN)
        at_k = pl.ds(pl.multiple_of(k * KN, KN), KN)
        dv = dot(p_ref[at_k, :].astype(BF), spread_heads(dmix_ref[at_q, :], lane_head))
        dk = dot(dsl_ref[at_k, :], spread_heads(q_ref[at_q, :], lane_head)) * scale
        dkv_ref[at_k, 0:256] = dk.astype(BF)
        dkv_ref[at_k, 256:512] = dv.astype(BF)
        own_ref[at_q, 0:256] = dk[0:QN]
        own_ref[at_q, 256:512] = dv[0:QN]
        after = jnp.concatenate([dk[QN : QN + RIM], dv[QN : QN + RIM]], axis=1)
        before = jnp.concatenate([dk[KN - RIM :], dv[KN - RIM :]], axis=1)
        return after, before

    def attend_back(pair, _):
        after0, before0 = back_class(pair * 2)
        after1, before1 = back_class(pair * 2 + 1)
        at = pl.ds(pl.multiple_of(pair * 2 * RIM, 2 * RIM), 2 * RIM)
        after = jnp.concatenate([after0, after1], axis=0)
        before = jnp.concatenate([before0, before1], axis=0)
        rimc_ref[at, :] = jnp.where(odd, before, after).astype(BF)
        rimz_ref[at, :] = jnp.where(odd, after, before).astype(BF)
        return 0

    lax.fori_loop(0, CLS // 2, attend_back, 0, unroll=8)


def early_grads(act_ref, dy_ref, a2_ref, dz_ref, mixed_ref, da_ref, fd, fu, fo):
    fd[...] = dot_tn(act_ref[...], dy_ref[...])
    fu[...] = dot_tn(a2_ref[...], dz_ref[...])
    fo[...] = dot_tn(mixed_ref[...], da_ref[...])


def output_kernel(x1_ref, act_ref, wd_ref, vec_ref, po_ref, out_ref):
    def result(rc, _):
        at = pl.ds(pl.multiple_of(rc * 192, 192), 192)
        res = x1_ref[at, :] + dot(act_ref[at, :], wd_ref[...]) + vec_ref[7:8, :]
        back = dot_tn(po_ref[...], res.astype(BF)).astype(BF)
        for i in range(4):
            out_ref[4 * i + rc] = back[48 * i : 48 * i + 48]
        return 0

    lax.fori_loop(0, 4, result, 0, unroll=4)


def late_grads(
    dsl_ref,
    k_ref,
    tacc_ref,
    xhat_ref,
    xk_ref,
    dkv_ref,
    wqkv_ref,
    vt_ref,
    sums_ref,
    zsum_ref,
    dq_ref,
    fq_ref,
    fv_ref,
    tgrad_ref,
):
    scale = 32 ** (-0.5)
    lane_head = lax.broadcasted_iota(jnp.int32, (QN, 128), 1) >> 5

    def query(k, _):
        at_q = pl.ds(pl.multiple_of(k * QN, QN), QN)
        at_k = pl.ds(pl.multiple_of(k * KN, KN), KN)
        dq = pick_heads(dot_tn(dsl_ref[at_k, :], k_ref[at_k, :]), lane_head) * scale
        dq_ref[at_q, :] = dq.astype(BF)
        return 0

    lax.fori_loop(0, CLS, query, 0, unroll=16)
    dq = dq_ref[...]
    gain, shift = vt_ref[:, 0:1], vt_ref[:, 1:2]
    qsum = jnp.sum(dq.astype(F32), axis=0, keepdims=True)
    m = dot_tn(xhat_ref[...].astype(BF), dq)
    weight = wqkv_ref[:, 0:256].astype(F32)
    fq_ref[:, 0:256] = gain * m + shift * qsum
    gain_grad = jnp.sum(weight * m, axis=1, keepdims=True)
    shift_grad = jnp.sum(weight * qsum, axis=1, keepdims=True)
    xk = xk_ref[...].astype(BF)
    for cols in (slice(256, 512), slice(512, 768)):
        dkv = dkv_ref[:, cols.start - 256 : cols.stop - 256]
        kvsum = jnp.sum(dkv.astype(F32), axis=0, keepdims=True)
        m = dot_tn(xk, dkv)
        weight = wqkv_ref[:, cols].astype(F32)
        fq_ref[:, cols] = gain * m + shift * kvsum
        gain_grad = gain_grad + jnp.sum(weight * m, axis=1, keepdims=True)
        shift_grad = shift_grad + jnp.sum(weight * kvsum, axis=1, keepdims=True)
    lines = jnp.concatenate(
        [jnp.zeros((2, 256), F32), qsum, kvsum, sums_ref[4:8, :]]
        + [zsum_ref[:, 256 * i : 256 * i + 256] for i in range(3)]
        + [jnp.zeros((117, 256), F32)],
        axis=0,
    )
    lane = lax.broadcasted_iota(jnp.int32, (256, 128), 1)
    fv_ref[...] = jnp.where(lane == 0, gain_grad, jnp.where(lane == 1, shift_grad, lines.T))

    flat = tacc_ref[...].T
    qi = lax.broadcasted_iota(jnp.int32, (QN, KN), 0)
    lines = []
    for h in range(HEADS):
        part = flat[h * QN : (h + 1) * QN]
        for bit in range(6):
            turned = pltpu.roll(part, KN - (1 << bit), 1)
            part = jnp.where((qi >> bit) & 1 == 1, turned, part)
        lines.append(jnp.sum(part, axis=0, keepdims=True))
    tgrad_ref[...] = jnp.concatenate(lines, axis=0)


def input_kernel(
    own_ref, gotc_ref, gotz_ref, dq_ref, dx1_ref, xhat_ref, rstd_ref, wqkv_ref, vec_ref, po_ref, tok_ref
):
    odd = (lax.axis_index("band") & 1) == 1

    def block(rc, _):
        at = pl.ds(pl.multiple_of(rc * 192, 192), 192)
        mine = own_ref[at, :]
        got_c = gotc_ref[pl.ds(pl.multiple_of(rc * 160, 160), 160), :].astype(F32)
        got_z = gotz_ref[pl.ds(pl.multiple_of(rc * 160, 160), 160), :].astype(F32)
        got_a = jnp.where(odd, got_c, got_z)
        got_b = jnp.where(odd, got_z, got_c)
        gap = jnp.zeros((QN - RIM, 512), F32)
        parts = []
        for i in range(4):
            a = jnp.concatenate([got_a[i * RIM : (i + 1) * RIM], gap], axis=0)
            b = jnp.concatenate([gap, got_b[i * RIM : (i + 1) * RIM]], axis=0)
            parts.append(mine[i * QN : (i + 1) * QN] + a + b)
        dkv = jnp.concatenate(parts, axis=0).astype(BF)
        dn = dot_nt(dq_ref[at, :], wqkv_ref[:, 0:256]) + dot_nt(dkv, wqkv_ref[:, 256:768])
        dx = dx1_ref[at, :] + norm_back(dn * vec_ref[0:1, :], xhat_ref[at, :], rstd_ref[at, 0:1])
        back = dot_tn(po_ref[...], dx.astype(BF)).astype(BF)
        for i in range(4):
            tok_ref[4 * i + rc] = back[48 * i : 48 * i + 48]
        return 0

    lax.fori_loop(0, 4, block, 0, unroll=4)


EARLY = 896
LATE = 512


def widen(v):
    return jnp.concatenate([v, jnp.zeros((v.shape[0], 128 - v.shape[1]), F32)], axis=1)


def pack(wqkv, wo, wu, wd, vec):
    pieces = [(wqkv, 0, 0), (wo, 0, 768), (wd, 0, 1024), (vec, 0, 1280)]
    pieces += [(wu, 8, 0), (wd, 0, 768), (wd, -8, 1024)]
    total = 0.0
    for p, row, lane in pieces:
        rows, lanes = p.shape
        zero = jnp.zeros((), F32)
        if rows == 24 and lane == 1024 and row == 0:
            p = lax.pad(p, zero, ((0, -16, 0), (0, 0, 0)))
            rows = 8
        elif rows == 24:
            p = lax.pad(p, zero, ((-8 + row, -8 - row, 0), (0, 0, 0)))
            row, rows = 8, 8
        total = total + lax.pad(p, zero, ((row, 16 - row - rows, 0), (lane, EARLY + LATE - lane - lanes, 0)))
    return total.astype(BF)


def own_index():
    return lax.axis_index("maps") * 8 + lax.axis_index("band")


def unpack(blocks, big_qkv, big_out, big_up, big_down, vec, vt, fq, fo, fu, fd):
    me = own_index()
    for index, block in enumerate(blocks):
        core, across = divmod(index, 4)
        for z in range(4):
            slab = block[z].astype(F32)
            o = me ^ (core | (z << 1) | (across << 3))
            at = pl.ds(pl.multiple_of(o * 8, 8), 8)
            fq[at, :] = slab[0:8, 0:768]
            vt[at, :] = slab[0:8, 1280:1408]
            for b, rows in enumerate((slab[0:8, 1024:1280], slab[8:16, 768:1024], slab[8:16, 1024:1280])):
                fd[pl.ds(pl.multiple_of(o * 24 + 8 * b, 8), 8), :] = rows
            fo[at, :] = slab[0:8, 768:1024]
            fu[at, :] = slab[8:16, 0:768]
    big_qkv[...] = fq[...].astype(BF)
    vec[...] = vt[...].T[0 : vec.shape[0]]
    big_out[...] = fo[...].astype(BF)
    big_up[...] = fu[...].astype(BF)
    big_down[...] = fd[...].astype(BF)


def main_kernel(*refs):
    blocks, (xhat, x, xz, xc, pk, xp, bias, limits, dy, dysum) = refs[:8], refs[8:18]
    act, dx1, x1, own, rimc, rimz, dq, out_ref, big_qkv, big_down, vec = refs[18:29]
    q, k, v, mixed, p, dz, a2, da, dmix, sums, zsum, dsl, tacc, dkv = refs[29:43]
    fq, fv, tgrad, fd, fu, fo, big_out, big_up, vt, xk, other, xhat1, rstd1 = refs[43:]
    halo_kernel(x, xc, xz, pk, xk)
    unpack(blocks, big_qkv, big_out, big_up, big_down, vec, vt, fq, fo, fu, fd)
    project_kernel(xhat, xk, big_qkv, vec, q, k, v)
    attend_kernel(limits, bias, q, k, v, mixed, p, other)
    feed_kernel(dy, dysum, mixed, xp, big_out, big_up, big_down, vec, act, dz, a2, da, dx1, x1, dmix, sums, zsum, xhat1, rstd1)
    back_kernel(q, v, p, dmix, own, rimc, rimz, dsl, tacc, dkv)
    early_grads(act, dy, a2, dz, mixed, da, fd, fu, fo)
    late_grads(dsl, k, tacc, xhat, xk, dkv, big_qkv, vt, sums, zsum, dq, fq, fv, tgrad)
    table = tgrad[...]
    me = own_index()
    for o in range(32):
        at = slice(8 * o, 8 * o + 8)
        top = [fd[24 * o + 8 * b : 24 * o + 8 * b + 8, :] for b in range(3)] + [fo[at, 0:128], fq[at, 0:512]]
        low = [fu[at, :], fo[at, 128:256], fq[at, 512:768], fv[at, :], table]
        both = jnp.concatenate([jnp.concatenate(top, axis=1), jnp.concatenate(low, axis=1)], axis=0)
        out_ref[frame_slot(me, o)] = both.astype(BF)


def frame_slot(me, o):
    m = me ^ o
    return (m & 1) * 16 + (m >> 3) * 4 + ((m >> 1) & 3)


def shard_grads(refs, vrows):
    total = refs[0][...] + sum(ref[...].astype(F32) for ref in refs[1:4])
    early, late = total[:, :EARLY], total[:, EARLY:]
    return [
        jnp.concatenate([late[0:8], late[8:16, 0:256]], axis=1),
        jnp.concatenate([early[0:8, 768:896], early[8:16, 768:896]], axis=1),
        early[8:16, 0:768],
        jnp.concatenate([early[0:8, 256 * b : 256 * b + 256] for b in range(3)], axis=0),
        late[8:16, 256 : 256 + vrows],
        lax.dot_general(
            late[8:16, 384:512],
            table_slots(),
            (((1,), (1,)), ((), ())),
            precision=lax.Precision.HIGHEST,
            preferred_element_type=F32,
        ),
    ]


def update_kernel(*refs):
    w, first, second, outs = refs[4:10], refs[10:16], refs[16:22], refs[22:]
    vrows = w[4].shape[1]
    grads = shard_grads(refs, vrows)
    row = lax.broadcasted_iota(jnp.int32, (8, 128), 0)
    lane = lax.broadcasted_iota(jnp.int32, (8, 128), 1)
    norms = jnp.zeros((8, 128), F32)
    for i in range(6):
        update = adam_parts(w[i][...], grads[i], first[i][...], second[i][...])[2]
        outs[i][...] = update
        for line, v in ((0, w[i][...]), (1, update)):
            sums = jnp.sum(v * v, axis=0, keepdims=True)
            if i == 4:
                sums = pltpu.roll(widen(sums), 4, 1)
                norms = jnp.where((row == line) & (lane >= 4) & (lane < 4 + vrows), sums, norms)
            else:
                at = i if i < 4 else 4 + vrows
                norms = jnp.where((row == line) & (lane == at), jnp.sum(sums, axis=1, keepdims=True), norms)
    outs[6][...] = norms


def moments_kernel(*refs):
    first, second, outs = refs[4:10], refs[10:16], refs[16:]
    grads = shard_grads(refs, first[4].shape[1])
    for i in range(6):
        new_first, new_second, _ = adam_parts(0.0, grads[i], first[i][...], second[i][...])
        outs[2 * i][...] = new_first
        outs[2 * i + 1][...] = new_second


def step_kernel(mine_ref, a_ref, b_ref, c_ref, d_ref, *refs):
    w, update, outs = refs[0:6], refs[6:12], refs[12:]
    vrows = w[4].shape[1]
    total = a_ref[...] + b_ref[...] + c_ref[...] + d_ref[...]
    lane = lax.broadcasted_iota(jnp.int32, (8, 128), 1)
    norms = jnp.sqrt(jnp.where(lane == 4 + vrows, mine_ref[...], total))
    outs[6][...] = norms[0:1, 0:16]
    outs[7][...] = norms[1:2, 0:16]
    rate = LEARN_RATE * norms[0:1] / (norms[1:2] + RATIO_EPS)
    for i in range(6):
        if i == 4:
            r = pltpu.roll(rate, 124, 1)[:, 0:vrows]
        else:
            at = i if i < 4 else 4 + vrows
            r = rate[:, at : at + 1]
        outs[i][...] = w[i][...] - r * update[i][...]


def stack_kernel(*refs):
    for i, ref in enumerate(refs[:4]):
        refs[4][i] = ref[...]


def call(kernel, out_shape, scratch, *args, smem=0, flops=10**8, vmem=16):
    vm = pl.BlockSpec(memory_space=pltpu.VMEM)
    specs = [pl.BlockSpec(memory_space=pltpu.SMEM)] * smem + [vm] * (len(args) - smem)
    return pl.pallas_call(
        kernel,
        out_shape=out_shape,
        in_specs=specs,
        out_specs=jax.tree.map(lambda _: vm, out_shape),
        scratch_shapes=scratch,
        compiler_params=pltpu.CompilerParams(vmem_limit_bytes=vmem * 2**20),
        cost_estimate=pl.CostEstimate(flops=flops, bytes_accessed=10**6, transcendentals=0),
    )(*args)


def sds(shape, dtype=BF):
    return jax.ShapeDtypeStruct(shape, dtype)


def exchange_groups(maps, band):
    zbits = band.bit_length() - 2
    mbits = maps.bit_length() - 1
    cut = lambda lo, n: [(lo + i, min(2, n - i)) for i in range(0, n, 2)]
    return cut(1, zbits) + cut(1 + zbits, mbits) + [(0, 1)]


def swap(block, mask, count):
    return lax.ppermute(block, AXES, [(k, k ^ mask) for k in range(count)])


def frame_masks(groups):
    masks = [0]
    for lo, bits in groups:
        masks = [m ^ (d << lo) for d in range(1 << bits) for m in masks]
    return masks


def gather_all(slab, groups, count):
    block = slab[None]
    for lo, bits in groups:
        block = jnp.concatenate(
            [block] + [swap(block, d << lo, count) for d in range(1, 1 << bits)], axis=0
        )
    return block


def scatter_sum(grads, groups, count):
    for lo, bits in reversed(groups):
        grads = add_stage(grads, lo, bits, count)
    return grads[0]


def adam_parts(weight, grad, first, second):
    new_first = BETA_FIRST * first + (1.0 - BETA_FIRST) * grad
    new_second = BETA_SECOND * second + (1.0 - BETA_SECOND) * grad * grad
    update = (
        new_first
        / (1.0 - BETA_FIRST**STEP)
        / (jnp.sqrt(new_second / (1.0 - BETA_SECOND**STEP)) + ADAM_EPS)
        + DECAY_RATE * weight
    )
    return (new_first, new_second, update)


def squares_of(matrices, rowwise):
    return jnp.concatenate(
        [
            jnp.stack([jnp.sum(matrix * matrix) for matrix in matrices]),
            jnp.sum(rowwise * rowwise, axis=1),
        ]
    )


def bias_outputs():
    return (sds((KN, 384), F32), sds((8, 128), jnp.int32), sds((4 * QN, 4 * 48)), sds((4 * KN, 10 * 48)))


def prep_outputs():
    return (
        sds((768, 256), F32),
        sds((768, 256), F32),
        sds((768, 128), F32),
        sds((768, 256)),
        sds((1, 256), F32),
        sds((12, 48, 256)),
        sds((12, 48, 256)),
    )


def project_outputs():
    return (sds((768, 256)), sds((CLS * KN, 256)), sds((CLS * KN, 256)))


def attend_outputs():
    return (sds((768, 256)), sds((CLS * KN, 384), F32))


def feed_outputs():
    return (
        sds((768, 768)),
        sds((768, 768)),
        sds((768, 256)),
        sds((768, 256)),
        sds((768, 256), F32),
        sds((768, 256), F32),
        sds((768, 256)),
        sds((8, 256), F32),
        sds((1, 768), F32),
    )


def back_outputs():
    return (
        sds((768, 512), F32),
        sds((CLS * RIM, 512)),
        sds((CLS * RIM, 512)),
        sds((CLS * KN, 384)),
        sds((KN, 384), F32),
        sds((CLS * KN, 512)),
    )


def late_outputs():
    return (
        sds((768, 256)),
        sds((256, 768), F32),
        sds((256, 128), F32),
        sds((HEADS, KN), F32),
    )


def beside(block, band):
    touching = [(b, b + 1 if b % 2 else b - 1) for b in range(band)]
    return (
        lax.ppermute(block[0], "band", [(b, b ^ 1) for b in range(band)]),
        lax.ppermute(block[1], "band", [(b, to) for b, to in touching if 0 <= to < band]),
    )


def packed_step(tokens_in, cotangent, map_sizes, weights, firsts, seconds):
    count = 32
    vrows = weights[4].shape[0]
    turn = lambda arrays: tuple(a.T if i == 4 else a for i, a in enumerate(arrays))
    weights, firsts, seconds = turn(weights), turn(firsts), turn(seconds)
    slab = pack(*weights[:5])
    slab, sizes = lax.optimization_barrier((slab, map_sizes))
    slabs = [slab] + [swap(slab, d << 1, count) for d in (1, 2, 3)]
    bias, limits, po, pk = call(bias_kernel, bias_outputs(), [], sizes, weights[5], smem=1, flops=10**9, vmem=4)
    *slabs, bias = lax.optimization_barrier((*slabs, bias))
    column = call(stack_kernel, sds((4, 16, EARLY + LATE)), [], *slabs, vmem=4)
    column, x = lax.optimization_barrier((column, tokens_in))
    blocks = [column] + [swap(column, d << 3, count) for d in (1, 2, 3)]
    xp, xhat, rstd, dy, dysum, *edges = call(prep_kernel, prep_outputs(), [], x, cotangent, po, flops=2 * 10**9, vmem=8)
    x_core, x_next = beside(edges, 8)
    *far, xp = lax.optimization_barrier((*blocks[1:], xp))
    blocks = [blocks[0]] + far + [swap(block, 1, count) for block in [blocks[0]] + far]
    act_s, dz_s, a2_s, da_s, dx1_s, x1_s, dmix_s, sums_s, zsum_s = feed_outputs()
    own_s, rimc_s, rimz_s, dsl_s, tacc_s, dkv_s = back_outputs()
    dq_s, fq_s, fv_s, tgrad_s = late_outputs()
    act, dx1, x1, own, rim_c, rim_z, dq, grads, big_qkv, big_down, vec = call(
        main_kernel,
        (act_s, dx1_s, x1_s, own_s, rimc_s, rimz_s, dq_s)
        + (sds((count, 16, EARLY + LATE)), sds((256, 768)), sds((768, 256)), sds((vrows, 256), F32)),
        [
            pltpu.VMEM(o.shape, o.dtype)
            for o in project_outputs()
            + attend_outputs()
            + (dz_s, a2_s, da_s, dmix_s, sums_s, zsum_s, dsl_s, tacc_s, dkv_s, fq_s, fv_s, tgrad_s)
            + (sds((768, 256), F32), sds((256, 768), F32), sds((256, 256), F32))
            + (sds((256, 256)), sds((256, 768)), sds((256, 128), F32), sds((CLS * KN, 256), F32), sds((KN, 384), F32))
            + (sds((768, 256), F32), sds((768, 128), F32))
        ],
        *blocks, xhat, x, x_next, x_core, pk, xp, bias, limits, dy, dysum,
        flops=15 * 10**9, vmem=24,
    )
    layer_out = call(output_kernel, sds((16, 48, 256)), [], x1, act, big_down, vec, po, flops=10**9, vmem=8)
    got_c, got_z = beside((rim_c, rim_z), 8)
    grads = add_stage(add_stage(grads, 0, 1, count), 3, 2, count)
    grads, own = lax.optimization_barrier((grads, own))
    tokens_grad = call(
        input_kernel, sds((16, 48, 256)), [], own, got_c, got_z, dq, dx1, xhat, rstd, big_qkv, vec, po,
        flops=10**9, vmem=8,
    )
    low = grads.astype(BF)
    parts = [grads[0]] + [swap(low[d], d << 1, count) for d in (1, 2, 3)]
    parts[0], tokens_grad, layer_out = lax.optimization_barrier((parts[0], tokens_grad, layer_out))

    shapes = [sds(w.shape, F32) for w in weights]
    *updates, mine = call(
        update_kernel, tuple(shapes) + (sds((8, 128), F32),), [], *parts, *weights, *firsts, *seconds, vmem=4
    )
    moments = call(
        moments_kernel, tuple(shape for shape in shapes for _ in range(2)), [], *parts, *firsts, *seconds, vmem=4
    )
    squares = mine + swap(mine, 1, count)
    squares = squares + swap(squares, 8, count) + swap(squares, 16, count) + swap(squares, 24, count)
    last = [swap(squares, d << 1, count) for d in (1, 2, 3)]
    squares, *moments = lax.optimization_barrier((squares, *moments))
    news = call(
        step_kernel,
        tuple(shapes) + (sds((1, 16), F32),) * 2,
        [],
        mine, squares, *last, *weights, *updates, vmem=4,
    )
    results = [layer_out, tokens_grad]
    for i in range(6):
        three = (moments[2 * i], moments[2 * i + 1], news[i])
        results += [a.T for a in three] if i == 4 else three
    return tuple(results) + (news[6].reshape(16), news[7].reshape(16))


def add_stage(grads, lo, bits, count):
    low = grads.astype(BF).reshape((1 << bits, -1) + grads.shape[1:])
    total = grads.reshape(low.shape)[0].astype(F32)
    for d in range(1, 1 << bits):
        total = total + swap(low[d], d << lo, count).astype(F32)
    return total


def per_device(
    maps,
    band,
    tokens_in,
    cotangent,
    map_sizes,
    w_qkv,
    w_out,
    w_up,
    w_down,
    vectors,
    pos_table,
    first_qkv,
    second_qkv,
    first_out,
    second_out,
    first_up,
    second_up,
    first_down,
    second_down,
    first_vectors,
    second_vectors,
    first_table,
    second_table,
):
    if w_qkv.shape[0] == 8 and (maps, band) == (4, 8):
        return packed_step(
            tokens_in, cotangent, map_sizes,
            (w_qkv, w_out, w_up, w_down, vectors, pos_table),
            (first_qkv, first_out, first_up, first_down, first_vectors, first_table),
            (second_qkv, second_out, second_up, second_down, second_vectors, second_table),
        )
    count = maps * band
    rows = w_qkv.shape[0]
    vrows = vectors.shape[0]
    groups = exchange_groups(maps, band)
    masks = np.array(frame_masks(groups))
    inverse = np.argsort(masks)
    me = lax.axis_index(AXES)
    def pack(qkv, out, upw, dnw, vec):
        dn = dnw.reshape(3, rows, 256).transpose(1, 0, 2).reshape(rows, 768)
        vt = jnp.pad(vec.T, ((0, 0), (0, 128 - vrows)))
        return jnp.concatenate([qkv, out, upw, dn, vt], axis=1)

    slab = pack(*(w.astype(BF) for w in (w_qkv, w_out, w_up, w_down, vectors)))
    block = gather_all(slab, groups, count)
    order = jnp.asarray(inverse, jnp.int32)[jnp.arange(count, dtype=jnp.int32) ^ me]
    whole = jnp.take(block, order, axis=0).reshape(256, -1)
    big_qkv = whole[:, 0:768]
    big_out = whole[:, 768:1024]
    big_up = whole[:, 1024:1792]
    big_down = (
        whole[:, 1792:2560].reshape(count, rows, 3, 256).transpose(0, 2, 1, 3).reshape(768, 256)
    )
    vt = whole[:, 2560:].astype(F32)
    vec = vt[:, :vrows].T

    bias, limits, po, pk = call(bias_kernel, bias_outputs(), [], map_sizes, pos_table, smem=1, flops=10**9)
    xp, xhat, rstd, dy, dysum, *edges = call(prep_kernel, prep_outputs(), [], tokens_in, cotangent, po, flops=2 * 10**9)
    x_core, x_next = beside(edges, band)
    xk = call(halo_kernel, sds((CLS * KN, 256), F32), [], tokens_in, x_core, x_next, pk, flops=10**9)
    queries, keys, values = call(project_kernel, project_outputs(), [], xhat, xk, big_qkv, vec, flops=10**9)
    mixed, probs = call(attend_kernel, attend_outputs(), [pltpu.VMEM((KN, 384), F32)], limits, bias, queries, keys, values, flops=3 * 10**9)
    act, dz, a2, da, dx1, x1, dmix, sums, zsum = call(
        feed_kernel,
        feed_outputs(),
        [pltpu.VMEM((768, 256), F32), pltpu.VMEM((768, 128), F32)],
        dy, dysum, mixed, xp, big_out, big_up, big_down, vec,
        flops=4 * 10**9,
    )
    own, rim_c, rim_z, dsl, tacc, dkv = call(
        back_kernel, back_outputs(), [], queries, values, probs, dmix, flops=4 * 10**9
    )
    got_c, got_z = beside((rim_c, rim_z), band)
    grad_down, grad_up, grad_out = call(
        early_grads,
        (sds((768, 256), F32), sds((256, 768), F32), sds((256, 256), F32)),
        [],
        act, dy, a2, dz, mixed, da,
        flops=10**9,
    )
    dq, grad_qkv, grad_vec, table_grad = call(
        late_grads,
        late_outputs(),
        [],
        dsl, keys, tacc, xhat, xk, dkv, big_qkv, vt, sums, zsum,
        flops=3 * 10**9,
    )
    layer_out = call(output_kernel, sds((16, 48, 256)), [], x1, act, big_down, vec, po, flops=10**9)
    tokens_grad = call(
        input_kernel, sds((16, 48, 256)), [], own, got_c, got_z, dq, dx1, xhat, rstd, big_qkv, vec, po, flops=10**9
    )

    packed = jnp.concatenate(
        [
            grad_qkv.reshape(count, rows, 768),
            grad_out.reshape(count, rows, 256),
            grad_up.reshape(count, rows, 768),
            grad_down.reshape(count, 3, rows, 256).transpose(0, 2, 1, 3).reshape(count, rows, 768),
            grad_vec.reshape(count, rows, 128),
        ],
        axis=2,
    )
    packed = jnp.take(packed, jnp.asarray(masks, jnp.int32) ^ me, axis=0)
    red = scatter_sum(packed, groups, count)
    red_qkv = red[:, 0:768]
    red_out = red[:, 768:1024]
    red_up = red[:, 1024:1792]
    red_down = red[:, 1792:2560].reshape(rows, 3, 256).transpose(1, 0, 2).reshape(3 * rows, 256)
    red_vec = red[:, 2560 : 2560 + vrows].T

    steps = np.arange(-3, 4)
    lanes = ((12 * steps[:, None] + steps[None, :]) % KN).reshape(-1)
    table_total = lax.psum(table_grad, AXES)[:, lanes]

    part_qkv = adam_parts(w_qkv, red_qkv, first_qkv, second_qkv)
    part_out = adam_parts(w_out, red_out, first_out, second_out)
    part_up = adam_parts(w_up, red_up, first_up, second_up)
    part_down = adam_parts(w_down, red_down, first_down, second_down)
    part_vec = adam_parts(vectors, red_vec, first_vectors, second_vectors)
    part_table = adam_parts(pos_table, table_total, first_table, second_table)
    local_weight_sq = squares_of((w_qkv, w_out, w_up, w_down), vectors)
    local_update_sq = squares_of((part_qkv[2], part_out[2], part_up[2], part_down[2]), part_vec[2])
    weight_sq, update_sq = lax.psum((local_weight_sq, local_update_sq), AXES)
    table_weight = jnp.sqrt(jnp.sum(pos_table * pos_table))
    table_update = jnp.sqrt(jnp.sum(part_table[2] * part_table[2]))
    weight_norms = jnp.concatenate([jnp.sqrt(weight_sq), table_weight[None]])
    update_norms = jnp.concatenate([jnp.sqrt(update_sq), table_update[None]])
    ratios = weight_norms / (update_norms + RATIO_EPS)
    next_qkv = w_qkv - LEARN_RATE * ratios[0] * part_qkv[2]
    next_out = w_out - LEARN_RATE * ratios[1] * part_out[2]
    next_up = w_up - LEARN_RATE * ratios[2] * part_up[2]
    next_down = w_down - LEARN_RATE * ratios[3] * part_down[2]
    next_vectors = vectors - LEARN_RATE * ratios[4 : 4 + vrows][:, None] * part_vec[2]
    next_table = pos_table - LEARN_RATE * ratios[4 + vrows] * part_table[2]
    return (
        layer_out,
        tokens_grad,
        part_qkv[0],
        part_qkv[1],
        next_qkv,
        part_out[0],
        part_out[1],
        next_out,
        part_up[0],
        part_up[1],
        next_up,
        part_down[0],
        part_down[1],
        next_down,
        part_vec[0],
        part_vec[1],
        next_vectors,
        part_table[0],
        part_table[1],
        next_table,
        weight_norms,
        update_norms,
    )


def solution(mesh):
    both = P(AXES, None)
    side = P(None, AXES)
    tall = P(AXES, None, None)
    copied = P()
    return jax.shard_map(
        functools.partial(per_device, mesh.shape["maps"], mesh.shape["band"]),
        mesh=mesh,
        in_specs=(tall, tall, P("maps", None))
        + (both,) * 4
        + (side, copied)
        + (both,) * 8
        + (side, side, copied, copied),
        out_specs=(tall, tall) + (both,) * 12 + (side,) * 3 + (copied,) * 5,
        check_vma=False,
    )
```

```python
import functools

import jax
import jax.numpy as jnp
import numpy as np
from jax import lax
from jax.experimental import pallas as pl
from jax.experimental.pallas import tpu as pltpu
from jax.sharding import PartitionSpec as P

HEADS = 8
WINDOW = 7
DIL = 4
STEP = 10
NORM_EPS = 1e-05
BETA_FIRST = 0.9
BETA_SECOND = 0.999
ADAM_EPS = 1e-06
DECAY_RATE = 0.01
LEARN_RATE = 0.2
RATIO_EPS = 1e-06
MASKED = -1e30
LOG2E = 1.4426950408889634
GELU0 = 0.7978845608028654
GELU1 = 0.044715
AXES = ("maps", "band")

BF = jnp.bfloat16
F32 = jnp.float32

CLS = DIL * DIL
QN = 48
KN = 128
RIM = 40


def dot(a, b):
    return lax.dot_general(a, b, (((1,), (0,)), ((), ())), preferred_element_type=F32)


def dot_nt(a, b):
    return lax.dot_general(a, b, (((1,), (1,)), ((), ())), preferred_element_type=F32)


def dot_tn(a, b):
    return lax.dot_general(a, b, (((0,), (0,)), ((), ())), preferred_element_type=F32)


def select(shape, source):
    o = lax.broadcasted_iota(jnp.int32, shape, 0)
    return (source(o) == lax.broadcasted_iota(jnp.int32, shape, 1)).astype(F32).astype(BF)


def own_source(o):
    cc = (o * 171) >> 13
    qr, qc = split12(o - QN * cc)
    return qr * 48 + qc * 4 + cc


def key_source(o):
    j = ((o & (KN - 1)) + 36) & (KN - 1)
    kr, kc = split12(j)
    return jnp.where(j < 120, kr * 48 + kc * 4 + (o >> 7), -1)


def normed(v):
    mean = jnp.mean(v, axis=-1, keepdims=True)
    cen = v - mean
    var = jnp.mean(cen * cen, axis=-1, keepdims=True)
    rstd = lax.rsqrt(var + NORM_EPS)
    return cen * rstd, rstd


def norm_back(g, xhat, rstd):
    m1 = jnp.mean(g, axis=-1, keepdims=True)
    m2 = jnp.mean(g * xhat, axis=-1, keepdims=True)
    return rstd * (g - m1 - xhat * m2)


def spread_heads(v, lane_head):
    zero = jnp.zeros((QN, 128), v.dtype)
    rows = []
    for h in range(HEADS):
        half = [zero, zero]
        half[h // 4] = jnp.where(lane_head == h % 4, v[:, 128 * (h // 4) : 128 * (h // 4) + 128], zero)
        rows.append(jnp.concatenate(half, axis=1))
    return jnp.concatenate(rows, axis=0)


def pick_heads(full, lane_head):
    halves = []
    for side in range(2):
        parts = [full[h * QN : (h + 1) * QN, 128 * side : 128 * side + 128] for h in range(4 * side, 4 * side + 4)]
        low = jnp.where(lane_head == 0, parts[0], parts[1])
        high = jnp.where(lane_head == 2, parts[2], parts[3])
        halves.append(jnp.where(lane_head < 2, low, high))
    return jnp.concatenate(halves, axis=1)


def split12(v):
    q = (v * 43) >> 9
    return q, v - 12 * q


def table_slots():
    n = lax.broadcasted_iota(jnp.int32, (WINDOW * WINDOW, KN), 0)
    lane = lax.broadcasted_iota(jnp.int32, (WINDOW * WINDOW, KN), 1)
    nr = (n * 37) >> 8
    nc = n - 7 * nr
    return (((12 * (nr - 3) + nc - 3) & (KN - 1)) == lane).astype(F32)


def bias_kernel(sizes_ref, table_ref, bias_ref, limits_ref, po_ref, pk_ref):
    po_ref[...] = select((4 * QN, 4 * 48), own_source)
    pk_ref[...] = select((4 * KN, 10 * 48), key_source)
    row = lax.broadcasted_iota(jnp.int32, (8, 128), 0)
    limits_ref[...] = jnp.where(row == 0, sizes_ref[0, 0] - lax.axis_index("band") * 16, sizes_ref[0, 1])

    slots = lax.dot_general(
        table_ref[...],
        table_slots(),
        (((1,), (0,)), ((), ())),
        precision=lax.Precision.HIGHEST,
        preferred_element_type=F32,
    )
    qi = lax.broadcasted_iota(jnp.int32, (QN, KN), 0)
    si = lax.broadcasted_iota(jnp.int32, (QN, KN), 1)
    ji = (si + 36) & (KN - 1)
    kr, kc = split12(ji)
    qr, qc = split12(qi)
    window = (jnp.abs(kc - qc) <= 3) & (jnp.abs(kr - qr - 3) <= 3) & (ji < 120)
    rows = []
    for h in range(HEADS):
        line = jnp.broadcast_to(slots[h : h + 1, :] * LOG2E, (QN, KN))
        line = pltpu.roll(line, 0, 1, stride=1, stride_axis=0)
        rows.append(jnp.where(window, line, MASKED))
    bias_ref[...] = jnp.concatenate(rows, axis=0).T


def prep_kernel(x_ref, cot_ref, po_ref, xp_ref, xhat_ref, rstd_ref, dy_ref, dysum_ref, toc_ref, toz_ref):
    odd = (lax.axis_index("band") & 1) == 1
    for i in range(12):
        toc_ref[i] = jnp.where(odd, x_ref[i], x_ref[4 + i])
        toz_ref[i] = jnp.where(odd, x_ref[4 + i], x_ref[i])

    def block(rc, _):
        at = pl.ds(pl.multiple_of(rc * 192, 192), 192)
        xp = dot(po_ref[...], jnp.concatenate([x_ref[4 * i + rc] for i in range(4)], axis=0))
        xp_ref[at, :] = xp
        xhat, rstd = normed(xp)
        xhat_ref[at, :] = xhat
        rstd_ref[at, :] = jnp.broadcast_to(rstd, (192, 128))
        dy = dot(po_ref[...], jnp.concatenate([cot_ref[4 * i + rc] for i in range(4)], axis=0))
        dy_ref[at, :] = dy.astype(BF)
        dysum_ref[...] += jnp.sum(dy, axis=0, keepdims=True)
        return 0

    dysum_ref[...] = jnp.zeros_like(dysum_ref)
    lax.fori_loop(0, 4, block, 0, unroll=4)


def halo_kernel(x_ref, xc_ref, xz_ref, pk_ref, xk_ref):
    odd = (lax.axis_index("band") & 1) == 1

    def block(rc, _):
        rows = [jnp.where(odd, xc_ref[4 * i + rc], xz_ref[4 * i + rc]) for i in range(3)]
        rows += [x_ref[4 * i + rc] for i in range(4)]
        rows += [jnp.where(odd, xz_ref[4 * i + rc], xc_ref[4 * i + rc]) for i in range(3)]
        xk = dot(pk_ref[...], jnp.concatenate(rows, axis=0))
        xk_ref[pl.ds(pl.multiple_of(rc * 512, 512), 512), :] = normed(xk)[0]
        return 0

    lax.fori_loop(0, 4, block, 0, unroll=4)


def project_kernel(xhat_ref, xk_ref, wqkv_ref, vec_ref, q_ref, k_ref, v_ref):
    def vrow(i):
        return vec_ref[i : i + 1, :]

    def block(rc, _):
        at = pl.ds(pl.multiple_of(rc * 192, 192), 192)
        a1 = (xhat_ref[at, :] * vrow(0) + vrow(1)).astype(BF)
        q_ref[at, :] = (dot(a1, wqkv_ref[:, 0:256]) + vrow(2)).astype(BF)
        at = pl.ds(pl.multiple_of(rc * 512, 512), 512)
        a1k = (xk_ref[at, :] * vrow(0) + vrow(1)).astype(BF)
        k_ref[at, :] = dot(a1k, wqkv_ref[:, 256:512]).astype(BF)
        v_ref[at, :] = (dot(a1k, wqkv_ref[:, 512:768]) + vrow(3)).astype(BF)
        return 0

    lax.fori_loop(0, 4, block, 0, unroll=4)


def attend_kernel(limits_ref, bias_ref, q_ref, k_ref, v_ref, mixed_ref, p_ref, other_ref):
    scale = 32 ** (-0.5)
    lane_head = lax.broadcasted_iota(jnp.int32, (QN, 128), 1) >> 5
    row0 = lax.axis_index("band") * 16
    height = limits_ref[0:1, 0:1]
    wide = limits_ref[1:2, 0:1]
    ks = lax.broadcasted_iota(jnp.int32, (KN, 384), 0)
    ql = lax.broadcasted_iota(jnp.int32, (KN, 384), 1)
    other_ref[...] = jnp.where(ks == ql - 48 * ((ql * 171) >> 13), 0.0, 1.0)
    krow, kcol = split12((lax.broadcasted_iota(jnp.int32, (KN, 128), 0) + 36) & (KN - 1))

    def attend(k, _):
        rc = k >> 2
        cc = k & 3
        at_q = pl.ds(pl.multiple_of(k * QN, QN), QN)
        at_k = pl.ds(pl.multiple_of(k * KN, KN), KN)
        qbd = spread_heads(q_ref[at_q, :], lane_head)
        r = krow * 4 + (rc - 12)
        c = kcol * 4 + cc
        off = jnp.where((r >= -row0) & (r < height) & (c < wide), 0.0, MASKED)
        off = bias_ref[...] + jnp.concatenate([off] * 3, axis=1) * other_ref[...]
        s = dot_nt(k_ref[at_k, :], qbd) * (scale * LOG2E) + off
        top = jnp.max(s, axis=0, keepdims=True)
        e = jnp.exp2(s - top)
        p = e * (1.0 / jnp.sum(e, axis=0, keepdims=True))
        p_ref[at_k, :] = p
        full = dot_tn(p.astype(BF), v_ref[at_k, :])
        mixed_ref[at_q, :] = pick_heads(full, lane_head).astype(BF)
        return 0

    lax.fori_loop(0, CLS, attend, 0, unroll=CLS)


def feed_kernel(
    dy_ref,
    dysum_ref,
    mixed_ref,
    xp_ref,
    wo_ref,
    wu_ref,
    wd_ref,
    vec_ref,
    act_ref,
    dz_ref,
    a2_ref,
    da_ref,
    dx1_ref,
    x1_ref,
    dmix_ref,
    sums_ref,
    zsum_ref,
    xhat_ref,
    rstd_ref,
):
    def vrow(i):
        return vec_ref[i : i + 1, :]

    sums_ref[...] = jnp.zeros_like(sums_ref)
    sums_ref[7:8, :] = dysum_ref[...]
    zsum_ref[...] = jnp.zeros_like(zsum_ref)

    def inner(rc, _):
        at = pl.ds(pl.multiple_of(rc * 192, 192), 192)
        x1 = xp_ref[at, :] + (dot(mixed_ref[at, :], wo_ref[...]) + vrow(4))
        x1_ref[at, :] = x1
        xhat, rstd = normed(x1)
        xhat_ref[at, :] = xhat
        rstd_ref[at, :] = jnp.broadcast_to(rstd, (192, 128))
        a2_ref[at, :] = (xhat * vrow(5) + vrow(6)).astype(BF)
        return 0

    lax.fori_loop(0, 4, inner, 0, unroll=4)

    def hidden(rc, _):
        at = pl.ds(pl.multiple_of(rc * 192, 192), 192)
        for part in range(3):
            cols = slice(256 * part, 256 * part + 256)
            z = dot(a2_ref[at, :], wu_ref[:, cols]) + vrow(8 + part)
            cube = (GELU0 * GELU1) * (z * z)
            up = 0.5 + 0.5 * jnp.tanh(z * (GELU0 + cube))
            act = z * up
            act_ref[at, cols] = act.astype(BF)
            slope = up * (1.0 + (z - act) * (2.0 * GELU0 + 6.0 * cube))
            dz = dot_nt(dy_ref[at, :], wd_ref[cols, :]) * slope
            zsum_ref[:, cols] += jnp.sum(dz, axis=0, keepdims=True)
            dz_ref[at, cols] = dz.astype(BF)
        return 0

    lax.fori_loop(0, 4, hidden, 0, unroll=4)

    def outer(rc, _):
        at = pl.ds(pl.multiple_of(rc * 192, 192), 192)
        dn = dot_nt(dz_ref[at, :], wu_ref[...])
        xhat = xhat_ref[at, :]
        dx1 = dy_ref[at, :].astype(F32) + norm_back(dn * vrow(5), xhat, rstd_ref[at, 0:1])
        dx1_ref[at, :] = dx1
        da_ref[at, :] = dx1.astype(BF)
        sums_ref[4:5, :] += jnp.sum(dx1, axis=0, keepdims=True)
        sums_ref[5:6, :] += jnp.sum(dn * xhat, axis=0, keepdims=True)
        sums_ref[6:7, :] += jnp.sum(dn, axis=0, keepdims=True)
        return 0

    lax.fori_loop(0, 4, outer, 0, unroll=4)
    dmix_ref[...] = dot_nt(da_ref[...], wo_ref[...]).astype(BF)


def back_kernel(
    q_ref,
    v_ref,
    p_ref,
    dmix_ref,
    own_ref,
    rimc_ref,
    rimz_ref,
    dsl_ref,
    tacc_ref,
    dkv_ref,
):
    odd = (lax.axis_index("band") & 1) == 1
    scale = 32 ** (-0.5)
    lane_head = lax.broadcasted_iota(jnp.int32, (QN, 128), 1) >> 5
    tacc_ref[...] = jnp.zeros_like(tacc_ref)

    def scores_back(k, _):
        at_q = pl.ds(pl.multiple_of(k * QN, QN), QN)
        at_k = pl.ds(pl.multiple_of(k * KN, KN), KN)
        dp = dot_nt(v_ref[at_k, :], spread_heads(dmix_ref[at_q, :], lane_head))
        p = p_ref[at_k, :]
        pdp = p * dp
        ds = pdp - p * jnp.sum(pdp, axis=0, keepdims=True)
        tacc_ref[...] += ds
        dsl_ref[at_k, :] = ds.astype(BF)
        return 0

    lax.fori_loop(0, CLS, scores_back, 0, unroll=CLS)

    def back_class(k):
        at_q = pl.ds(pl.multiple_of(k * QN, QN), QN)
        at_k = pl.ds(pl.multiple_of(k * KN, KN), KN)
        dv = dot(p_ref[at_k, :].astype(BF), spread_heads(dmix_ref[at_q, :], lane_head))
        dk = dot(dsl_ref[at_k, :], spread_heads(q_ref[at_q, :], lane_head)) * scale
        dkv_ref[at_k, 0:256] = dk.astype(BF)
        dkv_ref[at_k, 256:512] = dv.astype(BF)
        own_ref[at_q, 0:256] = dk[0:QN]
        own_ref[at_q, 256:512] = dv[0:QN]
        after = jnp.concatenate([dk[QN : QN + RIM], dv[QN : QN + RIM]], axis=1)
        before = jnp.concatenate([dk[KN - RIM :], dv[KN - RIM :]], axis=1)
        return after, before

    def attend_back(pair, _):
        after0, before0 = back_class(pair * 2)
        after1, before1 = back_class(pair * 2 + 1)
        at = pl.ds(pl.multiple_of(pair * 2 * RIM, 2 * RIM), 2 * RIM)
        after = jnp.concatenate([after0, after1], axis=0)
        before = jnp.concatenate([before0, before1], axis=0)
        rimc_ref[at, :] = jnp.where(odd, before, after).astype(BF)
        rimz_ref[at, :] = jnp.where(odd, after, before).astype(BF)
        return 0

    lax.fori_loop(0, CLS // 2, attend_back, 0, unroll=8)


def early_grads(act_ref, dy_ref, a2_ref, dz_ref, mixed_ref, da_ref, fd, fu, fo):
    fd[...] = dot_tn(act_ref[...], dy_ref[...])
    fu[...] = dot_tn(a2_ref[...], dz_ref[...])
    fo[...] = dot_tn(mixed_ref[...], da_ref[...])


def output_kernel(x1_ref, act_ref, wd_ref, vec_ref, po_ref, out_ref):
    def result(rc, _):
        at = pl.ds(pl.multiple_of(rc * 192, 192), 192)
        res = x1_ref[at, :] + dot(act_ref[at, :], wd_ref[...]) + vec_ref[7:8, :]
        back = dot_tn(po_ref[...], res.astype(BF)).astype(BF)
        for i in range(4):
            out_ref[4 * i + rc] = back[48 * i : 48 * i + 48]
        return 0

    lax.fori_loop(0, 4, result, 0, unroll=4)


def late_grads(
    dsl_ref,
    k_ref,
    tacc_ref,
    xhat_ref,
    xk_ref,
    dkv_ref,
    wqkv_ref,
    vt_ref,
    sums_ref,
    zsum_ref,
    dq_ref,
    fq_ref,
    fv_ref,
    tgrad_ref,
):
    scale = 32 ** (-0.5)
    lane_head = lax.broadcasted_iota(jnp.int32, (QN, 128), 1) >> 5

    def query(k, _):
        at_q = pl.ds(pl.multiple_of(k * QN, QN), QN)
        at_k = pl.ds(pl.multiple_of(k * KN, KN), KN)
        dq = pick_heads(dot_tn(dsl_ref[at_k, :], k_ref[at_k, :]), lane_head) * scale
        dq_ref[at_q, :] = dq.astype(BF)
        return 0

    lax.fori_loop(0, CLS, query, 0, unroll=16)
    dq = dq_ref[...]
    gain, shift = vt_ref[:, 0:1], vt_ref[:, 1:2]
    qsum = jnp.sum(dq.astype(F32), axis=0, keepdims=True)
    m = dot_tn(xhat_ref[...].astype(BF), dq)
    weight = wqkv_ref[:, 0:256].astype(F32)
    fq_ref[:, 0:256] = gain * m + shift * qsum
    gain_grad = jnp.sum(weight * m, axis=1, keepdims=True)
    shift_grad = jnp.sum(weight * qsum, axis=1, keepdims=True)
    xk = xk_ref[...].astype(BF)
    for cols in (slice(256, 512), slice(512, 768)):
        dkv = dkv_ref[:, cols.start - 256 : cols.stop - 256]
        kvsum = jnp.sum(dkv.astype(F32), axis=0, keepdims=True)
        m = dot_tn(xk, dkv)
        weight = wqkv_ref[:, cols].astype(F32)
        fq_ref[:, cols] = gain * m + shift * kvsum
        gain_grad = gain_grad + jnp.sum(weight * m, axis=1, keepdims=True)
        shift_grad = shift_grad + jnp.sum(weight * kvsum, axis=1, keepdims=True)
    lines = jnp.concatenate(
        [jnp.zeros((2, 256), F32), qsum, kvsum, sums_ref[4:8, :]]
        + [zsum_ref[:, 256 * i : 256 * i + 256] for i in range(3)]
        + [jnp.zeros((117, 256), F32)],
        axis=0,
    )
    lane = lax.broadcasted_iota(jnp.int32, (256, 128), 1)
    fv_ref[...] = jnp.where(lane == 0, gain_grad, jnp.where(lane == 1, shift_grad, lines.T))

    flat = tacc_ref[...].T
    qi = lax.broadcasted_iota(jnp.int32, (QN, KN), 0)
    lines = []
    for h in range(HEADS):
        part = flat[h * QN : (h + 1) * QN]
        for bit in range(6):
            turned = pltpu.roll(part, KN - (1 << bit), 1)
            part = jnp.where((qi >> bit) & 1 == 1, turned, part)
        lines.append(jnp.sum(part, axis=0, keepdims=True))
    tgrad_ref[...] = jnp.concatenate(lines, axis=0)


def input_kernel(
    own_ref, gotc_ref, gotz_ref, dq_ref, dx1_ref, xhat_ref, rstd_ref, wqkv_ref, vec_ref, po_ref, tok_ref
):
    odd = (lax.axis_index("band") & 1) == 1

    def block(rc, _):
        at = pl.ds(pl.multiple_of(rc * 192, 192), 192)
        mine = own_ref[at, :]
        got_c = gotc_ref[pl.ds(pl.multiple_of(rc * 160, 160), 160), :].astype(F32)
        got_z = gotz_ref[pl.ds(pl.multiple_of(rc * 160, 160), 160), :].astype(F32)
        got_a = jnp.where(odd, got_c, got_z)
        got_b = jnp.where(odd, got_z, got_c)
        gap = jnp.zeros((QN - RIM, 512), F32)
        parts = []
        for i in range(4):
            a = jnp.concatenate([got_a[i * RIM : (i + 1) * RIM], gap], axis=0)
            b = jnp.concatenate([gap, got_b[i * RIM : (i + 1) * RIM]], axis=0)
            parts.append(mine[i * QN : (i + 1) * QN] + a + b)
        dkv = jnp.concatenate(parts, axis=0).astype(BF)
        dn = dot_nt(dq_ref[at, :], wqkv_ref[:, 0:256]) + dot_nt(dkv, wqkv_ref[:, 256:768])
        dx = dx1_ref[at, :] + norm_back(dn * vec_ref[0:1, :], xhat_ref[at, :], rstd_ref[at, 0:1])
        back = dot_tn(po_ref[...], dx.astype(BF)).astype(BF)
        for i in range(4):
            tok_ref[4 * i + rc] = back[48 * i : 48 * i + 48]
        return 0

    lax.fori_loop(0, 4, block, 0, unroll=4)


EARLY = 896
LATE = 512


def widen(v):
    return jnp.concatenate([v, jnp.zeros((v.shape[0], 128 - v.shape[1]), F32)], axis=1)


def pack(wqkv, wo, wu, wd, vec):
    pieces = [(wqkv, 0, 0), (wo, 0, 768), (wd, 0, 1024), (vec, 0, 1280)]
    pieces += [(wu, 8, 0), (wd, 0, 768), (wd, -8, 1024)]
    total = 0.0
    for p, row, lane in pieces:
        rows, lanes = p.shape
        zero = jnp.zeros((), F32)
        if rows == 24 and lane == 1024 and row == 0:
            p = lax.pad(p, zero, ((0, -16, 0), (0, 0, 0)))
            rows = 8
        elif rows == 24:
            p = lax.pad(p, zero, ((-8 + row, -8 - row, 0), (0, 0, 0)))
            row, rows = 8, 8
        total = total + lax.pad(p, zero, ((row, 16 - row - rows, 0), (lane, EARLY + LATE - lane - lanes, 0)))
    return total.astype(BF)


def own_index():
    return lax.axis_index("maps") * 8 + lax.axis_index("band")


def unpack(blocks, big_qkv, big_out, big_up, big_down, vec, vt, fq, fo, fu, fd):
    me = own_index()
    for index, block in enumerate(blocks):
        core, across = divmod(index, 4)
        for z in range(4):
            slab = block[z].astype(F32)
            o = me ^ (core | (z << 1) | (across << 3))
            at = pl.ds(pl.multiple_of(o * 8, 8), 8)
            fq[at, :] = slab[0:8, 0:768]
            vt[at, :] = slab[0:8, 1280:1408]
            for b, rows in enumerate((slab[0:8, 1024:1280], slab[8:16, 768:1024], slab[8:16, 1024:1280])):
                fd[pl.ds(pl.multiple_of(o * 24 + 8 * b, 8), 8), :] = rows
            fo[at, :] = slab[0:8, 768:1024]
            fu[at, :] = slab[8:16, 0:768]
    big_qkv[...] = fq[...].astype(BF)
    vec[...] = vt[...].T[0 : vec.shape[0]]
    big_out[...] = fo[...].astype(BF)
    big_up[...] = fu[...].astype(BF)
    big_down[...] = fd[...].astype(BF)


def main_kernel(*refs):
    blocks, (xhat, x, xz, xc, pk, xp, bias, limits, dy, dysum) = refs[:8], refs[8:18]
    act, dx1, x1, own, rimc, rimz, dq, out_ref, big_qkv, big_down, vec = refs[18:29]
    q, k, v, mixed, p, dz, a2, da, dmix, sums, zsum, dsl, tacc, dkv = refs[29:43]
    fq, fv, tgrad, fd, fu, fo, big_out, big_up, vt, xk, other, xhat1, rstd1 = refs[43:]
    halo_kernel(x, xc, xz, pk, xk)
    unpack(blocks, big_qkv, big_out, big_up, big_down, vec, vt, fq, fo, fu, fd)
    project_kernel(xhat, xk, big_qkv, vec, q, k, v)
    attend_kernel(limits, bias, q, k, v, mixed, p, other)
    feed_kernel(dy, dysum, mixed, xp, big_out, big_up, big_down, vec, act, dz, a2, da, dx1, x1, dmix, sums, zsum, xhat1, rstd1)
    back_kernel(q, v, p, dmix, own, rimc, rimz, dsl, tacc, dkv)
    late_grads(dsl, k, tacc, xhat, xk, dkv, big_qkv, vt, sums, zsum, dq, fq, fv, tgrad)
    early_grads(act, dy, a2, dz, mixed, da, fd, fu, fo)
    table = tgrad[...]
    me = own_index()
    for o in range(32):
        at = slice(8 * o, 8 * o + 8)
        top = [fd[24 * o + 8 * b : 24 * o + 8 * b + 8, :] for b in range(3)] + [fo[at, 0:128], fq[at, 0:512]]
        low = [fu[at, :], fo[at, 128:256], fq[at, 512:768], fv[at, :], table]
        both = jnp.concatenate([jnp.concatenate(top, axis=1), jnp.concatenate(low, axis=1)], axis=0)
        out_ref[frame_slot(me, o)] = both.astype(BF)


def frame_slot(me, o):
    m = me ^ o
    return (m & 1) * 16 + (m >> 3) * 4 + ((m >> 1) & 3)


def shard_grads(refs, vrows):
    total = refs[0][...] + sum(ref[...].astype(F32) for ref in refs[1:4])
    early, late = total[:, :EARLY], total[:, EARLY:]
    return [
        jnp.concatenate([late[0:8], late[8:16, 0:256]], axis=1),
        jnp.concatenate([early[0:8, 768:896], early[8:16, 768:896]], axis=1),
        early[8:16, 0:768],
        jnp.concatenate([early[0:8, 256 * b : 256 * b + 256] for b in range(3)], axis=0),
        late[8:16, 256 : 256 + vrows],
        lax.dot_general(
            late[8:16, 384:512],
            table_slots(),
            (((1,), (1,)), ((), ())),
            precision=lax.Precision.HIGHEST,
            preferred_element_type=F32,
        ),
    ]


def update_kernel(*refs):
    w, first, second, outs = refs[4:10], refs[10:16], refs[16:22], refs[22:]
    vrows = w[4].shape[1]
    grads = shard_grads(refs, vrows)
    row = lax.broadcasted_iota(jnp.int32, (8, 128), 0)
    lane = lax.broadcasted_iota(jnp.int32, (8, 128), 1)
    norms = jnp.zeros((8, 128), F32)
    for i in range(6):
        update = adam_parts(w[i][...], grads[i], first[i][...], second[i][...])[2]
        outs[i][...] = update
        for line, v in ((0, w[i][...]), (1, update)):
            sums = jnp.sum(v * v, axis=0, keepdims=True)
            if i == 4:
                sums = pltpu.roll(widen(sums), 4, 1)
                norms = jnp.where((row == line) & (lane >= 4) & (lane < 4 + vrows), sums, norms)
            else:
                at = i if i < 4 else 4 + vrows
                norms = jnp.where((row == line) & (lane == at), jnp.sum(sums, axis=1, keepdims=True), norms)
    outs[6][...] = norms


def moments_kernel(*refs):
    first, second, outs = refs[4:10], refs[10:16], refs[16:]
    grads = shard_grads(refs, first[4].shape[1])
    for i in range(6):
        new_first, new_second, _ = adam_parts(0.0, grads[i], first[i][...], second[i][...])
        outs[2 * i][...] = new_first
        outs[2 * i + 1][...] = new_second


def step_kernel(mine_ref, a_ref, b_ref, c_ref, d_ref, *refs):
    w, update, outs = refs[0:6], refs[6:12], refs[12:]
    vrows = w[4].shape[1]
    total = a_ref[...] + b_ref[...] + c_ref[...] + d_ref[...]
    lane = lax.broadcasted_iota(jnp.int32, (8, 128), 1)
    norms = jnp.sqrt(jnp.where(lane == 4 + vrows, mine_ref[...], total))
    outs[6][...] = norms[0:1, 0:16]
    outs[7][...] = norms[1:2, 0:16]
    rate = LEARN_RATE * norms[0:1] / (norms[1:2] + RATIO_EPS)
    for i in range(6):
        if i == 4:
            r = pltpu.roll(rate, 124, 1)[:, 0:vrows]
        else:
            at = i if i < 4 else 4 + vrows
            r = rate[:, at : at + 1]
        outs[i][...] = w[i][...] - r * update[i][...]


def stack_kernel(*refs):
    for i, ref in enumerate(refs[:4]):
        refs[4][i] = ref[...]


def call(kernel, out_shape, scratch, *args, smem=0, flops=10**8, vmem=16):
    vm = pl.BlockSpec(memory_space=pltpu.VMEM)
    specs = [pl.BlockSpec(memory_space=pltpu.SMEM)] * smem + [vm] * (len(args) - smem)
    return pl.pallas_call(
        kernel,
        out_shape=out_shape,
        in_specs=specs,
        out_specs=jax.tree.map(lambda _: vm, out_shape),
        scratch_shapes=scratch,
        compiler_params=pltpu.CompilerParams(vmem_limit_bytes=vmem * 2**20),
        cost_estimate=pl.CostEstimate(flops=flops, bytes_accessed=10**6, transcendentals=0),
    )(*args)


def sds(shape, dtype=BF):
    return jax.ShapeDtypeStruct(shape, dtype)


def exchange_groups(maps, band):
    zbits = band.bit_length() - 2
    mbits = maps.bit_length() - 1
    cut = lambda lo, n: [(lo + i, min(2, n - i)) for i in range(0, n, 2)]
    return cut(1, zbits) + cut(1 + zbits, mbits) + [(0, 1)]


def swap(block, mask, count):
    return lax.ppermute(block, AXES, [(k, k ^ mask) for k in range(count)])


def frame_masks(groups):
    masks = [0]
    for lo, bits in groups:
        masks = [m ^ (d << lo) for d in range(1 << bits) for m in masks]
    return masks


def gather_all(slab, groups, count):
    block = slab[None]
    for lo, bits in groups:
        block = jnp.concatenate(
            [block] + [swap(block, d << lo, count) for d in range(1, 1 << bits)], axis=0
        )
    return block


def scatter_sum(grads, groups, count):
    for lo, bits in reversed(groups):
        grads = add_stage(grads, lo, bits, count)
    return grads[0]


def adam_parts(weight, grad, first, second):
    new_first = BETA_FIRST * first + (1.0 - BETA_FIRST) * grad
    new_second = BETA_SECOND * second + (1.0 - BETA_SECOND) * grad * grad
    update = (
        new_first
        / (1.0 - BETA_FIRST**STEP)
        / (jnp.sqrt(new_second / (1.0 - BETA_SECOND**STEP)) + ADAM_EPS)
        + DECAY_RATE * weight
    )
    return (new_first, new_second, update)


def squares_of(matrices, rowwise):
    return jnp.concatenate(
        [
            jnp.stack([jnp.sum(matrix * matrix) for matrix in matrices]),
            jnp.sum(rowwise * rowwise, axis=1),
        ]
    )


def bias_outputs():
    return (sds((KN, 384), F32), sds((8, 128), jnp.int32), sds((4 * QN, 4 * 48)), sds((4 * KN, 10 * 48)))


def prep_outputs():
    return (
        sds((768, 256), F32),
        sds((768, 256), F32),
        sds((768, 128), F32),
        sds((768, 256)),
        sds((1, 256), F32),
        sds((12, 48, 256)),
        sds((12, 48, 256)),
    )


def project_outputs():
    return (sds((768, 256)), sds((CLS * KN, 256)), sds((CLS * KN, 256)))


def attend_outputs():
    return (sds((768, 256)), sds((CLS * KN, 384), F32))


def feed_outputs():
    return (
        sds((768, 768)),
        sds((768, 768)),
        sds((768, 256)),
        sds((768, 256)),
        sds((768, 256), F32),
        sds((768, 256), F32),
        sds((768, 256)),
        sds((8, 256), F32),
        sds((1, 768), F32),
    )


def back_outputs():
    return (
        sds((768, 512), F32),
        sds((CLS * RIM, 512)),
        sds((CLS * RIM, 512)),
        sds((CLS * KN, 384)),
        sds((KN, 384), F32),
        sds((CLS * KN, 512)),
    )


def late_outputs():
    return (
        sds((768, 256)),
        sds((256, 768), F32),
        sds((256, 128), F32),
        sds((HEADS, KN), F32),
    )


def beside(block, band):
    touching = [(b, b + 1 if b % 2 else b - 1) for b in range(band)]
    return (
        lax.ppermute(block[0], "band", [(b, b ^ 1) for b in range(band)]),
        lax.ppermute(block[1], "band", [(b, to) for b, to in touching if 0 <= to < band]),
    )


def packed_step(tokens_in, cotangent, map_sizes, weights, firsts, seconds):
    count = 32
    vrows = weights[4].shape[0]
    turn = lambda arrays: tuple(a.T if i == 4 else a for i, a in enumerate(arrays))
    weights, firsts, seconds = turn(weights), turn(firsts), turn(seconds)
    slab = pack(*weights[:5])
    slab, sizes = lax.optimization_barrier((slab, map_sizes))
    slabs = [slab] + [swap(slab, d << 1, count) for d in (1, 2, 3)]
    bias, limits, po, pk = call(bias_kernel, bias_outputs(), [], sizes, weights[5], smem=1, flops=10**9, vmem=4)
    *slabs, bias = lax.optimization_barrier((*slabs, bias))
    column = call(stack_kernel, sds((4, 16, EARLY + LATE)), [], *slabs, vmem=4)
    column, x = lax.optimization_barrier((column, tokens_in))
    blocks = [column] + [swap(column, d << 3, count) for d in (1, 2, 3)]
    xp, xhat, rstd, dy, dysum, *edges = call(prep_kernel, prep_outputs(), [], x, cotangent, po, flops=2 * 10**9, vmem=8)
    x_core, x_next = beside(edges, 8)
    *far, xp = lax.optimization_barrier((*blocks[1:], xp))
    blocks = [blocks[0]] + far + [swap(block, 1, count) for block in [blocks[0]] + far]
    act_s, dz_s, a2_s, da_s, dx1_s, x1_s, dmix_s, sums_s, zsum_s = feed_outputs()
    own_s, rimc_s, rimz_s, dsl_s, tacc_s, dkv_s = back_outputs()
    dq_s, fq_s, fv_s, tgrad_s = late_outputs()
    act, dx1, x1, own, rim_c, rim_z, dq, grads, big_qkv, big_down, vec = call(
        main_kernel,
        (act_s, dx1_s, x1_s, own_s, rimc_s, rimz_s, dq_s)
        + (sds((count, 16, EARLY + LATE)), sds((256, 768)), sds((768, 256)), sds((vrows, 256), F32)),
        [
            pltpu.VMEM(o.shape, o.dtype)
            for o in project_outputs()
            + attend_outputs()
            + (dz_s, a2_s, da_s, dmix_s, sums_s, zsum_s, dsl_s, tacc_s, dkv_s, fq_s, fv_s, tgrad_s)
            + (sds((768, 256), F32), sds((256, 768), F32), sds((256, 256), F32))
            + (sds((256, 256)), sds((256, 768)), sds((256, 128), F32), sds((CLS * KN, 256), F32), sds((KN, 384), F32))
            + (sds((768, 256), F32), sds((768, 128), F32))
        ],
        *blocks, xhat, x, x_next, x_core, pk, xp, bias, limits, dy, dysum,
        flops=15 * 10**9, vmem=24,
    )
    layer_out = call(output_kernel, sds((16, 48, 256)), [], x1, act, big_down, vec, po, flops=10**9, vmem=8)
    got_c, got_z = beside((rim_c, rim_z), 8)
    grads = add_stage(add_stage(grads, 0, 1, count), 3, 2, count)
    grads, own = lax.optimization_barrier((grads, own))
    tokens_grad = call(
        input_kernel, sds((16, 48, 256)), [], own, got_c, got_z, dq, dx1, xhat, rstd, big_qkv, vec, po,
        flops=10**9, vmem=8,
    )
    low = grads.astype(BF)
    parts = [grads[0]] + [swap(low[d], d << 1, count) for d in (1, 2, 3)]
    parts[0], tokens_grad, layer_out = lax.optimization_barrier((parts[0], tokens_grad, layer_out))

    shapes = [sds(w.shape, F32) for w in weights]
    *updates, mine = call(
        update_kernel, tuple(shapes) + (sds((8, 128), F32),), [], *parts, *weights, *firsts, *seconds, vmem=4
    )
    moments = call(
        moments_kernel, tuple(shape for shape in shapes for _ in range(2)), [], *parts, *firsts, *seconds, vmem=4
    )
    squares = mine + swap(mine, 1, count)
    squares = squares + swap(squares, 8, count) + swap(squares, 16, count) + swap(squares, 24, count)
    last = [swap(squares, d << 1, count) for d in (1, 2, 3)]
    squares, *moments = lax.optimization_barrier((squares, *moments))
    news = call(
        step_kernel,
        tuple(shapes) + (sds((1, 16), F32),) * 2,
        [],
        mine, squares, *last, *weights, *updates, vmem=4,
    )
    results = [layer_out, tokens_grad]
    for i in range(6):
        three = (moments[2 * i], moments[2 * i + 1], news[i])
        results += [a.T for a in three] if i == 4 else three
    return tuple(results) + (news[6].reshape(16), news[7].reshape(16))


def add_stage(grads, lo, bits, count):
    low = grads.astype(BF).reshape((1 << bits, -1) + grads.shape[1:])
    total = grads.reshape(low.shape)[0].astype(F32)
    for d in range(1, 1 << bits):
        total = total + swap(low[d], d << lo, count).astype(F32)
    return total


def per_device(
    maps,
    band,
    tokens_in,
    cotangent,
    map_sizes,
    w_qkv,
    w_out,
    w_up,
    w_down,
    vectors,
    pos_table,
    first_qkv,
    second_qkv,
    first_out,
    second_out,
    first_up,
    second_up,
    first_down,
    second_down,
    first_vectors,
    second_vectors,
    first_table,
    second_table,
):
    if w_qkv.shape[0] == 8 and (maps, band) == (4, 8):
        return packed_step(
            tokens_in, cotangent, map_sizes,
            (w_qkv, w_out, w_up, w_down, vectors, pos_table),
            (first_qkv, first_out, first_up, first_down, first_vectors, first_table),
            (second_qkv, second_out, second_up, second_down, second_vectors, second_table),
        )
    count = maps * band
    rows = w_qkv.shape[0]
    vrows = vectors.shape[0]
    groups = exchange_groups(maps, band)
    masks = np.array(frame_masks(groups))
    inverse = np.argsort(masks)
    me = lax.axis_index(AXES)
    def pack(qkv, out, upw, dnw, vec):
        dn = dnw.reshape(3, rows, 256).transpose(1, 0, 2).reshape(rows, 768)
        vt = jnp.pad(vec.T, ((0, 0), (0, 128 - vrows)))
        return jnp.concatenate([qkv, out, upw, dn, vt], axis=1)

    slab = pack(*(w.astype(BF) for w in (w_qkv, w_out, w_up, w_down, vectors)))
    block = gather_all(slab, groups, count)
    order = jnp.asarray(inverse, jnp.int32)[jnp.arange(count, dtype=jnp.int32) ^ me]
    whole = jnp.take(block, order, axis=0).reshape(256, -1)
    big_qkv = whole[:, 0:768]
    big_out = whole[:, 768:1024]
    big_up = whole[:, 1024:1792]
    big_down = (
        whole[:, 1792:2560].reshape(count, rows, 3, 256).transpose(0, 2, 1, 3).reshape(768, 256)
    )
    vt = whole[:, 2560:].astype(F32)
    vec = vt[:, :vrows].T

    bias, limits, po, pk = call(bias_kernel, bias_outputs(), [], map_sizes, pos_table, smem=1, flops=10**9)
    xp, xhat, rstd, dy, dysum, *edges = call(prep_kernel, prep_outputs(), [], tokens_in, cotangent, po, flops=2 * 10**9)
    x_core, x_next = beside(edges, band)
    xk = call(halo_kernel, sds((CLS * KN, 256), F32), [], tokens_in, x_core, x_next, pk, flops=10**9)
    queries, keys, values = call(project_kernel, project_outputs(), [], xhat, xk, big_qkv, vec, flops=10**9)
    mixed, probs = call(attend_kernel, attend_outputs(), [pltpu.VMEM((KN, 384), F32)], limits, bias, queries, keys, values, flops=3 * 10**9)
    act, dz, a2, da, dx1, x1, dmix, sums, zsum = call(
        feed_kernel,
        feed_outputs(),
        [pltpu.VMEM((768, 256), F32), pltpu.VMEM((768, 128), F32)],
        dy, dysum, mixed, xp, big_out, big_up, big_down, vec,
        flops=4 * 10**9,
    )
    own, rim_c, rim_z, dsl, tacc, dkv = call(
        back_kernel, back_outputs(), [], queries, values, probs, dmix, flops=4 * 10**9
    )
    got_c, got_z = beside((rim_c, rim_z), band)
    grad_down, grad_up, grad_out = call(
        early_grads,
        (sds((768, 256), F32), sds((256, 768), F32), sds((256, 256), F32)),
        [],
        act, dy, a2, dz, mixed, da,
        flops=10**9,
    )
    dq, grad_qkv, grad_vec, table_grad = call(
        late_grads,
        late_outputs(),
        [],
        dsl, keys, tacc, xhat, xk, dkv, big_qkv, vt, sums, zsum,
        flops=3 * 10**9,
    )
    layer_out = call(output_kernel, sds((16, 48, 256)), [], x1, act, big_down, vec, po, flops=10**9)
    tokens_grad = call(
        input_kernel, sds((16, 48, 256)), [], own, got_c, got_z, dq, dx1, xhat, rstd, big_qkv, vec, po, flops=10**9
    )

    packed = jnp.concatenate(
        [
            grad_qkv.reshape(count, rows, 768),
            grad_out.reshape(count, rows, 256),
            grad_up.reshape(count, rows, 768),
            grad_down.reshape(count, 3, rows, 256).transpose(0, 2, 1, 3).reshape(count, rows, 768),
            grad_vec.reshape(count, rows, 128),
        ],
        axis=2,
    )
    packed = jnp.take(packed, jnp.asarray(masks, jnp.int32) ^ me, axis=0)
    red = scatter_sum(packed, groups, count)
    red_qkv = red[:, 0:768]
    red_out = red[:, 768:1024]
    red_up = red[:, 1024:1792]
    red_down = red[:, 1792:2560].reshape(rows, 3, 256).transpose(1, 0, 2).reshape(3 * rows, 256)
    red_vec = red[:, 2560 : 2560 + vrows].T

    steps = np.arange(-3, 4)
    lanes = ((12 * steps[:, None] + steps[None, :]) % KN).reshape(-1)
    table_total = lax.psum(table_grad, AXES)[:, lanes]

    part_qkv = adam_parts(w_qkv, red_qkv, first_qkv, second_qkv)
    part_out = adam_parts(w_out, red_out, first_out, second_out)
    part_up = adam_parts(w_up, red_up, first_up, second_up)
    part_down = adam_parts(w_down, red_down, first_down, second_down)
    part_vec = adam_parts(vectors, red_vec, first_vectors, second_vectors)
    part_table = adam_parts(pos_table, table_total, first_table, second_table)
    local_weight_sq = squares_of((w_qkv, w_out, w_up, w_down), vectors)
    local_update_sq = squares_of((part_qkv[2], part_out[2], part_up[2], part_down[2]), part_vec[2])
    weight_sq, update_sq = lax.psum((local_weight_sq, local_update_sq), AXES)
    table_weight = jnp.sqrt(jnp.sum(pos_table * pos_table))
    table_update = jnp.sqrt(jnp.sum(part_table[2] * part_table[2]))
    weight_norms = jnp.concatenate([jnp.sqrt(weight_sq), table_weight[None]])
    update_norms = jnp.concatenate([jnp.sqrt(update_sq), table_update[None]])
    ratios = weight_norms / (update_norms + RATIO_EPS)
    next_qkv = w_qkv - LEARN_RATE * ratios[0] * part_qkv[2]
    next_out = w_out - LEARN_RATE * ratios[1] * part_out[2]
    next_up = w_up - LEARN_RATE * ratios[2] * part_up[2]
    next_down = w_down - LEARN_RATE * ratios[3] * part_down[2]
    next_vectors = vectors - LEARN_RATE * ratios[4 : 4 + vrows][:, None] * part_vec[2]
    next_table = pos_table - LEARN_RATE * ratios[4 + vrows] * part_table[2]
    return (
        layer_out,
        tokens_grad,
        part_qkv[0],
        part_qkv[1],
        next_qkv,
        part_out[0],
        part_out[1],
        next_out,
        part_up[0],
        part_up[1],
        next_up,
        part_down[0],
        part_down[1],
        next_down,
        part_vec[0],
        part_vec[1],
        next_vectors,
        part_table[0],
        part_table[1],
        next_table,
        weight_norms,
        update_norms,
    )


def solution(mesh):
    both = P(AXES, None)
    side = P(None, AXES)
    tall = P(AXES, None, None)
    copied = P()
    return jax.shard_map(
        functools.partial(per_device, mesh.shape["maps"], mesh.shape["band"]),
        mesh=mesh,
        in_specs=(tall, tall, P("maps", None))
        + (both,) * 4
        + (side, copied)
        + (both,) * 8
        + (side, side, copied, copied),
        out_specs=(tall, tall) + (both,) * 12 + (side,) * 3 + (copied,) * 5,
        check_vma=False,
    )
```

```python
import functools

import jax
import jax.numpy as jnp
import numpy as np
from jax import lax
from jax.experimental import pallas as pl
from jax.experimental.pallas import tpu as pltpu
from jax.sharding import PartitionSpec as P

HEADS = 8
WINDOW = 7
DIL = 4
STEP = 10
NORM_EPS = 1e-05
BETA_FIRST = 0.9
BETA_SECOND = 0.999
ADAM_EPS = 1e-06
DECAY_RATE = 0.01
LEARN_RATE = 0.2
RATIO_EPS = 1e-06
MASKED = -1e30
LOG2E = 1.4426950408889634
GELU0 = 0.7978845608028654
GELU1 = 0.044715
AXES = ("maps", "band")

BF = jnp.bfloat16
F32 = jnp.float32

CLS = DIL * DIL
QN = 48
KN = 128
RIM = 40


def dot(a, b):
    return lax.dot_general(a, b, (((1,), (0,)), ((), ())), preferred_element_type=F32)


def dot_nt(a, b):
    return lax.dot_general(a, b, (((1,), (1,)), ((), ())), preferred_element_type=F32)


def dot_tn(a, b):
    return lax.dot_general(a, b, (((0,), (0,)), ((), ())), preferred_element_type=F32)


def select(shape, source):
    o = lax.broadcasted_iota(jnp.int32, shape, 0)
    return (source(o) == lax.broadcasted_iota(jnp.int32, shape, 1)).astype(F32).astype(BF)


def own_source(o):
    cc = (o * 171) >> 13
    qr, qc = split12(o - QN * cc)
    return qr * 48 + qc * 4 + cc


def key_source(o):
    j = ((o & (KN - 1)) + 36) & (KN - 1)
    kr, kc = split12(j)
    return jnp.where(j < 120, kr * 48 + kc * 4 + (o >> 7), -1)


def normed(v):
    mean = jnp.mean(v, axis=-1, keepdims=True)
    cen = v - mean
    var = jnp.mean(cen * cen, axis=-1, keepdims=True)
    rstd = lax.rsqrt(var + NORM_EPS)
    return cen * rstd, rstd


def norm_back(g, xhat, rstd):
    m1 = jnp.mean(g, axis=-1, keepdims=True)
    m2 = jnp.mean(g * xhat, axis=-1, keepdims=True)
    return rstd * (g - m1 - xhat * m2)


def spread_heads(v, lane_head):
    zero = jnp.zeros((QN, 128), v.dtype)
    rows = []
    for h in range(HEADS):
        half = [zero, zero]
        half[h // 4] = jnp.where(lane_head == h % 4, v[:, 128 * (h // 4) : 128 * (h // 4) + 128], zero)
        rows.append(jnp.concatenate(half, axis=1))
    return jnp.concatenate(rows, axis=0)


def pick_heads(full, lane_head):
    halves = []
    for side in range(2):
        parts = [full[h * QN : (h + 1) * QN, 128 * side : 128 * side + 128] for h in range(4 * side, 4 * side + 4)]
        low = jnp.where(lane_head == 0, parts[0], parts[1])
        high = jnp.where(lane_head == 2, parts[2], parts[3])
        halves.append(jnp.where(lane_head < 2, low, high))
    return jnp.concatenate(halves, axis=1)


def split12(v):
    q = (v * 43) >> 9
    return q, v - 12 * q


def table_slots():
    n = lax.broadcasted_iota(jnp.int32, (WINDOW * WINDOW, KN), 0)
    lane = lax.broadcasted_iota(jnp.int32, (WINDOW * WINDOW, KN), 1)
    nr = (n * 37) >> 8
    nc = n - 7 * nr
    return (((12 * (nr - 3) + nc - 3) & (KN - 1)) == lane).astype(F32)


def bias_kernel(sizes_ref, table_ref, bias_ref, limits_ref, po_ref, pk_ref):
    po_ref[...] = select((4 * QN, 4 * 48), own_source)
    pk_ref[...] = select((4 * KN, 10 * 48), key_source)
    row = lax.broadcasted_iota(jnp.int32, (8, 128), 0)
    limits_ref[...] = jnp.where(row == 0, sizes_ref[0, 0] - lax.axis_index("band") * 16, sizes_ref[0, 1])

    slots = lax.dot_general(
        table_ref[...],
        table_slots(),
        (((1,), (0,)), ((), ())),
        precision=lax.Precision.HIGHEST,
        preferred_element_type=F32,
    )
    qi = lax.broadcasted_iota(jnp.int32, (QN, KN), 0)
    si = lax.broadcasted_iota(jnp.int32, (QN, KN), 1)
    ji = (si + 36) & (KN - 1)
    kr, kc = split12(ji)
    qr, qc = split12(qi)
    window = (jnp.abs(kc - qc) <= 3) & (jnp.abs(kr - qr - 3) <= 3) & (ji < 120)
    rows = []
    for h in range(HEADS):
        line = jnp.broadcast_to(slots[h : h + 1, :] * LOG2E, (QN, KN))
        line = pltpu.roll(line, 0, 1, stride=1, stride_axis=0)
        rows.append(jnp.where(window, line, MASKED))
    bias_ref[...] = jnp.concatenate(rows, axis=0).T


def prep_kernel(x_ref, cot_ref, po_ref, xp_ref, xhat_ref, rstd_ref, dy_ref, dysum_ref, toc_ref, toz_ref):
    odd = (lax.axis_index("band") & 1) == 1
    for i in range(12):
        toc_ref[i] = jnp.where(odd, x_ref[i], x_ref[4 + i])
        toz_ref[i] = jnp.where(odd, x_ref[4 + i], x_ref[i])

    def block(rc, _):
        at = pl.ds(pl.multiple_of(rc * 192, 192), 192)
        xp = dot(po_ref[...], jnp.concatenate([x_ref[4 * i + rc] for i in range(4)], axis=0))
        xp_ref[at, :] = xp
        xhat, rstd = normed(xp)
        xhat_ref[at, :] = xhat
        rstd_ref[at, :] = jnp.broadcast_to(rstd, (192, 128))
        dy = dot(po_ref[...], jnp.concatenate([cot_ref[4 * i + rc] for i in range(4)], axis=0))
        dy_ref[at, :] = dy.astype(BF)
        dysum_ref[...] += jnp.sum(dy, axis=0, keepdims=True)
        return 0

    dysum_ref[...] = jnp.zeros_like(dysum_ref)
    lax.fori_loop(0, 4, block, 0, unroll=4)


def halo_kernel(x_ref, xc_ref, xz_ref, pk_ref, xk_ref):
    odd = (lax.axis_index("band") & 1) == 1

    def block(rc, _):
        rows = [jnp.where(odd, xc_ref[4 * i + rc], xz_ref[4 * i + rc]) for i in range(3)]
        rows += [x_ref[4 * i + rc] for i in range(4)]
        rows += [jnp.where(odd, xz_ref[4 * i + rc], xc_ref[4 * i + rc]) for i in range(3)]
        xk = dot(pk_ref[...], jnp.concatenate(rows, axis=0))
        xk_ref[pl.ds(pl.multiple_of(rc * 512, 512), 512), :] = normed(xk)[0]
        return 0

    lax.fori_loop(0, 4, block, 0, unroll=4)


def project_kernel(xhat_ref, xk_ref, wqkv_ref, vec_ref, q_ref, k_ref, v_ref):
    def vrow(i):
        return vec_ref[i : i + 1, :]

    def block(rc, _):
        at = pl.ds(pl.multiple_of(rc * 192, 192), 192)
        a1 = (xhat_ref[at, :] * vrow(0) + vrow(1)).astype(BF)
        q_ref[at, :] = (dot(a1, wqkv_ref[:, 0:256]) + vrow(2)).astype(BF)
        at = pl.ds(pl.multiple_of(rc * 512, 512), 512)
        a1k = (xk_ref[at, :] * vrow(0) + vrow(1)).astype(BF)
        k_ref[at, :] = dot(a1k, wqkv_ref[:, 256:512]).astype(BF)
        v_ref[at, :] = (dot(a1k, wqkv_ref[:, 512:768]) + vrow(3)).astype(BF)
        return 0

    lax.fori_loop(0, 4, block, 0, unroll=4)


def attend_kernel(limits_ref, bias_ref, q_ref, k_ref, v_ref, mixed_ref, p_ref, other_ref):
    scale = 32 ** (-0.5)
    lane_head = lax.broadcasted_iota(jnp.int32, (QN, 128), 1) >> 5
    row0 = lax.axis_index("band") * 16
    height = limits_ref[0:1, 0:1]
    wide = limits_ref[1:2, 0:1]
    ks = lax.broadcasted_iota(jnp.int32, (KN, 384), 0)
    ql = lax.broadcasted_iota(jnp.int32, (KN, 384), 1)
    other_ref[...] = jnp.where(ks == ql - 48 * ((ql * 171) >> 13), 0.0, 1.0)
    krow, kcol = split12((lax.broadcasted_iota(jnp.int32, (KN, 128), 0) + 36) & (KN - 1))

    def attend(k, _):
        rc = k >> 2
        cc = k & 3
        at_q = pl.ds(pl.multiple_of(k * QN, QN), QN)
        at_k = pl.ds(pl.multiple_of(k * KN, KN), KN)
        qbd = spread_heads(q_ref[at_q, :], lane_head)
        r = krow * 4 + (rc - 12)
        c = kcol * 4 + cc
        off = jnp.where((r >= -row0) & (r < height) & (c < wide), 0.0, MASKED)
        off = bias_ref[...] + jnp.concatenate([off] * 3, axis=1) * other_ref[...]
        s = dot_nt(k_ref[at_k, :], qbd) * (scale * LOG2E) + off
        top = jnp.max(s, axis=0, keepdims=True)
        e = jnp.exp2(s - top)
        p = e * (1.0 / jnp.sum(e, axis=0, keepdims=True))
        p_ref[at_k, :] = p
        full = dot_tn(p.astype(BF), v_ref[at_k, :])
        mixed_ref[at_q, :] = pick_heads(full, lane_head).astype(BF)
        return 0

    lax.fori_loop(0, CLS, attend, 0, unroll=CLS)


def feed_kernel(
    dy_ref,
    dysum_ref,
    mixed_ref,
    xp_ref,
    wo_ref,
    wu_ref,
    wd_ref,
    vec_ref,
    act_ref,
    dz_ref,
    a2_ref,
    da_ref,
    dx1_ref,
    x1_ref,
    dmix_ref,
    sums_ref,
    zsum_ref,
    xhat_ref,
    rstd_ref,
):
    def vrow(i):
        return vec_ref[i : i + 1, :]

    sums_ref[...] = jnp.zeros_like(sums_ref)
    sums_ref[7:8, :] = dysum_ref[...]
    zsum_ref[...] = jnp.zeros_like(zsum_ref)

    def inner(rc, _):
        at = pl.ds(pl.multiple_of(rc * 192, 192), 192)
        x1 = xp_ref[at, :] + (dot(mixed_ref[at, :], wo_ref[...]) + vrow(4))
        x1_ref[at, :] = x1
        xhat, rstd = normed(x1)
        xhat_ref[at, :] = xhat
        rstd_ref[at, :] = jnp.broadcast_to(rstd, (192, 128))
        a2_ref[at, :] = (xhat * vrow(5) + vrow(6)).astype(BF)
        return 0

    lax.fori_loop(0, 4, inner, 0, unroll=4)

    def hidden(rc, _):
        at = pl.ds(pl.multiple_of(rc * 192, 192), 192)
        for part in range(3):
            cols = slice(256 * part, 256 * part + 256)
            z = dot(a2_ref[at, :], wu_ref[:, cols]) + vrow(8 + part)
            cube = (GELU0 * GELU1) * (z * z)
            up = 0.5 + 0.5 * jnp.tanh(z * (GELU0 + cube))
            act = z * up
            act_ref[at, cols] = act.astype(BF)
            slope = up * (1.0 + (z - act) * (2.0 * GELU0 + 6.0 * cube))
            dz = dot_nt(dy_ref[at, :], wd_ref[cols, :]) * slope
            zsum_ref[:, cols] += jnp.sum(dz, axis=0, keepdims=True)
            dz_ref[at, cols] = dz.astype(BF)
        return 0

    lax.fori_loop(0, 4, hidden, 0, unroll=4)

    def outer(rc, _):
        at = pl.ds(pl.multiple_of(rc * 192, 192), 192)
        dn = dot_nt(dz_ref[at, :], wu_ref[...])
        xhat = xhat_ref[at, :]
        dx1 = dy_ref[at, :].astype(F32) + norm_back(dn * vrow(5), xhat, rstd_ref[at, 0:1])
        dx1_ref[at, :] = dx1
        da_ref[at, :] = dx1.astype(BF)
        sums_ref[4:5, :] += jnp.sum(dx1, axis=0, keepdims=True)
        sums_ref[5:6, :] += jnp.sum(dn * xhat, axis=0, keepdims=True)
        sums_ref[6:7, :] += jnp.sum(dn, axis=0, keepdims=True)
        return 0

    lax.fori_loop(0, 4, outer, 0, unroll=4)
    dmix_ref[...] = dot_nt(da_ref[...], wo_ref[...]).astype(BF)


def back_kernel(
    q_ref,
    v_ref,
    p_ref,
    dmix_ref,
    own_ref,
    rimc_ref,
    rimz_ref,
    dsl_ref,
    tacc_ref,
    dkv_ref,
):
    odd = (lax.axis_index("band") & 1) == 1
    scale = 32 ** (-0.5)
    lane_head = lax.broadcasted_iota(jnp.int32, (QN, 128), 1) >> 5
    tacc_ref[...] = jnp.zeros_like(tacc_ref)

    def scores_back(k, _):
        at_q = pl.ds(pl.multiple_of(k * QN, QN), QN)
        at_k = pl.ds(pl.multiple_of(k * KN, KN), KN)
        dp = dot_nt(v_ref[at_k, :], spread_heads(dmix_ref[at_q, :], lane_head))
        p = p_ref[at_k, :]
        pdp = p * dp
        ds = pdp - p * jnp.sum(pdp, axis=0, keepdims=True)
        tacc_ref[...] += ds
        dsl_ref[at_k, :] = ds.astype(BF)
        return 0

    lax.fori_loop(0, CLS, scores_back, 0, unroll=CLS)

    def back_class(k):
        at_q = pl.ds(pl.multiple_of(k * QN, QN), QN)
        at_k = pl.ds(pl.multiple_of(k * KN, KN), KN)
        dv = dot(p_ref[at_k, :].astype(BF), spread_heads(dmix_ref[at_q, :], lane_head))
        dk = dot(dsl_ref[at_k, :], spread_heads(q_ref[at_q, :], lane_head)) * scale
        dkv_ref[at_k, 0:256] = dk.astype(BF)
        dkv_ref[at_k, 256:512] = dv.astype(BF)
        own_ref[at_q, 0:256] = dk[0:QN]
        own_ref[at_q, 256:512] = dv[0:QN]
        after = jnp.concatenate([dk[QN : QN + RIM], dv[QN : QN + RIM]], axis=1)
        before = jnp.concatenate([dk[KN - RIM :], dv[KN - RIM :]], axis=1)
        return after, before

    def attend_back(pair, _):
        after0, before0 = back_class(pair * 2)
        after1, before1 = back_class(pair * 2 + 1)
        at = pl.ds(pl.multiple_of(pair * 2 * RIM, 2 * RIM), 2 * RIM)
        after = jnp.concatenate([after0, after1], axis=0)
        before = jnp.concatenate([before0, before1], axis=0)
        rimc_ref[at, :] = jnp.where(odd, before, after).astype(BF)
        rimz_ref[at, :] = jnp.where(odd, after, before).astype(BF)
        return 0

    lax.fori_loop(0, CLS // 2, attend_back, 0, unroll=8)


def early_grads(act_ref, dy_ref, a2_ref, dz_ref, mixed_ref, da_ref, fd, fu, fo):
    fd[...] = dot_tn(act_ref[...], dy_ref[...])
    fu[...] = dot_tn(a2_ref[...], dz_ref[...])
    fo[...] = dot_tn(mixed_ref[...], da_ref[...])


def output_kernel(x1_ref, act_ref, wd_ref, vec_ref, po_ref, out_ref):
    def result(rc, _):
        at = pl.ds(pl.multiple_of(rc * 192, 192), 192)
        res = x1_ref[at, :] + dot(act_ref[at, :], wd_ref[...]) + vec_ref[7:8, :]
        back = dot_tn(po_ref[...], res.astype(BF)).astype(BF)
        for i in range(4):
            out_ref[4 * i + rc] = back[48 * i : 48 * i + 48]
        return 0

    lax.fori_loop(0, 4, result, 0, unroll=4)


def late_grads(
    dsl_ref,
    k_ref,
    tacc_ref,
    xhat_ref,
    xk_ref,
    dkv_ref,
    wqkv_ref,
    vt_ref,
    sums_ref,
    zsum_ref,
    dq_ref,
    fq_ref,
    fv_ref,
    tgrad_ref,
):
    scale = 32 ** (-0.5)
    lane_head = lax.broadcasted_iota(jnp.int32, (QN, 128), 1) >> 5

    def query(k, _):
        at_q = pl.ds(pl.multiple_of(k * QN, QN), QN)
        at_k = pl.ds(pl.multiple_of(k * KN, KN), KN)
        dq = pick_heads(dot_tn(dsl_ref[at_k, :], k_ref[at_k, :]), lane_head) * scale
        dq_ref[at_q, :] = dq.astype(BF)
        return 0

    lax.fori_loop(0, CLS, query, 0, unroll=16)
    dq = dq_ref[...]
    gain, shift = vt_ref[:, 0:1], vt_ref[:, 1:2]
    qsum = jnp.sum(dq.astype(F32), axis=0, keepdims=True)
    m = dot_tn(xhat_ref[...].astype(BF), dq)
    weight = wqkv_ref[:, 0:256].astype(F32)
    fq_ref[:, 0:256] = gain * m + shift * qsum
    gain_grad = jnp.sum(weight * m, axis=1, keepdims=True)
    shift_grad = jnp.sum(weight * qsum, axis=1, keepdims=True)
    xk = xk_ref[...].astype(BF)
    for cols in (slice(256, 512), slice(512, 768)):
        dkv = dkv_ref[:, cols.start - 256 : cols.stop - 256]
        kvsum = jnp.sum(dkv.astype(F32), axis=0, keepdims=True)
        m = dot_tn(xk, dkv)
        weight = wqkv_ref[:, cols].astype(F32)
        fq_ref[:, cols] = gain * m + shift * kvsum
        gain_grad = gain_grad + jnp.sum(weight * m, axis=1, keepdims=True)
        shift_grad = shift_grad + jnp.sum(weight * kvsum, axis=1, keepdims=True)
    lines = jnp.concatenate(
        [jnp.zeros((2, 256), F32), qsum, kvsum, sums_ref[4:8, :]]
        + [zsum_ref[:, 256 * i : 256 * i + 256] for i in range(3)]
        + [jnp.zeros((117, 256), F32)],
        axis=0,
    )
    lane = lax.broadcasted_iota(jnp.int32, (256, 128), 1)
    fv_ref[...] = jnp.where(lane == 0, gain_grad, jnp.where(lane == 1, shift_grad, lines.T))

    flat = tacc_ref[...].T
    qi = lax.broadcasted_iota(jnp.int32, (QN, KN), 0)
    lines = []
    for h in range(HEADS):
        part = flat[h * QN : (h + 1) * QN]
        for bit in range(6):
            turned = pltpu.roll(part, KN - (1 << bit), 1)
            part = jnp.where((qi >> bit) & 1 == 1, turned, part)
        lines.append(jnp.sum(part, axis=0, keepdims=True))
    tgrad_ref[...] = jnp.concatenate(lines, axis=0)


def input_kernel(
    own_ref, gotc_ref, gotz_ref, dq_ref, dx1_ref, xhat_ref, rstd_ref, wqkv_ref, vec_ref, po_ref, tok_ref
):
    odd = (lax.axis_index("band") & 1) == 1

    def block(rc, _):
        at = pl.ds(pl.multiple_of(rc * 192, 192), 192)
        mine = own_ref[at, :]
        got_c = gotc_ref[pl.ds(pl.multiple_of(rc * 160, 160), 160), :].astype(F32)
        got_z = gotz_ref[pl.ds(pl.multiple_of(rc * 160, 160), 160), :].astype(F32)
        got_a = jnp.where(odd, got_c, got_z)
        got_b = jnp.where(odd, got_z, got_c)
        gap = jnp.zeros((QN - RIM, 512), F32)
        parts = []
        for i in range(4):
            a = jnp.concatenate([got_a[i * RIM : (i + 1) * RIM], gap], axis=0)
            b = jnp.concatenate([gap, got_b[i * RIM : (i + 1) * RIM]], axis=0)
            parts.append(mine[i * QN : (i + 1) * QN] + a + b)
        dkv = jnp.concatenate(parts, axis=0).astype(BF)
        dn = dot_nt(dq_ref[at, :], wqkv_ref[:, 0:256]) + dot_nt(dkv, wqkv_ref[:, 256:768])
        dx = dx1_ref[at, :] + norm_back(dn * vec_ref[0:1, :], xhat_ref[at, :], rstd_ref[at, 0:1])
        back = dot_tn(po_ref[...], dx.astype(BF)).astype(BF)
        for i in range(4):
            tok_ref[4 * i + rc] = back[48 * i : 48 * i + 48]
        return 0

    lax.fori_loop(0, 4, block, 0, unroll=4)


EARLY = 896
LATE = 512


def widen(v):
    return jnp.concatenate([v, jnp.zeros((v.shape[0], 128 - v.shape[1]), F32)], axis=1)


def pack(wqkv, wo, wu, wd, vec):
    pieces = [(wqkv, 0, 0), (wo, 0, 768), (wd, 0, 1024), (vec, 0, 1280)]
    pieces += [(wu, 8, 0), (wd, 0, 768), (wd, -8, 1024)]
    total = 0.0
    for p, row, lane in pieces:
        rows, lanes = p.shape
        zero = jnp.zeros((), F32)
        if rows == 24 and lane == 1024 and row == 0:
            p = lax.pad(p, zero, ((0, -16, 0), (0, 0, 0)))
            rows = 8
        elif rows == 24:
            p = lax.pad(p, zero, ((-8 + row, -8 - row, 0), (0, 0, 0)))
            row, rows = 8, 8
        total = total + lax.pad(p, zero, ((row, 16 - row - rows, 0), (lane, EARLY + LATE - lane - lanes, 0)))
    return total.astype(BF)


def own_index():
    return lax.axis_index("maps") * 8 + lax.axis_index("band")


def unpack(blocks, big_qkv, big_out, big_up, big_down, vec, vt, fq, fo, fu, fd):
    me = own_index()
    for index, block in enumerate(blocks):
        core, across = divmod(index, 4)
        for z in range(4):
            slab = block[z].astype(F32)
            o = me ^ (core | (z << 1) | (across << 3))
            at = pl.ds(pl.multiple_of(o * 8, 8), 8)
            fq[at, :] = slab[0:8, 0:768]
            vt[at, :] = slab[0:8, 1280:1408]
            for b, rows in enumerate((slab[0:8, 1024:1280], slab[8:16, 768:1024], slab[8:16, 1024:1280])):
                fd[pl.ds(pl.multiple_of(o * 24 + 8 * b, 8), 8), :] = rows
            fo[at, :] = slab[0:8, 768:1024]
            fu[at, :] = slab[8:16, 0:768]
    big_qkv[...] = fq[...].astype(BF)
    vec[...] = vt[...].T[0 : vec.shape[0]]
    big_out[...] = fo[...].astype(BF)
    big_up[...] = fu[...].astype(BF)
    big_down[...] = fd[...].astype(BF)


def main_kernel(*refs):
    blocks, (xhat, x, xz, xc, pk, xp, bias, limits, dy, dysum) = refs[:8], refs[8:18]
    act, dx1, x1, own, rimc, rimz, dq, out_ref, big_qkv, big_down, vec = refs[18:29]
    q, k, v, mixed, p, dz, a2, da, dmix, sums, zsum, dsl, tacc, dkv = refs[29:43]
    fq, fv, tgrad, fd, fu, fo, big_out, big_up, vt, xk, other, xhat1, rstd1 = refs[43:]
    halo_kernel(x, xc, xz, pk, xk)
    unpack(blocks, big_qkv, big_out, big_up, big_down, vec, vt, fq, fo, fu, fd)
    project_kernel(xhat, xk, big_qkv, vec, q, k, v)
    attend_kernel(limits, bias, q, k, v, mixed, p, other)
    feed_kernel(dy, dysum, mixed, xp, big_out, big_up, big_down, vec, act, dz, a2, da, dx1, x1, dmix, sums, zsum, xhat1, rstd1)
    back_kernel(q, v, p, dmix, own, rimc, rimz, dsl, tacc, dkv)
    late_grads(dsl, k, tacc, xhat, xk, dkv, big_qkv, vt, sums, zsum, dq, fq, fv, tgrad)
    early_grads(act, dy, a2, dz, mixed, da, fd, fu, fo)
    table = tgrad[...]
    me = own_index()
    for o in range(32):
        at = slice(8 * o, 8 * o + 8)
        top = [fd[24 * o + 8 * b : 24 * o + 8 * b + 8, :] for b in range(3)] + [fo[at, 0:128], fq[at, 0:512]]
        low = [fu[at, :], fo[at, 128:256], fq[at, 512:768], fv[at, :], table]
        both = jnp.concatenate([jnp.concatenate(top, axis=1), jnp.concatenate(low, axis=1)], axis=0)
        out_ref[frame_slot(me, o)] = both.astype(BF)


def frame_slot(me, o):
    m = me ^ o
    return (m & 1) * 16 + (m >> 3) * 4 + ((m >> 1) & 3)


def shard_grads(refs, vrows):
    total = refs[0][...] + sum(ref[...].astype(F32) for ref in refs[1:4])
    early, late = total[:, :EARLY], total[:, EARLY:]
    return [
        jnp.concatenate([late[0:8], late[8:16, 0:256]], axis=1),
        jnp.concatenate([early[0:8, 768:896], early[8:16, 768:896]], axis=1),
        early[8:16, 0:768],
        jnp.concatenate([early[0:8, 256 * b : 256 * b + 256] for b in range(3)], axis=0),
        late[8:16, 256 : 256 + vrows],
        lax.dot_general(
            late[8:16, 384:512],
            table_slots(),
            (((1,), (1,)), ((), ())),
            precision=lax.Precision.HIGHEST,
            preferred_element_type=F32,
        ),
    ]


def update_kernel(*refs):
    w, first, second, outs = refs[4:10], refs[10:16], refs[16:22], refs[22:]
    vrows = w[4].shape[1]
    grads = shard_grads(refs, vrows)
    row = lax.broadcasted_iota(jnp.int32, (8, 128), 0)
    lane = lax.broadcasted_iota(jnp.int32, (8, 128), 1)
    norms = jnp.zeros((8, 128), F32)
    for i in range(6):
        update = adam_parts(w[i][...], grads[i], first[i][...], second[i][...])[2]
        outs[i][...] = update
        for line, v in ((0, w[i][...]), (1, update)):
            sums = jnp.sum(v * v, axis=0, keepdims=True)
            if i == 4:
                sums = pltpu.roll(widen(sums), 4, 1)
                norms = jnp.where((row == line) & (lane >= 4) & (lane < 4 + vrows), sums, norms)
            else:
                at = i if i < 4 else 4 + vrows
                norms = jnp.where((row == line) & (lane == at), jnp.sum(sums, axis=1, keepdims=True), norms)
    outs[6][...] = norms


def moments_kernel(*refs):
    first, second, outs = refs[4:10], refs[10:16], refs[16:]
    grads = shard_grads(refs, first[4].shape[1])
    for i in range(6):
        new_first, new_second, _ = adam_parts(0.0, grads[i], first[i][...], second[i][...])
        outs[2 * i][...] = new_first
        outs[2 * i + 1][...] = new_second


def step_kernel(mine_ref, a_ref, b_ref, c_ref, d_ref, *refs):
    w, update, outs = refs[0:6], refs[6:12], refs[12:]
    vrows = w[4].shape[1]
    total = a_ref[...] + b_ref[...] + c_ref[...] + d_ref[...]
    lane = lax.broadcasted_iota(jnp.int32, (8, 128), 1)
    norms = jnp.sqrt(jnp.where(lane == 4 + vrows, mine_ref[...], total))
    outs[6][...] = norms[0:1, 0:16]
    outs[7][...] = norms[1:2, 0:16]
    rate = LEARN_RATE * norms[0:1] / (norms[1:2] + RATIO_EPS)
    for i in range(6):
        if i == 4:
            r = pltpu.roll(rate, 124, 1)[:, 0:vrows]
        else:
            at = i if i < 4 else 4 + vrows
            r = rate[:, at : at + 1]
        outs[i][...] = w[i][...] - r * update[i][...]


def stack_kernel(*refs):
    for i, ref in enumerate(refs[:4]):
        refs[4][i] = ref[...]


def call(kernel, out_shape, scratch, *args, smem=0, flops=10**8, vmem=16):
    vm = pl.BlockSpec(memory_space=pltpu.VMEM)
    specs = [pl.BlockSpec(memory_space=pltpu.SMEM)] * smem + [vm] * (len(args) - smem)
    return pl.pallas_call(
        kernel,
        out_shape=out_shape,
        in_specs=specs,
        out_specs=jax.tree.map(lambda _: vm, out_shape),
        scratch_shapes=scratch,
        compiler_params=pltpu.CompilerParams(vmem_limit_bytes=vmem * 2**20),
        cost_estimate=pl.CostEstimate(flops=flops, bytes_accessed=10**6, transcendentals=0),
    )(*args)


def sds(shape, dtype=BF):
    return jax.ShapeDtypeStruct(shape, dtype)


def exchange_groups(maps, band):
    zbits = band.bit_length() - 2
    mbits = maps.bit_length() - 1
    cut = lambda lo, n: [(lo + i, min(2, n - i)) for i in range(0, n, 2)]
    return cut(1, zbits) + cut(1 + zbits, mbits) + [(0, 1)]


def swap(block, mask, count):
    return lax.ppermute(block, AXES, [(k, k ^ mask) for k in range(count)])


def frame_masks(groups):
    masks = [0]
    for lo, bits in groups:
        masks = [m ^ (d << lo) for d in range(1 << bits) for m in masks]
    return masks


def gather_all(slab, groups, count):
    block = slab[None]
    for lo, bits in groups:
        block = jnp.concatenate(
            [block] + [swap(block, d << lo, count) for d in range(1, 1 << bits)], axis=0
        )
    return block


def scatter_sum(grads, groups, count):
    for lo, bits in reversed(groups):
        grads = add_stage(grads, lo, bits, count)
    return grads[0]


def adam_parts(weight, grad, first, second):
    new_first = BETA_FIRST * first + (1.0 - BETA_FIRST) * grad
    new_second = BETA_SECOND * second + (1.0 - BETA_SECOND) * grad * grad
    update = (
        new_first
        / (1.0 - BETA_FIRST**STEP)
        / (jnp.sqrt(new_second / (1.0 - BETA_SECOND**STEP)) + ADAM_EPS)
        + DECAY_RATE * weight
    )
    return (new_first, new_second, update)


def squares_of(matrices, rowwise):
    return jnp.concatenate(
        [
            jnp.stack([jnp.sum(matrix * matrix) for matrix in matrices]),
            jnp.sum(rowwise * rowwise, axis=1),
        ]
    )


def bias_outputs():
    return (sds((KN, 384), F32), sds((8, 128), jnp.int32), sds((4 * QN, 4 * 48)), sds((4 * KN, 10 * 48)))


def prep_outputs():
    return (
        sds((768, 256), F32),
        sds((768, 256), F32),
        sds((768, 128), F32),
        sds((768, 256)),
        sds((1, 256), F32),
        sds((12, 48, 256)),
        sds((12, 48, 256)),
    )


def project_outputs():
    return (sds((768, 256)), sds((CLS * KN, 256)), sds((CLS * KN, 256)))


def attend_outputs():
    return (sds((768, 256)), sds((CLS * KN, 384), F32))


def feed_outputs():
    return (
        sds((768, 768)),
        sds((768, 768)),
        sds((768, 256)),
        sds((768, 256)),
        sds((768, 256), F32),
        sds((768, 256), F32),
        sds((768, 256)),
        sds((8, 256), F32),
        sds((1, 768), F32),
    )


def back_outputs():
    return (
        sds((768, 512), F32),
        sds((CLS * RIM, 512)),
        sds((CLS * RIM, 512)),
        sds((CLS * KN, 384)),
        sds((KN, 384), F32),
        sds((CLS * KN, 512)),
    )


def late_outputs():
    return (
        sds((768, 256)),
        sds((256, 768), F32),
        sds((256, 128), F32),
        sds((HEADS, KN), F32),
    )


def beside(block, band):
    touching = [(b, b + 1 if b % 2 else b - 1) for b in range(band)]
    return (
        lax.ppermute(block[0], "band", [(b, b ^ 1) for b in range(band)]),
        lax.ppermute(block[1], "band", [(b, to) for b, to in touching if 0 <= to < band]),
    )


def packed_step(tokens_in, cotangent, map_sizes, weights, firsts, seconds):
    count = 32
    vrows = weights[4].shape[0]
    turn = lambda arrays: tuple(a.T if i == 4 else a for i, a in enumerate(arrays))
    weights, firsts, seconds = turn(weights), turn(firsts), turn(seconds)
    slab = pack(*weights[:5])
    slab, sizes = lax.optimization_barrier((slab, map_sizes))
    slabs = [slab] + [swap(slab, d << 1, count) for d in (1, 2, 3)]
    bias, limits, po, pk = call(bias_kernel, bias_outputs(), [], sizes, weights[5], smem=1, flops=10**9, vmem=4)
    *slabs, bias = lax.optimization_barrier((*slabs, bias))
    column = call(stack_kernel, sds((4, 16, EARLY + LATE)), [], *slabs, vmem=4)
    column, x = lax.optimization_barrier((column, tokens_in))
    blocks = [column] + [swap(column, d << 3, count) for d in (1, 2, 3)]
    xp, xhat, rstd, dy, dysum, *edges = call(prep_kernel, prep_outputs(), [], x, cotangent, po, flops=2 * 10**9, vmem=8)
    x_core, x_next = beside(edges, 8)
    *far, xp = lax.optimization_barrier((*blocks[1:], xp))
    blocks = [blocks[0]] + far + [swap(block, 1, count) for block in [blocks[0]] + far]
    act_s, dz_s, a2_s, da_s, dx1_s, x1_s, dmix_s, sums_s, zsum_s = feed_outputs()
    own_s, rimc_s, rimz_s, dsl_s, tacc_s, dkv_s = back_outputs()
    dq_s, fq_s, fv_s, tgrad_s = late_outputs()
    act, dx1, x1, own, rim_c, rim_z, dq, grads, big_qkv, big_down, vec = call(
        main_kernel,
        (act_s, dx1_s, x1_s, own_s, rimc_s, rimz_s, dq_s)
        + (sds((count, 16, EARLY + LATE)), sds((256, 768)), sds((768, 256)), sds((vrows, 256), F32)),
        [
            pltpu.VMEM(o.shape, o.dtype)
            for o in project_outputs()
            + attend_outputs()
            + (dz_s, a2_s, da_s, dmix_s, sums_s, zsum_s, dsl_s, tacc_s, dkv_s, fq_s, fv_s, tgrad_s)
            + (sds((768, 256), F32), sds((256, 768), F32), sds((256, 256), F32))
            + (sds((256, 256)), sds((256, 768)), sds((256, 128), F32), sds((CLS * KN, 256), F32), sds((KN, 384), F32))
            + (sds((768, 256), F32), sds((768, 128), F32))
        ],
        *blocks, xhat, x, x_next, x_core, pk, xp, bias, limits, dy, dysum,
        flops=15 * 10**9, vmem=24,
    )
    layer_out = call(output_kernel, sds((16, 48, 256)), [], x1, act, big_down, vec, po, flops=10**9, vmem=8)
    got_c, got_z = beside((rim_c, rim_z), 8)
    grads = add_stage(add_stage(grads, 0, 1, count), 3, 2, count)
    grads, own = lax.optimization_barrier((grads, own))
    tokens_grad = call(
        input_kernel, sds((16, 48, 256)), [], own, got_c, got_z, dq, dx1, xhat, rstd, big_qkv, vec, po,
        flops=10**9, vmem=8,
    )
    low = grads.astype(BF)
    parts = [grads[0]] + [swap(low[d], d << 1, count) for d in (1, 2, 3)]
    parts[0], tokens_grad, layer_out = lax.optimization_barrier((parts[0], tokens_grad, layer_out))

    shapes = [sds(w.shape, F32) for w in weights]
    *updates, mine = call(
        update_kernel, tuple(shapes) + (sds((8, 128), F32),), [], *parts, *weights, *firsts, *seconds, vmem=4
    )
    moments = call(
        moments_kernel, tuple(shape for shape in shapes for _ in range(2)), [], *parts, *firsts, *seconds, vmem=4
    )
    squares = mine + swap(mine, 1, count)
    squares = squares + swap(squares, 2, count) + swap(squares, 4, count) + swap(squares, 6, count)
    last = [swap(squares, d << 3, count) for d in (1, 2, 3)]
    squares, *moments = lax.optimization_barrier((squares, *moments))
    news = call(
        step_kernel,
        tuple(shapes) + (sds((1, 16), F32),) * 2,
        [],
        mine, squares, *last, *weights, *updates, vmem=4,
    )
    results = [layer_out, tokens_grad]
    for i in range(6):
        three = (moments[2 * i], moments[2 * i + 1], news[i])
        results += [a.T for a in three] if i == 4 else three
    return tuple(results) + (news[6].reshape(16), news[7].reshape(16))


def add_stage(grads, lo, bits, count):
    low = grads.astype(BF).reshape((1 << bits, -1) + grads.shape[1:])
    total = grads.reshape(low.shape)[0].astype(F32)
    for d in range(1, 1 << bits):
        total = total + swap(low[d], d << lo, count).astype(F32)
    return total


def per_device(
    maps,
    band,
    tokens_in,
    cotangent,
    map_sizes,
    w_qkv,
    w_out,
    w_up,
    w_down,
    vectors,
    pos_table,
    first_qkv,
    second_qkv,
    first_out,
    second_out,
    first_up,
    second_up,
    first_down,
    second_down,
    first_vectors,
    second_vectors,
    first_table,
    second_table,
):
    if w_qkv.shape[0] == 8 and (maps, band) == (4, 8):
        return packed_step(
            tokens_in, cotangent, map_sizes,
            (w_qkv, w_out, w_up, w_down, vectors, pos_table),
            (first_qkv, first_out, first_up, first_down, first_vectors, first_table),
            (second_qkv, second_out, second_up, second_down, second_vectors, second_table),
        )
    count = maps * band
    rows = w_qkv.shape[0]
    vrows = vectors.shape[0]
    groups = exchange_groups(maps, band)
    masks = np.array(frame_masks(groups))
    inverse = np.argsort(masks)
    me = lax.axis_index(AXES)
    def pack(qkv, out, upw, dnw, vec):
        dn = dnw.reshape(3, rows, 256).transpose(1, 0, 2).reshape(rows, 768)
        vt = jnp.pad(vec.T, ((0, 0), (0, 128 - vrows)))
        return jnp.concatenate([qkv, out, upw, dn, vt], axis=1)

    slab = pack(*(w.astype(BF) for w in (w_qkv, w_out, w_up, w_down, vectors)))
    block = gather_all(slab, groups, count)
    order = jnp.asarray(inverse, jnp.int32)[jnp.arange(count, dtype=jnp.int32) ^ me]
    whole = jnp.take(block, order, axis=0).reshape(256, -1)
    big_qkv = whole[:, 0:768]
    big_out = whole[:, 768:1024]
    big_up = whole[:, 1024:1792]
    big_down = (
        whole[:, 1792:2560].reshape(count, rows, 3, 256).transpose(0, 2, 1, 3).reshape(768, 256)
    )
    vt = whole[:, 2560:].astype(F32)
    vec = vt[:, :vrows].T

    bias, limits, po, pk = call(bias_kernel, bias_outputs(), [], map_sizes, pos_table, smem=1, flops=10**9)
    xp, xhat, rstd, dy, dysum, *edges = call(prep_kernel, prep_outputs(), [], tokens_in, cotangent, po, flops=2 * 10**9)
    x_core, x_next = beside(edges, band)
    xk = call(halo_kernel, sds((CLS * KN, 256), F32), [], tokens_in, x_core, x_next, pk, flops=10**9)
    queries, keys, values = call(project_kernel, project_outputs(), [], xhat, xk, big_qkv, vec, flops=10**9)
    mixed, probs = call(attend_kernel, attend_outputs(), [pltpu.VMEM((KN, 384), F32)], limits, bias, queries, keys, values, flops=3 * 10**9)
    act, dz, a2, da, dx1, x1, dmix, sums, zsum = call(
        feed_kernel,
        feed_outputs(),
        [pltpu.VMEM((768, 256), F32), pltpu.VMEM((768, 128), F32)],
        dy, dysum, mixed, xp, big_out, big_up, big_down, vec,
        flops=4 * 10**9,
    )
    own, rim_c, rim_z, dsl, tacc, dkv = call(
        back_kernel, back_outputs(), [], queries, values, probs, dmix, flops=4 * 10**9
    )
    got_c, got_z = beside((rim_c, rim_z), band)
    grad_down, grad_up, grad_out = call(
        early_grads,
        (sds((768, 256), F32), sds((256, 768), F32), sds((256, 256), F32)),
        [],
        act, dy, a2, dz, mixed, da,
        flops=10**9,
    )
    dq, grad_qkv, grad_vec, table_grad = call(
        late_grads,
        late_outputs(),
        [],
        dsl, keys, tacc, xhat, xk, dkv, big_qkv, vt, sums, zsum,
        flops=3 * 10**9,
    )
    layer_out = call(output_kernel, sds((16, 48, 256)), [], x1, act, big_down, vec, po, flops=10**9)
    tokens_grad = call(
        input_kernel, sds((16, 48, 256)), [], own, got_c, got_z, dq, dx1, xhat, rstd, big_qkv, vec, po, flops=10**9
    )

    packed = jnp.concatenate(
        [
            grad_qkv.reshape(count, rows, 768),
            grad_out.reshape(count, rows, 256),
            grad_up.reshape(count, rows, 768),
            grad_down.reshape(count, 3, rows, 256).transpose(0, 2, 1, 3).reshape(count, rows, 768),
            grad_vec.reshape(count, rows, 128),
        ],
        axis=2,
    )
    packed = jnp.take(packed, jnp.asarray(masks, jnp.int32) ^ me, axis=0)
    red = scatter_sum(packed, groups, count)
    red_qkv = red[:, 0:768]
    red_out = red[:, 768:1024]
    red_up = red[:, 1024:1792]
    red_down = red[:, 1792:2560].reshape(rows, 3, 256).transpose(1, 0, 2).reshape(3 * rows, 256)
    red_vec = red[:, 2560 : 2560 + vrows].T

    steps = np.arange(-3, 4)
    lanes = ((12 * steps[:, None] + steps[None, :]) % KN).reshape(-1)
    table_total = lax.psum(table_grad, AXES)[:, lanes]

    part_qkv = adam_parts(w_qkv, red_qkv, first_qkv, second_qkv)
    part_out = adam_parts(w_out, red_out, first_out, second_out)
    part_up = adam_parts(w_up, red_up, first_up, second_up)
    part_down = adam_parts(w_down, red_down, first_down, second_down)
    part_vec = adam_parts(vectors, red_vec, first_vectors, second_vectors)
    part_table = adam_parts(pos_table, table_total, first_table, second_table)
    local_weight_sq = squares_of((w_qkv, w_out, w_up, w_down), vectors)
    local_update_sq = squares_of((part_qkv[2], part_out[2], part_up[2], part_down[2]), part_vec[2])
    weight_sq, update_sq = lax.psum((local_weight_sq, local_update_sq), AXES)
    table_weight = jnp.sqrt(jnp.sum(pos_table * pos_table))
    table_update = jnp.sqrt(jnp.sum(part_table[2] * part_table[2]))
    weight_norms = jnp.concatenate([jnp.sqrt(weight_sq), table_weight[None]])
    update_norms = jnp.concatenate([jnp.sqrt(update_sq), table_update[None]])
    ratios = weight_norms / (update_norms + RATIO_EPS)
    next_qkv = w_qkv - LEARN_RATE * ratios[0] * part_qkv[2]
    next_out = w_out - LEARN_RATE * ratios[1] * part_out[2]
    next_up = w_up - LEARN_RATE * ratios[2] * part_up[2]
    next_down = w_down - LEARN_RATE * ratios[3] * part_down[2]
    next_vectors = vectors - LEARN_RATE * ratios[4 : 4 + vrows][:, None] * part_vec[2]
    next_table = pos_table - LEARN_RATE * ratios[4 + vrows] * part_table[2]
    return (
        layer_out,
        tokens_grad,
        part_qkv[0],
        part_qkv[1],
        next_qkv,
        part_out[0],
        part_out[1],
        next_out,
        part_up[0],
        part_up[1],
        next_up,
        part_down[0],
        part_down[1],
        next_down,
        part_vec[0],
        part_vec[1],
        next_vectors,
        part_table[0],
        part_table[1],
        next_table,
        weight_norms,
        update_norms,
    )


def solution(mesh):
    both = P(AXES, None)
    side = P(None, AXES)
    tall = P(AXES, None, None)
    copied = P()
    return jax.shard_map(
        functools.partial(per_device, mesh.shape["maps"], mesh.shape["band"]),
        mesh=mesh,
        in_specs=(tall, tall, P("maps", None))
        + (both,) * 4
        + (side, copied)
        + (both,) * 8
        + (side, side, copied, copied),
        out_specs=(tall, tall) + (both,) * 12 + (side,) * 3 + (copied,) * 5,
        check_vma=False,
    )
```

```python
import functools

import jax
import jax.numpy as jnp
import numpy as np
from jax import lax
from jax.experimental import pallas as pl
from jax.experimental.pallas import tpu as pltpu
from jax.sharding import PartitionSpec as P

HEADS = 8
WINDOW = 7
DIL = 4
STEP = 10
NORM_EPS = 1e-05
BETA_FIRST = 0.9
BETA_SECOND = 0.999
ADAM_EPS = 1e-06
DECAY_RATE = 0.01
LEARN_RATE = 0.2
RATIO_EPS = 1e-06
MASKED = -1e30
LOG2E = 1.4426950408889634
GELU0 = 0.7978845608028654
GELU1 = 0.044715
AXES = ("maps", "band")

BF = jnp.bfloat16
F32 = jnp.float32

CLS = DIL * DIL
QN = 48
KN = 128
RIM = 40


def dot(a, b):
    return lax.dot_general(a, b, (((1,), (0,)), ((), ())), preferred_element_type=F32)


def dot_nt(a, b):
    return lax.dot_general(a, b, (((1,), (1,)), ((), ())), preferred_element_type=F32)


def dot_tn(a, b):
    return lax.dot_general(a, b, (((0,), (0,)), ((), ())), preferred_element_type=F32)


def select(shape, source):
    o = lax.broadcasted_iota(jnp.int32, shape, 0)
    return (source(o) == lax.broadcasted_iota(jnp.int32, shape, 1)).astype(F32).astype(BF)


def own_source(o):
    cc = (o * 171) >> 13
    qr, qc = split12(o - QN * cc)
    return qr * 48 + qc * 4 + cc


def key_source(o):
    j = ((o & (KN - 1)) + 36) & (KN - 1)
    kr, kc = split12(j)
    return jnp.where(j < 120, kr * 48 + kc * 4 + (o >> 7), -1)


def normed(v):
    mean = jnp.mean(v, axis=-1, keepdims=True)
    cen = v - mean
    var = jnp.mean(cen * cen, axis=-1, keepdims=True)
    rstd = lax.rsqrt(var + NORM_EPS)
    return cen * rstd, rstd


def norm_back(g, xhat, rstd):
    m1 = jnp.mean(g, axis=-1, keepdims=True)
    m2 = jnp.mean(g * xhat, axis=-1, keepdims=True)
    return rstd * (g - m1 - xhat * m2)


def spread_heads(v, lane_head):
    zero = jnp.zeros((QN, 128), v.dtype)
    rows = []
    for h in range(HEADS):
        half = [zero, zero]
        half[h // 4] = jnp.where(lane_head == h % 4, v[:, 128 * (h // 4) : 128 * (h // 4) + 128], zero)
        rows.append(jnp.concatenate(half, axis=1))
    return jnp.concatenate(rows, axis=0)


def pick_heads(full, lane_head):
    halves = []
    for side in range(2):
        parts = [full[h * QN : (h + 1) * QN, 128 * side : 128 * side + 128] for h in range(4 * side, 4 * side + 4)]
        low = jnp.where(lane_head == 0, parts[0], parts[1])
        high = jnp.where(lane_head == 2, parts[2], parts[3])
        halves.append(jnp.where(lane_head < 2, low, high))
    return jnp.concatenate(halves, axis=1)


def split12(v):
    q = (v * 43) >> 9
    return q, v - 12 * q


def table_slots():
    n = lax.broadcasted_iota(jnp.int32, (WINDOW * WINDOW, KN), 0)
    lane = lax.broadcasted_iota(jnp.int32, (WINDOW * WINDOW, KN), 1)
    nr = (n * 37) >> 8
    nc = n - 7 * nr
    return (((12 * (nr - 3) + nc - 3) & (KN - 1)) == lane).astype(F32)


def bias_kernel(sizes_ref, table_ref, bias_ref, limits_ref, po_ref, pk_ref):
    po_ref[...] = select((4 * QN, 4 * 48), own_source)
    pk_ref[...] = select((4 * KN, 10 * 48), key_source)
    row = lax.broadcasted_iota(jnp.int32, (8, 128), 0)
    limits_ref[...] = jnp.where(row == 0, sizes_ref[0, 0] - lax.axis_index("band") * 16, sizes_ref[0, 1])

    slots = lax.dot_general(
        table_ref[...],
        table_slots(),
        (((1,), (0,)), ((), ())),
        precision=lax.Precision.HIGHEST,
        preferred_element_type=F32,
    )
    qi = lax.broadcasted_iota(jnp.int32, (QN, KN), 0)
    si = lax.broadcasted_iota(jnp.int32, (QN, KN), 1)
    ji = (si + 36) & (KN - 1)
    kr, kc = split12(ji)
    qr, qc = split12(qi)
    window = (jnp.abs(kc - qc) <= 3) & (jnp.abs(kr - qr - 3) <= 3) & (ji < 120)
    rows = []
    for h in range(HEADS):
        line = jnp.broadcast_to(slots[h : h + 1, :] * LOG2E, (QN, KN))
        line = pltpu.roll(line, 0, 1, stride=1, stride_axis=0)
        rows.append(jnp.where(window, line, MASKED))
    bias_ref[...] = jnp.concatenate(rows, axis=0).T


def prep_kernel(x_ref, cot_ref, po_ref, xp_ref, xhat_ref, rstd_ref, dy_ref, dysum_ref, toc_ref, toz_ref):
    odd = (lax.axis_index("band") & 1) == 1
    for i in range(12):
        toc_ref[i] = jnp.where(odd, x_ref[i], x_ref[4 + i])
        toz_ref[i] = jnp.where(odd, x_ref[4 + i], x_ref[i])

    def block(rc, _):
        at = pl.ds(pl.multiple_of(rc * 192, 192), 192)
        xp = dot(po_ref[...], jnp.concatenate([x_ref[4 * i + rc] for i in range(4)], axis=0))
        xp_ref[at, :] = xp
        xhat, rstd = normed(xp)
        xhat_ref[at, :] = xhat
        rstd_ref[at, :] = jnp.broadcast_to(rstd, (192, 128))
        dy = dot(po_ref[...], jnp.concatenate([cot_ref[4 * i + rc] for i in range(4)], axis=0))
        dy_ref[at, :] = dy.astype(BF)
        dysum_ref[...] += jnp.sum(dy, axis=0, keepdims=True)
        return 0

    dysum_ref[...] = jnp.zeros_like(dysum_ref)
    lax.fori_loop(0, 4, block, 0, unroll=4)


def halo_kernel(x_ref, xc_ref, xz_ref, pk_ref, xk_ref):
    odd = (lax.axis_index("band") & 1) == 1

    def block(rc, _):
        rows = [jnp.where(odd, xc_ref[4 * i + rc], xz_ref[4 * i + rc]) for i in range(3)]
        rows += [x_ref[4 * i + rc] for i in range(4)]
        rows += [jnp.where(odd, xz_ref[4 * i + rc], xc_ref[4 * i + rc]) for i in range(3)]
        xk = dot(pk_ref[...], jnp.concatenate(rows, axis=0))
        xk_ref[pl.ds(pl.multiple_of(rc * 512, 512), 512), :] = normed(xk)[0]
        return 0

    lax.fori_loop(0, 4, block, 0, unroll=4)


def project_kernel(xhat_ref, xk_ref, wqkv_ref, vec_ref, q_ref, k_ref, v_ref):
    def vrow(i):
        return vec_ref[i : i + 1, :]

    def block(rc, _):
        at = pl.ds(pl.multiple_of(rc * 192, 192), 192)
        a1 = (xhat_ref[at, :] * vrow(0) + vrow(1)).astype(BF)
        q_ref[at, :] = (dot(a1, wqkv_ref[:, 0:256]) + vrow(2)).astype(BF)
        at = pl.ds(pl.multiple_of(rc * 512, 512), 512)
        a1k = (xk_ref[at, :] * vrow(0) + vrow(1)).astype(BF)
        k_ref[at, :] = dot(a1k, wqkv_ref[:, 256:512]).astype(BF)
        v_ref[at, :] = (dot(a1k, wqkv_ref[:, 512:768]) + vrow(3)).astype(BF)
        return 0

    lax.fori_loop(0, 4, block, 0, unroll=4)


def attend_kernel(limits_ref, bias_ref, q_ref, k_ref, v_ref, mixed_ref, p_ref, other_ref):
    scale = 32 ** (-0.5)
    lane_head = lax.broadcasted_iota(jnp.int32, (QN, 128), 1) >> 5
    row0 = lax.axis_index("band") * 16
    height = limits_ref[0:1, 0:1]
    wide = limits_ref[1:2, 0:1]
    ks = lax.broadcasted_iota(jnp.int32, (KN, 384), 0)
    ql = lax.broadcasted_iota(jnp.int32, (KN, 384), 1)
    other_ref[...] = jnp.where(ks == ql - 48 * ((ql * 171) >> 13), 0.0, 1.0)
    krow, kcol = split12((lax.broadcasted_iota(jnp.int32, (KN, 128), 0) + 36) & (KN - 1))

    def attend(k, _):
        rc = k >> 2
        cc = k & 3
        at_q = pl.ds(pl.multiple_of(k * QN, QN), QN)
        at_k = pl.ds(pl.multiple_of(k * KN, KN), KN)
        qbd = spread_heads(q_ref[at_q, :], lane_head)
        r = krow * 4 + (rc - 12)
        c = kcol * 4 + cc
        off = jnp.where((r >= -row0) & (r < height) & (c < wide), 0.0, MASKED)
        off = bias_ref[...] + jnp.concatenate([off] * 3, axis=1) * other_ref[...]
        s = dot_nt(k_ref[at_k, :], qbd) * (scale * LOG2E) + off
        top = jnp.max(s, axis=0, keepdims=True)
        e = jnp.exp2(s - top)
        p = e * (1.0 / jnp.sum(e, axis=0, keepdims=True))
        p_ref[at_k, :] = p
        full = dot_tn(p.astype(BF), v_ref[at_k, :])
        mixed_ref[at_q, :] = pick_heads(full, lane_head).astype(BF)
        return 0

    lax.fori_loop(0, CLS, attend, 0, unroll=CLS)


def feed_kernel(
    dy_ref,
    dysum_ref,
    mixed_ref,
    xp_ref,
    wo_ref,
    wu_ref,
    wd_ref,
    vec_ref,
    act_ref,
    dz_ref,
    a2_ref,
    da_ref,
    dx1_ref,
    x1_ref,
    dmix_ref,
    sums_ref,
    zsum_ref,
    xhat_ref,
    rstd_ref,
):
    def vrow(i):
        return vec_ref[i : i + 1, :]

    sums_ref[...] = jnp.zeros_like(sums_ref)
    sums_ref[7:8, :] = dysum_ref[...]
    zsum_ref[...] = jnp.zeros_like(zsum_ref)

    def inner(rc, _):
        at = pl.ds(pl.multiple_of(rc * 192, 192), 192)
        x1 = xp_ref[at, :] + (dot(mixed_ref[at, :], wo_ref[...]) + vrow(4))
        x1_ref[at, :] = x1
        xhat, rstd = normed(x1)
        xhat_ref[at, :] = xhat
        rstd_ref[at, :] = jnp.broadcast_to(rstd, (192, 128))
        a2_ref[at, :] = (xhat * vrow(5) + vrow(6)).astype(BF)
        return 0

    lax.fori_loop(0, 4, inner, 0, unroll=4)

    def hidden(rc, _):
        at = pl.ds(pl.multiple_of(rc * 192, 192), 192)
        for part in range(3):
            cols = slice(256 * part, 256 * part + 256)
            z = dot(a2_ref[at, :], wu_ref[:, cols]) + vrow(8 + part)
            cube = (GELU0 * GELU1) * (z * z)
            up = 0.5 + 0.5 * jnp.tanh(z * (GELU0 + cube))
            act = z * up
            act_ref[at, cols] = act.astype(BF)
            slope = up * (1.0 + (z - act) * (2.0 * GELU0 + 6.0 * cube))
            dz = dot_nt(dy_ref[at, :], wd_ref[cols, :]) * slope
            zsum_ref[:, cols] += jnp.sum(dz, axis=0, keepdims=True)
            dz_ref[at, cols] = dz.astype(BF)
        return 0

    lax.fori_loop(0, 4, hidden, 0, unroll=4)

    def outer(rc, _):
        at = pl.ds(pl.multiple_of(rc * 192, 192), 192)
        dn = dot_nt(dz_ref[at, :], wu_ref[...])
        xhat = xhat_ref[at, :]
        dx1 = dy_ref[at, :].astype(F32) + norm_back(dn * vrow(5), xhat, rstd_ref[at, 0:1])
        dx1_ref[at, :] = dx1
        da_ref[at, :] = dx1.astype(BF)
        sums_ref[4:5, :] += jnp.sum(dx1, axis=0, keepdims=True)
        sums_ref[5:6, :] += jnp.sum(dn * xhat, axis=0, keepdims=True)
        sums_ref[6:7, :] += jnp.sum(dn, axis=0, keepdims=True)
        return 0

    lax.fori_loop(0, 4, outer, 0, unroll=4)
    dmix_ref[...] = dot_nt(da_ref[...], wo_ref[...]).astype(BF)


def back_kernel(
    q_ref,
    v_ref,
    p_ref,
    dmix_ref,
    own_ref,
    rimc_ref,
    rimz_ref,
    dsl_ref,
    tacc_ref,
    dkv_ref,
    kvsum_ref,
):
    odd = (lax.axis_index("band") & 1) == 1
    scale = 32 ** (-0.5)
    lane_head = lax.broadcasted_iota(jnp.int32, (QN, 128), 1) >> 5
    tacc_ref[...] = jnp.zeros_like(tacc_ref)
    kvsum_ref[...] = jnp.zeros_like(kvsum_ref)

    def scores_back(k, _):
        at_q = pl.ds(pl.multiple_of(k * QN, QN), QN)
        at_k = pl.ds(pl.multiple_of(k * KN, KN), KN)
        dp = dot_nt(v_ref[at_k, :], spread_heads(dmix_ref[at_q, :], lane_head))
        p = p_ref[at_k, :]
        pdp = p * dp
        ds = pdp - p * jnp.sum(pdp, axis=0, keepdims=True)
        tacc_ref[...] += ds
        dsl_ref[at_k, :] = ds.astype(BF)
        return 0

    lax.fori_loop(0, CLS, scores_back, 0, unroll=CLS)

    def back_class(k):
        at_q = pl.ds(pl.multiple_of(k * QN, QN), QN)
        at_k = pl.ds(pl.multiple_of(k * KN, KN), KN)
        dv = dot(p_ref[at_k, :].astype(BF), spread_heads(dmix_ref[at_q, :], lane_head))
        dk = dot(dsl_ref[at_k, :], spread_heads(q_ref[at_q, :], lane_head)) * scale
        dkv_ref[at_k, 0:256] = dk.astype(BF)
        dkv_ref[at_k, 256:512] = dv.astype(BF)
        kvsum_ref[:, 0:256] += jnp.sum(dk, axis=0, keepdims=True)
        kvsum_ref[:, 256:512] += jnp.sum(dv, axis=0, keepdims=True)
        own_ref[at_q, 0:256] = dk[0:QN]
        own_ref[at_q, 256:512] = dv[0:QN]
        after = jnp.concatenate([dk[QN : QN + RIM], dv[QN : QN + RIM]], axis=1)
        before = jnp.concatenate([dk[KN - RIM :], dv[KN - RIM :]], axis=1)
        return after, before

    def attend_back(pair, _):
        after0, before0 = back_class(pair * 2)
        after1, before1 = back_class(pair * 2 + 1)
        at = pl.ds(pl.multiple_of(pair * 2 * RIM, 2 * RIM), 2 * RIM)
        after = jnp.concatenate([after0, after1], axis=0)
        before = jnp.concatenate([before0, before1], axis=0)
        rimc_ref[at, :] = jnp.where(odd, before, after).astype(BF)
        rimz_ref[at, :] = jnp.where(odd, after, before).astype(BF)
        return 0

    lax.fori_loop(0, CLS // 2, attend_back, 0, unroll=8)


def early_grads(act_ref, dy_ref, a2_ref, dz_ref, mixed_ref, da_ref, fd, fu, fo):
    fd[...] = dot_tn(act_ref[...], dy_ref[...])
    fu[...] = dot_tn(a2_ref[...], dz_ref[...])
    fo[...] = dot_tn(mixed_ref[...], da_ref[...])


def output_kernel(x1_ref, act_ref, wd_ref, vec_ref, po_ref, out_ref):
    def result(rc, _):
        at = pl.ds(pl.multiple_of(rc * 192, 192), 192)
        res = x1_ref[at, :] + dot(act_ref[at, :], wd_ref[...]) + vec_ref[7:8, :]
        back = dot_tn(po_ref[...], res.astype(BF)).astype(BF)
        for i in range(4):
            out_ref[4 * i + rc] = back[48 * i : 48 * i + 48]
        return 0

    lax.fori_loop(0, 4, result, 0, unroll=4)


def late_grads(
    dsl_ref,
    k_ref,
    tacc_ref,
    xhat_ref,
    xk_ref,
    dkv_ref,
    kvsum_ref,
    wqkv_ref,
    vt_ref,
    sums_ref,
    zsum_ref,
    dq_ref,
    fq_ref,
    fv_ref,
    tgrad_ref,
):
    scale = 32 ** (-0.5)
    lane_head = lax.broadcasted_iota(jnp.int32, (QN, 128), 1) >> 5

    def query(k, _):
        at_q = pl.ds(pl.multiple_of(k * QN, QN), QN)
        at_k = pl.ds(pl.multiple_of(k * KN, KN), KN)
        dq = pick_heads(dot_tn(dsl_ref[at_k, :], k_ref[at_k, :]), lane_head) * scale
        dq_ref[at_q, :] = dq.astype(BF)
        return 0

    lax.fori_loop(0, CLS, query, 0, unroll=16)
    dq = dq_ref[...]
    gain, shift = vt_ref[:, 0:1], vt_ref[:, 1:2]
    qsum = jnp.sum(dq.astype(F32), axis=0, keepdims=True)
    m = dot_tn(xhat_ref[...].astype(BF), dq)
    weight = wqkv_ref[:, 0:256].astype(F32)
    fq_ref[:, 0:256] = gain * m + shift * qsum
    gain_grad = jnp.sum(weight * m, axis=1, keepdims=True)
    shift_grad = jnp.sum(weight * qsum, axis=1, keepdims=True)
    xk = xk_ref[...].astype(BF)
    for cols in (slice(256, 512), slice(512, 768)):
        dkv = dkv_ref[:, cols.start - 256 : cols.stop - 256]
        kvsum = kvsum_ref[:, cols.start - 256 : cols.stop - 256]
        m = dot_tn(xk, dkv)
        weight = wqkv_ref[:, cols].astype(F32)
        fq_ref[:, cols] = gain * m + shift * kvsum
        gain_grad = gain_grad + jnp.sum(weight * m, axis=1, keepdims=True)
        shift_grad = shift_grad + jnp.sum(weight * kvsum, axis=1, keepdims=True)
    lines = jnp.concatenate(
        [jnp.zeros((2, 256), F32), qsum, kvsum, sums_ref[4:8, :]]
        + [zsum_ref[:, 256 * i : 256 * i + 256] for i in range(3)]
        + [jnp.zeros((117, 256), F32)],
        axis=0,
    )
    lane = lax.broadcasted_iota(jnp.int32, (256, 128), 1)
    fv_ref[...] = jnp.where(lane == 0, gain_grad, jnp.where(lane == 1, shift_grad, lines.T))

    flat = tacc_ref[...].T
    qi = lax.broadcasted_iota(jnp.int32, (QN, KN), 0)
    lines = []
    for h in range(HEADS):
        part = flat[h * QN : (h + 1) * QN]
        for bit in range(6):
            turned = pltpu.roll(part, KN - (1 << bit), 1)
            part = jnp.where((qi >> bit) & 1 == 1, turned, part)
        lines.append(jnp.sum(part, axis=0, keepdims=True))
    tgrad_ref[...] = jnp.concatenate(lines, axis=0)


def input_kernel(
    own_ref, gotc_ref, gotz_ref, dq_ref, dx1_ref, xhat_ref, rstd_ref, wqkv_ref, vec_ref, po_ref, tok_ref
):
    odd = (lax.axis_index("band") & 1) == 1

    def block(rc, _):
        at = pl.ds(pl.multiple_of(rc * 192, 192), 192)
        mine = own_ref[at, :]
        got_c = gotc_ref[pl.ds(pl.multiple_of(rc * 160, 160), 160), :].astype(F32)
        got_z = gotz_ref[pl.ds(pl.multiple_of(rc * 160, 160), 160), :].astype(F32)
        got_a = jnp.where(odd, got_c, got_z)
        got_b = jnp.where(odd, got_z, got_c)
        gap = jnp.zeros((QN - RIM, 512), F32)
        parts = []
        for i in range(4):
            a = jnp.concatenate([got_a[i * RIM : (i + 1) * RIM], gap], axis=0)
            b = jnp.concatenate([gap, got_b[i * RIM : (i + 1) * RIM]], axis=0)
            parts.append(mine[i * QN : (i + 1) * QN] + a + b)
        dkv = jnp.concatenate(parts, axis=0).astype(BF)
        dn = dot_nt(dq_ref[at, :], wqkv_ref[:, 0:256]) + dot_nt(dkv, wqkv_ref[:, 256:768])
        dx = dx1_ref[at, :] + norm_back(dn * vec_ref[0:1, :], xhat_ref[at, :], rstd_ref[at, 0:1])
        back = dot_tn(po_ref[...], dx.astype(BF)).astype(BF)
        for i in range(4):
            tok_ref[4 * i + rc] = back[48 * i : 48 * i + 48]
        return 0

    lax.fori_loop(0, 4, block, 0, unroll=4)


EARLY = 896
LATE = 512


def widen(v):
    return jnp.concatenate([v, jnp.zeros((v.shape[0], 128 - v.shape[1]), F32)], axis=1)


def pack(wqkv, wo, wu, wd, vec):
    pieces = [(wqkv, 0, 0), (wo, 0, 768), (wd, 0, 1024), (vec, 0, 1280)]
    pieces += [(wu, 8, 0), (wd, 0, 768), (wd, -8, 1024)]
    total = 0.0
    for p, row, lane in pieces:
        rows, lanes = p.shape
        zero = jnp.zeros((), F32)
        if rows == 24 and lane == 1024 and row == 0:
            p = lax.pad(p, zero, ((0, -16, 0), (0, 0, 0)))
            rows = 8
        elif rows == 24:
            p = lax.pad(p, zero, ((-8 + row, -8 - row, 0), (0, 0, 0)))
            row, rows = 8, 8
        total = total + lax.pad(p, zero, ((row, 16 - row - rows, 0), (lane, EARLY + LATE - lane - lanes, 0)))
    return total.astype(BF)


def own_index():
    return lax.axis_index("maps") * 8 + lax.axis_index("band")


def unpack(blocks, big_qkv, big_out, big_up, big_down, vec, vt):
    me = own_index()
    odd = (me & 1) == 1
    for across in range(4):
        for z in range(4):
            mine, other = blocks[across][z].astype(F32), blocks[across + 4][z].astype(F32)
            pair = (jnp.where(odd, other, mine), jnp.where(odd, mine, other))
            o = (me ^ ((z << 1) | (across << 3))) >> 1
            at = pl.ds(pl.multiple_of(o * 16, 16), 16)
            both = lambda rows, lanes: [slab[rows, lanes] for slab in pair]
            top, low = slice(0, 8), slice(8, 16)
            big_qkv[at, :] = jnp.concatenate(both(top, slice(0, 768)), axis=0).astype(BF)
            big_out[at, :] = jnp.concatenate(both(top, slice(768, 1024)), axis=0).astype(BF)
            big_up[at, :] = jnp.concatenate(both(low, slice(0, 768)), axis=0).astype(BF)
            vt[at, :] = jnp.concatenate(both(top, slice(1280, 1408)), axis=0)
            tall = [[s[0:8, 1024:1280], s[8:16, 768:1024], s[8:16, 1024:1280]] for s in pair]
            big_down[pl.ds(pl.multiple_of(o * 48, 16), 48), :] = jnp.concatenate(tall[0] + tall[1], axis=0).astype(BF)
    vec[...] = vt[...].T[0 : vec.shape[0]]


def main_kernel(*refs):
    blocks, (xhat, x, xz, xc, pk, xp, bias, limits, dy, dysum) = refs[:8], refs[8:18]
    act, dx1, x1, own, rimc, rimz, dq, out_ref, big_qkv, big_down, vec = refs[18:29]
    q, k, v, mixed, p, dz, a2, da, dmix, sums, zsum, dsl, tacc, dkv, kvsum = refs[29:44]
    fq, fv, tgrad, fd, fu, fo, big_out, big_up, vt, xk, other, xhat1, rstd1 = refs[44:]
    halo_kernel(x, xc, xz, pk, xk)
    unpack(blocks, big_qkv, big_out, big_up, big_down, vec, vt)
    project_kernel(xhat, xk, big_qkv, vec, q, k, v)
    attend_kernel(limits, bias, q, k, v, mixed, p, other)
    feed_kernel(dy, dysum, mixed, xp, big_out, big_up, big_down, vec, act, dz, a2, da, dx1, x1, dmix, sums, zsum, xhat1, rstd1)
    back_kernel(q, v, p, dmix, own, rimc, rimz, dsl, tacc, dkv, kvsum)
    late_grads(dsl, k, tacc, xhat, xk, dkv, kvsum, big_qkv, vt, sums, zsum, dq, fq, fv, tgrad)
    early_grads(act, dy, a2, dz, mixed, da, fd, fu, fo)
    table = tgrad[...]
    me = own_index()
    for o in range(32):
        at = slice(8 * o, 8 * o + 8)
        top = [fd[24 * o + 8 * b : 24 * o + 8 * b + 8, :] for b in range(3)] + [fo[at, 0:128], fq[at, 0:512]]
        low = [fu[at, :], fo[at, 128:256], fq[at, 512:768], fv[at, :], table]
        both = jnp.concatenate([jnp.concatenate(top, axis=1), jnp.concatenate(low, axis=1)], axis=0)
        out_ref[frame_slot(me, o)] = both.astype(BF)


def frame_slot(me, o):
    m = me ^ o
    return (m & 1) * 16 + (m >> 3) * 4 + ((m >> 1) & 3)


def shard_grads(refs, vrows):
    total = refs[0][...] + sum(ref[...].astype(F32) for ref in refs[1:4])
    early, late = total[:, :EARLY], total[:, EARLY:]
    return [
        jnp.concatenate([late[0:8], late[8:16, 0:256]], axis=1),
        jnp.concatenate([early[0:8, 768:896], early[8:16, 768:896]], axis=1),
        early[8:16, 0:768],
        jnp.concatenate([early[0:8, 256 * b : 256 * b + 256] for b in range(3)], axis=0),
        late[8:16, 256 : 256 + vrows],
        lax.dot_general(
            late[8:16, 384:512],
            table_slots(),
            (((1,), (1,)), ((), ())),
            precision=lax.Precision.HIGHEST,
            preferred_element_type=F32,
        ),
    ]


def update_kernel(*refs):
    w, first, second, outs = refs[4:10], refs[10:16], refs[16:22], refs[22:]
    vrows = w[4].shape[1]
    grads = shard_grads(refs, vrows)
    row = lax.broadcasted_iota(jnp.int32, (8, 128), 0)
    lane = lax.broadcasted_iota(jnp.int32, (8, 128), 1)
    norms = jnp.zeros((8, 128), F32)
    for i in range(6):
        update = adam_parts(w[i][...], grads[i], first[i][...], second[i][...])[2]
        outs[i][...] = update
        for line, v in ((0, w[i][...]), (1, update)):
            sums = jnp.sum(v * v, axis=0, keepdims=True)
            if i == 4:
                sums = pltpu.roll(widen(sums), 4, 1)
                norms = jnp.where((row == line) & (lane >= 4) & (lane < 4 + vrows), sums, norms)
            else:
                at = i if i < 4 else 4 + vrows
                norms = jnp.where((row == line) & (lane == at), jnp.sum(sums, axis=1, keepdims=True), norms)
    outs[6][...] = norms


def moments_kernel(*refs):
    first, second, outs = refs[4:10], refs[10:16], refs[16:]
    grads = shard_grads(refs, first[4].shape[1])
    for i in range(6):
        new_first, new_second, _ = adam_parts(0.0, grads[i], first[i][...], second[i][...])
        outs[2 * i][...] = new_first
        outs[2 * i + 1][...] = new_second


def step_kernel(mine_ref, a_ref, b_ref, c_ref, d_ref, *refs):
    w, update, outs = refs[0:6], refs[6:12], refs[12:]
    vrows = w[4].shape[1]
    total = a_ref[...] + b_ref[...] + c_ref[...] + d_ref[...]
    lane = lax.broadcasted_iota(jnp.int32, (8, 128), 1)
    norms = jnp.sqrt(jnp.where(lane == 4 + vrows, mine_ref[...], total))
    outs[6][...] = norms[0:1, 0:16]
    outs[7][...] = norms[1:2, 0:16]
    rate = LEARN_RATE * norms[0:1] / (norms[1:2] + RATIO_EPS)
    for i in range(6):
        if i == 4:
            r = pltpu.roll(rate, 124, 1)[:, 0:vrows]
        else:
            at = i if i < 4 else 4 + vrows
            r = rate[:, at : at + 1]
        outs[i][...] = w[i][...] - r * update[i][...]


def stack_kernel(*refs):
    for i, ref in enumerate(refs[:4]):
        refs[4][i] = ref[...]


def call(kernel, out_shape, scratch, *args, smem=0, flops=10**8, vmem=16):
    vm = pl.BlockSpec(memory_space=pltpu.VMEM)
    specs = [pl.BlockSpec(memory_space=pltpu.SMEM)] * smem + [vm] * (len(args) - smem)
    return pl.pallas_call(
        kernel,
        out_shape=out_shape,
        in_specs=specs,
        out_specs=jax.tree.map(lambda _: vm, out_shape),
        scratch_shapes=scratch,
        compiler_params=pltpu.CompilerParams(vmem_limit_bytes=vmem * 2**20),
        cost_estimate=pl.CostEstimate(flops=flops, bytes_accessed=10**6, transcendentals=0),
    )(*args)


def sds(shape, dtype=BF):
    return jax.ShapeDtypeStruct(shape, dtype)


def exchange_groups(maps, band):
    zbits = band.bit_length() - 2
    mbits = maps.bit_length() - 1
    cut = lambda lo, n: [(lo + i, min(2, n - i)) for i in range(0, n, 2)]
    return cut(1, zbits) + cut(1 + zbits, mbits) + [(0, 1)]


def swap(block, mask, count):
    return lax.ppermute(block, AXES, [(k, k ^ mask) for k in range(count)])


def frame_masks(groups):
    masks = [0]
    for lo, bits in groups:
        masks = [m ^ (d << lo) for d in range(1 << bits) for m in masks]
    return masks


def gather_all(slab, groups, count):
    block = slab[None]
    for lo, bits in groups:
        block = jnp.concatenate(
            [block] + [swap(block, d << lo, count) for d in range(1, 1 << bits)], axis=0
        )
    return block


def scatter_sum(grads, groups, count):
    for lo, bits in reversed(groups):
        grads = add_stage(grads, lo, bits, count)
    return grads[0]


def adam_parts(weight, grad, first, second):
    new_first = BETA_FIRST * first + (1.0 - BETA_FIRST) * grad
    new_second = BETA_SECOND * second + (1.0 - BETA_SECOND) * grad * grad
    update = (
        new_first
        / (1.0 - BETA_FIRST**STEP)
        / (jnp.sqrt(new_second / (1.0 - BETA_SECOND**STEP)) + ADAM_EPS)
        + DECAY_RATE * weight
    )
    return (new_first, new_second, update)


def squares_of(matrices, rowwise):
    return jnp.concatenate(
        [
            jnp.stack([jnp.sum(matrix * matrix) for matrix in matrices]),
            jnp.sum(rowwise * rowwise, axis=1),
        ]
    )


def bias_outputs():
    return (sds((KN, 384), F32), sds((8, 128), jnp.int32), sds((4 * QN, 4 * 48)), sds((4 * KN, 10 * 48)))


def prep_outputs():
    return (
        sds((768, 256), F32),
        sds((768, 256), F32),
        sds((768, 128), F32),
        sds((768, 256)),
        sds((1, 256), F32),
        sds((12, 48, 256)),
        sds((12, 48, 256)),
    )


def project_outputs():
    return (sds((768, 256)), sds((CLS * KN, 256)), sds((CLS * KN, 256)))


def attend_outputs():
    return (sds((768, 256)), sds((CLS * KN, 384), F32))


def feed_outputs():
    return (
        sds((768, 768)),
        sds((768, 768)),
        sds((768, 256)),
        sds((768, 256)),
        sds((768, 256), F32),
        sds((768, 256), F32),
        sds((768, 256)),
        sds((8, 256), F32),
        sds((1, 768), F32),
    )


def back_outputs():
    return (
        sds((768, 512), F32),
        sds((CLS * RIM, 512)),
        sds((CLS * RIM, 512)),
        sds((CLS * KN, 384)),
        sds((KN, 384), F32),
        sds((CLS * KN, 512)),
        sds((1, 512), F32),
    )


def late_outputs():
    return (
        sds((768, 256)),
        sds((256, 768), F32),
        sds((256, 128), F32),
        sds((HEADS, KN), F32),
    )


def beside(block, band):
    touching = [(b, b + 1 if b % 2 else b - 1) for b in range(band)]
    return (
        lax.ppermute(block[0], "band", [(b, b ^ 1) for b in range(band)]),
        lax.ppermute(block[1], "band", [(b, to) for b, to in touching if 0 <= to < band]),
    )


def packed_step(tokens_in, cotangent, map_sizes, weights, firsts, seconds):
    count = 32
    vrows = weights[4].shape[0]
    turn = lambda arrays: tuple(a.T if i == 4 else a for i, a in enumerate(arrays))
    weights, firsts, seconds = turn(weights), turn(firsts), turn(seconds)
    slab = pack(*weights[:5])
    slab, sizes = lax.optimization_barrier((slab, map_sizes))
    slabs = [slab] + [swap(slab, d << 1, count) for d in (1, 2, 3)]
    bias, limits, po, pk = call(bias_kernel, bias_outputs(), [], sizes, weights[5], smem=1, flops=10**9, vmem=4)
    *slabs, bias = lax.optimization_barrier((*slabs, bias))
    column = call(stack_kernel, sds((4, 16, EARLY + LATE)), [], *slabs, vmem=4)
    column, x = lax.optimization_barrier((column, tokens_in))
    blocks = [column] + [swap(column, d << 3, count) for d in (1, 2, 3)]
    xp, xhat, rstd, dy, dysum, *edges = call(prep_kernel, prep_outputs(), [], x, cotangent, po, flops=2 * 10**9, vmem=8)
    x_core, x_next = beside(edges, 8)
    *far, xp = lax.optimization_barrier((*blocks[1:], xp))
    blocks = [blocks[0]] + far + [swap(block, 1, count) for block in [blocks[0]] + far]
    act_s, dz_s, a2_s, da_s, dx1_s, x1_s, dmix_s, sums_s, zsum_s = feed_outputs()
    own_s, rimc_s, rimz_s, dsl_s, tacc_s, dkv_s, kvsum_s = back_outputs()
    dq_s, fq_s, fv_s, tgrad_s = late_outputs()
    act, dx1, x1, own, rim_c, rim_z, dq, grads, big_qkv, big_down, vec = call(
        main_kernel,
        (act_s, dx1_s, x1_s, own_s, rimc_s, rimz_s, dq_s)
        + (sds((count, 16, EARLY + LATE)), sds((256, 768)), sds((768, 256)), sds((vrows, 256), F32)),
        [
            pltpu.VMEM(o.shape, o.dtype)
            for o in project_outputs()
            + attend_outputs()
            + (dz_s, a2_s, da_s, dmix_s, sums_s, zsum_s, dsl_s, tacc_s, dkv_s, kvsum_s, fq_s, fv_s, tgrad_s)
            + (sds((768, 256), F32), sds((256, 768), F32), sds((256, 256), F32))
            + (sds((256, 256)), sds((256, 768)), sds((256, 128), F32), sds((CLS * KN, 256), F32), sds((KN, 384), F32))
            + (sds((768, 256), F32), sds((768, 128), F32))
        ],
        *blocks, xhat, x, x_next, x_core, pk, xp, bias, limits, dy, dysum,
        flops=15 * 10**9, vmem=24,
    )
    layer_out = call(output_kernel, sds((16, 48, 256)), [], x1, act, big_down, vec, po, flops=10**9, vmem=8)
    got_c, got_z = beside((rim_c, rim_z), 8)
    grads = add_stage(add_stage(grads, 0, 1, count), 3, 2, count)
    grads, own = lax.optimization_barrier((grads, own))
    tokens_grad = call(
        input_kernel, sds((16, 48, 256)), [], own, got_c, got_z, dq, dx1, xhat, rstd, big_qkv, vec, po,
        flops=10**9, vmem=8,
    )
    low = grads.astype(BF)
    parts = [grads[0]] + [swap(low[d], d << 1, count) for d in (1, 2, 3)]
    parts[0], tokens_grad, layer_out = lax.optimization_barrier((parts[0], tokens_grad, layer_out))

    shapes = [sds(w.shape, F32) for w in weights]
    *updates, mine = call(
        update_kernel, tuple(shapes) + (sds((8, 128), F32),), [], *parts, *weights, *firsts, *seconds, vmem=4
    )
    moments = call(
        moments_kernel, tuple(shape for shape in shapes for _ in range(2)), [], *parts, *firsts, *seconds, vmem=4
    )
    squares = mine + swap(mine, 1, count)
    squares = squares + swap(squares, 2, count) + swap(squares, 4, count) + swap(squares, 6, count)
    last = [swap(squares, d << 3, count) for d in (1, 2, 3)]
    squares, *moments = lax.optimization_barrier((squares, *moments))
    news = call(
        step_kernel,
        tuple(shapes) + (sds((1, 16), F32),) * 2,
        [],
        mine, squares, *last, *weights, *updates, vmem=4,
    )
    results = [layer_out, tokens_grad]
    for i in range(6):
        three = (moments[2 * i], moments[2 * i + 1], news[i])
        results += [a.T for a in three] if i == 4 else three
    return tuple(results) + (news[6].reshape(16), news[7].reshape(16))


def add_stage(grads, lo, bits, count):
    low = grads.astype(BF).reshape((1 << bits, -1) + grads.shape[1:])
    total = grads.reshape(low.shape)[0].astype(F32)
    for d in range(1, 1 << bits):
        total = total + swap(low[d], d << lo, count).astype(F32)
    return total


def per_device(
    maps,
    band,
    tokens_in,
    cotangent,
    map_sizes,
    w_qkv,
    w_out,
    w_up,
    w_down,
    vectors,
    pos_table,
    first_qkv,
    second_qkv,
    first_out,
    second_out,
    first_up,
    second_up,
    first_down,
    second_down,
    first_vectors,
    second_vectors,
    first_table,
    second_table,
):
    if w_qkv.shape[0] == 8 and (maps, band) == (4, 8):
        return packed_step(
            tokens_in, cotangent, map_sizes,
            (w_qkv, w_out, w_up, w_down, vectors, pos_table),
            (first_qkv, first_out, first_up, first_down, first_vectors, first_table),
            (second_qkv, second_out, second_up, second_down, second_vectors, second_table),
        )
    count = maps * band
    rows = w_qkv.shape[0]
    vrows = vectors.shape[0]
    groups = exchange_groups(maps, band)
    masks = np.array(frame_masks(groups))
    inverse = np.argsort(masks)
    me = lax.axis_index(AXES)
    def pack(qkv, out, upw, dnw, vec):
        dn = dnw.reshape(3, rows, 256).transpose(1, 0, 2).reshape(rows, 768)
        vt = jnp.pad(vec.T, ((0, 0), (0, 128 - vrows)))
        return jnp.concatenate([qkv, out, upw, dn, vt], axis=1)

    slab = pack(*(w.astype(BF) for w in (w_qkv, w_out, w_up, w_down, vectors)))
    block = gather_all(slab, groups, count)
    order = jnp.asarray(inverse, jnp.int32)[jnp.arange(count, dtype=jnp.int32) ^ me]
    whole = jnp.take(block, order, axis=0).reshape(256, -1)
    big_qkv = whole[:, 0:768]
    big_out = whole[:, 768:1024]
    big_up = whole[:, 1024:1792]
    big_down = (
        whole[:, 1792:2560].reshape(count, rows, 3, 256).transpose(0, 2, 1, 3).reshape(768, 256)
    )
    vt = whole[:, 2560:].astype(F32)
    vec = vt[:, :vrows].T

    bias, limits, po, pk = call(bias_kernel, bias_outputs(), [], map_sizes, pos_table, smem=1, flops=10**9)
    xp, xhat, rstd, dy, dysum, *edges = call(prep_kernel, prep_outputs(), [], tokens_in, cotangent, po, flops=2 * 10**9)
    x_core, x_next = beside(edges, band)
    xk = call(halo_kernel, sds((CLS * KN, 256), F32), [], tokens_in, x_core, x_next, pk, flops=10**9)
    queries, keys, values = call(project_kernel, project_outputs(), [], xhat, xk, big_qkv, vec, flops=10**9)
    mixed, probs = call(attend_kernel, attend_outputs(), [pltpu.VMEM((KN, 384), F32)], limits, bias, queries, keys, values, flops=3 * 10**9)
    act, dz, a2, da, dx1, x1, dmix, sums, zsum = call(
        feed_kernel,
        feed_outputs(),
        [pltpu.VMEM((768, 256), F32), pltpu.VMEM((768, 128), F32)],
        dy, dysum, mixed, xp, big_out, big_up, big_down, vec,
        flops=4 * 10**9,
    )
    own, rim_c, rim_z, dsl, tacc, dkv, kvsum = call(
        back_kernel, back_outputs(), [], queries, values, probs, dmix, flops=4 * 10**9
    )
    got_c, got_z = beside((rim_c, rim_z), band)
    grad_down, grad_up, grad_out = call(
        early_grads,
        (sds((768, 256), F32), sds((256, 768), F32), sds((256, 256), F32)),
        [],
        act, dy, a2, dz, mixed, da,
        flops=10**9,
    )
    dq, grad_qkv, grad_vec, table_grad = call(
        late_grads,
        late_outputs(),
        [],
        dsl, keys, tacc, xhat, xk, dkv, kvsum, big_qkv, vt, sums, zsum,
        flops=3 * 10**9,
    )
    layer_out = call(output_kernel, sds((16, 48, 256)), [], x1, act, big_down, vec, po, flops=10**9)
    tokens_grad = call(
        input_kernel, sds((16, 48, 256)), [], own, got_c, got_z, dq, dx1, xhat, rstd, big_qkv, vec, po, flops=10**9
    )

    packed = jnp.concatenate(
        [
            grad_qkv.reshape(count, rows, 768),
            grad_out.reshape(count, rows, 256),
            grad_up.reshape(count, rows, 768),
            grad_down.reshape(count, 3, rows, 256).transpose(0, 2, 1, 3).reshape(count, rows, 768),
            grad_vec.reshape(count, rows, 128),
        ],
        axis=2,
    )
    packed = jnp.take(packed, jnp.asarray(masks, jnp.int32) ^ me, axis=0)
    red = scatter_sum(packed, groups, count)
    red_qkv = red[:, 0:768]
    red_out = red[:, 768:1024]
    red_up = red[:, 1024:1792]
    red_down = red[:, 1792:2560].reshape(rows, 3, 256).transpose(1, 0, 2).reshape(3 * rows, 256)
    red_vec = red[:, 2560 : 2560 + vrows].T

    steps = np.arange(-3, 4)
    lanes = ((12 * steps[:, None] + steps[None, :]) % KN).reshape(-1)
    table_total = lax.psum(table_grad, AXES)[:, lanes]

    part_qkv = adam_parts(w_qkv, red_qkv, first_qkv, second_qkv)
    part_out = adam_parts(w_out, red_out, first_out, second_out)
    part_up = adam_parts(w_up, red_up, first_up, second_up)
    part_down = adam_parts(w_down, red_down, first_down, second_down)
    part_vec = adam_parts(vectors, red_vec, first_vectors, second_vectors)
    part_table = adam_parts(pos_table, table_total, first_table, second_table)
    local_weight_sq = squares_of((w_qkv, w_out, w_up, w_down), vectors)
    local_update_sq = squares_of((part_qkv[2], part_out[2], part_up[2], part_down[2]), part_vec[2])
    weight_sq, update_sq = lax.psum((local_weight_sq, local_update_sq), AXES)
    table_weight = jnp.sqrt(jnp.sum(pos_table * pos_table))
    table_update = jnp.sqrt(jnp.sum(part_table[2] * part_table[2]))
    weight_norms = jnp.concatenate([jnp.sqrt(weight_sq), table_weight[None]])
    update_norms = jnp.concatenate([jnp.sqrt(update_sq), table_update[None]])
    ratios = weight_norms / (update_norms + RATIO_EPS)
    next_qkv = w_qkv - LEARN_RATE * ratios[0] * part_qkv[2]
    next_out = w_out - LEARN_RATE * ratios[1] * part_out[2]
    next_up = w_up - LEARN_RATE * ratios[2] * part_up[2]
    next_down = w_down - LEARN_RATE * ratios[3] * part_down[2]
    next_vectors = vectors - LEARN_RATE * ratios[4 : 4 + vrows][:, None] * part_vec[2]
    next_table = pos_table - LEARN_RATE * ratios[4 + vrows] * part_table[2]
    return (
        layer_out,
        tokens_grad,
        part_qkv[0],
        part_qkv[1],
        next_qkv,
        part_out[0],
        part_out[1],
        next_out,
        part_up[0],
        part_up[1],
        next_up,
        part_down[0],
        part_down[1],
        next_down,
        part_vec[0],
        part_vec[1],
        next_vectors,
        part_table[0],
        part_table[1],
        next_table,
        weight_norms,
        update_norms,
    )


def solution(mesh):
    both = P(AXES, None)
    side = P(None, AXES)
    tall = P(AXES, None, None)
    copied = P()
    return jax.shard_map(
        functools.partial(per_device, mesh.shape["maps"], mesh.shape["band"]),
        mesh=mesh,
        in_specs=(tall, tall, P("maps", None))
        + (both,) * 4
        + (side, copied)
        + (both,) * 8
        + (side, side, copied, copied),
        out_specs=(tall, tall) + (both,) * 12 + (side,) * 3 + (copied,) * 5,
        check_vma=False,
    )
```
